32 devices in a mesh: dp: 4 (over y, core), fsdp: 8 (over z, x).
Axes of the slice: x: 2, y: 2, z: 4, core: 2. Of those that a mesh axis runs over, the one named last changes fastest.
Arguments:
- tokens: bfloat16 [32, 256, 2048], P(('dp', 'fsdp')), may hold values from -6 to 6
- labels: int32 [32], P(('dp', 'fsdp')), may hold values from 0 to 2
- counts: int32 [3], replicated, may hold values from 1365 to 4095
- grad_out: bfloat16 [32, 256, 2048], P(('dp', 'fsdp')), may hold values from -6 to 6
- w_query: bfloat16 [2048, 2048], P(('dp', 'fsdp')), may hold values from -0.125 to 0.125
- w_key: bfloat16 [2048, 2048], P(('dp', 'fsdp')), may hold values from -0.125 to 0.125
- w_value: bfloat16 [2048, 2048], P(('dp', 'fsdp')), may hold values from -0.125 to 0.125
- w_out: bfloat16 [2048, 2048], P(('dp', 'fsdp')), may hold values from -0.375 to 0.375
- gain_attn: bfloat16 [2048], P(('dp', 'fsdp')), may hold values from 0.099609375 to 1.8984375
- gain_mlp: bfloat16 [2048], P(('dp', 'fsdp')), may hold values from 0.099609375 to 1.8984375
- w_gate: bfloat16 [2048, 8192], P(('dp', 'fsdp')), may hold values from -0.125 to 0.125
- w_up: bfloat16 [2048, 8192], P(('dp', 'fsdp')), may hold values from -0.125 to 0.125
- w_down: bfloat16 [8192, 2048], P(('dp', 'fsdp')), may hold values from -0.0625 to 0.0625
Outputs:
- layer_out: bfloat16 [32, 256, 2048], P(('dp', 'fsdp'))
- grad_tokens: float32 [32, 256, 2048], P(('dp', 'fsdp'))
- grad_query: float32 [2048, 2048], P(('dp', 'fsdp'))
- grad_key: float32 [2048, 2048], P(('dp', 'fsdp'))
- grad_value: float32 [2048, 2048], P(('dp', 'fsdp'))
- grad_out_proj: float32 [2048, 2048], P(('dp', 'fsdp'))
- grad_gain_attn: float32 [2048], P(('dp', 'fsdp'))
- grad_gain_mlp: float32 [2048], P(('dp', 'fsdp'))
- grad_gate: float32 [2048, 8192], P(('dp', 'fsdp'))
- grad_up: float32 [2048, 8192], P(('dp', 'fsdp'))
- grad_down: float32 [8192, 2048], P(('dp', 'fsdp'))
The draws below stay inside these ranges and needn't reach their ends.
All inputs are finite; a program needn't handle non-finite values.
Results may differ from the reference program's by a relative error of at most 0.014.
Values may be sent and summed in bfloat16 or wider, within the bound.
A program may use at most 704 MiB of HBM per device.

```python
import jax
import jax.numpy as jnp
from jax import lax

D = 2048
FF = 8192
HEAD_DIM = 64
SEQ = 256
BATCH = 32


def place_ends(entries, key, smallest, largest):
    place = [jax.random.randint(jax.random.fold_in(key, axis), (), 0, length) for axis, length in enumerate(entries.shape)]
    longest = entries.shape.index(max(entries.shape))
    next_to = place[:longest] + [(place[longest] + 1) % entries.shape[longest]] + place[longest + 1:]
    return entries.at[tuple(place)].set(smallest).at[tuple(next_to)].set(largest)


def raised(values, rng, source, target, blocks, factor):
    def block_of(axis_at):
        return (jnp.arange(values.shape[axis_at]) // (values.shape[axis_at] // blocks)).reshape((-1,) + (1,) * (values.ndim - 1 - axis_at))

    one_side = jax.random.permutation(rng, blocks)[block_of(target)]
    second = (block_of(target) + blocks // 2) % blocks
    return jnp.where((block_of(source) == one_side) | (block_of(source) == second), factor * values, values)


def block_levels(key, extent, cuts, least, top_value):
    def one(position, blocks):
        heights = jax.random.uniform(jax.random.fold_in(jax.random.fold_in(key, 6), position), (blocks,), jnp.float32, least / len(cuts), top_value / len(cuts))
        return jnp.repeat(jnp.exp(heights), extent[position] // blocks).reshape((-1,) + (1,) * (len(extent) - position - 1))

    level = one(*cuts[0])
    for cut in cuts[1:]:
        level = level * one(*cut)
    return level


def noise(stream_key, extent, width, reach, shards=(), dtype=jnp.bfloat16):
    entries = jax.random.normal(stream_key, extent, jnp.float32) * width
    if len(shards) > 0:
        entries = block_levels(stream_key, extent, shards, -0.22, 0.18) * entries
    return jnp.clip(entries, min=-reach, max=reach).astype(dtype)


def bell_draw_with(stream_key, dims, spread, reach, shards, heavy, dtype=jnp.bfloat16):
    array = spread * jax.random.normal(stream_key, dims, jnp.float32)
    if shards:
        array = array * block_levels(stream_key, dims, shards, -0.22, 0.18)
    return jnp.clip(raised(array, jax.random.fold_in(stream_key, 3), *heavy), -reach, reach).astype(dtype)


def setup_inputs(seed: int = 0) -> dict:
    key_list = jax.random.split(jax.random.key(seed), 14)
    tokens = bell_draw_with(key_list[0], (BATCH, SEQ, D), 1.0, 6.0, ((0, 32),), (0, 2, 32, 2.75))
    labels = place_ends(jax.random.randint(key_list[1], (BATCH,), 0, 3), jax.random.fold_in(key_list[1], 1), 0, 2).astype(jnp.int32)
    counts = jax.random.randint(key_list[2], (3,), SEQ * BATCH // 6, SEQ * BATCH // 2).astype(jnp.int32)
    grad_out = noise(key_list[3], (BATCH, SEQ, D), 1.0, 6.0, ((0, 32),))
    w_query = noise(key_list[4], (D, D), D ** -0.5, 0.125, ((0, 32),))
    w_key = noise(key_list[5], (D, D), D ** -0.5, 0.125, ((0, 32),))
    w_value = noise(key_list[6], (D, D), D ** -0.5, 0.125, ((0, 32),))
    w_out = noise(key_list[7], (D, D), (D // 8) ** -0.5, 0.375, ((0, 32),))
    gain_attn = jnp.clip(1.0 + 0.18 * jax.random.normal(key_list[8], (D,), jnp.float32), 0.099609375, 1.8984375).astype(jnp.bfloat16)
    gain_mlp = jnp.clip(1.0 + 0.18 * jax.random.normal(key_list[9], (D,), jnp.float32), 0.099609375, 1.8984375).astype(jnp.bfloat16)
    w_gate = noise(key_list[10], (D, FF), D ** -0.5, 0.125, ((0, 32),))
    w_up = noise(key_list[11], (D, FF), D ** -0.5, 0.125, ((0, 32),))
    w_down = noise(key_list[12], (FF, D), FF ** -0.5, 0.0625, ((0, 32),))
    return {"tokens": tokens, "labels": labels, "counts": counts, "grad_out": grad_out, "w_query": w_query, "w_key": w_key, "w_value": w_value, "w_out": w_out, "gain_attn": gain_attn, "gain_mlp": gain_mlp, "w_gate": w_gate, "w_up": w_up, "w_down": w_down}


epsilon = 1e-05
rope_base = 130000.0

@jax.custom_vjp
def low(v):
    return lax.optimization_barrier(v.astype(jnp.bfloat16)).astype(jnp.float32)

@jax.custom_vjp
def low_back(v):
    return v

def low_keep(v):
    return (low(v), None)

def low_pass(kept, grad):
    return (grad,)

def back_keep(v):
    return (v, None)

def back_low(kept, grad):
    return (low(grad),)
low.defvjp(low_keep, low_pass)
low_back.defvjp(back_keep, back_low)

def rope_tables(seq_len, head_dim):
    half_dim = head_dim // 2
    frequency = rope_base ** (-(jnp.arange(half_dim).astype(jnp.float32) * 2.0) / head_dim)
    angles = jnp.arange(seq_len).astype(jnp.float32)[:, None] * frequency[None, :]
    angles = jnp.concatenate([angles, angles], axis=1)
    return (jnp.cos(angles), jnp.sin(angles))

def rotate(tensor, cosine, sine):
    half_dim = tensor.shape[-1] // 2
    turned = jnp.concatenate([-tensor[..., half_dim:], tensor[..., :half_dim]], axis=-1)
    return tensor * cosine[:, None, :] + turned * sine[:, None, :]

def norm_scale(values, gain):
    return values * lax.rsqrt(lax.optimization_barrier(jnp.mean(values * values, axis=-1, keepdims=True)) + epsilon) * gain

def project(acts, weight):
    return jnp.einsum('gsd,df->gsf', acts, weight, precision=lax.Precision.HIGHEST)

def head_attend(block_items):
    queries, keys_rot, values = block_items
    seq_len = queries.shape[1]
    scores = jnp.einsum('gqd,gkd->gqk', queries, keys_rot, precision=lax.Precision.HIGHEST)
    scores = low_back(scores * queries.shape[2] ** (-0.5))
    causal = lax.broadcasted_iota(jnp.int32, (seq_len, seq_len), 1) <= lax.broadcasted_iota(jnp.int32, (seq_len, seq_len), 0)
    scores = jnp.where(causal, scores, -1e+30)
    soft = low(jax.nn.softmax(scores, axis=-1))
    return jnp.einsum('gqk,gkd->gqd', soft, values, precision=lax.Precision.HIGHEST)

def layer_forward(token_rows, w_query, w_key, w_value, w_out, gain_attn, gain_mlp, w_gate, w_up, w_down):
    group, seq_len, model_width = token_rows.shape
    head_count = model_width // HEAD_DIM
    four_shape = (group, seq_len, head_count, HEAD_DIM)
    act_one = low(norm_scale(token_rows, gain_attn))
    queries = low_back(project(act_one, w_query))
    keys_raw = low_back(project(act_one, w_key))
    values = low(low_back(project(act_one, w_value)))
    cosine, sine = rope_tables(seq_len, HEAD_DIM)
    q_rot = low(rotate(queries.reshape(four_shape), cosine, sine))
    k_rot = low(rotate(keys_raw.reshape(four_shape), cosine, sine))
    mixed = lax.map(jax.checkpoint(head_attend), (q_rot.transpose(2, 0, 1, 3), k_rot.transpose(2, 0, 1, 3), values.reshape(four_shape).transpose(2, 0, 1, 3)))
    attended = low(low_back(mixed.transpose(1, 2, 0, 3).reshape(group, seq_len, model_width)))
    resid = token_rows + low_back(project(attended, w_out))
    act_two = low(norm_scale(resid, gain_mlp))
    gate_pre = low_back(project(act_two, w_gate))
    up_proj = low_back(project(act_two, w_up))
    middle = low(jax.nn.silu(gate_pre) * up_proj)
    return resid + low_back(project(middle, w_down))

def reference(tokens, labels, counts, grad_out, w_query, w_key, w_value, w_out, gain_attn, gain_mlp, w_gate, w_up, w_down):
    weights = tuple((weight_arg.astype(jnp.float32) for weight_arg in (w_query, w_key, w_value, w_out, gain_attn, gain_mlp, w_gate, w_up, w_down)))
    picked = counts[labels].astype(jnp.float32)
    factor = SEQ * BATCH / (3.0 * picked)
    cotangent = grad_out.astype(jnp.float32) * factor[:, None, None]
    group = min(BATCH, max(1, 4096 // SEQ))
    token_groups = tokens.astype(jnp.float32).reshape(BATCH // group, group, SEQ, D)
    cotangent_groups = cotangent.reshape(BATCH // group, group, SEQ, D)

    def group_step(grad_sums, group_pair):
        token_rows, cot_rows = group_pair
        result, pullback = jax.vjp(layer_forward, token_rows, *weights)
        grads = pullback(cot_rows)
        summed = tuple((total + added for total, added in zip(grad_sums, grads[1:])))
        return (summed, (result.astype(jnp.bfloat16), grads[0]))
    zeros = tuple((jnp.zeros_like(weight_arg) for weight_arg in weights))
    grad_sums, (outputs, input_grads) = lax.scan(group_step, zeros, (token_groups, cotangent_groups))
    layer_out = outputs.reshape(BATCH, SEQ, D)
    grad_tokens = input_grads.reshape(BATCH, SEQ, D)
    return (layer_out, grad_tokens, grad_sums[0], grad_sums[1], grad_sums[2], grad_sums[3], grad_sums[4], grad_sums[5], grad_sums[6], grad_sums[7], grad_sums[8])
```

```python
import jax
import jax.numpy as jnp
from jax import lax
from jax.sharding import PartitionSpec as P

HEAD_DIM = 64
AXES = ("dp", "fsdp")
QUAD = 4

epsilon = 1e-05
rope_base = 130000.0
bf16 = jnp.bfloat16
f32 = jnp.float32


def rope_tables(seq_len, head_dim):
    half_dim = head_dim // 2
    frequency = rope_base ** (-(jnp.arange(half_dim).astype(f32) * 2.0) / head_dim)
    angles = jnp.arange(seq_len).astype(f32)[:, None] * frequency[None, :]
    angles = jnp.concatenate([angles, angles], axis=1)
    return (jnp.cos(angles), jnp.sin(angles))


def rotate(tensor, cosine, sine):
    half_dim = tensor.shape[-1] // 2
    turned = jnp.concatenate([-tensor[..., half_dim:], tensor[..., :half_dim]], axis=-1)
    return tensor * cosine[:, None, :] + turned * sine[:, None, :]


def unrotate(grads, cosine, sine):
    half_dim = grads.shape[-1] // 2
    turned = grads * sine[:, None, :]
    return grads * cosine[:, None, :] + jnp.concatenate(
        [turned[..., half_dim:], -turned[..., :half_dim]], axis=-1
    )


def mm(left, right):
    return jnp.dot(left, right, preferred_element_type=f32)


def outer_sum(left, right):
    return lax.dot_general(left, right, (((0,), (0,)), ((), ())), preferred_element_type=f32)


def times_transposed(left, weight):
    return lax.dot_general(left, weight, (((1,), (1,)), ((), ())), preferred_element_type=f32)


def causal_mask(seq_len):
    return lax.broadcasted_iota(jnp.int32, (seq_len, seq_len), 1) <= lax.broadcasted_iota(
        jnp.int32, (seq_len, seq_len), 0
    )


def attend(queries, keys_rot, values):
    scale_factor = queries.shape[-1] ** (-0.5)
    scores = (
        jnp.einsum("bqhd,bkhd->bhqk", queries, keys_rot, preferred_element_type=f32) * scale_factor
    )
    scores = jnp.where(causal_mask(scores.shape[-1]), scores, -1e30)
    row_max = jnp.max(scores, axis=-1, keepdims=True)
    exp_scores = jnp.exp(scores - row_max)
    row_total = jnp.sum(exp_scores, axis=-1, keepdims=True)
    soft = (exp_scores / row_total).astype(bf16)
    mixed = jnp.einsum("bhqk,bkhd->bqhd", soft, values, preferred_element_type=f32)
    return (mixed, (row_max + jnp.log(row_total))[..., 0])


def attend_back(queries, keys_rot, values, grad_mixed, log_total):
    scale_factor = queries.shape[-1] ** (-0.5)
    scores = (
        jnp.einsum("bqhd,bkhd->bhqk", queries, keys_rot, preferred_element_type=f32) * scale_factor
    )
    soft = jnp.where(causal_mask(scores.shape[-1]), jnp.exp(scores - log_total[..., None]), 0.0)
    grad_soft = jnp.einsum("bqhd,bkhd->bhqk", grad_mixed, values, preferred_element_type=f32)
    grad_scores = (soft * (grad_soft - jnp.sum(soft * grad_soft, axis=-1, keepdims=True))).astype(
        bf16
    )
    grad_queries = (
        jnp.einsum("bhqk,bkhd->bqhd", grad_scores, keys_rot, preferred_element_type=f32)
        * scale_factor
    )
    grad_keys = (
        jnp.einsum("bhqk,bqhd->bkhd", grad_scores, queries, preferred_element_type=f32)
        * scale_factor
    )
    grad_values = jnp.einsum(
        "bhqk,bqhd->bkhd", soft.astype(bf16), grad_mixed, preferred_element_type=f32
    )
    return (grad_queries, grad_keys, grad_values)


class Plan:
    def __init__(self, outer, inner, rows):
        self.count = outer * inner
        self.inner = inner
        self.span = max(1, HEAD_DIM // rows)
        self.bit_a = self.span
        self.bit_b = 2 * self.span
        self.bit_core = inner
        flat = lax.axis_index("dp") * inner + lax.axis_index("fsdp")
        self.flat = flat
        self.core = (flat // inner) % 2
        self.quad = (flat // self.span) % QUAD
        self.me = self.core * QUAD + self.quad
        dims = []
        bit = outer * inner // 2
        while bit > inner:
            dims.append(bit)
            bit //= 2
        self.upper = dims
        mid = []
        bit = inner // 2
        while bit >= QUAD * self.span:
            mid.append(bit)
            bit //= 2
        self.mid = mid
        low = []
        bit = self.span // 2
        while bit >= 1:
            low.append(bit)
            bit //= 2
        self.low = low
        self.data_bits = low + mid + dims
        self.deltas = [
            c * self.bit_core + q * self.span for c in range(2) for q in range(QUAD)
        ]

    def send(self, array, bit):
        return lax.ppermute(array, AXES, [(r, r ^ bit) for r in range(self.count)])

    def mine(self, bit):
        return (self.flat // bit) % 2

    def column_dims(self):
        return (
            (2,) * len(self.upper) + (2,) + (2,) * len(self.mid) + (QUAD,) + (2,) * len(self.low)
        )

    def row_dims(self):
        return (2,) * (len(self.upper) + len(self.mid) + len(self.low))

    def axes(self, with_columns):
        skip_core = 1 if with_columns else 0
        skip_quad = skip_core + (1 if with_columns else 0)
        found = {}
        place = 0
        for bit in self.upper:
            found[bit] = place
            place += 1
        place += skip_core
        for bit in self.mid:
            found[bit] = place
            place += 1
        place += skip_quad - skip_core
        for bit in self.low:
            found[bit] = place
            place += 1
        return found

    def cut_columns(self, weight):
        rows, width = weight.shape
        chunk = width // (self.count // self.span)
        ahead = 2 ** len(self.upper)
        middle = 2 ** len(self.mid)
        parts = weight.reshape(rows, ahead, 2, middle, QUAD, chunk)
        return parts.transpose(2, 4, 0, 1, 3, 5).reshape(2 * QUAD, rows, width // (2 * QUAD))

    def join_columns(self, parts):
        eight, rows, narrow = parts.shape
        width = eight * narrow
        chunk = width // (self.count // self.span)
        ahead = 2 ** len(self.upper)
        middle = 2 ** len(self.mid)
        parts = parts.reshape(2, QUAD, rows, ahead, middle, chunk)
        return parts.transpose(2, 3, 0, 4, 1, 5).reshape(rows, width)

    def swap(self, parts):
        got = jnp.zeros_like(parts)
        for index, delta in enumerate(self.deltas):
            other = self.me ^ index
            block = lax.dynamic_index_in_dim(parts, other, 0, keepdims=True)
            if index:
                block = self.send(block, delta)
            got = lax.dynamic_update_slice_in_dim(got, block, other, 0)
        return got

    def gather(self, block, with_columns):
        held = {0: block}
        for bit in self.data_bits:
            for key in list(held):
                held[key ^ bit] = self.send(held[key], bit)
        found = self.axes(with_columns)
        if with_columns:
            dims = self.column_dims()
            piece = [1] * len(dims)
            piece[len(self.upper)] = 2
            piece[len(self.upper) + 1 + len(self.mid)] = QUAD
        else:
            dims = self.row_dims()
            piece = [1] * len(dims)
        tail = block.shape[-2:]
        whole = jnp.zeros(tuple(dims) + tail, block.dtype)
        for key, array in held.items():
            start = [0] * (len(dims) + 2)
            for bit, place in found.items():
                start[place] = self.mine(bit) ^ (1 if key & bit else 0)
            whole = lax.dynamic_update_slice(whole, array.reshape(tuple(piece) + tail), start)
        return whole.reshape(-1, tail[1])

    def scatter(self, total, rows, with_columns):
        dims = self.column_dims() if with_columns else self.row_dims()
        found = self.axes(with_columns)
        total = total.reshape(dims + (rows, total.shape[-1]))
        for bit in reversed(self.data_bits):
            place = found[bit]
            here = self.mine(bit)
            away = lax.dynamic_slice_in_dim(total, 1 - here, 1, place).astype(bf16)
            kept = lax.dynamic_slice_in_dim(total, here, 1, place)
            total = kept + self.send(away, bit).astype(f32)
        if with_columns:
            return total.reshape(2 * QUAD, rows, total.shape[-1])
        return total.reshape(rows, total.shape[-1])

    def share_tokens(self, block):
        half = block.shape[0] // 2
        from_a = self.send(block, self.bit_a)
        from_b = self.send(block, self.bit_b)
        first = self.send(from_a[:half], self.bit_b)
        second = self.send(from_b[half:], self.bit_a)
        four = jnp.concatenate([block, from_a, from_b, first, second], axis=0)
        return jnp.concatenate([four, self.send(four, self.bit_core)], axis=0)

    def sum_tokens(self, left, product):
        count = left.shape[0] // 2
        far = product(left[count:]).astype(bf16)
        four = product(left[:count]) + self.send(far, self.bit_core).astype(f32)
        size = count // 4
        half = size // 2
        own, for_a, for_b, for_ab = (four[i * size : (i + 1) * size] for i in range(4))
        first = self.send(for_ab[:half].astype(bf16), self.bit_b)
        second = self.send(for_ab[half:].astype(bf16), self.bit_a)
        for_a = jnp.concatenate([for_a[:half] + first.astype(f32), for_a[half:]]).astype(bf16)
        for_b = jnp.concatenate([for_b[:half], for_b[half:] + second.astype(f32)]).astype(bf16)
        return (
            own
            + self.send(for_a, self.bit_a).astype(f32)
            + self.send(for_b, self.bit_b).astype(f32)
        )

    def gather_gains(self, gains):
        bits = []
        bit = self.count // 2
        while bit >= 1:
            bits.append(bit)
            bit //= 2
        for bit in reversed(bits):
            other = self.send(gains, bit)
            low = self.mine(bit) == 0
            gains = jnp.concatenate(
                [jnp.where(low, gains, other), jnp.where(low, other, gains)], axis=1
            )
        return gains

    def scatter_gains(self, totals):
        bit = self.count // 2
        while bit >= 1:
            half = totals.shape[1] // 2
            low = self.mine(bit) == 0
            kept = jnp.where(low, totals[:, :half], totals[:, half:])
            away = jnp.where(low, totals[:, half:], totals[:, :half])
            totals = kept + self.send(away, bit)
            bit //= 2
        return totals


def on_device(
    tokens,
    labels,
    counts,
    grad_out,
    w_query,
    w_key,
    w_value,
    w_out,
    gain_attn,
    gain_mlp,
    w_gate,
    w_up,
    w_down,
):
    batch_size, seq_len, width = tokens.shape
    outer_count = lax.axis_size("dp")
    inner_count = lax.axis_size("fsdp")
    rows = w_query.shape[0]
    hidden_rows = w_down.shape[0]
    plan = Plan(outer_count, inner_count, rows)
    x_rows = tokens.reshape(-1, width).astype(f32)

    gains = plan.gather_gains(jnp.stack([gain_attn, gain_mlp])).astype(f32)
    gain_one, gain_two = gains[0:1], gains[1:2]

    inv_one = lax.rsqrt(jnp.mean(x_rows * x_rows, axis=-1, keepdims=True) + epsilon)
    act_one_own = (x_rows * inv_one * gain_one).astype(bf16)
    act_one = plan.share_tokens(act_one_own)

    qkv_parts = plan.swap(
        jnp.concatenate([plan.cut_columns(w) for w in (w_query, w_key, w_value)], axis=2)
    )
    w_qkv = plan.gather(qkv_parts, True)
    w_o = plan.gather(w_out, False)
    gu_parts = plan.swap(jnp.concatenate([plan.cut_columns(w) for w in (w_gate, w_up)], axis=2))
    w_gu = plan.gather(gu_parts, True)
    w_d = plan.gather(w_down, False)

    token_total = float(seq_len * batch_size * outer_count * inner_count)
    picked_counts = jnp.sum(
        jnp.where(labels[:, None] == jnp.arange(3)[None, :], counts[None, :], 0), axis=1
    ).astype(f32)
    factor = token_total / (3.0 * picked_counts)
    cotangent = (grad_out.astype(f32) * factor[:, None, None]).reshape(-1, width)
    dy = plan.share_tokens(cotangent.astype(bf16))

    narrow = w_qkv.shape[1] // 3
    hidden = w_gu.shape[1] // 2
    head_count = narrow // HEAD_DIM
    four_shape = (-1, seq_len, head_count, HEAD_DIM)
    cosine, sine = rope_tables(seq_len, HEAD_DIM)

    qkv = mm(act_one, w_qkv)
    q_rot = rotate(qkv[:, :narrow].reshape(four_shape), cosine, sine).astype(bf16)
    k_rot = rotate(qkv[:, narrow : 2 * narrow].reshape(four_shape), cosine, sine).astype(bf16)
    values = qkv[:, 2 * narrow :].astype(bf16).reshape(four_shape)
    mixed, log_total = attend(q_rot, k_rot, values)
    attended = mixed.reshape(-1, narrow).astype(bf16)

    resid = x_rows + plan.sum_tokens(attended, lambda part: mm(part, w_o))
    inv_two = lax.rsqrt(jnp.mean(resid * resid, axis=-1, keepdims=True) + epsilon)
    act_two = plan.share_tokens((resid * inv_two * gain_two).astype(bf16))

    gu = mm(act_two, w_gu)
    gate_pre, up_proj = gu[:, :hidden], gu[:, hidden:]
    sigmoid_gate = jax.nn.sigmoid(gate_pre)
    middle = (gate_pre * sigmoid_gate * up_proj).astype(bf16)

    grad_middle = times_transposed(dy, w_d)
    grad_gate_pre = (
        grad_middle * up_proj * sigmoid_gate * (1.0 + gate_pre * (1.0 - sigmoid_gate))
    ).astype(bf16)
    grad_up_proj = (grad_middle * gate_pre * sigmoid_gate).astype(bf16)
    grad_gu_cols = jnp.concatenate([grad_gate_pre, grad_up_proj], axis=1)

    added = plan.sum_tokens(grad_gu_cols, lambda part: times_transposed(part, w_gu))
    down_grad = plan.scatter(outer_sum(middle, dy), hidden_rows, False)
    gu_grad = plan.swap(plan.scatter(outer_sum(act_two, grad_gu_cols), rows, True).astype(bf16))
    gate_grad = plan.join_columns(gu_grad[:, :, :hidden]).astype(f32)
    up_grad = plan.join_columns(gu_grad[:, :, hidden:]).astype(f32)

    layer_out = (
        (resid + plan.sum_tokens(middle, lambda part: mm(part, w_d)))
        .astype(bf16)
        .reshape(tokens.shape)
    )

    grad_gain_two = jnp.sum(added * resid * inv_two, axis=0, keepdims=True)
    scaled_two = gain_two * added
    grad_resid = (
        cotangent
        + inv_two * scaled_two
        - resid * inv_two**3 * jnp.mean(scaled_two * resid, axis=-1, keepdims=True)
    )
    grad_branch = plan.share_tokens(grad_resid.astype(bf16))
    grad_attended = times_transposed(grad_branch, w_o).astype(bf16).reshape(four_shape)
    out_grad = plan.scatter(outer_sum(attended, grad_branch), rows, False)
    grad_q_rot, grad_k_rot, grad_v = attend_back(q_rot, k_rot, values, grad_attended, log_total)
    grad_qkv_cols = jnp.concatenate(
        [
            unrotate(grad_q_rot, cosine, sine).reshape(-1, narrow).astype(bf16),
            unrotate(grad_k_rot, cosine, sine).reshape(-1, narrow).astype(bf16),
            grad_v.reshape(-1, narrow).astype(bf16),
        ],
        axis=1,
    )
    qkv_grad = plan.swap(plan.scatter(outer_sum(act_one, grad_qkv_cols), rows, True).astype(bf16))
    query_grad, key_grad, value_grad = (
        plan.join_columns(qkv_grad[:, :, i * narrow : (i + 1) * narrow]).astype(f32)
        for i in range(3)
    )
    grad_act_one = plan.sum_tokens(grad_qkv_cols, lambda part: times_transposed(part, w_qkv))
    grad_gain_one = jnp.sum(grad_act_one * x_rows * inv_one, axis=0, keepdims=True)
    scaled_one = gain_one * grad_act_one
    grad_rows = (
        grad_resid
        + inv_one * scaled_one
        - x_rows * inv_one**3 * jnp.mean(scaled_one * x_rows, axis=-1, keepdims=True)
    )
    gain_grads = plan.scatter_gains(jnp.concatenate([grad_gain_one, grad_gain_two], axis=0))
    return (
        layer_out,
        grad_rows.reshape(tokens.shape),
        query_grad,
        key_grad,
        value_grad,
        out_grad,
        gain_grads[0],
        gain_grads[1],
        gate_grad,
        up_grad,
        down_grad,
    )


def solution(mesh):
    rows = P(AXES, None)
    vector = P(AXES)
    three = P(AXES, None, None)
    in_specs = (three, vector, P(), three, rows, rows, rows, rows, vector, vector, rows, rows, rows)
    out_specs = (three, three, rows, rows, rows, rows, vector, vector, rows, rows, rows)
    return jax.shard_map(
        on_device, mesh=mesh, in_specs=in_specs, out_specs=out_specs, check_vma=False
    )
```

```python
import functools

import jax
import jax.numpy as jnp
from jax import lax
from jax.experimental import pallas as pl
from jax.experimental.pallas import tpu as pltpu
from jax.sharding import PartitionSpec as P

HEAD_DIM = 64
AXES = ("dp", "fsdp")
QUAD = 4

epsilon = 1e-05
rope_base = 130000.0
bf16 = jnp.bfloat16
f32 = jnp.float32
MESH = pl.DeviceIdType.MESH


def rope_tables(seq_len, head_dim):
    half_dim = head_dim // 2
    frequency = rope_base ** (-(jnp.arange(half_dim).astype(f32) * 2.0) / head_dim)
    angles = jnp.arange(seq_len).astype(f32)[:, None] * frequency[None, :]
    angles = jnp.concatenate([angles, angles], axis=1)
    return (jnp.cos(angles), jnp.sin(angles))


def rotate(tensor, cosine, sine):
    half_dim = tensor.shape[-1] // 2
    turned = jnp.concatenate([-tensor[..., half_dim:], tensor[..., :half_dim]], axis=-1)
    return tensor * cosine[:, None, :] + turned * sine[:, None, :]


def unrotate(grads, cosine, sine):
    half_dim = grads.shape[-1] // 2
    turned = grads * sine[:, None, :]
    return grads * cosine[:, None, :] + jnp.concatenate(
        [turned[..., half_dim:], -turned[..., :half_dim]], axis=-1
    )


def mm(left, right):
    return jnp.dot(left, right, preferred_element_type=f32)


def outer_sum(left, right):
    return lax.dot_general(left, right, (((0,), (0,)), ((), ())), preferred_element_type=f32)


def times_transposed(left, weight):
    return lax.dot_general(left, weight, (((1,), (1,)), ((), ())), preferred_element_type=f32)


def causal_mask(seq_len):
    return lax.broadcasted_iota(jnp.int32, (seq_len, seq_len), 1) <= lax.broadcasted_iota(
        jnp.int32, (seq_len, seq_len), 0
    )


def attend_back(queries, keys_rot, values, grad_mixed):
    scale_factor = queries.shape[-1] ** (-0.5)
    scores = (
        jnp.einsum("bqhd,bkhd->bhqk", queries, keys_rot, preferred_element_type=f32) * scale_factor
    )
    soft = jax.nn.softmax(jnp.where(causal_mask(scores.shape[-1]), scores, -1e30), axis=-1)
    grad_soft = jnp.einsum("bqhd,bkhd->bhqk", grad_mixed, values, preferred_element_type=f32)
    grad_scores = (soft * (grad_soft - jnp.sum(soft * grad_soft, axis=-1, keepdims=True))).astype(
        bf16
    )
    grad_queries = (
        jnp.einsum("bhqk,bkhd->bqhd", grad_scores, keys_rot, preferred_element_type=f32)
        * scale_factor
    )
    grad_keys = (
        jnp.einsum("bhqk,bqhd->bkhd", grad_scores, queries, preferred_element_type=f32)
        * scale_factor
    )
    grad_values = jnp.einsum(
        "bhqk,bqhd->bkhd", soft.astype(bf16), grad_mixed, preferred_element_type=f32
    )
    return (grad_queries, grad_keys, grad_values)


class Plan:
    def __init__(self, outer, inner, rows):
        self.count = outer * inner
        self.inner = inner
        self.span = max(1, HEAD_DIM // rows)
        self.bit_a = self.span
        self.bit_b = 2 * self.span
        self.bit_core = inner
        flat = lax.axis_index("dp") * inner + lax.axis_index("fsdp")
        self.flat = flat
        self.core = (flat // inner) % 2
        self.quad = (flat // self.span) % QUAD
        self.me = self.core * QUAD + self.quad
        dims = []
        bit = outer * inner // 2
        while bit > inner:
            dims.append(bit)
            bit //= 2
        self.upper = dims
        mid = []
        bit = inner // 2
        while bit >= QUAD * self.span:
            mid.append(bit)
            bit //= 2
        self.mid = mid
        low = []
        bit = self.span // 2
        while bit >= 1:
            low.append(bit)
            bit //= 2
        self.low = low
        self.data_bits = low + mid + dims
        self.deltas = [
            c * self.bit_core + q * self.span for c in range(2) for q in range(QUAD)
        ]

    def send(self, array, bit):
        return lax.ppermute(array, AXES, [(r, r ^ bit) for r in range(self.count)])

    def mine(self, bit):
        return (self.flat // bit) % 2

    def column_dims(self):
        return (
            (2,) * len(self.upper) + (2,) + (2,) * len(self.mid) + (QUAD,) + (2,) * len(self.low)
        )

    def row_dims(self):
        return (2,) * (len(self.upper) + len(self.mid) + len(self.low))

    def axes(self, with_columns):
        skip_core = 1 if with_columns else 0
        skip_quad = skip_core + (1 if with_columns else 0)
        found = {}
        place = 0
        for bit in self.upper:
            found[bit] = place
            place += 1
        place += skip_core
        for bit in self.mid:
            found[bit] = place
            place += 1
        place += skip_quad - skip_core
        for bit in self.low:
            found[bit] = place
            place += 1
        return found

    def cut_columns(self, weight):
        rows, width = weight.shape
        chunk = width // (self.count // self.span)
        ahead = 2 ** len(self.upper)
        middle = 2 ** len(self.mid)
        parts = weight.reshape(rows, ahead, 2, middle, QUAD, chunk)
        return parts.transpose(2, 4, 0, 1, 3, 5).reshape(2 * QUAD, rows, width // (2 * QUAD))

    def join_columns(self, parts):
        eight, rows, narrow = parts.shape
        width = eight * narrow
        chunk = width // (self.count // self.span)
        ahead = 2 ** len(self.upper)
        middle = 2 ** len(self.mid)
        parts = parts.reshape(2, QUAD, rows, ahead, middle, chunk)
        return parts.transpose(2, 3, 0, 4, 1, 5).reshape(rows, width)

    def swap(self, parts):
        got = jnp.zeros_like(parts)
        for index, delta in enumerate(self.deltas):
            other = self.me ^ index
            block = lax.dynamic_index_in_dim(parts, other, 0, keepdims=True)
            if index:
                block = self.send(block, delta)
            got = lax.dynamic_update_slice_in_dim(got, block, other, 0)
        return got

    def gather(self, block, with_columns):
        held = {0: block}
        for bit in self.data_bits:
            for key in list(held):
                held[key ^ bit] = self.send(held[key], bit)
        found = self.axes(with_columns)
        if with_columns:
            dims = self.column_dims()
            piece = [1] * len(dims)
            piece[len(self.upper)] = 2
            piece[len(self.upper) + 1 + len(self.mid)] = QUAD
        else:
            dims = self.row_dims()
            piece = [1] * len(dims)
        tail = block.shape[-2:]
        whole = jnp.zeros(tuple(dims) + tail, block.dtype)
        for key, array in held.items():
            start = [0] * (len(dims) + 2)
            for bit, place in found.items():
                start[place] = self.mine(bit) ^ (1 if key & bit else 0)
            whole = lax.dynamic_update_slice(whole, array.reshape(tuple(piece) + tail), start)
        return whole.reshape(-1, tail[1])

    def scatter(self, total, rows, with_columns):
        dims = self.column_dims() if with_columns else self.row_dims()
        found = self.axes(with_columns)
        total = total.reshape(dims + (rows, total.shape[-1]))
        for bit in reversed(self.data_bits):
            place = found[bit]
            here = self.mine(bit)
            away = lax.dynamic_slice_in_dim(total, 1 - here, 1, place).astype(bf16)
            kept = lax.dynamic_slice_in_dim(total, here, 1, place)
            total = kept + self.send(away, bit).astype(f32)
        if with_columns:
            return total.reshape(2 * QUAD, rows, total.shape[-1])
        return total.reshape(rows, total.shape[-1])

    def share_tokens(self, block):
        half = block.shape[0] // 2
        from_a = self.send(block, self.bit_a)
        from_b = self.send(block, self.bit_b)
        first = self.send(from_a[:half], self.bit_b)
        second = self.send(from_b[half:], self.bit_a)
        four = jnp.concatenate([block, from_a, from_b, first, second], axis=0)
        return jnp.concatenate([four, self.send(four, self.bit_core)], axis=0)

    def sum_tokens(self, left, product):
        count = left.shape[0] // 2
        far = product(left[count:]).astype(bf16)
        four = product(left[:count]) + self.send(far, self.bit_core).astype(f32)
        size = count // 4
        half = size // 2
        own, for_a, for_b, for_ab = (four[i * size : (i + 1) * size] for i in range(4))
        first = self.send(for_ab[:half].astype(bf16), self.bit_b)
        second = self.send(for_ab[half:].astype(bf16), self.bit_a)
        for_a = jnp.concatenate([for_a[:half] + first.astype(f32), for_a[half:]]).astype(bf16)
        for_b = jnp.concatenate([for_b[:half], for_b[half:] + second.astype(f32)]).astype(bf16)
        return (
            own
            + self.send(for_a, self.bit_a).astype(f32)
            + self.send(for_b, self.bit_b).astype(f32)
        )

    def gather_gains(self, gains):
        bits = []
        bit = self.count // 2
        while bit >= 1:
            bits.append(bit)
            bit //= 2
        for bit in reversed(bits):
            other = self.send(gains, bit)
            low = self.mine(bit) == 0
            gains = jnp.concatenate(
                [jnp.where(low, gains, other), jnp.where(low, other, gains)], axis=1
            )
        return gains

    def scatter_gains(self, totals):
        bit = self.count // 2
        while bit >= 1:
            half = totals.shape[1] // 2
            low = self.mine(bit) == 0
            kept = jnp.where(low, totals[:, :half], totals[:, half:])
            away = jnp.where(low, totals[:, half:], totals[:, :half])
            totals = kept + self.send(away, bit)
            bit //= 2
        return totals


class Ring:
    def __init__(self, outer, inner, rows):
        self.count = outer * inner
        self.inner = inner
        self.span = max(1, HEAD_DIM // rows)
        self.bit_a = self.span
        self.bit_b = 2 * self.span
        self.bit_core = inner
        self.low = powers(1, self.span)
        self.mid = powers(QUAD * self.span, inner)
        self.upper = powers(2 * inner, self.count)
        self.data_bits = self.low + self.mid + self.upper
        self.deltas = [
            (self.bit_core if t // QUAD else 0) + (t % QUAD) * self.span for t in range(2 * QUAD)
        ]
        self.across = inner // (QUAD * self.span)
        self.upper_size = outer // 2
        self.flat = lax.axis_index("dp") * inner + lax.axis_index("fsdp")

    def flip(self, flat, bits):
        bit = 1
        while bit <= bits:
            if bits & bit:
                flat = flat + bit * (1 - 2 * ((flat // bit) % 2))
            bit *= 2
        return flat

    def where(self, bits):
        other = self.flip(self.flat, bits)
        return (other // self.inner, other % self.inner)

    def team(self, flat):
        return ((flat // self.inner) % 2) * QUAD + (flat // self.span) % QUAD

    def place(self, flat):
        return (
            (flat // (2 * self.inner)) * self.across + (flat % self.inner) // (QUAD * self.span)
        ) * self.span + flat % self.span

    def runs(self, flat, rows):
        lowest = flat - self.span * ((flat // self.span) % QUAD)
        lowest = lowest - self.inner * ((flat // self.inner) % 2)
        found = []
        for core in range(2):
            start = lowest + core * self.inner
            if self.span == 1:
                found.append((start * rows, QUAD * rows))
            else:
                found += [((start + q * self.span) * rows, rows) for q in range(QUAD)]
        return found

    def greet(self):
        partners = self.deltas[1:] + self.data_bits
        barrier = pltpu.get_barrier_semaphore()
        for bits in partners:
            pl.semaphore_signal(barrier, 1, device_id=self.where(bits), device_id_type=MESH)
        pl.semaphore_wait(barrier, len(partners))


def powers(first, end):
    found = []
    while first < end:
        found.append(first)
        first *= 2
    return found


class Mail:
    def __init__(self, ring, send_sems, recv_sems, local_sems):
        self.ring, self.send_sems, self.recv_sems, self.local_sems = ring, send_sems, recv_sems, local_sems
        self.used = 0
        self.used_local = 0
        self.sent = []
        self.kept = []

    def post(self, src, dst, bits):
        copy = pltpu.make_async_remote_copy(
            src_ref=src,
            dst_ref=dst,
            send_sem=self.send_sems.at[self.used],
            recv_sem=self.recv_sems.at[self.used],
            device_id=self.ring.where(bits),
            device_id_type=MESH,
        )
        self.used += 1
        copy.start()
        self.sent.append(copy)
        return copy

    def keep(self, src, dst):
        copy = pltpu.make_async_copy(src, dst, self.local_sems.at[self.used_local])
        self.used_local += 1
        copy.start()
        self.kept.append(copy)
        return copy

    def finish(self):
        for copy in self.sent:
            copy.wait_send()
        for copy in self.kept:
            copy.wait()


class Spread:
    def __init__(self, mail, views, bits):
        self.mail, self.views, self.bits = mail, views, bits
        self.came = {}

    def start(self, key, stage):
        bit = self.bits[stage]
        self.came[key + bit] = [self.mail.post(ref, ref, bit) for ref in self.views(key)]

    def start_from(self, key, first):
        for stage in range(first, len(self.bits)):
            self.start(key, stage)

    def pass_on(self, stage):
        for low in range(2**stage):
            key = sum(b for i, b in enumerate(self.bits[:stage]) if low >> i & 1) + self.bits[stage]
            for later in range(stage + 1, len(self.bits)):
                self.came[key + self.bits[later]] = []
            for copy, ref in zip(self.came[key], self.views(key)):
                copy.wait_recv()
                for later in range(stage + 1, len(self.bits)):
                    bit = self.bits[later]
                    self.came[key + bit].append(self.mail.post(ref, ref, bit))
            self.came[key] = []

    def pass_all(self):
        for stage in range(len(self.bits) - 1):
            self.pass_on(stage)

    def done(self):
        for copies in self.came.values():
            for copy in copies:
                copy.wait_recv()


class Share:
    def __init__(self, mail, whole, own):
        self.mail, self.whole, self.own = mail, whole, own
        self.half = own.shape[0] // 2

    def first(self):
        ring = self.mail.ring
        self.from_a = self.mail.post(self.own, self.whole.at[1], ring.bit_a)
        self.from_b = self.mail.post(self.own, self.whole.at[2], ring.bit_b)
        self.core = [self.mail.post(self.own, self.whole.at[QUAD], ring.bit_core)]

    def second(self):
        ring = self.mail.ring
        top, end = pl.ds(0, self.half), pl.ds(self.half, self.half)
        self.from_a.wait_recv()
        self.one = self.mail.post(self.whole.at[1, top], self.whole.at[3, top], ring.bit_b)
        self.core.append(self.mail.post(self.whole.at[1], self.whole.at[QUAD + 1], ring.bit_core))
        self.from_b.wait_recv()
        self.two = self.mail.post(self.whole.at[2, end], self.whole.at[3, end], ring.bit_a)
        self.core.append(self.mail.post(self.whole.at[2], self.whole.at[QUAD + 2], ring.bit_core))

    def third(self):
        self.one.wait_recv()
        self.two.wait_recv()
        self.core.append(
            self.mail.post(self.whole.at[3], self.whole.at[QUAD + 3], self.mail.ring.bit_core)
        )

    def done(self):
        for copy in self.core:
            copy.wait_recv()


def head_mask(width, head):
    lanes = lax.broadcasted_iota(jnp.int32, (1, width), 1)
    return (lanes >= head * HEAD_DIM) & (lanes < (head + 1) * HEAD_DIM)


def turn(u, cosine, signed_sine):
    width = u.shape[-1]
    half = HEAD_DIM // 2
    lanes = lax.broadcasted_iota(jnp.int32, (1, width), 1)
    lower = lanes % HEAD_DIM < half
    turned = jnp.where(lower, pltpu.roll(u, width - half, 1), pltpu.roll(u, half, 1))
    return u * cosine + turned * signed_sine


def front_kernel(
    outer, inner, seq_len,
    x_ref, go_ref, factor_ref, gain_ref, wq_ref, wk_ref, wv_ref, cos_ref, sin_ref,
    wo_ref, wg_ref, wu_ref, wd_ref,
    act_one, w_qkv, w_o, q_out, k_out, v_out, att_out, resid_out, gains_out,
    act_two, dy, w_gu, w_d,
    cut, gain_in, far, core_in, near, own_sum, half_a, half_b, in_a, in_b, act_two_own, dy_own,
    send_sems, recv_sems, local_sems, far_send, far_recv,
):
    rows = wq_ref.shape[0]
    width = wq_ref.shape[1]
    hidden_rows = wd_ref.shape[0]
    narrow = width // (2 * QUAD)
    hidden = w_gu.shape[1] // 2
    ring = Ring(outer, inner, rows)
    mail = Mail(ring, send_sems, recv_sems, local_sems)
    ring.greet()
    bits = ring.data_bits
    flat = ring.flat

    def by_place(ref, size):
        return lambda key: [ref.at[pl.ds(pl.multiple_of(ring.place(ring.flip(flat, key)) * size, 16), size)]]

    def by_runs(ref):
        return lambda key: [
            ref.at[pl.ds(pl.multiple_of(start, 16), size)]
            for start, size in ring.runs(ring.flip(flat, key), rows)
        ]

    mine_o = w_o.at[pl.ds(pl.multiple_of(ring.place(flat) * rows, 16), rows)]
    mine_d = w_d.at[pl.ds(pl.multiple_of(ring.place(flat) * hidden_rows, 16), hidden_rows)]
    keep_o = mail.keep(wo_ref, mine_o)
    keep_d = mail.keep(wd_ref, mine_d)

    heads = ring.upper_size * ring.across
    chunk = HEAD_DIM
    for t in range(2 * QUAD):
        for j, ref in enumerate((wq_ref, wk_ref, wv_ref)):
            parts = []
            for y in range(ring.upper_size):
                for o in range(ring.across):
                    head = ((y * 2 + t // QUAD) * ring.across + o) * QUAD + t % QUAD
                    parts.append(ref[:, head * chunk : (head + 1) * chunk])
            cut[t, :, j * narrow : (j + 1) * narrow] = jnp.concatenate(parts, axis=1)
    here = pl.ds(pl.multiple_of(flat * rows, 16), rows)
    keep_qkv = mail.keep(cut.at[ring.team(flat)], w_qkv.at[here])
    qkv_swap = []
    for delta in ring.deltas[1:]:
        other = ring.flip(flat, delta)
        qkv_swap.append(mail.post(cut.at[ring.team(other)], w_qkv.at[here], delta))
    keep_o.wait()
    mail.kept = [c for c in mail.kept if c is not keep_o]
    spread_o = Spread(mail, by_place(w_o, rows), bits)
    spread_o.start_from(0, 0)

    block = ring.span * hidden_rows
    gu_swap = []
    for delta in ring.deltas:
        other = ring.flip(flat, delta)
        team = ring.team(other)
        pieces = []
        for j, ref in enumerate((wg_ref, wu_ref)):
            for y in range(ring.upper_size):
                for o in range(ring.across):
                    source = ((y * 2 + team // QUAD) * ring.across + o) * QUAD + team % QUAD
                    target = j * hidden + (y * ring.across + o) * block
                    src = ref.at[:, pl.ds(pl.multiple_of(source * block, 128), block)]
                    dst = w_gu.at[here, pl.ds(target, block)]
                    pieces.append(mail.post(src, dst, delta) if delta else mail.keep(src, dst))
        gu_swap.append(pieces)

    step = 0
    gains_out[...] = gain_ref[...]
    for bit in [ring.bit_core, ring.bit_a, ring.bit_b] + bits:
        copy = mail.post(gains_out, gain_in.at[step], bit)
        copy.wait()
        mail.sent = [c for c in mail.sent if c is not copy]
        gains_out[...] = gains_out[...] + gain_in[step]
        step += 1
    keep_qkv.wait()
    mail.kept = [c for c in mail.kept if c is not keep_qkv]
    for copy in qkv_swap:
        copy.wait_recv()
    spread_qkv = Spread(mail, by_runs(w_qkv), bits)
    spread_qkv.start_from(0, 0)

    size = act_one.shape[1]
    strip = 32

    def norm_one(i, carry):
        part = pl.ds(pl.multiple_of(i * strip, strip), strip)
        x = x_ref[part, :].astype(f32)
        inv = lax.rsqrt(jnp.mean(x * x, axis=-1, keepdims=True) + epsilon)
        act_one[0, part, :] = (x * inv * gains_out[0:1, :]).astype(bf16)
        dy_own[part, :] = (go_ref[part, :].astype(f32) * factor_ref[part, :]).astype(bf16)
        return carry

    lax.fori_loop(0, size // strip, norm_one, 0)
    share_one = Share(mail, act_one, act_one.at[0])
    share_one.first()
    mail.keep(dy_own, dy.at[0])
    share_one.second()
    spread_o.pass_all()
    share_one.third()
    share_dy = Share(mail, dy, dy_own)
    share_dy.first()
    spread_qkv.pass_all()
    keep_d.wait()
    mail.kept = [c for c in mail.kept if c is not keep_d]
    for index, pieces in enumerate(gu_swap):
        for copy in pieces:
            if index:
                copy.wait_recv()
            else:
                copy.wait()
                mail.kept = [c for c in mail.kept if c is not copy]
    spread_d = Spread(mail, by_place(w_d, hidden_rows), bits)
    spread_gu = Spread(mail, by_runs(w_gu), bits)
    spread_d.start_from(0, 0)
    spread_gu.start_from(0, 0)
    share_one.done()

    scale = HEAD_DIM**-0.5
    cosine, sine = cos_ref[...], sin_ref[...]
    per_block = act_one.shape[1] // seq_len

    def attend_block(place):
        qkv = jnp.dot(act_one[place], w_qkv[...], preferred_element_type=f32)
        causal = lax.broadcasted_iota(jnp.int32, (seq_len, seq_len), 1) <= lax.broadcasted_iota(
            jnp.int32, (seq_len, seq_len), 0
        )
        for b in range(per_block):
            span = slice(b * seq_len, (b + 1) * seq_len)
            q = turn(qkv[span, :narrow], cosine, sine).astype(bf16)
            k = turn(qkv[span, narrow : 2 * narrow], cosine, sine).astype(bf16)
            v = qkv[span, 2 * narrow :].astype(bf16)
            q_out[place, span] = q
            k_out[place, span] = k
            v_out[place, span] = v
            mixed = jnp.zeros((seq_len, narrow), f32)
            for head in range(narrow // HEAD_DIM):
                mask = head_mask(narrow, head)
                kh = jnp.where(mask, k, jnp.zeros_like(k))
                vh = jnp.where(mask, v, jnp.zeros_like(v))
                scores = lax.dot_general(
                    q, kh, (((1,), (1,)), ((), ())), preferred_element_type=f32
                )
                scores = jnp.where(causal, scores * scale, -1e30)
                top = jnp.max(scores, axis=-1, keepdims=True)
                grown = jnp.exp(scores - top)
                soft = (grown / jnp.sum(grown, axis=-1, keepdims=True)).astype(bf16)
                mixed = mixed + jnp.dot(soft, vh, preferred_element_type=f32)
            att_out[place, span] = mixed.astype(bf16)
        return jnp.dot(att_out[place], w_o[...], preferred_element_type=f32)

    def far_copy(j):
        return pltpu.make_async_remote_copy(
            src_ref=far.at[j],
            dst_ref=core_in.at[j],
            send_sem=far_send.at[j],
            recv_sem=far_recv.at[j],
            device_id=ring.where(ring.bit_core),
            device_id_type=MESH,
        )

    spread_o.done()
    spread_qkv.done()

    def far_step(i, carry):
        j = QUAD - 1 - i
        far[j] = attend_block(QUAD + j).astype(bf16)
        far_copy(j).start()
        return carry

    lax.fori_loop(0, QUAD, far_step, 0)
    share_dy.second()

    def near_step(i, carry):
        j = QUAD - 1 - i
        part = attend_block(j)
        far_copy(j).wait_recv()
        own_sum[...] = part + core_in[j].astype(f32)
        near[j] = own_sum[...].astype(bf16)
        return carry

    lax.fori_loop(0, QUAD, near_step, 0)
    for j in range(QUAD):
        far_copy(j).wait_send()
    half = size // 2
    top, end = pl.ds(0, half), pl.ds(half, half)
    sum_one = mail.post(near.at[3, top], half_a, ring.bit_b)
    sum_two = mail.post(near.at[3, end], half_b, ring.bit_a)
    share_dy.third()
    sum_one.wait_recv()
    near[1, :half] = (near[1, :half].astype(f32) + half_a[...].astype(f32)).astype(bf16)
    for_a = mail.post(near.at[1], in_a, ring.bit_a)
    sum_two.wait_recv()
    near[2, half:] = (near[2, half:].astype(f32) + half_b[...].astype(f32)).astype(bf16)
    for_b = mail.post(near.at[2], in_b, ring.bit_b)
    spread_d.pass_on(0)
    for_a.wait_recv()
    for_b.wait_recv()

    def norm_two(i, carry):
        part = pl.ds(pl.multiple_of(i * strip, strip), strip)
        resid = (
            x_ref[part, :].astype(f32)
            + own_sum[part, :]
            + in_a[part, :].astype(f32)
            + in_b[part, :].astype(f32)
        )
        resid_out[part, :] = resid
        inv = lax.rsqrt(jnp.mean(resid * resid, axis=-1, keepdims=True) + epsilon)
        act_two_own[part, :] = (resid * inv * gains_out[1:2, :]).astype(bf16)
        return carry

    lax.fori_loop(0, size // strip, norm_two, 0)
    mail.keep(act_two_own, act_two.at[0])
    share_two = Share(mail, act_two, act_two_own)
    share_two.first()
    share_two.second()
    share_two.third()
    for stage in range(1, len(bits) - 1):
        spread_d.pass_on(stage)
    spread_gu.pass_all()
    spread_d.done()
    spread_gu.done()
    share_two.done()
    share_dy.done()
    mail.finish()


def front(outer, inner, batch_size, seq_len, tokens, grad_out, factor_rows, gain_rows, w_query, w_key, w_value, cosine, signed_sine, w_out, w_gate, w_up, w_down):
    size, width = tokens.shape
    rows, hidden_all = w_gate.shape
    hidden_rows = w_down.shape[0]
    narrow, hidden = width // (2 * QUAD), hidden_all // (2 * QUAD)
    span = max(1, HEAD_DIM // rows)
    places = outer * inner // (2 * QUAD)
    pieces = 2 if span == 1 else 2 * QUAD
    remote = 2 * (places - 1) * (pieces + 1) + 7 + 14 * places // span + 8 + 24 + 8
    local = 8 + 2 * places // span
    vm = pl.BlockSpec(memory_space=pltpu.VMEM)
    hbm = pl.BlockSpec(memory_space=pl.ANY)
    eight = (2 * QUAD, size)
    sds = jax.ShapeDtypeStruct
    out_shape = (
        sds(eight + (width,), bf16),
        sds((width, 3 * narrow), bf16),
        sds((narrow, width), bf16),
        sds(eight + (narrow,), bf16),
        sds(eight + (narrow,), bf16),
        sds(eight + (narrow,), bf16),
        sds(eight + (narrow,), bf16),
        sds((size, width), f32),
        sds((8, width), f32),
        sds(eight + (width,), bf16),
        sds(eight + (width,), bf16),
        sds((width, 2 * hidden), bf16),
        sds((hidden, width), bf16),
    )
    return pl.pallas_call(
        functools.partial(front_kernel, outer, inner, seq_len),
        out_shape=out_shape,
        in_specs=[vm] * 9 + [hbm] * 4,
        out_specs=tuple([vm] * 9 + [hbm] * 4),
        scratch_shapes=[
            pltpu.VMEM((2 * QUAD, rows, 3 * narrow), bf16),
            pltpu.VMEM((8, 8, width), f32),
            pltpu.VMEM((QUAD, size, width), bf16),
            pltpu.VMEM((QUAD, size, width), bf16),
            pltpu.VMEM((QUAD, size, width), bf16),
            pltpu.VMEM((size, width), f32),
            pltpu.VMEM((size // 2, width), bf16),
            pltpu.VMEM((size // 2, width), bf16),
            pltpu.VMEM((size, width), bf16),
            pltpu.VMEM((size, width), bf16),
            pltpu.VMEM((size, width), bf16),
            pltpu.VMEM((size, width), bf16),
            pltpu.SemaphoreType.DMA((remote,)),
            pltpu.SemaphoreType.DMA((remote,)),
            pltpu.SemaphoreType.DMA((local,)),
            pltpu.SemaphoreType.DMA((QUAD,)),
            pltpu.SemaphoreType.DMA((QUAD,)),
        ],
        compiler_params=pltpu.CompilerParams(
            collective_id=0, has_side_effects=True, vmem_limit_bytes=60 * 1024 * 1024
        ),
        name="front",
    )(tokens, grad_out, factor_rows, gain_rows, w_query, w_key, w_value, cosine, signed_sine, w_out, w_gate, w_up, w_down)


def on_device(
    tokens,
    labels,
    counts,
    grad_out,
    w_query,
    w_key,
    w_value,
    w_out,
    gain_attn,
    gain_mlp,
    w_gate,
    w_up,
    w_down,
):
    batch_size, seq_len, width = tokens.shape
    outer_count = lax.axis_size("dp")
    inner_count = lax.axis_size("fsdp")
    rows = w_query.shape[0]
    hidden_rows = w_down.shape[0]
    plan = Plan(outer_count, inner_count, rows)
    x_rows = tokens.reshape(-1, width).astype(f32)

    token_total = float(seq_len * batch_size * outer_count * inner_count)
    picked_counts = jnp.sum(
        jnp.where(labels[:, None] == jnp.arange(3)[None, :], counts[None, :], 0), axis=1
    ).astype(f32)
    factor = token_total / (3.0 * picked_counts)
    cotangent = (grad_out.astype(f32) * factor[:, None, None]).reshape(-1, width)
    cosine, sine = rope_tables(seq_len, HEAD_DIM)
    head_count = width // (2 * QUAD) // HEAD_DIM
    four_shape = (-1, seq_len, head_count, HEAD_DIM)
    sign = jnp.where(jnp.arange(HEAD_DIM) < HEAD_DIM // 2, -1.0, 1.0)
    gain_rows = lax.dynamic_update_slice(
        jnp.zeros((8, width), f32),
        jnp.stack([gain_attn, gain_mlp]).astype(f32),
        (0, plan.flat * rows),
    )
    factor_rows = jnp.repeat(factor, seq_len)[:, None]
    (
        act_one, w_qkv, w_o, q_rot, k_rot, values, attended, resid, gains, act_two, dy, w_gu, w_d,
    ) = front(
        outer_count, inner_count, batch_size, seq_len,
        tokens.reshape(-1, width), grad_out.reshape(-1, width), factor_rows, gain_rows,
        w_query, w_key, w_value,
        jnp.tile(cosine, (1, head_count)), jnp.tile(sine * sign, (1, head_count)),
        w_out, w_gate, w_up, w_down,
    )
    narrow = w_o.shape[0]
    hidden = w_d.shape[0]
    gain_one, gain_two = gains[0:1], gains[1:2]
    act_one, act_two, dy = (a.reshape(-1, width) for a in (act_one, act_two, dy))
    attended = attended.reshape(-1, narrow)
    q_rot, k_rot, values = (a.reshape(four_shape) for a in (q_rot, k_rot, values))
    inv_one = lax.rsqrt(jnp.mean(x_rows * x_rows, axis=-1, keepdims=True) + epsilon)
    inv_two = lax.rsqrt(jnp.mean(resid * resid, axis=-1, keepdims=True) + epsilon)

    gu = mm(act_two, w_gu)
    gate_pre, up_proj = gu[:, :hidden], gu[:, hidden:]
    sigmoid_gate = jax.nn.sigmoid(gate_pre)
    middle = (gate_pre * sigmoid_gate * up_proj).astype(bf16)

    grad_middle = times_transposed(dy, w_d)
    grad_gate_pre = (
        grad_middle * up_proj * sigmoid_gate * (1.0 + gate_pre * (1.0 - sigmoid_gate))
    ).astype(bf16)
    grad_up_proj = (grad_middle * gate_pre * sigmoid_gate).astype(bf16)
    grad_gu_cols = jnp.concatenate([grad_gate_pre, grad_up_proj], axis=1)

    added = plan.sum_tokens(grad_gu_cols, lambda part: times_transposed(part, w_gu))
    down_grad = plan.scatter(outer_sum(middle, dy), hidden_rows, False)
    gu_grad = plan.swap(plan.scatter(outer_sum(act_two, grad_gu_cols), rows, True).astype(bf16))
    gate_grad = plan.join_columns(gu_grad[:, :, :hidden]).astype(f32)
    up_grad = plan.join_columns(gu_grad[:, :, hidden:]).astype(f32)

    layer_out = (
        (resid + plan.sum_tokens(middle, lambda part: mm(part, w_d)))
        .astype(bf16)
        .reshape(tokens.shape)
    )

    grad_gain_two = jnp.sum(added * resid * inv_two, axis=0, keepdims=True)
    scaled_two = gain_two * added
    grad_resid = (
        cotangent
        + inv_two * scaled_two
        - resid * inv_two**3 * jnp.mean(scaled_two * resid, axis=-1, keepdims=True)
    )
    grad_branch = plan.share_tokens(grad_resid.astype(bf16))
    grad_attended = times_transposed(grad_branch, w_o).astype(bf16).reshape(four_shape)
    out_grad = plan.scatter(outer_sum(attended, grad_branch), rows, False)
    grad_q_rot, grad_k_rot, grad_v = attend_back(q_rot, k_rot, values, grad_attended)
    grad_qkv_cols = jnp.concatenate(
        [
            unrotate(grad_q_rot, cosine, sine).reshape(-1, narrow).astype(bf16),
            unrotate(grad_k_rot, cosine, sine).reshape(-1, narrow).astype(bf16),
            grad_v.reshape(-1, narrow).astype(bf16),
        ],
        axis=1,
    )
    qkv_grad = plan.swap(plan.scatter(outer_sum(act_one, grad_qkv_cols), rows, True).astype(bf16))
    query_grad, key_grad, value_grad = (
        plan.join_columns(qkv_grad[:, :, i * narrow : (i + 1) * narrow]).astype(f32)
        for i in range(3)
    )
    grad_act_one = plan.sum_tokens(grad_qkv_cols, lambda part: times_transposed(part, w_qkv))
    grad_gain_one = jnp.sum(grad_act_one * x_rows * inv_one, axis=0, keepdims=True)
    scaled_one = gain_one * grad_act_one
    grad_rows = (
        grad_resid
        + inv_one * scaled_one
        - x_rows * inv_one**3 * jnp.mean(scaled_one * x_rows, axis=-1, keepdims=True)
    )
    gain_grads = plan.scatter_gains(jnp.concatenate([grad_gain_one, grad_gain_two], axis=0))
    return (
        layer_out,
        grad_rows.reshape(tokens.shape),
        query_grad,
        key_grad,
        value_grad,
        out_grad,
        gain_grads[0],
        gain_grads[1],
        gate_grad,
        up_grad,
        down_grad,
    )


def solution(mesh):
    rows = P(AXES, None)
    vector = P(AXES)
    three = P(AXES, None, None)
    in_specs = (three, vector, P(), three, rows, rows, rows, rows, vector, vector, rows, rows, rows)
    out_specs = (three, three, rows, rows, rows, rows, vector, vector, rows, rows, rows)
    return jax.shard_map(
        on_device, mesh=mesh, in_specs=in_specs, out_specs=out_specs, check_vma=False
    )
```

```python
import functools

import jax
import jax.numpy as jnp
from jax import lax
from jax.experimental import pallas as pl
from jax.experimental.pallas import tpu as pltpu
from jax.sharding import PartitionSpec as P

HEAD_DIM = 64
AXES = ("dp", "fsdp")
QUAD = 4

epsilon = 1e-05
rope_base = 130000.0
bf16 = jnp.bfloat16
f32 = jnp.float32
MESH = pl.DeviceIdType.MESH


def rope_tables(seq_len, head_dim):
    half_dim = head_dim // 2
    frequency = rope_base ** (-(jnp.arange(half_dim).astype(f32) * 2.0) / head_dim)
    angles = jnp.arange(seq_len).astype(f32)[:, None] * frequency[None, :]
    angles = jnp.concatenate([angles, angles], axis=1)
    return (jnp.cos(angles), jnp.sin(angles))


def rotate(tensor, cosine, sine):
    half_dim = tensor.shape[-1] // 2
    turned = jnp.concatenate([-tensor[..., half_dim:], tensor[..., :half_dim]], axis=-1)
    return tensor * cosine[:, None, :] + turned * sine[:, None, :]


def unrotate(grads, cosine, sine):
    half_dim = grads.shape[-1] // 2
    turned = grads * sine[:, None, :]
    return grads * cosine[:, None, :] + jnp.concatenate(
        [turned[..., half_dim:], -turned[..., :half_dim]], axis=-1
    )


def mm(left, right):
    return jnp.dot(left, right, preferred_element_type=f32)


def outer_sum(left, right):
    return lax.dot_general(left, right, (((0,), (0,)), ((), ())), preferred_element_type=f32)


def times_transposed(left, weight):
    return lax.dot_general(left, weight, (((1,), (1,)), ((), ())), preferred_element_type=f32)


def causal_mask(seq_len):
    return lax.broadcasted_iota(jnp.int32, (seq_len, seq_len), 1) <= lax.broadcasted_iota(
        jnp.int32, (seq_len, seq_len), 0
    )


def attend_back(queries, keys_rot, values, grad_mixed):
    scale_factor = queries.shape[-1] ** (-0.5)
    scores = (
        jnp.einsum("bqhd,bkhd->bhqk", queries, keys_rot, preferred_element_type=f32) * scale_factor
    )
    soft = jax.nn.softmax(jnp.where(causal_mask(scores.shape[-1]), scores, -1e30), axis=-1)
    grad_soft = jnp.einsum("bqhd,bkhd->bhqk", grad_mixed, values, preferred_element_type=f32)
    grad_scores = (soft * (grad_soft - jnp.sum(soft * grad_soft, axis=-1, keepdims=True))).astype(
        bf16
    )
    grad_queries = (
        jnp.einsum("bhqk,bkhd->bqhd", grad_scores, keys_rot, preferred_element_type=f32)
        * scale_factor
    )
    grad_keys = (
        jnp.einsum("bhqk,bqhd->bkhd", grad_scores, queries, preferred_element_type=f32)
        * scale_factor
    )
    grad_values = jnp.einsum(
        "bhqk,bqhd->bkhd", soft.astype(bf16), grad_mixed, preferred_element_type=f32
    )
    return (grad_queries, grad_keys, grad_values)


class Plan:
    def __init__(self, outer, inner, rows):
        self.count = outer * inner
        self.inner = inner
        self.span = max(1, HEAD_DIM // rows)
        self.bit_a = self.span
        self.bit_b = 2 * self.span
        self.bit_core = inner
        flat = lax.axis_index("dp") * inner + lax.axis_index("fsdp")
        self.flat = flat
        self.core = (flat // inner) % 2
        self.quad = (flat // self.span) % QUAD
        self.me = self.core * QUAD + self.quad
        dims = []
        bit = outer * inner // 2
        while bit > inner:
            dims.append(bit)
            bit //= 2
        self.upper = dims
        mid = []
        bit = inner // 2
        while bit >= QUAD * self.span:
            mid.append(bit)
            bit //= 2
        self.mid = mid
        low = []
        bit = self.span // 2
        while bit >= 1:
            low.append(bit)
            bit //= 2
        self.low = low
        self.data_bits = low + mid + dims
        self.deltas = [
            c * self.bit_core + q * self.span for c in range(2) for q in range(QUAD)
        ]

    def send(self, array, bit):
        return lax.ppermute(array, AXES, [(r, r ^ bit) for r in range(self.count)])

    def mine(self, bit):
        return (self.flat // bit) % 2

    def column_dims(self):
        return (
            (2,) * len(self.upper) + (2,) + (2,) * len(self.mid) + (QUAD,) + (2,) * len(self.low)
        )

    def row_dims(self):
        return (2,) * (len(self.upper) + len(self.mid) + len(self.low))

    def axes(self, with_columns):
        skip_core = 1 if with_columns else 0
        skip_quad = skip_core + (1 if with_columns else 0)
        found = {}
        place = 0
        for bit in self.upper:
            found[bit] = place
            place += 1
        place += skip_core
        for bit in self.mid:
            found[bit] = place
            place += 1
        place += skip_quad - skip_core
        for bit in self.low:
            found[bit] = place
            place += 1
        return found

    def cut_columns(self, weight):
        rows, width = weight.shape
        chunk = width // (self.count // self.span)
        ahead = 2 ** len(self.upper)
        middle = 2 ** len(self.mid)
        parts = weight.reshape(rows, ahead, 2, middle, QUAD, chunk)
        return parts.transpose(2, 4, 0, 1, 3, 5).reshape(2 * QUAD, rows, width // (2 * QUAD))

    def join_columns(self, parts):
        eight, rows, narrow = parts.shape
        width = eight * narrow
        chunk = width // (self.count // self.span)
        ahead = 2 ** len(self.upper)
        middle = 2 ** len(self.mid)
        parts = parts.reshape(2, QUAD, rows, ahead, middle, chunk)
        return parts.transpose(2, 3, 0, 4, 1, 5).reshape(rows, width)

    def swap(self, parts):
        got = jnp.zeros_like(parts)
        for index, delta in enumerate(self.deltas):
            other = self.me ^ index
            block = lax.dynamic_index_in_dim(parts, other, 0, keepdims=True)
            if index:
                block = self.send(block, delta)
            got = lax.dynamic_update_slice_in_dim(got, block, other, 0)
        return got

    def gather(self, block, with_columns):
        held = {0: block}
        for bit in self.data_bits:
            for key in list(held):
                held[key ^ bit] = self.send(held[key], bit)
        found = self.axes(with_columns)
        if with_columns:
            dims = self.column_dims()
            piece = [1] * len(dims)
            piece[len(self.upper)] = 2
            piece[len(self.upper) + 1 + len(self.mid)] = QUAD
        else:
            dims = self.row_dims()
            piece = [1] * len(dims)
        tail = block.shape[-2:]
        whole = jnp.zeros(tuple(dims) + tail, block.dtype)
        for key, array in held.items():
            start = [0] * (len(dims) + 2)
            for bit, place in found.items():
                start[place] = self.mine(bit) ^ (1 if key & bit else 0)
            whole = lax.dynamic_update_slice(whole, array.reshape(tuple(piece) + tail), start)
        return whole.reshape(-1, tail[1])

    def scatter(self, total, rows, with_columns):
        dims = self.column_dims() if with_columns else self.row_dims()
        found = self.axes(with_columns)
        total = total.reshape(dims + (rows, total.shape[-1]))
        for bit in reversed(self.data_bits):
            place = found[bit]
            here = self.mine(bit)
            away = lax.dynamic_slice_in_dim(total, 1 - here, 1, place).astype(bf16)
            kept = lax.dynamic_slice_in_dim(total, here, 1, place)
            total = kept + self.send(away, bit).astype(f32)
        if with_columns:
            return total.reshape(2 * QUAD, rows, total.shape[-1])
        return total.reshape(rows, total.shape[-1])

    def share_tokens(self, block):
        half = block.shape[0] // 2
        from_a = self.send(block, self.bit_a)
        from_b = self.send(block, self.bit_b)
        first = self.send(from_a[:half], self.bit_b)
        second = self.send(from_b[half:], self.bit_a)
        four = jnp.concatenate([block, from_a, from_b, first, second], axis=0)
        return jnp.concatenate([four, self.send(four, self.bit_core)], axis=0)

    def sum_tokens(self, left, product):
        count = left.shape[0] // 2
        far = product(left[count:]).astype(bf16)
        four = product(left[:count]) + self.send(far, self.bit_core).astype(f32)
        size = count // 4
        half = size // 2
        own, for_a, for_b, for_ab = (four[i * size : (i + 1) * size] for i in range(4))
        first = self.send(for_ab[:half].astype(bf16), self.bit_b)
        second = self.send(for_ab[half:].astype(bf16), self.bit_a)
        for_a = jnp.concatenate([for_a[:half] + first.astype(f32), for_a[half:]]).astype(bf16)
        for_b = jnp.concatenate([for_b[:half], for_b[half:] + second.astype(f32)]).astype(bf16)
        return (
            own
            + self.send(for_a, self.bit_a).astype(f32)
            + self.send(for_b, self.bit_b).astype(f32)
        )

    def gather_gains(self, gains):
        bits = []
        bit = self.count // 2
        while bit >= 1:
            bits.append(bit)
            bit //= 2
        for bit in reversed(bits):
            other = self.send(gains, bit)
            low = self.mine(bit) == 0
            gains = jnp.concatenate(
                [jnp.where(low, gains, other), jnp.where(low, other, gains)], axis=1
            )
        return gains

    def scatter_gains(self, totals):
        bit = self.count // 2
        while bit >= 1:
            half = totals.shape[1] // 2
            low = self.mine(bit) == 0
            kept = jnp.where(low, totals[:, :half], totals[:, half:])
            away = jnp.where(low, totals[:, half:], totals[:, :half])
            totals = kept + self.send(away, bit)
            bit //= 2
        return totals


class Ring:
    def __init__(self, outer, inner, rows):
        self.count = outer * inner
        self.inner = inner
        self.span = max(1, HEAD_DIM // rows)
        self.bit_a = self.span
        self.bit_b = 2 * self.span
        self.bit_core = inner
        self.low = powers(1, self.span)
        self.mid = powers(QUAD * self.span, inner)
        self.upper = powers(2 * inner, self.count)
        self.data_bits = self.low + self.mid + self.upper
        self.deltas = [
            (self.bit_core if t // QUAD else 0) + (t % QUAD) * self.span for t in range(2 * QUAD)
        ]
        self.across = inner // (QUAD * self.span)
        self.upper_size = outer // 2
        self.flat = lax.axis_index("dp") * inner + lax.axis_index("fsdp")

    def flip(self, flat, bits):
        bit = 1
        while bit <= bits:
            if bits & bit:
                flat = flat + bit * (1 - 2 * ((flat // bit) % 2))
            bit *= 2
        return flat

    def where(self, bits):
        other = self.flip(self.flat, bits)
        return (other // self.inner, other % self.inner)

    def team(self, flat):
        return ((flat // self.inner) % 2) * QUAD + (flat // self.span) % QUAD

    def place(self, flat):
        return (
            (flat // (2 * self.inner)) * self.across + (flat % self.inner) // (QUAD * self.span)
        ) * self.span + flat % self.span

    def runs(self, flat, rows):
        lowest = flat - self.span * ((flat // self.span) % QUAD)
        lowest = lowest - self.inner * ((flat // self.inner) % 2)
        found = []
        for core in range(2):
            start = lowest + core * self.inner
            if self.span == 1:
                found.append((start * rows, QUAD * rows))
            else:
                found += [((start + q * self.span) * rows, rows) for q in range(QUAD)]
        return found

    def greet(self):
        partners = self.deltas[1:] + self.data_bits
        barrier = pltpu.get_barrier_semaphore()
        for bits in partners:
            pl.semaphore_signal(barrier, 1, device_id=self.where(bits), device_id_type=MESH)
        pl.semaphore_wait(barrier, len(partners))


def powers(first, end):
    found = []
    while first < end:
        found.append(first)
        first *= 2
    return found


class Mail:
    def __init__(self, ring, send_sems, recv_sems, local_sems):
        self.ring, self.send_sems, self.recv_sems, self.local_sems = ring, send_sems, recv_sems, local_sems
        self.used = 0
        self.used_local = 0
        self.sent = []
        self.kept = []

    def post(self, src, dst, bits):
        copy = pltpu.make_async_remote_copy(
            src_ref=src,
            dst_ref=dst,
            send_sem=self.send_sems.at[self.used],
            recv_sem=self.recv_sems.at[self.used],
            device_id=self.ring.where(bits),
            device_id_type=MESH,
        )
        self.used += 1
        copy.start()
        self.sent.append(copy)
        return copy

    def keep(self, src, dst):
        copy = pltpu.make_async_copy(src, dst, self.local_sems.at[self.used_local])
        self.used_local += 1
        copy.start()
        self.kept.append(copy)
        return copy

    def finish(self):
        for copy in self.sent:
            copy.wait_send()
        for copy in self.kept:
            copy.wait()


class Spread:
    def __init__(self, mail, views, bits):
        self.mail, self.views, self.bits = mail, views, bits
        self.came = {}

    def start(self, key, stage):
        bit = self.bits[stage]
        self.came[key + bit] = [self.mail.post(ref, ref, bit) for ref in self.views(key)]

    def start_from(self, key, first):
        for stage in range(first, len(self.bits)):
            self.start(key, stage)

    def pass_on(self, stage):
        for low in range(2**stage):
            key = sum(b for i, b in enumerate(self.bits[:stage]) if low >> i & 1) + self.bits[stage]
            for later in range(stage + 1, len(self.bits)):
                self.came[key + self.bits[later]] = []
            for copy, ref in zip(self.came[key], self.views(key)):
                copy.wait_recv()
                for later in range(stage + 1, len(self.bits)):
                    bit = self.bits[later]
                    self.came[key + bit].append(self.mail.post(ref, ref, bit))
            self.came[key] = []

    def pass_all(self):
        for stage in range(len(self.bits) - 1):
            self.pass_on(stage)

    def done(self):
        for copies in self.came.values():
            for copy in copies:
                copy.wait_recv()


class Share:
    def __init__(self, mail, whole, own):
        self.mail, self.whole, self.own = mail, whole, own
        self.half = own.shape[0] // 2

    def first(self):
        ring = self.mail.ring
        self.from_a = self.mail.post(self.own, self.whole.at[1], ring.bit_a)
        self.from_b = self.mail.post(self.own, self.whole.at[2], ring.bit_b)
        self.core = [self.mail.post(self.own, self.whole.at[QUAD], ring.bit_core)]

    def second(self):
        ring = self.mail.ring
        top, end = pl.ds(0, self.half), pl.ds(self.half, self.half)
        self.from_a.wait_recv()
        self.one = self.mail.post(self.whole.at[1, top], self.whole.at[3, top], ring.bit_b)
        self.core.append(self.mail.post(self.whole.at[1], self.whole.at[QUAD + 1], ring.bit_core))
        self.from_b.wait_recv()
        self.two = self.mail.post(self.whole.at[2, end], self.whole.at[3, end], ring.bit_a)
        self.core.append(self.mail.post(self.whole.at[2], self.whole.at[QUAD + 2], ring.bit_core))

    def third(self):
        self.one.wait_recv()
        self.two.wait_recv()
        self.core.append(
            self.mail.post(self.whole.at[3], self.whole.at[QUAD + 3], self.mail.ring.bit_core)
        )

    def done(self):
        for copy in self.core:
            copy.wait_recv()


def head_mask(width, head):
    lanes = lax.broadcasted_iota(jnp.int32, (1, width), 1)
    return (lanes >= head * HEAD_DIM) & (lanes < (head + 1) * HEAD_DIM)


def turn(u, cosine, signed_sine):
    width = u.shape[-1]
    half = HEAD_DIM // 2
    lanes = lax.broadcasted_iota(jnp.int32, (1, width), 1)
    lower = lanes % HEAD_DIM < half
    turned = jnp.where(lower, pltpu.roll(u, width - half, 1), pltpu.roll(u, half, 1))
    return u * cosine + turned * signed_sine


def front_kernel(
    outer, inner, seq_len,
    x_ref, go_ref, factor_ref, gain_ref, wq_ref, wk_ref, wv_ref, cos_ref, sin_ref,
    wo_ref, wg_ref, wu_ref, wd_ref,
    act_one, w_qkv, w_o, q_out, k_out, v_out, att_out, resid_out, gains_out,
    act_two, dy, w_gu, w_d,
    cut, gain_in, far, core_in, near, own_sum, half_a, half_b, in_a, in_b, act_two_own, dy_own,
    send_sems, recv_sems, local_sems, far_send, far_recv,
):
    rows = wq_ref.shape[0]
    width = wq_ref.shape[1]
    hidden_rows = wd_ref.shape[0]
    narrow = width // (2 * QUAD)
    hidden = w_gu.shape[1] // 2
    ring = Ring(outer, inner, rows)
    mail = Mail(ring, send_sems, recv_sems, local_sems)
    ring.greet()
    bits = ring.data_bits
    flat = ring.flat

    def by_place(ref, size):
        return lambda key: [ref.at[pl.ds(pl.multiple_of(ring.place(ring.flip(flat, key)) * size, 16), size)]]

    def by_runs(ref):
        return lambda key: [
            ref.at[pl.ds(pl.multiple_of(start, 16), size)]
            for start, size in ring.runs(ring.flip(flat, key), rows)
        ]

    mine_o = w_o.at[pl.ds(pl.multiple_of(ring.place(flat) * rows, 16), rows)]
    mine_d = w_d.at[pl.ds(pl.multiple_of(ring.place(flat) * hidden_rows, 16), hidden_rows)]
    keep_o = mail.keep(wo_ref, mine_o)
    keep_d = mail.keep(wd_ref, mine_d)

    heads = ring.upper_size * ring.across
    chunk = HEAD_DIM
    for t in range(2 * QUAD):
        for j, ref in enumerate((wq_ref, wk_ref, wv_ref)):
            parts = []
            for y in range(ring.upper_size):
                for o in range(ring.across):
                    head = ((y * 2 + t // QUAD) * ring.across + o) * QUAD + t % QUAD
                    parts.append(ref[:, head * chunk : (head + 1) * chunk])
            cut[t, :, j * narrow : (j + 1) * narrow] = jnp.concatenate(parts, axis=1)
    here = pl.ds(pl.multiple_of(flat * rows, 16), rows)
    keep_qkv = mail.keep(cut.at[ring.team(flat)], w_qkv.at[here])
    qkv_swap = []
    for delta in ring.deltas[1:]:
        other = ring.flip(flat, delta)
        qkv_swap.append(mail.post(cut.at[ring.team(other)], w_qkv.at[here], delta))
    keep_o.wait()
    mail.kept = [c for c in mail.kept if c is not keep_o]
    spread_o = Spread(mail, by_place(w_o, rows), bits)
    spread_o.start_from(0, 0)

    block = ring.span * hidden_rows
    gu_swap = []
    for delta in ring.deltas:
        other = ring.flip(flat, delta)
        team = ring.team(other)
        pieces = []
        for j, ref in enumerate((wg_ref, wu_ref)):
            for y in range(ring.upper_size):
                for o in range(ring.across):
                    source = ((y * 2 + team // QUAD) * ring.across + o) * QUAD + team % QUAD
                    target = j * hidden + (y * ring.across + o) * block
                    src = ref.at[:, pl.ds(pl.multiple_of(source * block, 128), block)]
                    dst = w_gu.at[here, pl.ds(target, block)]
                    pieces.append(mail.post(src, dst, delta) if delta else mail.keep(src, dst))
        gu_swap.append(pieces)

    step = 0
    gains_out[...] = gain_ref[...]
    for bit in [ring.bit_core, ring.bit_a, ring.bit_b] + bits:
        copy = mail.post(gains_out, gain_in.at[step], bit)
        copy.wait()
        mail.sent = [c for c in mail.sent if c is not copy]
        gains_out[...] = gains_out[...] + gain_in[step]
        step += 1
    keep_qkv.wait()
    mail.kept = [c for c in mail.kept if c is not keep_qkv]
    for copy in qkv_swap:
        copy.wait_recv()
    spread_qkv = Spread(mail, by_runs(w_qkv), bits)
    spread_qkv.start_from(0, 0)

    size = act_one.shape[1]
    strip = 32

    def norm_one(i, carry):
        part = pl.ds(pl.multiple_of(i * strip, strip), strip)
        x = x_ref[part, :].astype(f32)
        inv = lax.rsqrt(jnp.mean(x * x, axis=-1, keepdims=True) + epsilon)
        act_one[0, part, :] = (x * inv * gains_out[0:1, :]).astype(bf16)
        dy_own[part, :] = (go_ref[part, :].astype(f32) * factor_ref[part, :]).astype(bf16)
        return carry

    lax.fori_loop(0, size // strip, norm_one, 0)
    share_one = Share(mail, act_one, act_one.at[0])
    share_one.first()
    mail.keep(dy_own, dy.at[0])
    share_one.second()
    spread_o.pass_all()
    share_one.third()
    share_dy = Share(mail, dy, dy_own)
    share_dy.first()
    spread_qkv.pass_all()
    keep_d.wait()
    mail.kept = [c for c in mail.kept if c is not keep_d]
    for index, pieces in enumerate(gu_swap):
        for copy in pieces:
            if index:
                copy.wait_recv()
            else:
                copy.wait()
                mail.kept = [c for c in mail.kept if c is not copy]
    spread_d = Spread(mail, by_place(w_d, hidden_rows), bits)
    spread_gu = Spread(mail, by_runs(w_gu), bits)
    spread_d.start_from(0, 0)
    spread_gu.start_from(0, 0)
    share_one.done()

    scale = HEAD_DIM**-0.5
    cosine, sine = cos_ref[...], sin_ref[...]
    per_block = act_one.shape[1] // seq_len

    def attend_block(place):
        qkv = jnp.dot(act_one[place], w_qkv[...], preferred_element_type=f32)
        causal = lax.broadcasted_iota(jnp.int32, (seq_len, seq_len), 1) <= lax.broadcasted_iota(
            jnp.int32, (seq_len, seq_len), 0
        )
        for b in range(per_block):
            span = slice(b * seq_len, (b + 1) * seq_len)
            q = turn(qkv[span, :narrow], cosine, sine).astype(bf16)
            k = turn(qkv[span, narrow : 2 * narrow], cosine, sine).astype(bf16)
            v = qkv[span, 2 * narrow :].astype(bf16)
            q_out[place, span] = q
            k_out[place, span] = k
            v_out[place, span] = v
            mixed = jnp.zeros((seq_len, narrow), f32)
            for head in range(narrow // HEAD_DIM):
                mask = head_mask(narrow, head)
                kh = jnp.where(mask, k, jnp.zeros_like(k))
                vh = jnp.where(mask, v, jnp.zeros_like(v))
                scores = lax.dot_general(
                    q, kh, (((1,), (1,)), ((), ())), preferred_element_type=f32
                )
                scores = jnp.where(causal, scores * scale, -1e30)
                top = jnp.max(scores, axis=-1, keepdims=True)
                grown = jnp.exp(scores - top)
                soft = (grown / jnp.sum(grown, axis=-1, keepdims=True)).astype(bf16)
                mixed = mixed + jnp.dot(soft, vh, preferred_element_type=f32)
            att_out[place, span] = mixed.astype(bf16)
        return jnp.dot(att_out[place], w_o[...], preferred_element_type=f32)

    def far_copy(j):
        return pltpu.make_async_remote_copy(
            src_ref=far.at[j],
            dst_ref=core_in.at[j],
            send_sem=far_send.at[j],
            recv_sem=far_recv.at[j],
            device_id=ring.where(ring.bit_core),
            device_id_type=MESH,
        )

    spread_o.done()
    spread_qkv.done()

    def far_step(i, carry):
        j = QUAD - 1 - i
        far[j] = attend_block(QUAD + j).astype(bf16)
        far_copy(j).start()
        return carry

    lax.fori_loop(0, QUAD, far_step, 0)
    share_dy.second()

    def near_step(i, carry):
        j = QUAD - 1 - i
        part = attend_block(j)
        far_copy(j).wait_recv()
        own_sum[...] = part + core_in[j].astype(f32)
        near[j] = own_sum[...].astype(bf16)
        return carry

    lax.fori_loop(0, QUAD, near_step, 0)
    for j in range(QUAD):
        far_copy(j).wait_send()
    half = size // 2
    top, end = pl.ds(0, half), pl.ds(half, half)
    sum_one = mail.post(near.at[3, top], half_a, ring.bit_b)
    sum_two = mail.post(near.at[3, end], half_b, ring.bit_a)
    share_dy.third()
    sum_one.wait_recv()
    near[1, :half] = (near[1, :half].astype(f32) + half_a[...].astype(f32)).astype(bf16)
    for_a = mail.post(near.at[1], in_a, ring.bit_a)
    sum_two.wait_recv()
    near[2, half:] = (near[2, half:].astype(f32) + half_b[...].astype(f32)).astype(bf16)
    for_b = mail.post(near.at[2], in_b, ring.bit_b)
    spread_d.pass_on(0)
    for_a.wait_recv()
    for_b.wait_recv()

    def norm_two(i, carry):
        part = pl.ds(pl.multiple_of(i * strip, strip), strip)
        resid = (
            x_ref[part, :].astype(f32)
            + own_sum[part, :]
            + in_a[part, :].astype(f32)
            + in_b[part, :].astype(f32)
        )
        resid_out[part, :] = resid
        inv = lax.rsqrt(jnp.mean(resid * resid, axis=-1, keepdims=True) + epsilon)
        act_two_own[part, :] = (resid * inv * gains_out[1:2, :]).astype(bf16)
        return carry

    lax.fori_loop(0, size // strip, norm_two, 0)
    mail.keep(act_two_own, act_two.at[0])
    share_two = Share(mail, act_two, act_two_own)
    share_two.first()
    share_two.second()
    share_two.third()
    for stage in range(1, len(bits) - 1):
        spread_d.pass_on(stage)
    spread_gu.pass_all()
    spread_d.done()
    spread_gu.done()
    share_two.done()
    share_dy.done()
    mail.finish()


def front(outer, inner, batch_size, seq_len, tokens, grad_out, factor_rows, gain_rows, w_query, w_key, w_value, cosine, signed_sine, w_out, w_gate, w_up, w_down):
    size, width = tokens.shape
    rows, hidden_all = w_gate.shape
    hidden_rows = w_down.shape[0]
    narrow, hidden = width // (2 * QUAD), hidden_all // (2 * QUAD)
    span = max(1, HEAD_DIM // rows)
    places = outer * inner // (2 * QUAD)
    pieces = 2 if span == 1 else 2 * QUAD
    remote = 2 * (places - 1) * (pieces + 1) + 7 + 14 * places // span + 8 + 24 + 8
    local = 8 + 2 * places // span
    vm = pl.BlockSpec(memory_space=pltpu.VMEM)
    hbm = pl.BlockSpec(memory_space=pl.ANY)
    eight = (2 * QUAD, size)
    sds = jax.ShapeDtypeStruct
    out_shape = (
        sds(eight + (width,), bf16),
        sds((width, 3 * narrow), bf16),
        sds((narrow, width), bf16),
        sds(eight + (narrow,), bf16),
        sds(eight + (narrow,), bf16),
        sds(eight + (narrow,), bf16),
        sds(eight + (narrow,), bf16),
        sds((size, width), f32),
        sds((8, width), f32),
        sds(eight + (width,), bf16),
        sds(eight + (width,), bf16),
        sds((width, 2 * hidden), bf16),
        sds((hidden, width), bf16),
    )
    return pl.pallas_call(
        functools.partial(front_kernel, outer, inner, seq_len),
        out_shape=out_shape,
        in_specs=[vm] * 9 + [hbm] * 4,
        out_specs=tuple([vm] * 9 + [hbm] * 4),
        scratch_shapes=[
            pltpu.VMEM((2 * QUAD, rows, 3 * narrow), bf16),
            pltpu.VMEM((8, 8, width), f32),
            pltpu.VMEM((QUAD, size, width), bf16),
            pltpu.VMEM((QUAD, size, width), bf16),
            pltpu.VMEM((QUAD, size, width), bf16),
            pltpu.VMEM((size, width), f32),
            pltpu.VMEM((size // 2, width), bf16),
            pltpu.VMEM((size // 2, width), bf16),
            pltpu.VMEM((size, width), bf16),
            pltpu.VMEM((size, width), bf16),
            pltpu.VMEM((size, width), bf16),
            pltpu.VMEM((size, width), bf16),
            pltpu.SemaphoreType.DMA((remote,)),
            pltpu.SemaphoreType.DMA((remote,)),
            pltpu.SemaphoreType.DMA((local,)),
            pltpu.SemaphoreType.DMA((QUAD,)),
            pltpu.SemaphoreType.DMA((QUAD,)),
        ],
        compiler_params=pltpu.CompilerParams(
            collective_id=0, has_side_effects=True, vmem_limit_bytes=60 * 1024 * 1024
        ),
        name="front",
    )(tokens, grad_out, factor_rows, gain_rows, w_query, w_key, w_value, cosine, signed_sine, w_out, w_gate, w_up, w_down)


def add_far(target, left, right):
    rows, width = left.shape
    strip = min(64, rows)

    def body(left_ref, right_ref, target_ref):
        target_ref[...] = (left_ref[...].astype(f32) + right_ref[...].astype(f32)).astype(
            target_ref.dtype
        )

    spec = pl.BlockSpec((strip, width), lambda i: (i, 0))
    pltpu.emit_pipeline(body, grid=(rows // strip,), in_specs=[spec, spec], out_specs=[spec])(
        left, right, target
    )


def add_near(target, left, right):
    rows = left.shape[0]
    strip = min(32, rows)

    def step(i, carry):
        part = pl.ds(pl.multiple_of(i * strip, strip), strip)
        target[part, :] = (left[part, :].astype(f32) + right[part, :].astype(f32)).astype(
            target.dtype
        )
        return carry

    lax.fori_loop(0, rows // strip, step, 0)


def keys_below(bits, stage):
    return [
        sum(b for i, b in enumerate(bits[:stage]) if low >> i & 1) for low in range(2**stage)
    ]


class Collect:
    def __init__(self, mail, bits, views, landed, sums, last, add):
        self.mail, self.bits, self.views = mail, bits, views
        self.landed, self.sums, self.last, self.add = landed, sums, last, add
        self.came = {}
        self.added = set()
        self.pieces = len(views(0))

    def slot(self, stage, sub, piece):
        return (2**stage - 1 + keys_below(self.bits, stage).index(sub)) * self.pieces + piece

    def current(self, sub, piece):
        if (sub, piece) not in self.added:
            return self.views(sub)[piece]
        return self.sums.at[keys_below(self.bits, len(self.bits)).index(sub) * self.pieces + piece]

    def send(self, stage, sub, piece):
        bit = self.bits[stage]
        self.came[stage, sub, piece] = self.mail.post(
            self.current(bit + sub, piece), self.landed.at[self.slot(stage, sub, piece)], bit
        )

    def start(self, which=None):
        stage = len(self.bits) - 1
        for sub in reversed(keys_below(self.bits, stage)):
            if which is None or (sub != 0) == which:
                for piece in range(self.pieces):
                    self.send(stage, sub, piece)

    def take(self, stage, sub, piece):
        self.came[stage, sub, piece].wait_recv()
        here = self.current(sub, piece)
        landed = self.landed.at[self.slot(stage, sub, piece)]
        if stage == 0:
            self.add(self.last(piece), here, landed)
            return
        place = keys_below(self.bits, len(self.bits)).index(sub) * self.pieces + piece
        self.add(self.sums.at[place], here, landed)
        self.added.add((sub, piece))
        below = self.bits[stage - 1]
        if (sub // below) % 2:
            self.send(stage - 1, sub - below, piece)

    def take_away(self, stage, piece):
        below = self.bits[stage - 1]
        for sub in keys_below(self.bits, stage):
            if (sub // below) % 2:
                self.take(stage, sub, piece)

    def take_here(self, stage, piece):
        below = self.bits[stage - 1] if stage else 0
        for sub in keys_below(self.bits, stage):
            if not stage or not (sub // below) % 2:
                self.take(stage, sub, piece)

    def finish_piece(self, piece):
        top = len(self.bits) - 1
        for stage in range(top, -1, -1):
            if stage and stage != top:
                self.take_away(stage, piece)
            self.take_here(stage, piece)


class Total:
    def __init__(self, mail, near, own, half_a, half_b, in_a, in_b):
        self.mail, self.near, self.own = mail, near, own
        self.half_a, self.half_b, self.in_a, self.in_b = half_a, half_b, in_a, in_b
        self.half = near.shape[1] // 2
        self.top, self.end = pl.ds(0, self.half), pl.ds(self.half, self.half)

    def first(self):
        ring = self.mail.ring
        self.one = self.mail.post(self.near.at[3, self.top], self.half_a, ring.bit_b)
        self.two = self.mail.post(self.near.at[3, self.end], self.half_b, ring.bit_a)

    def second(self):
        ring = self.mail.ring
        self.one.wait_recv()
        part = self.near.at[1, self.top]
        add_near(part, part, self.half_a)
        self.for_a = self.mail.post(self.near.at[1], self.in_a, ring.bit_a)
        self.two.wait_recv()
        part = self.near.at[2, self.end]
        add_near(part, part, self.half_b)
        self.for_b = self.mail.post(self.near.at[2], self.in_b, ring.bit_b)

    def arrive(self):
        self.for_a.wait_recv()
        self.for_b.wait_recv()

    def value(self, part):
        return self.own[part, :] + self.in_a[part, :].astype(f32) + self.in_b[part, :].astype(f32)


def norm_back(total, base, gain):
    inv = lax.rsqrt(jnp.mean(base * base, axis=-1, keepdims=True) + epsilon)
    scaled = gain * total
    grads = inv * scaled - base * inv**3 * jnp.mean(scaled * base, axis=-1, keepdims=True)
    return grads, total * base * inv


def back_kernel(
    outer, inner, seq_len,
    x_ref, go_ref, factor_ref, gains_ref, q_ref, k_ref, v_ref, att_ref, w_qkv, w_o, cos_ref, sin_ref,
    p_gu, p_d, far_two, near_two, act_one, resid_ref,
    grad_tokens, out_q, out_k, out_v, out_o, gain_grads,
    out_gate, out_up, out_d, land_gu, land_d, sum_gu, sum_d, fin_gu,
    near, core_in, far, own_sum, grad_resid, branch,
    half_a, half_b, in_a, in_b,
    acts, d_qkv, p_qkv, p_o, p_o_sum, land_qkv, land_o, sum_qkv, sum_o, fin_qkv, qkv_in, gain_in,
    send_sems, recv_sems, local_sems, core_send, core_recv, far_send, far_recv, act_sems, near_sems,
):
    size, width = x_ref.shape
    rows = out_q.shape[0]
    hidden_rows = out_d.shape[0]
    narrow = w_o.shape[0]
    hidden = p_d.shape[0]
    ring = Ring(outer, inner, rows)
    mail = Mail(ring, send_sems, recv_sems, local_sems)
    ring.greet()
    bits = ring.data_bits
    flat = ring.flat
    strip = 32
    core_partner = ring.where(ring.bit_core)

    def strips(step):
        def run(i, carry):
            step(pl.ds(pl.multiple_of(i * strip, strip), strip))
            return carry

        lax.fori_loop(0, size // strip, run, 0)

    def by_place(ref, count):
        return lambda key: [
            ref.at[pl.ds(pl.multiple_of(ring.place(ring.flip(flat, key)) * count, 16), count)]
        ]

    def by_runs(ref):
        return lambda key: [
            ref.at[pl.ds(pl.multiple_of(start, 16), count)]
            for start, count in ring.runs(ring.flip(flat, key), rows)
        ]

    run_rows = ring.runs(flat, rows)[0][1]
    top_stage = len(bits) - 1
    collect_gu = Collect(
        mail, bits, by_runs(p_gu), land_gu, sum_gu,
        lambda piece: fin_gu.at[pl.ds(piece * run_rows, run_rows)], add_far,
    )
    collect_d = Collect(
        mail, bits, by_place(p_d, hidden_rows), land_d, sum_d, lambda piece: out_d, add_far
    )

    def core_copy(j):
        return pltpu.make_async_remote_copy(
            src_ref=far_two.at[j],
            dst_ref=core_in.at[j],
            send_sem=core_send.at[j],
            recv_sem=core_recv.at[j],
            device_id=core_partner,
            device_id_type=MESH,
        )

    load_resid = mail.keep(resid_ref, grad_resid)
    order = (3, 1, 2, 0)
    for j in order:
        core_copy(j).start()
        pltpu.make_async_copy(near_two.at[j], near.at[j], near_sems.at[j]).start()
    collect_gu.start(True)
    collect_d.start(True)
    collect_gu.start(False)
    collect_d.start(False)

    total_two = Total(mail, near, own_sum, half_a, half_b, in_a, in_b)
    for j in order:
        pltpu.make_async_copy(near_two.at[j], near.at[j], near_sems.at[j]).wait()
        core_copy(j).wait_recv()
        if j:
            add_near(near.at[j], near.at[j], core_in.at[j])
        else:
            add_near(own_sum, near.at[j], core_in.at[j])
        if j == 3:
            total_two.first()
    total_two.second()
    collect_gu.take_away(top_stage, 0)
    total_two.arrive()

    gain_grads[...] = jnp.zeros_like(gain_grads)
    load_resid.wait()
    mail.kept = [c for c in mail.kept if c is not load_resid]

    def second_norm(part):
        resid = grad_resid[part, :]
        grads, terms = norm_back(total_two.value(part), resid, gains_ref[1:2, :])
        grads = grads + go_ref[part, :].astype(f32) * factor_ref[part, :]
        grad_resid[part, :] = grads
        branch[0, part, :] = grads.astype(bf16)
        gain_grads[1:2, :] = gain_grads[1:2, :] + jnp.sum(terms, axis=0, keepdims=True)

    strips(second_norm)
    share = Share(mail, branch, branch.at[0])
    share.first()
    for piece in range(1, collect_gu.pieces):
        collect_gu.take_away(top_stage, piece)
    share.second()
    share.third()
    collect_d.take_away(top_stage, 0)
    p_o_sum[...] = jnp.zeros_like(p_o_sum)
    for j in range(QUAD):
        core_copy(j).wait_send()
    share.done()

    scale = HEAD_DIM**-0.5
    cosine, sine = cos_ref[...], sin_ref[...]
    per_block = size // seq_len

    def dot(left, right, left_dim, right_dim):
        return lax.dot_general(
            left, right, (((left_dim,), (right_dim,)), ((), ())), preferred_element_type=f32
        )

    def attend_block(place):
        grads = branch[place]
        grad_att = dot(grads, w_o[...], 1, 1).astype(bf16)
        p_o_sum[...] = p_o_sum[...] + dot(att_ref[place], grads, 0, 0)
        causal = lax.broadcasted_iota(jnp.int32, (seq_len, seq_len), 1) <= lax.broadcasted_iota(
            jnp.int32, (seq_len, seq_len), 0
        )
        for b in range(per_block):
            span = slice(b * seq_len, (b + 1) * seq_len)
            q, k, v = q_ref[place, span], k_ref[place, span], v_ref[place, span]
            ga = grad_att[span]
            dq = jnp.zeros((seq_len, narrow), f32)
            dk = jnp.zeros((seq_len, narrow), f32)
            dv = jnp.zeros((seq_len, narrow), f32)
            for head in range(narrow // HEAD_DIM):
                mask = head_mask(narrow, head)
                kh = jnp.where(mask, k, jnp.zeros_like(k))
                vh = jnp.where(mask, v, jnp.zeros_like(v))
                qh = jnp.where(mask, q, jnp.zeros_like(q))
                gh = jnp.where(mask, ga, jnp.zeros_like(ga))
                scores = jnp.where(causal, dot(q, kh, 1, 1) * scale, -1e30)
                grown = jnp.exp(scores - jnp.max(scores, axis=-1, keepdims=True))
                soft = grown / jnp.sum(grown, axis=-1, keepdims=True)
                grad_soft = dot(ga, vh, 1, 1)
                grad_scores = (
                    soft * (grad_soft - jnp.sum(soft * grad_soft, axis=-1, keepdims=True))
                ).astype(bf16)
                dq = dq + dot(grad_scores, kh, 1, 0)
                dk = dk + dot(grad_scores, qh, 0, 0)
                dv = dv + dot(soft.astype(bf16), gh, 0, 0)
            d_qkv[place, span, :narrow] = turn(dq * scale, cosine, -sine).astype(bf16)
            d_qkv[place, span, narrow : 2 * narrow] = turn(dk * scale, cosine, -sine).astype(bf16)
            d_qkv[place, span, 2 * narrow :] = dv.astype(bf16)
        return dot(d_qkv[place], w_qkv[...], 1, 1)

    def far_copy(j):
        return pltpu.make_async_remote_copy(
            src_ref=far.at[j % 2],
            dst_ref=core_in.at[j],
            send_sem=far_send.at[j],
            recv_sem=far_recv.at[j],
            device_id=core_partner,
            device_id_type=MESH,
        )

    def far_step(i, carry):
        j = QUAD - 1 - i
        part = attend_block(QUAD + j).astype(bf16)

        @pl.when(i >= 2)
        def _():
            far_copy(j + 2).wait_send()

        far[j % 2] = part
        far_copy(j).start()
        return carry

    lax.fori_loop(0, QUAD, far_step, 0)
    for j in range(2):
        far_copy(j).wait_send()
    for copy in (total_two.one, total_two.two, total_two.for_a, total_two.for_b):
        copy.wait_send()
        mail.sent = [c for c in mail.sent if c is not copy]

    def near_step(i, carry):
        j = QUAD - 1 - i
        part = attend_block(j)
        far_copy(j).wait_recv()
        own_sum[...] = part + core_in[j].astype(f32)
        near[j] = own_sum[...].astype(bf16)
        return carry

    lax.fori_loop(0, QUAD, near_step, 0)
    total_one = Total(mail, near, own_sum, half_a, half_b, in_a, in_b)
    total_one.first()

    collect_o = Collect(
        mail, bits, by_place(p_o, rows), land_o, sum_o, lambda piece: out_o, add_near
    )
    collect_qkv = Collect(
        mail, bits, by_runs(p_qkv), land_qkv, sum_qkv,
        lambda piece: fin_qkv.at[pl.ds(piece * run_rows, run_rows)], add_near,
    )
    p_o[...] = p_o_sum[...].astype(bf16)
    collect_o.start()
    cut = acts.shape[3]
    cuts = width // cut
    shift = (1 - flat // (ring.count // 2)) * (cuts // 2)

    def chunk_at(i):
        return pl.multiple_of(((i + shift) % cuts) * cut, cut)

    def act_copy(i):
        return pltpu.make_async_copy(
            act_one.at[:, :, pl.ds(chunk_at(i), cut)], acts.at[i % 2], act_sems.at[i % 2]
        )

    act_copy(0).start()

    def chunk_step(i, carry):
        act_copy(i).wait()

        @pl.when(i + 1 < cuts)
        def _():
            act_copy(i + 1).start()

        left = acts[i % 2].reshape(2 * QUAD * size, cut)
        right = d_qkv[...].reshape(2 * QUAD * size, 3 * narrow)
        p_qkv[pl.ds(chunk_at(i), cut), :] = dot(left, right, 0, 0).astype(bf16)
        return carry

    lax.fori_loop(0, cuts // 2, chunk_step, 0)
    collect_qkv.start()
    total_one.second()
    lax.fori_loop(cuts // 2, cuts, chunk_step, 0)

    for piece in range(collect_gu.pieces):
        collect_gu.finish_piece(piece)
    block = ring.span * hidden_rows
    gu_swap = []
    team = ring.team(flat)
    for delta in ring.deltas:
        other = ring.team(ring.flip(flat, delta))
        part = pl.ds(pl.multiple_of(other * rows, 16), rows)
        for j, ref in enumerate((out_gate, out_up)):
            for y in range(ring.upper_size):
                for o in range(ring.across):
                    target = ((y * 2 + team // QUAD) * ring.across + o) * QUAD + team % QUAD
                    source = j * hidden + (y * ring.across + o) * block
                    src = fin_gu.at[part, pl.ds(source, block)]
                    dst = ref.at[:, pl.ds(pl.multiple_of(target * block, 128), block)]
                    if delta:
                        gu_swap.append(mail.post(src, dst, delta))
                    else:
                        mail.keep(src, dst)

    total_one.arrive()

    def first_norm(part):
        x = x_ref[part, :].astype(f32)
        grads, terms = norm_back(total_one.value(part), x, gains_ref[0:1, :])
        grad_tokens[part, :] = grad_resid[part, :] + grads
        gain_grads[0:1, :] = gain_grads[0:1, :] + jnp.sum(terms, axis=0, keepdims=True)

    strips(first_norm)
    collect_d.finish_piece(0)

    collect_o.take_away(top_stage, 0)
    for piece in range(collect_qkv.pieces):
        collect_qkv.take_away(top_stage, piece)
    for step, bit in enumerate([ring.bit_core, ring.bit_a, ring.bit_b] + bits):
        copy = mail.post(gain_grads, gain_in.at[step], bit)
        copy.wait()
        mail.sent = [c for c in mail.sent if c is not copy]
        gain_grads[...] = gain_grads[...] + gain_in[step]
    for piece in range(collect_qkv.pieces):
        collect_qkv.finish_piece(piece)
    collect_o.finish_piece(0)

    swaps = []
    for delta in ring.deltas:
        other = ring.team(ring.flip(flat, delta))
        src = fin_qkv.at[pl.ds(pl.multiple_of(other * rows, 16), rows)]
        dst = qkv_in.at[team]
        if delta:
            swaps.append(mail.post(src, dst, delta))
        else:
            kept = mail.keep(src, dst)
    kept.wait()
    mail.kept = [c for c in mail.kept if c is not kept]
    for copy in swaps:
        copy.wait_recv()
    for j, ref in enumerate((out_q, out_k, out_v)):
        parts = []
        for y in range(ring.upper_size):
            for c in range(2):
                for o in range(ring.across):
                    for q in range(QUAD):
                        start = j * narrow + (y * ring.across + o) * HEAD_DIM
                        parts.append(qkv_in[c * QUAD + q, :, start : start + HEAD_DIM])
        ref[...] = jnp.concatenate(parts, axis=1).astype(f32)
    for copy in gu_swap:
        copy.wait_recv()
    mail.finish()


def back(outer, inner, seq_len, near_args, far_args):
    tokens, w_qkv, w_o = near_args[0], near_args[8], near_args[9]
    p_gu, p_d = far_args[0], far_args[1]
    size, width = tokens.shape
    narrow = w_o.shape[0]
    hidden = p_d.shape[0]
    places = outer * inner // (2 * QUAD)
    rows = width // (outer * inner)
    hidden_rows = hidden // places
    span = max(1, HEAD_DIM // rows)
    pieces = 2 if span == 1 else 2 * QUAD
    run_rows = 2 * QUAD * rows // pieces
    remote = 2 * (places - 1) * (pieces + 1) + 7 + 14 * places // span + 8 + 24
    local = 8 + 2 * places // span
    vm = pl.BlockSpec(memory_space=pltpu.VMEM)
    hbm = pl.BlockSpec(memory_space=pl.ANY)
    sds = jax.ShapeDtypeStruct
    out_shape = (
        sds((size, width), f32),
        sds((rows, width), f32),
        sds((rows, width), f32),
        sds((rows, width), f32),
        sds((rows, width), f32),
        sds((8, width), f32),
        sds((rows, 2 * QUAD * hidden), bf16),
        sds((rows, 2 * QUAD * hidden), bf16),
        sds((hidden_rows, width), f32),
        sds(((places - 1) * pieces, run_rows, 2 * hidden), bf16),
        sds((places - 1, hidden_rows, width), bf16),
        sds((places // 2 * pieces, run_rows, 2 * hidden), bf16),
        sds((places // 2, hidden_rows, width), bf16),
        sds((2 * QUAD * rows, 2 * hidden), bf16),
    )
    wide = pltpu.VMEM((size, width), bf16)
    half = pltpu.VMEM((size // 2, width), bf16)
    four = pltpu.VMEM((QUAD, size, width), bf16)
    cut = min(256, width // 2)
    four_sems = pltpu.SemaphoreType.DMA((QUAD,))
    return pl.pallas_call(
        functools.partial(back_kernel, outer, inner, seq_len),
        out_shape=out_shape,
        in_specs=[vm] * len(near_args) + [hbm] * len(far_args),
        out_specs=tuple([vm] * 6 + [hbm] * 8),
        scratch_shapes=[
            four, four, pltpu.VMEM((2, size, width), bf16),
            pltpu.VMEM((size, width), f32),
            pltpu.VMEM((size, width), f32),
            pltpu.VMEM((2 * QUAD, size, width), bf16),
            half, half, wide, wide,
            pltpu.VMEM((2, 2 * QUAD, size, cut), bf16),
            pltpu.VMEM((2 * QUAD, size, 3 * narrow), bf16),
            pltpu.VMEM((width, 3 * narrow), bf16),
            pltpu.VMEM((narrow, width), bf16),
            pltpu.VMEM((narrow, width), f32),
            pltpu.VMEM(((places - 1) * pieces, run_rows, 3 * narrow), bf16),
            pltpu.VMEM((places - 1, rows, width), bf16),
            pltpu.VMEM((places // 2 * pieces, run_rows, 3 * narrow), bf16),
            pltpu.VMEM((places // 2, rows, width), bf16),
            pltpu.VMEM((2 * QUAD * rows, 3 * narrow), bf16),
            pltpu.VMEM((2 * QUAD, rows, 3 * narrow), bf16),
            pltpu.VMEM((8, 8, width), f32),
            pltpu.SemaphoreType.DMA((remote,)),
            pltpu.SemaphoreType.DMA((remote,)),
            pltpu.SemaphoreType.DMA((local,)),
            four_sems, four_sems, four_sems, four_sems,
            pltpu.SemaphoreType.DMA((2,)),
            four_sems,
        ],
        compiler_params=pltpu.CompilerParams(
            collective_id=1, has_side_effects=True, vmem_limit_bytes=63 * 1024 * 1024
        ),
        name="back",
    )(*near_args, *far_args)


def on_device(
    tokens,
    labels,
    counts,
    grad_out,
    w_query,
    w_key,
    w_value,
    w_out,
    gain_attn,
    gain_mlp,
    w_gate,
    w_up,
    w_down,
):
    batch_size, seq_len, width = tokens.shape
    outer_count = lax.axis_size("dp")
    inner_count = lax.axis_size("fsdp")
    rows = w_query.shape[0]
    hidden_rows = w_down.shape[0]
    plan = Plan(outer_count, inner_count, rows)
    x_rows = tokens.reshape(-1, width)

    token_total = float(seq_len * batch_size * outer_count * inner_count)
    picked_counts = jnp.sum(
        jnp.where(labels[:, None] == jnp.arange(3)[None, :], counts[None, :], 0), axis=1
    ).astype(f32)
    factor = token_total / (3.0 * picked_counts)
    cosine, sine = rope_tables(seq_len, HEAD_DIM)
    head_count = width // (2 * QUAD) // HEAD_DIM
    sign = jnp.where(jnp.arange(HEAD_DIM) < HEAD_DIM // 2, -1.0, 1.0)
    wide_cosine = jnp.tile(cosine, (1, head_count))
    wide_sine = jnp.tile(sine * sign, (1, head_count))
    gain_rows = lax.dynamic_update_slice(
        jnp.zeros((8, width), f32),
        jnp.stack([gain_attn, gain_mlp]).astype(f32),
        (0, plan.flat * rows),
    )
    factor_rows = jnp.repeat(factor, seq_len)[:, None]
    (
        act_one, w_qkv, w_o, q_rot, k_rot, values, attended, resid, gains, act_two, dy, w_gu, w_d,
    ) = front(
        outer_count, inner_count, batch_size, seq_len,
        x_rows, grad_out.reshape(-1, width), factor_rows, gain_rows,
        w_query, w_key, w_value,
        wide_cosine, wide_sine,
        w_out, w_gate, w_up, w_down,
    )
    narrow = w_o.shape[0]
    hidden = w_d.shape[0]
    act_two, dy = (a.reshape(-1, width) for a in (act_two, dy))
    gu = mm(act_two, w_gu)
    gate_pre, up_proj = gu[:, :hidden], gu[:, hidden:]
    sigmoid_gate = jax.nn.sigmoid(gate_pre)
    middle = (gate_pre * sigmoid_gate * up_proj).astype(bf16)

    grad_middle = times_transposed(dy, w_d)
    grad_gate_pre = (
        grad_middle * up_proj * sigmoid_gate * (1.0 + gate_pre * (1.0 - sigmoid_gate))
    ).astype(bf16)
    grad_up_proj = (grad_middle * gate_pre * sigmoid_gate).astype(bf16)
    grad_gu_cols = jnp.concatenate([grad_gate_pre, grad_up_proj], axis=1)

    count = middle.shape[0] // 2
    four_blocks = (QUAD, -1, width)
    far_two = times_transposed(grad_gu_cols[count:], w_gu).astype(bf16).reshape(four_blocks)
    near_two = times_transposed(grad_gu_cols[:count], w_gu).astype(bf16).reshape(four_blocks)
    p_d = outer_sum(middle, dy).astype(bf16)
    p_gu = outer_sum(act_two, grad_gu_cols).astype(bf16)
    layer_out = (
        (resid + plan.sum_tokens(middle, lambda part: mm(part, w_d)))
        .astype(bf16)
        .reshape(tokens.shape)
    )
    p_gu, layer_out = lax.optimization_barrier((p_gu, layer_out))
    results = back(
        outer_count, inner_count, seq_len,
        (
            x_rows, grad_out.reshape(-1, width), factor_rows, gains, q_rot, k_rot, values, attended,
            w_qkv, w_o, wide_cosine, wide_sine,
        ),
        (p_gu, p_d, far_two, near_two, act_one, resid),
    )
    grad_tokens, query_grad, key_grad, value_grad, out_grad, gain_grads = results[:6]
    gate_grad, up_grad, down_grad = (a.astype(f32) for a in results[6:9])
    gain_grads = lax.dynamic_slice(gain_grads, (0, plan.flat * rows), (2, rows))
    return (
        layer_out,
        grad_tokens.reshape(tokens.shape),
        query_grad,
        key_grad,
        value_grad,
        out_grad,
        gain_grads[0],
        gain_grads[1],
        gate_grad,
        up_grad,
        down_grad,
    )


def solution(mesh):
    rows = P(AXES, None)
    vector = P(AXES)
    three = P(AXES, None, None)
    in_specs = (three, vector, P(), three, rows, rows, rows, rows, vector, vector, rows, rows, rows)
    out_specs = (three, three, rows, rows, rows, rows, vector, vector, rows, rows, rows)
    return jax.shard_map(
        on_device, mesh=mesh, in_specs=in_specs, out_specs=out_specs, check_vma=False
    )
```

```python
import functools

import jax
import jax.numpy as jnp
from jax import lax
from jax.experimental import pallas as pl
from jax.experimental.pallas import tpu as pltpu
from jax.sharding import PartitionSpec as P

HEAD_DIM = 64
AXES = ("dp", "fsdp")
QUAD = 4

epsilon = 1e-05
rope_base = 130000.0
bf16 = jnp.bfloat16
f32 = jnp.float32
MESH = pl.DeviceIdType.MESH


def rope_tables(seq_len, head_dim):
    half_dim = head_dim // 2
    frequency = rope_base ** (-(jnp.arange(half_dim).astype(f32) * 2.0) / head_dim)
    angles = jnp.arange(seq_len).astype(f32)[:, None] * frequency[None, :]
    angles = jnp.concatenate([angles, angles], axis=1)
    return (jnp.cos(angles), jnp.sin(angles))


def mm(left, right):
    return jnp.dot(left, right, preferred_element_type=f32)


def outer_sum(left, right):
    return lax.dot_general(left, right, (((0,), (0,)), ((), ())), preferred_element_type=f32)


def times_transposed(left, weight):
    return lax.dot_general(left, weight, (((1,), (1,)), ((), ())), preferred_element_type=f32)


class Plan:
    def __init__(self, outer, inner, rows):
        self.count = outer * inner
        self.bit_a = max(1, HEAD_DIM // rows)
        self.bit_b = 2 * self.bit_a
        self.bit_core = inner
        self.flat = lax.axis_index("dp") * inner + lax.axis_index("fsdp")

    def send(self, array, bit):
        return lax.ppermute(array, AXES, [(r, r ^ bit) for r in range(self.count)])

    def sum_upper(self, total):
        bit = self.count // 2
        rows = total.shape[0] // 2
        here = (self.flat // bit) % 2
        away = lax.dynamic_slice_in_dim(total, (1 - here) * rows, rows, 0)
        kept = lax.dynamic_slice_in_dim(total, here * rows, rows, 0)
        return (kept.astype(f32) + self.send(away, bit).astype(f32)).astype(bf16)

    def sum_four(self, near, core):
        size = near.shape[0] // QUAD
        half = size // 2
        own, for_a, for_b, for_ab = (
            near[i * size : (i + 1) * size] + core[i * size : (i + 1) * size].astype(f32)
            for i in range(QUAD)
        )
        first = self.send(for_ab[:half].astype(bf16), self.bit_b)
        second = self.send(for_ab[half:].astype(bf16), self.bit_a)
        for_a = jnp.concatenate([for_a[:half] + first.astype(f32), for_a[half:]]).astype(bf16)
        for_b = jnp.concatenate([for_b[:half], for_b[half:] + second.astype(f32)]).astype(bf16)
        return (
            own
            + self.send(for_a, self.bit_a).astype(f32)
            + self.send(for_b, self.bit_b).astype(f32)
        )


class Ring:
    def __init__(self, outer, inner, rows):
        self.count = outer * inner
        self.inner = inner
        self.span = max(1, HEAD_DIM // rows)
        self.bit_a = self.span
        self.bit_b = 2 * self.span
        self.bit_core = inner
        self.low = powers(1, self.span)
        self.mid = powers(QUAD * self.span, inner)
        self.upper = powers(2 * inner, self.count)
        self.data_bits = self.low + self.mid + self.upper
        self.deltas = [
            (self.bit_core if t // QUAD else 0) + (t % QUAD) * self.span for t in range(2 * QUAD)
        ]
        self.across = inner // (QUAD * self.span)
        self.upper_size = outer // 2
        self.flat = lax.axis_index("dp") * inner + lax.axis_index("fsdp")

    def flip(self, flat, bits):
        bit = 1
        while bit <= bits:
            if bits & bit:
                flat = flat + bit * (1 - 2 * ((flat // bit) % 2))
            bit *= 2
        return flat

    def where(self, bits):
        other = self.flip(self.flat, bits)
        return (other // self.inner, other % self.inner)

    def team(self, flat):
        return ((flat // self.inner) % 2) * QUAD + (flat // self.span) % QUAD

    def place(self, flat):
        return (
            (flat // (2 * self.inner)) * self.across + (flat % self.inner) // (QUAD * self.span)
        ) * self.span + flat % self.span

    def runs(self, flat, rows):
        lowest = flat - self.span * ((flat // self.span) % QUAD)
        lowest = lowest - self.inner * ((flat // self.inner) % 2)
        found = []
        for core in range(2):
            start = lowest + core * self.inner
            if self.span == 1:
                found.append((start * rows, QUAD * rows))
            else:
                found += [((start + q * self.span) * rows, rows) for q in range(QUAD)]
        return found

    def greet(self):
        partners = self.deltas[1:] + self.data_bits
        barrier = pltpu.get_barrier_semaphore()
        for bits in partners:
            pl.semaphore_signal(barrier, 1, device_id=self.where(bits), device_id_type=MESH)
        pl.semaphore_wait(barrier, len(partners))


def powers(first, end):
    found = []
    while first < end:
        found.append(first)
        first *= 2
    return found


class Mail:
    def __init__(self, ring, send_sems, recv_sems, local_sems):
        self.ring, self.send_sems, self.recv_sems, self.local_sems = ring, send_sems, recv_sems, local_sems
        self.used = 0
        self.used_local = 0
        self.sent = []
        self.kept = []

    def post(self, src, dst, bits):
        copy = pltpu.make_async_remote_copy(
            src_ref=src,
            dst_ref=dst,
            send_sem=self.send_sems.at[self.used],
            recv_sem=self.recv_sems.at[self.used],
            device_id=self.ring.where(bits),
            device_id_type=MESH,
        )
        self.used += 1
        copy.start()
        self.sent.append(copy)
        return copy

    def keep(self, src, dst):
        copy = pltpu.make_async_copy(src, dst, self.local_sems.at[self.used_local])
        self.used_local += 1
        copy.start()
        self.kept.append(copy)
        return copy

    def drop(self, copy):
        self.sent = [c for c in self.sent if c is not copy]

    def finish(self):
        for copy in self.sent:
            copy.wait_send()
        for copy in self.kept:
            copy.wait()


class Spread:
    def __init__(self, mail, views, bits):
        self.mail, self.views, self.bits = mail, views, bits
        self.pieces = len(views(0))
        self.came = {}

    def start(self, key, piece, first):
        ref = self.views(key)[piece]
        for bit in self.bits[first:]:
            self.came[key + bit, piece] = self.mail.post(ref, ref, bit)

    def begin(self, piece=None):
        for p in range(self.pieces) if piece is None else (piece,):
            self.start(0, p, 0)

    def pass_on(self, stage, piece=None):
        for p in range(self.pieces) if piece is None else (piece,):
            for key in keys_below(self.bits, stage):
                key += self.bits[stage]
                self.came.pop((key, p)).wait_recv()
                self.start(key, p, stage + 1)

    def pass_all(self, piece=None):
        for stage in range(len(self.bits) - 1):
            self.pass_on(stage, piece)

    def done(self):
        for copy in self.came.values():
            copy.wait_recv()


def keys_below(bits, stage):
    return [
        sum(b for i, b in enumerate(bits[:stage]) if low >> i & 1) for low in range(2**stage)
    ]


class Adding:
    def __init__(self, mail, ref, came_in, bits):
        self.mail, self.ref, self.came_in, self.bits = mail, ref, came_in, bits
        self.step = 0

    def post(self):
        self.copy = self.mail.post(
            self.ref, self.came_in.at[self.step], self.bits[self.step]
        )

    def take(self):
        self.copy.wait()
        self.mail.drop(self.copy)
        self.ref[...] = self.ref[...] + self.came_in[self.step]
        self.step += 1


class Share:
    def __init__(self, mail, whole, own):
        self.mail, self.whole, self.own = mail, whole, own
        self.core = []

    def first_core(self):
        self.to_core(self.own, 0)

    def first_a(self):
        self.from_a = self.mail.post(self.own, self.whole.at[1], self.mail.ring.bit_a)

    def first_b(self):
        self.from_b = self.mail.post(self.own, self.whole.at[2], self.mail.ring.bit_b)

    def first(self):
        self.first_a()
        self.first_b()
        self.first_core()

    def to_core(self, ref, place):
        self.core.append(
            self.mail.post(ref, self.whole.at[QUAD + place], self.mail.ring.bit_core)
        )

    def second_a(self):
        self.from_a.wait_recv()
        self.to_core(self.whole.at[1], 1)

    def second_b(self):
        self.from_b.wait_recv()
        self.both = self.mail.post(self.whole.at[2], self.whole.at[3], self.mail.ring.bit_a)
        self.to_core(self.whole.at[2], 2)

    def second(self):
        self.second_a()
        self.second_b()

    def third(self):
        self.both.wait_recv()
        self.to_core(self.whole.at[3], 3)

    def done(self, places=range(QUAD)):
        for place in places:
            self.core[place].wait_recv()


def add_near(target, left, right):
    rows = left.shape[0]
    strip = min(32, rows)

    def step(i, carry):
        part = pl.ds(pl.multiple_of(i * strip, strip), strip)
        target[part, :] = (left[part, :].astype(f32) + right[part, :].astype(f32)).astype(
            target.dtype
        )
        return carry

    lax.fori_loop(0, rows // strip, step, 0)


class Total:
    def __init__(self, mail, near, own, mid, in_a, in_b):
        self.mail, self.near, self.own = mail, near, own
        self.mid, self.in_a, self.in_b = mid, in_a, in_b

    def first(self):
        self.over = self.mail.post(self.near.at[3], self.mid, self.mail.ring.bit_a)

    def first_a(self):
        self.for_a = self.mail.post(self.near.at[1], self.in_a, self.mail.ring.bit_a)

    def second(self):
        self.over.wait_recv()
        add_near(self.near.at[2], self.near.at[2], self.mid)
        self.for_b = self.mail.post(self.near.at[2], self.in_b, self.mail.ring.bit_b)

    def arrive(self):
        self.for_a.wait_recv()
        self.for_b.wait_recv()

    def value(self, part):
        return self.own[part, :] + self.in_a[part, :].astype(f32) + self.in_b[part, :].astype(f32)


def head_mask(width, head):
    lanes = lax.broadcasted_iota(jnp.int32, (1, width), 1)
    return (lanes >= head * HEAD_DIM) & (lanes < (head + 1) * HEAD_DIM)


def turn(u, cosine, signed_sine):
    width = u.shape[-1]
    half = HEAD_DIM // 2
    lanes = lax.broadcasted_iota(jnp.int32, (1, width), 1)
    lower = lanes % HEAD_DIM < half
    turned = jnp.where(lower, pltpu.roll(u, width - half, 1), pltpu.roll(u, half, 1))
    return u * cosine + turned * signed_sine


def front_kernel(
    outer, inner, seq_len,
    x_ref, gain_ref, wq_ref, wk_ref, wv_ref, cos_ref, sin_ref,
    wo_ref, wg_ref, wu_ref, wd_ref,
    act_one, w_qkv, w_o, q_out, k_out, v_out, att_out, resid_out, gains_out,
    act_two, w_g, w_u, w_d,
    cut, gain_in, x_all, far, core_in, near, own_sum, mid, in_a, in_b, act_two_own,
    send_sems, recv_sems, local_sems, far_send, far_recv,
):
    rows = wq_ref.shape[0]
    width = wq_ref.shape[1]
    hidden_rows = wd_ref.shape[0]
    narrow = width // (2 * QUAD)
    ring = Ring(outer, inner, rows)
    mail = Mail(ring, send_sems, recv_sems, local_sems)
    ring.greet()
    bits = ring.data_bits
    flat = ring.flat

    def by_place(ref, size, pieces):
        step = size // pieces
        return lambda key: [
            ref.at[
                pl.ds(
                    pl.multiple_of(ring.place(ring.flip(flat, key)) * size + p * step, 16), step
                )
            ]
            for p in range(pieces)
        ]

    def by_runs(ref):
        return lambda key: [
            ref.at[pl.ds(pl.multiple_of(start, 16), size)]
            for start, size in ring.runs(ring.flip(flat, key), rows)
        ]

    def settle(copy):
        copy.wait()
        mail.kept = [c for c in mail.kept if c is not copy]

    mine_o = w_o.at[pl.ds(pl.multiple_of(ring.place(flat) * rows, 16), rows)]
    mine_d = w_d.at[pl.ds(pl.multiple_of(ring.place(flat) * hidden_rows, 16), hidden_rows)]
    keep_o = mail.keep(wo_ref, mine_o)
    keep_d = mail.keep(wd_ref, mine_d)
    keep_x = mail.keep(x_ref, x_all.at[0])

    chunk = HEAD_DIM
    for t in range(2 * QUAD):
        for j, ref in enumerate((wq_ref, wk_ref, wv_ref)):
            parts = []
            for y in range(ring.upper_size):
                for o in range(ring.across):
                    head = ((y * 2 + t // QUAD) * ring.across + o) * QUAD + t % QUAD
                    parts.append(ref[:, head * chunk : (head + 1) * chunk])
            cut[t, :, j * narrow : (j + 1) * narrow] = jnp.concatenate(parts, axis=1)
    here = pl.ds(pl.multiple_of(flat * rows, 16), rows)
    keep_qkv = mail.keep(cut.at[ring.team(flat)], w_qkv.at[here])
    qkv_swap = []
    for delta in ring.deltas[1:]:
        other = ring.flip(flat, delta)
        qkv_swap.append(mail.post(cut.at[ring.team(other)], w_qkv.at[here], delta))

    gains_out[...] = gain_ref[...]
    gains = Adding(
        mail, gains_out, gain_in, [ring.bit_core, ring.bit_a, ring.bit_b] + bits
    )
    gains.post()
    settle(keep_o)
    spread_o = Spread(mail, by_place(w_o, rows, 1), bits)
    spread_o.begin()
    gains.take()
    gains.post()
    share_x = Share(mail, x_all, x_ref)
    share_x.first_core()
    share_x.first_a()
    settle(keep_qkv)
    for copy in qkv_swap:
        copy.wait_recv()
    spread_qkv = Spread(mail, by_runs(w_qkv), bits)
    spread_qkv.begin()
    gains.take()
    gains.post()
    share_x.first_b()
    spread_o.pass_all()

    gains.take()
    gains.post()
    share_x.second_a()
    for piece in range(spread_qkv.pieces):
        spread_qkv.pass_all(piece)
    while gains.step < len(gains.bits) - 1:
        gains.take()
        gains.post()
    spread_d = Spread(mail, by_place(w_d, hidden_rows, 2), bits)
    settle(keep_d)
    share_x.second_b()
    block = ring.span * hidden_rows
    gate_swap, up_swap = [], []
    for ref, whole, swap in ((wg_ref, w_g, gate_swap), (wu_ref, w_u, up_swap)):
        for delta in ring.deltas:
            team = ring.team(ring.flip(flat, delta))
            for y in range(ring.upper_size):
                for o in range(ring.across):
                    source = ((y * 2 + team // QUAD) * ring.across + o) * QUAD + team % QUAD
                    src = ref.at[:, pl.ds(pl.multiple_of(source * block, 128), block)]
                    dst = whole.at[here, pl.ds((y * ring.across + o) * block, block)]
                    if delta:
                        swap.append((mail.post(src, dst, delta), True))
                    else:
                        swap.append((mail.keep(src, dst), False))

    def swapped(swap):
        for copy, remote in swap:
            if remote:
                copy.wait_recv()
            else:
                settle(copy)

    spread_d.begin()
    gains.take()

    size = act_one.shape[1]
    strip = 32

    def norm_block(place):
        def norm_one(i, carry):
            part = pl.ds(pl.multiple_of(i * strip, strip), strip)
            x = x_all[place, part, :].astype(f32)
            inv = lax.rsqrt(jnp.mean(x * x, axis=-1, keepdims=True) + epsilon)
            act_one[place, part, :] = (x * inv * gains_out[0:1, :]).astype(bf16)
            return carry

        lax.fori_loop(0, size // strip, norm_one, 0)

    settle(keep_x)
    share_x.done(range(QUAD - 1))

    def norm_early(i, carry):
        norm_block(lax.rem(i, QUAD - 1) + QUAD * (i // (QUAD - 1)))
        return carry

    lax.fori_loop(0, 2 * (QUAD - 1), norm_early, 0)
    spread_o.done()
    spread_qkv.done()

    scale = HEAD_DIM**-0.5
    cosine, sine = cos_ref[...], sin_ref[...]
    per_block = act_one.shape[1] // seq_len

    def attend_block(place):
        qkv = jnp.dot(act_one[place], w_qkv[...], preferred_element_type=f32)
        causal = lax.broadcasted_iota(jnp.int32, (seq_len, seq_len), 1) <= lax.broadcasted_iota(
            jnp.int32, (seq_len, seq_len), 0
        )
        for b in range(per_block):
            span = slice(b * seq_len, (b + 1) * seq_len)
            q = turn(qkv[span, :narrow], cosine, sine).astype(bf16)
            k = turn(qkv[span, narrow : 2 * narrow], cosine, sine).astype(bf16)
            v = qkv[span, 2 * narrow :].astype(bf16)
            q_out[place, span] = q
            k_out[place, span] = k
            v_out[place, span] = v
            mixed = jnp.zeros((seq_len, narrow), f32)
            for head in range(narrow // HEAD_DIM):
                mask = head_mask(narrow, head)
                kh = jnp.where(mask, k, jnp.zeros_like(k))
                vh = jnp.where(mask, v, jnp.zeros_like(v))
                scores = lax.dot_general(
                    q, kh, (((1,), (1,)), ((), ())), preferred_element_type=f32
                )
                scores = jnp.where(causal, scores * scale, -1e30)
                top = jnp.max(scores, axis=-1, keepdims=True)
                grown = jnp.exp(scores - top)
                soft = (grown / jnp.sum(grown, axis=-1, keepdims=True)).astype(bf16)
                mixed = mixed + jnp.dot(soft, vh, preferred_element_type=f32)
            att_out[place, span] = mixed.astype(bf16)
        return jnp.dot(att_out[place], w_o[...], preferred_element_type=f32)

    def far_copy(j):
        return pltpu.make_async_remote_copy(
            src_ref=far.at[j],
            dst_ref=core_in.at[j],
            send_sem=far_send.at[j],
            recv_sem=far_recv.at[j],
            device_id=ring.where(ring.bit_core),
            device_id_type=MESH,
        )

    def far_step(j, carry):
        far[j] = attend_block(QUAD + j).astype(bf16)
        far_copy(j).start()
        return carry

    def near_step(j, carry):
        part = attend_block(j)
        far_copy(j).wait_recv()
        total = part + core_in[j].astype(f32)
        near[j] = total.astype(bf16)

        @pl.when(j == 0)
        def _():
            own_sum[...] = total

        return carry

    lax.fori_loop(0, QUAD - 1, far_step, 0)
    spread_g = Spread(mail, by_runs(w_g), bits)
    spread_u = Spread(mail, by_runs(w_u), bits)
    swapped(gate_swap)
    spread_g.begin()
    share_x.third()
    lax.fori_loop(0, QUAD - 1, near_step, 0)
    norm_block(QUAD - 1)
    share_x.done((QUAD - 1,))
    norm_block(2 * QUAD - 1)
    far_step(QUAD - 1, 0)
    near_step(QUAD - 1, 0)
    for j in range(QUAD):
        far_copy(j).wait_send()
    total = Total(mail, near, own_sum, mid, in_a, in_b)
    total.first()
    total.first_a()
    swapped(up_swap)
    spread_u.begin()
    for piece in range(spread_d.pieces):
        spread_d.pass_on(0, piece)
    total.second()
    spread_g.pass_on(0, 0)
    total.arrive()

    def norm_two(i, carry):
        part = pl.ds(pl.multiple_of(i * strip, strip), strip)
        resid = (
            x_ref[part, :].astype(f32) + total.value(part)
        )
        resid_out[part, :] = resid
        inv = lax.rsqrt(jnp.mean(resid * resid, axis=-1, keepdims=True) + epsilon)
        act_two_own[part, :] = (resid * inv * gains_out[1:2, :]).astype(bf16)
        return carry

    lax.fori_loop(0, size // strip, norm_two, 0)
    mail.keep(act_two_own, act_two.at[0])
    share_two = Share(mail, act_two, act_two_own)
    share_two.first()
    for piece in range(1, spread_g.pieces):
        spread_g.pass_on(0, piece)
    share_two.second()
    spread_u.pass_on(0)
    share_two.third()
    for stage in range(1, len(bits) - 1):
        for spread in (spread_d, spread_g, spread_u):
            spread.pass_on(stage)
    spread_d.done()
    spread_g.done()
    spread_u.done()
    share_two.done()
    mail.finish()


def front(outer, inner, seq_len, tokens, gain_rows, w_query, w_key, w_value, cosine, signed_sine, w_out, w_gate, w_up, w_down):
    size, width = tokens.shape
    rows, hidden_all = w_gate.shape
    hidden_rows = w_down.shape[0]
    narrow, hidden = width // (2 * QUAD), hidden_all // (2 * QUAD)
    span = max(1, HEAD_DIM // rows)
    places = outer * inner // (2 * QUAD)
    pieces = 2 if span == 1 else 2 * QUAD
    remote = (places - 1) * (3 * pieces + 3) + 7 + 14 * places // span + 8 + 24
    local = 8 + 2 * places // span
    vm = pl.BlockSpec(memory_space=pltpu.VMEM)
    hbm = pl.BlockSpec(memory_space=pl.ANY)
    eight = (2 * QUAD, size)
    sds = jax.ShapeDtypeStruct
    out_shape = (
        sds(eight + (width,), bf16),
        sds((width, 3 * narrow), bf16),
        sds((narrow, width), bf16),
        sds(eight + (narrow,), bf16),
        sds(eight + (narrow,), bf16),
        sds(eight + (narrow,), bf16),
        sds(eight + (narrow,), bf16),
        sds((size, width), f32),
        sds((8, width), f32),
        sds(eight + (width,), bf16),
        sds((width, hidden), bf16),
        sds((width, hidden), bf16),
        sds((hidden, width), bf16),
    )
    return pl.pallas_call(
        functools.partial(front_kernel, outer, inner, seq_len),
        out_shape=out_shape,
        in_specs=[vm] * 7 + [hbm] * 4,
        out_specs=tuple([vm] * 9 + [hbm] * 4),
        scratch_shapes=[
            pltpu.VMEM((2 * QUAD, rows, 3 * narrow), bf16),
            pltpu.VMEM((8, 8, width), f32),
            pltpu.VMEM((2 * QUAD, size, width), bf16),
            pltpu.VMEM((QUAD, size, width), bf16),
            pltpu.VMEM((QUAD, size, width), bf16),
            pltpu.VMEM((QUAD, size, width), bf16),
            pltpu.VMEM((size, width), f32),
            pltpu.VMEM((size, width), bf16),
            pltpu.VMEM((size, width), bf16),
            pltpu.VMEM((size, width), bf16),
            pltpu.VMEM((size, width), bf16),
            pltpu.SemaphoreType.DMA((remote,)),
            pltpu.SemaphoreType.DMA((remote,)),
            pltpu.SemaphoreType.DMA((local,)),
            pltpu.SemaphoreType.DMA((QUAD,)),
            pltpu.SemaphoreType.DMA((QUAD,)),
        ],
        compiler_params=pltpu.CompilerParams(
            collective_id=0, has_side_effects=True, vmem_limit_bytes=60 * 1024 * 1024
        ),
        name="front",
    )(tokens, gain_rows, w_query, w_key, w_value, cosine, signed_sine, w_out, w_gate, w_up, w_down)


def add_far(target, left, right):
    rows, width = left.shape
    strip = min(64, rows)

    def body(left_ref, right_ref, target_ref):
        target_ref[...] = (left_ref[...].astype(f32) + right_ref[...].astype(f32)).astype(
            target_ref.dtype
        )

    spec = pl.BlockSpec((strip, width), lambda i: (i, 0))
    pltpu.emit_pipeline(body, grid=(rows // strip,), in_specs=[spec, spec], out_specs=[spec])(
        left, right, target
    )


class Collect:
    def __init__(self, mail, bits, views, landed, sums, last, add):
        self.mail, self.bits, self.views = mail, bits, views
        self.landed, self.sums, self.last, self.add = landed, sums, last, add
        self.came = {}
        self.added = set()
        self.pieces = len(views(0))

    def slot(self, stage, sub, piece):
        return (2**stage - 1 + keys_below(self.bits, stage).index(sub)) * self.pieces + piece

    def current(self, sub, piece):
        if (sub, piece) not in self.added:
            return self.views(sub)[piece]
        return self.sums.at[keys_below(self.bits, len(self.bits)).index(sub) * self.pieces + piece]

    def send(self, stage, sub, piece):
        bit = self.bits[stage]
        self.came[stage, sub, piece] = self.mail.post(
            self.current(bit + sub, piece), self.landed.at[self.slot(stage, sub, piece)], bit
        )

    def start(self, which=None):
        stage = len(self.bits) - 1
        for sub in reversed(keys_below(self.bits, stage)):
            if which is None or (sub != 0) == which:
                for piece in range(self.pieces):
                    self.send(stage, sub, piece)

    def take(self, stage, sub, piece):
        self.came[stage, sub, piece].wait_recv()
        here = self.current(sub, piece)
        landed = self.landed.at[self.slot(stage, sub, piece)]
        if stage == 0:
            self.add(self.last(piece), here, landed)
            return
        place = keys_below(self.bits, len(self.bits)).index(sub) * self.pieces + piece
        self.add(self.sums.at[place], here, landed)
        self.added.add((sub, piece))
        below = self.bits[stage - 1]
        if (sub // below) % 2:
            self.send(stage - 1, sub - below, piece)

    def take_away(self, stage, piece):
        below = self.bits[stage - 1]
        for sub in keys_below(self.bits, stage):
            if (sub // below) % 2:
                self.take(stage, sub, piece)

    def take_here(self, stage, piece):
        below = self.bits[stage - 1] if stage else 0
        for sub in keys_below(self.bits, stage):
            if not stage or not (sub // below) % 2:
                self.take(stage, sub, piece)

    def finish_piece(self, piece):
        top = len(self.bits) - 1
        for stage in range(top, -1, -1):
            if stage and stage != top:
                self.take_away(stage, piece)
            self.take_here(stage, piece)


def norm_back(total, base, gain):
    inv = lax.rsqrt(jnp.mean(base * base, axis=-1, keepdims=True) + epsilon)
    scaled = gain * total
    grads = inv * scaled - base * inv**3 * jnp.mean(scaled * base, axis=-1, keepdims=True)
    return grads, total * base * inv


def back_kernel(
    outer, inner, seq_len,
    x_ref, go_ref, factor_ref, gains_ref, q_ref, k_ref, v_ref, att_ref, w_qkv, w_o, cos_ref, sin_ref,
    p_g, p_u, half_d, act_one, resid_ref, two_ref,
    out_q, out_k, out_v, out_o, gain_grads,
    out_gate, out_up, out_d, land_g, land_u, land_d, sum_g, sum_u, sum_d, fin_g, fin_u, land_qkv, land_o, grad_tokens,
    near, core_in, far, own_sum, grad_resid, branch,
    mid, in_a, in_b,
    acts, d_qkv, p_qkv, p_o, p_o_sum, sum_qkv, sum_o, fin_qkv, qkv_in, gain_in,
    send_sems, recv_sems, local_sems, far_send, far_recv, act_sems, add_buf, add_sem,
):
    size, width = x_ref.shape
    rows = out_q.shape[0]
    hidden_rows = out_d.shape[0]
    narrow = w_o.shape[0]
    hidden = p_g.shape[1]
    ring = Ring(outer, inner, rows)
    mail = Mail(ring, send_sems, recv_sems, local_sems)
    ring.greet()
    bits = ring.data_bits
    flat = ring.flat
    strip = 32
    core_partner = ring.where(ring.bit_core)

    def strips(step):
        def run(i, carry):
            step(pl.ds(pl.multiple_of(i * strip, strip), strip))
            return carry

        lax.fori_loop(0, size // strip, run, 0)

    def by_place(ref, count):
        return lambda key: [
            ref.at[pl.ds(pl.multiple_of(ring.place(ring.flip(flat, key)) * count, 16), count)]
        ]

    def by_runs(ref):
        return lambda key: [
            ref.at[pl.ds(pl.multiple_of(start, 16), count)]
            for start, count in ring.runs(ring.flip(flat, key), rows)
        ]

    def dot(left, right, left_dim, right_dim):
        return lax.dot_general(
            left, right, (((left_dim,), (right_dim,)), ((), ())), preferred_element_type=f32
        )

    run_rows = ring.runs(flat, rows)[0][1]
    top_stage = len(bits) - 1
    collect_g, collect_u = (
        Collect(
            mail, bits, by_runs(partial), landed, sums,
            lambda piece, last=last: last.at[pl.ds(piece * run_rows, run_rows)], add_far,
        )
        for partial, landed, sums, last in (
            (p_g, land_g, sum_g, fin_g), (p_u, land_u, sum_u, fin_u)
        )
    )
    share_count = half_d.shape[0] // hidden_rows

    def half_place(key):
        place = ring.place(ring.flip(flat, key)) % share_count
        return [half_d.at[pl.ds(pl.multiple_of(place * hidden_rows, 16), hidden_rows)]]

    collect_d = Collect(mail, bits[:-1], half_place, land_d, sum_d, lambda piece: out_d, add_far)

    load_resid = mail.keep(resid_ref, grad_resid)
    load_two = mail.keep(two_ref, own_sum)
    collect_d.start()
    for which in (True, False):
        collect_g.start(which)
        collect_u.start(which)
    gain_grads[...] = jnp.zeros_like(gain_grads)
    for copy in (load_resid, load_two):
        copy.wait()
        mail.kept = [c for c in mail.kept if c is not copy]

    def second_norm(part):
        resid = grad_resid[part, :]
        grads, terms = norm_back(own_sum[part, :], resid, gains_ref[1:2, :])
        grads = grads + go_ref[part, :].astype(f32) * factor_ref[part, :]
        grad_resid[part, :] = grads
        branch[0, part, :] = grads.astype(bf16)
        gain_grads[1:2, :] = gain_grads[1:2, :] + jnp.sum(terms, axis=0, keepdims=True)

    strips(second_norm)
    share = Share(mail, branch, branch.at[0])
    share.first()
    for piece in range(collect_g.pieces):
        collect_g.take_away(top_stage, piece)
    share.second()
    for piece in range(collect_u.pieces):
        collect_u.take_away(top_stage, piece)
    share.third()
    p_o_sum[...] = jnp.zeros_like(p_o_sum)
    share.done()

    scale = HEAD_DIM**-0.5
    cosine, sine = cos_ref[...], sin_ref[...]
    per_block = size // seq_len

    def attend_block(place):
        grads = branch[place]
        grad_att = dot(grads, w_o[...], 1, 1).astype(bf16)
        p_o_sum[...] = p_o_sum[...] + dot(att_ref[place], grads, 0, 0)
        causal = lax.broadcasted_iota(jnp.int32, (seq_len, seq_len), 1) <= lax.broadcasted_iota(
            jnp.int32, (seq_len, seq_len), 0
        )
        for b in range(per_block):
            span = slice(b * seq_len, (b + 1) * seq_len)
            q, k, v = q_ref[place, span], k_ref[place, span], v_ref[place, span]
            ga = grad_att[span]
            dq = jnp.zeros((seq_len, narrow), f32)
            dk = jnp.zeros((seq_len, narrow), f32)
            dv = jnp.zeros((seq_len, narrow), f32)
            for head in range(narrow // HEAD_DIM):
                mask = head_mask(narrow, head)
                kh = jnp.where(mask, k, jnp.zeros_like(k))
                vh = jnp.where(mask, v, jnp.zeros_like(v))
                qh = jnp.where(mask, q, jnp.zeros_like(q))
                gh = jnp.where(mask, ga, jnp.zeros_like(ga))
                scores = jnp.where(causal, dot(q, kh, 1, 1) * scale, -1e30)
                grown = jnp.exp(scores - jnp.max(scores, axis=-1, keepdims=True))
                soft = grown / jnp.sum(grown, axis=-1, keepdims=True)
                grad_soft = dot(ga, vh, 1, 1)
                grad_scores = (
                    soft * (grad_soft - jnp.sum(soft * grad_soft, axis=-1, keepdims=True))
                ).astype(bf16)
                dq = dq + dot(grad_scores, kh, 1, 0)
                dk = dk + dot(grad_scores, qh, 0, 0)
                dv = dv + dot(soft.astype(bf16), gh, 0, 0)
            d_qkv[place, span, :narrow] = turn(dq * scale, cosine, -sine).astype(bf16)
            d_qkv[place, span, narrow : 2 * narrow] = turn(dk * scale, cosine, -sine).astype(bf16)
            d_qkv[place, span, 2 * narrow :] = dv.astype(bf16)
        return dot(d_qkv[place], w_qkv[...], 1, 1)

    def far_copy(j):
        return pltpu.make_async_remote_copy(
            src_ref=far.at[j % 2],
            dst_ref=core_in.at[j],
            send_sem=far_send.at[j],
            recv_sem=far_recv.at[j],
            device_id=core_partner,
            device_id_type=MESH,
        )

    def far_step(i, carry):
        j = QUAD - 1 - i
        part = attend_block(QUAD + j).astype(bf16)

        @pl.when(i >= 2)
        def _():
            far_copy(j + 2).wait_send()

        far[j % 2] = part
        far_copy(j).start()
        return carry

    lax.fori_loop(0, QUAD, far_step, 0)
    for j in range(2):
        far_copy(j).wait_send()
    def near_step(i, carry):
        j = QUAD - 1 - i
        part = attend_block(j)
        far_copy(j).wait_recv()
        own_sum[...] = part + core_in[j].astype(f32)
        near[j] = own_sum[...].astype(bf16)
        return carry

    lax.fori_loop(0, QUAD, near_step, 0)
    total_one = Total(mail, near, own_sum, mid, in_a, in_b)
    total_one.first()
    total_one.first_a()

    def add_mixed(target, left, landed):
        count, across = landed.shape
        buffer = add_buf.at[pl.ds(0, count), pl.ds(0, across)]
        copy = pltpu.make_async_copy(landed, buffer, add_sem.at[0])
        copy.start()
        copy.wait()
        add_near(target, left, buffer)

    collect_o = Collect(
        mail, bits, by_place(p_o, rows), land_o, sum_o, lambda piece: out_o, add_mixed
    )
    collect_qkv = Collect(
        mail, bits, by_runs(p_qkv), land_qkv, sum_qkv,
        lambda piece: fin_qkv.at[pl.ds(piece * run_rows, run_rows)], add_mixed,
    )
    p_o[...] = p_o_sum[...].astype(bf16)
    collect_o.start()
    cut = acts.shape[3]
    cuts = width // cut
    shift = (1 - flat // (ring.count // 2)) * (cuts // 2)

    def chunk_at(i):
        return pl.multiple_of(((i + shift) % cuts) * cut, cut)

    def act_copy(i):
        return pltpu.make_async_copy(
            act_one.at[:, :, pl.ds(chunk_at(i), cut)], acts.at[i % 2], act_sems.at[i % 2]
        )

    act_copy(0).start()

    def chunk_step(i, carry):
        act_copy(i).wait()

        @pl.when(i + 1 < cuts)
        def _():
            act_copy(i + 1).start()

        left = acts[i % 2].reshape(2 * QUAD * size, cut)
        right = d_qkv[...].reshape(2 * QUAD * size, 3 * narrow)
        p_qkv[pl.ds(chunk_at(i), cut), :] = dot(left, right, 0, 0).astype(bf16)
        return carry

    lax.fori_loop(0, cuts // 2, chunk_step, 0)
    collect_qkv.start()
    total_one.second()
    lax.fori_loop(cuts // 2, cuts, chunk_step, 0)
    if len(bits) > 2:
        collect_d.take_away(top_stage - 1, 0)
    collect_d.finish_piece(0)

    block = ring.span * hidden_rows
    gu_swap = []
    team = ring.team(flat)

    def hand_out(last, ref):
        for delta in ring.deltas:
            other = ring.team(ring.flip(flat, delta))
            part = pl.ds(pl.multiple_of(other * rows, 16), rows)
            for y in range(ring.upper_size):
                for o in range(ring.across):
                    target = ((y * 2 + team // QUAD) * ring.across + o) * QUAD + team % QUAD
                    src = last.at[part, pl.ds((y * ring.across + o) * block, block)]
                    dst = ref.at[:, pl.ds(pl.multiple_of(target * block, 128), block)]
                    if delta:
                        gu_swap.append(mail.post(src, dst, delta))
                    else:
                        mail.keep(src, dst)

    for piece in range(collect_g.pieces):
        collect_g.finish_piece(piece)
    hand_out(fin_g, out_gate)
    collect_o.take_away(top_stage, 0)
    for piece in range(collect_qkv.pieces):
        collect_qkv.take_away(top_stage, piece)
    for piece in range(collect_u.pieces):
        collect_u.finish_piece(piece)
    hand_out(fin_u, out_up)
    total_one.arrive()

    def first_norm(part):
        x = x_ref[part, :].astype(f32)
        grads, terms = norm_back(total_one.value(part), x, gains_ref[0:1, :])
        grad_resid[part, :] = grad_resid[part, :] + grads
        gain_grads[0:1, :] = gain_grads[0:1, :] + jnp.sum(terms, axis=0, keepdims=True)

    strips(first_norm)
    mail.keep(grad_resid, grad_tokens)
    for step, bit in enumerate([ring.bit_core, ring.bit_a, ring.bit_b] + bits):
        copy = mail.post(gain_grads, gain_in.at[step], bit)
        copy.wait()
        mail.sent = [c for c in mail.sent if c is not copy]
        gain_grads[...] = gain_grads[...] + gain_in[step]
    for piece in range(collect_qkv.pieces):
        collect_qkv.finish_piece(piece)
    collect_o.finish_piece(0)

    swaps = []
    for delta in ring.deltas:
        other = ring.team(ring.flip(flat, delta))
        src = fin_qkv.at[pl.ds(pl.multiple_of(other * rows, 16), rows)]
        dst = qkv_in.at[team]
        if delta:
            swaps.append(mail.post(src, dst, delta))
        else:
            kept = mail.keep(src, dst)
    kept.wait()
    mail.kept = [c for c in mail.kept if c is not kept]
    for copy in swaps:
        copy.wait_recv()
    for j, ref in enumerate((out_q, out_k, out_v)):
        parts = []
        for y in range(ring.upper_size):
            for c in range(2):
                for o in range(ring.across):
                    for q in range(QUAD):
                        start = j * narrow + (y * ring.across + o) * HEAD_DIM
                        parts.append(qkv_in[c * QUAD + q, :, start : start + HEAD_DIM])
        ref[...] = jnp.concatenate(parts, axis=1).astype(f32)
    for copy in gu_swap:
        copy.wait_recv()
    mail.finish()


def back(outer, inner, seq_len, near_args, far_args):
    tokens, w_qkv, w_o = near_args[0], near_args[8], near_args[9]
    size, width = tokens.shape
    narrow = w_o.shape[0]
    hidden = far_args[0].shape[1]
    places = outer * inner // (2 * QUAD)
    rows = width // (outer * inner)
    hidden_rows = hidden // places
    span = max(1, HEAD_DIM // rows)
    pieces = 2 if span == 1 else 2 * QUAD
    run_rows = 2 * QUAD * rows // pieces
    remote = (places - 1) * (3 * pieces + 2) + 7 + 14 * places // span + 8 + 24
    local = 8 + 2 * places // span
    vm = pl.BlockSpec(memory_space=pltpu.VMEM)
    hbm = pl.BlockSpec(memory_space=pl.ANY)
    sds = jax.ShapeDtypeStruct
    out_shape = (
        sds((rows, width), f32),
        sds((rows, width), f32),
        sds((rows, width), f32),
        sds((rows, width), f32),
        sds((8, width), f32),
        sds((rows, 2 * QUAD * hidden), bf16),
        sds((rows, 2 * QUAD * hidden), bf16),
        sds((hidden_rows, width), f32),
        sds(((places - 1) * pieces, run_rows, hidden), bf16),
        sds(((places - 1) * pieces, run_rows, hidden), bf16),
        sds((places // 2, hidden_rows, width), bf16),
        sds((places // 2 * pieces, run_rows, hidden), bf16),
        sds((places // 2 * pieces, run_rows, hidden), bf16),
        sds((places // 2, hidden_rows, width), bf16),
        sds((2 * QUAD * rows, hidden), bf16),
        sds((2 * QUAD * rows, hidden), bf16),
        sds(((places - 1) * pieces, run_rows, 3 * narrow), bf16),
        sds((places - 1, rows, width), bf16),
        sds((size, width), f32),
    )
    wide = pltpu.VMEM((size, width), bf16)
    four = pltpu.VMEM((QUAD, size, width), bf16)
    cut = min(256, width // 2)
    four_sems = pltpu.SemaphoreType.DMA((QUAD,))
    return pl.pallas_call(
        functools.partial(back_kernel, outer, inner, seq_len),
        out_shape=out_shape,
        in_specs=[vm] * len(near_args) + [hbm] * len(far_args),
        out_specs=tuple([vm] * 5 + [hbm] * 14),
        scratch_shapes=[
            four, four, pltpu.VMEM((2, size, width), bf16),
            pltpu.VMEM((size, width), f32),
            pltpu.VMEM((size, width), f32),
            pltpu.VMEM((2 * QUAD, size, width), bf16),
            wide, wide, wide,
            pltpu.VMEM((2, 2 * QUAD, size, cut), bf16),
            pltpu.VMEM((2 * QUAD, size, 3 * narrow), bf16),
            pltpu.VMEM((width, 3 * narrow), bf16),
            pltpu.VMEM((narrow, width), bf16),
            pltpu.VMEM((narrow, width), f32),
            pltpu.VMEM((places // 2 * pieces, run_rows, 3 * narrow), bf16),
            pltpu.VMEM((places // 2, rows, width), bf16),
            pltpu.VMEM((2 * QUAD * rows, 3 * narrow), bf16),
            pltpu.VMEM((2 * QUAD, rows, 3 * narrow), bf16),
            pltpu.VMEM((8, 8, width), f32),
            pltpu.SemaphoreType.DMA((remote,)),
            pltpu.SemaphoreType.DMA((remote,)),
            pltpu.SemaphoreType.DMA((local,)),
            four_sems, four_sems,
            pltpu.SemaphoreType.DMA((2,)),
            pltpu.VMEM((run_rows, width), bf16),
            pltpu.SemaphoreType.DMA((1,)),
        ],
        compiler_params=pltpu.CompilerParams(
            collective_id=1, has_side_effects=True, vmem_limit_bytes=63 * 1024 * 1024
        ),
        name="back",
    )(*near_args, *far_args)


def on_device(
    tokens,
    labels,
    counts,
    grad_out,
    w_query,
    w_key,
    w_value,
    w_out,
    gain_attn,
    gain_mlp,
    w_gate,
    w_up,
    w_down,
):
    batch_size, seq_len, width = tokens.shape
    outer_count = lax.axis_size("dp")
    inner_count = lax.axis_size("fsdp")
    rows = w_query.shape[0]
    hidden_rows = w_down.shape[0]
    plan = Plan(outer_count, inner_count, rows)
    x_rows = tokens.reshape(-1, width)

    token_total = float(seq_len * batch_size * outer_count * inner_count)
    picked_counts = jnp.sum(
        jnp.where(labels[:, None] == jnp.arange(3)[None, :], counts[None, :], 0), axis=1
    ).astype(f32)
    factor = token_total / (3.0 * picked_counts)
    cosine, sine = rope_tables(seq_len, HEAD_DIM)
    head_count = width // (2 * QUAD) // HEAD_DIM
    sign = jnp.where(jnp.arange(HEAD_DIM) < HEAD_DIM // 2, -1.0, 1.0)
    wide_cosine = jnp.tile(cosine, (1, head_count))
    wide_sine = jnp.tile(sine * sign, (1, head_count))
    gain_rows = lax.dynamic_update_slice(
        jnp.zeros((8, width), f32),
        jnp.stack([gain_attn, gain_mlp]).astype(f32),
        (0, plan.flat * rows),
    )
    factor_rows = jnp.repeat(factor, seq_len)[:, None]
    (
        act_one, w_qkv, w_o, q_rot, k_rot, values, attended, resid, gains, act_two, w_g, w_u, w_d,
    ) = front(
        outer_count, inner_count, seq_len,
        x_rows, gain_rows,
        w_query, w_key, w_value,
        wide_cosine, wide_sine,
        w_out, w_gate, w_up, w_down,
    )
    narrow = w_o.shape[0]
    hidden = w_d.shape[0]
    act_two = act_two.reshape(-1, width)
    dy_own = (grad_out.reshape(-1, width).astype(f32) * factor_rows).astype(bf16)
    dy_own, act_two = lax.optimization_barrier((dy_own, act_two))
    held = lax.optimization_barrier
    count = act_two.shape[0] // 2
    dy_a, dy_b = plan.send(dy_own, plan.bit_a), plan.send(dy_own, plan.bit_b)
    gate_pre, up_proj = mm(act_two, w_g), mm(act_two, w_u)
    gate_pre, up_proj, dy_a, dy_b = held((gate_pre, up_proj, dy_a, dy_b))

    half = dy_a.shape[0] // 2
    dy_first, dy_second = plan.send(dy_a[:half], plan.bit_b), plan.send(dy_b[half:], plan.bit_a)
    sigmoid_gate = jax.nn.sigmoid(gate_pre)
    middle = (gate_pre * sigmoid_gate * up_proj).astype(bf16)
    down_far = mm(middle[count:], w_d).astype(bf16)
    down_far, dy_first, dy_second = held((down_far, dy_first, dy_second))

    dy_near = jnp.concatenate([dy_own, dy_a, dy_b, dy_first, dy_second], axis=0)
    dy_far = plan.send(dy_near, plan.bit_core)
    down_near = mm(middle[:count], w_d)
    down_near, dy_far = held((down_near, dy_far))
    dy = jnp.concatenate([dy_near, dy_far], axis=0)
    down_core = plan.send(down_far, plan.bit_core)
    grad_middle = times_transposed(dy, w_d)
    grad_gate_pre = (
        grad_middle * up_proj * sigmoid_gate * (1.0 + gate_pre * (1.0 - sigmoid_gate))
    ).astype(bf16)
    grad_up_proj = (grad_middle * gate_pre * sigmoid_gate).astype(bf16)
    grad_gate_pre, grad_up_proj, down_core = held((grad_gate_pre, grad_up_proj, down_core))

    def back_two(part):
        return times_transposed(grad_gate_pre[part], w_g) + times_transposed(
            grad_up_proj[part], w_u
        )

    down = plan.sum_four(down_near, down_core)
    two_far = back_two(slice(count, None)).astype(bf16)
    two_far, middle, dy = held((two_far, middle, dy))
    two_core = plan.send(two_far, plan.bit_core)
    p_d = outer_sum(middle, dy).astype(bf16)
    p_d, two_core = held((p_d, two_core))
    half_d = plan.sum_upper(p_d)
    added = plan.sum_four(back_two(slice(0, count)), two_core)
    p_g = outer_sum(act_two, grad_gate_pre).astype(bf16)
    p_u = outer_sum(act_two, grad_up_proj).astype(bf16)
    layer_out = (resid + down).astype(bf16).reshape(tokens.shape)
    added, layer_out = held((added, layer_out))
    results = back(
        outer_count, inner_count, seq_len,
        (
            x_rows, grad_out.reshape(-1, width), factor_rows, gains, q_rot, k_rot, values, attended,
            w_qkv, w_o, wide_cosine, wide_sine,
        ),
        (p_g, p_u, half_d, act_one, resid, added),
    )
    query_grad, key_grad, value_grad, out_grad, gain_grads = results[:5]
    gate_grad, up_grad, down_grad = (a.astype(f32) for a in results[5:8])
    grad_tokens = results[-1]
    gain_grads = lax.dynamic_slice(gain_grads, (0, plan.flat * rows), (2, rows))
    return (
        layer_out,
        grad_tokens.reshape(tokens.shape),
        query_grad,
        key_grad,
        value_grad,
        out_grad,
        gain_grads[0],
        gain_grads[1],
        gate_grad,
        up_grad,
        down_grad,
    )


def solution(mesh):
    rows = P(AXES, None)
    vector = P(AXES)
    three = P(AXES, None, None)
    in_specs = (three, vector, P(), three, rows, rows, rows, rows, vector, vector, rows, rows, rows)
    out_specs = (three, three, rows, rows, rows, rows, vector, vector, rows, rows, rows)
    return jax.shard_map(
        on_device, mesh=mesh, in_specs=in_specs, out_specs=out_specs, check_vma=False
    )
```

```python
import functools

import jax
import jax.numpy as jnp
from jax import lax
from jax.experimental import pallas as pl
from jax.experimental.pallas import tpu as pltpu
from jax.sharding import PartitionSpec as P

HEAD_DIM = 64
AXES = ("dp", "fsdp")
QUAD = 4

epsilon = 1e-05
rope_base = 130000.0
bf16 = jnp.bfloat16
f32 = jnp.float32
MESH = pl.DeviceIdType.MESH


def rope_tables(seq_len, head_dim):
    half_dim = head_dim // 2
    frequency = rope_base ** (-(jnp.arange(half_dim).astype(f32) * 2.0) / head_dim)
    angles = jnp.arange(seq_len).astype(f32)[:, None] * frequency[None, :]
    angles = jnp.concatenate([angles, angles], axis=1)
    return (jnp.cos(angles), jnp.sin(angles))


class Ring:
    def __init__(self, outer, inner, rows):
        self.known = {}
        self.count = outer * inner
        self.inner = inner
        self.span = max(1, HEAD_DIM // rows)
        self.bit_a = self.span
        self.bit_b = 2 * self.span
        self.bit_core = inner
        self.low = powers(1, self.span)
        self.mid = powers(QUAD * self.span, inner)
        self.upper = powers(2 * inner, self.count)
        self.data_bits = self.low + self.mid + self.upper
        self.deltas = [
            (self.bit_core if t // QUAD else 0) + (t % QUAD) * self.span for t in range(2 * QUAD)
        ]
        self.across = inner // (QUAD * self.span)
        self.upper_size = outer // 2
        self.flat = lax.axis_index("dp") * inner + lax.axis_index("fsdp")

    def flip(self, flat, bits):
        bit = 1
        while bit <= bits:
            if bits & bit:
                flat = flat + bit * (1 - 2 * ((flat // bit) % 2))
            bit *= 2
        return flat

    def where(self, bits):
        if bits not in self.known:
            other = self.flip(self.flat, bits)
            self.known[bits] = (other // self.inner, other % self.inner)
        return self.known[bits]

    def team(self, flat):
        return ((flat // self.inner) % 2) * QUAD + (flat // self.span) % QUAD

    def place(self, flat):
        return (
            (flat // (2 * self.inner)) * self.across + (flat % self.inner) // (QUAD * self.span)
        ) * self.span + flat % self.span

    def runs(self, flat, rows):
        lowest = flat - self.span * ((flat // self.span) % QUAD)
        lowest = lowest - self.inner * ((flat // self.inner) % 2)
        found = []
        for core in range(2):
            start = lowest + core * self.inner
            if self.span == 1:
                found.append((start * rows, QUAD * rows))
            else:
                found += [((start + q * self.span) * rows, rows) for q in range(QUAD)]
        return found

    def greet(self):
        partners = self.deltas[1:] + self.data_bits
        barrier = pltpu.get_barrier_semaphore()
        for bits in partners:
            pl.semaphore_signal(barrier, 1, device_id=self.where(bits), device_id_type=MESH)
        pl.semaphore_wait(barrier, len(partners))


def powers(first, end):
    found = []
    while first < end:
        found.append(first)
        first *= 2
    return found


class Mail:
    def __init__(self, ring, send_sems, recv_sems, local_sems):
        self.ring, self.send_sems, self.recv_sems, self.local_sems = ring, send_sems, recv_sems, local_sems
        self.used = 0
        self.used_local = 0
        self.sent = []
        self.kept = []

    def post(self, src, dst, bits):
        copy = pltpu.make_async_remote_copy(
            src_ref=src,
            dst_ref=dst,
            send_sem=self.send_sems.at[self.used],
            recv_sem=self.recv_sems.at[self.used],
            device_id=self.ring.where(bits),
            device_id_type=MESH,
        )
        self.used += 1
        copy.start()
        self.sent.append(copy)
        return copy

    def keep(self, src, dst):
        copy = pltpu.make_async_copy(src, dst, self.local_sems.at[self.used_local])
        self.used_local += 1
        copy.start()
        self.kept.append(copy)
        return copy

    def drop(self, copy):
        self.sent = [c for c in self.sent if c is not copy]

    def finish(self):
        for copy in self.sent:
            copy.wait_send()
        for copy in self.kept:
            copy.wait()


class Spread:
    def __init__(self, mail, views, bits):
        self.mail, self.views, self.bits = mail, views, bits
        self.pieces = len(views(0))
        self.came = {}

    def start(self, key, piece, first):
        ref = self.views(key)[piece]
        for bit in self.bits[first:]:
            self.came[key + bit, piece] = self.mail.post(ref, ref, bit)

    def begin(self, piece=None):
        for p in range(self.pieces) if piece is None else (piece,):
            self.start(0, p, 0)

    def pass_on(self, stage, piece=None):
        for p in range(self.pieces) if piece is None else (piece,):
            for key in keys_below(self.bits, stage):
                key += self.bits[stage]
                self.came.pop((key, p)).wait_recv()
                self.start(key, p, stage + 1)

    def pass_all(self, piece=None):
        for stage in range(len(self.bits) - 1):
            self.pass_on(stage, piece)

    def done(self):
        for copy in self.came.values():
            copy.wait_recv()


def keys_below(bits, stage):
    return [
        sum(b for i, b in enumerate(bits[:stage]) if low >> i & 1) for low in range(2**stage)
    ]


class Adding:
    def __init__(self, mail, ref, came_in, bits):
        self.mail, self.ref, self.came_in, self.bits = mail, ref, came_in, bits
        self.step = 0

    def post(self):
        self.copy = self.mail.post(
            self.ref, self.came_in.at[self.step], self.bits[self.step]
        )

    def take(self):
        self.copy.wait()
        self.mail.drop(self.copy)
        self.ref[...] = self.ref[...] + self.came_in[self.step]
        self.step += 1


class Share:
    def __init__(self, mail, whole, own):
        self.mail, self.whole, self.own = mail, whole, own
        self.core = []

    def first_core(self):
        self.to_core(self.own, 0)

    def first_a(self):
        self.from_a = self.mail.post(self.own, self.whole.at[1], self.mail.ring.bit_a)

    def first_b(self):
        self.from_b = self.mail.post(self.own, self.whole.at[2], self.mail.ring.bit_b)

    def first(self):
        self.first_a()
        self.first_b()
        self.first_core()

    def to_core(self, ref, place):
        self.core.append(
            self.mail.post(ref, self.whole.at[QUAD + place], self.mail.ring.bit_core)
        )

    def second_a(self):
        self.from_a.wait_recv()
        self.to_core(self.whole.at[1], 1)

    def second_b(self):
        self.from_b.wait_recv()
        self.both = self.mail.post(self.whole.at[2], self.whole.at[3], self.mail.ring.bit_a)
        self.to_core(self.whole.at[2], 2)

    def second(self):
        self.second_a()
        self.second_b()

    def third(self):
        self.both.wait_recv()
        self.to_core(self.whole.at[3], 3)

    def done(self, places=range(QUAD)):
        for place in places:
            self.core[place].wait_recv()


def add_near(target, left, right):
    rows = left.shape[0]
    strip = min(32, rows)

    def step(i, carry):
        part = pl.ds(pl.multiple_of(i * strip, strip), strip)
        target[part, :] = (left[part, :].astype(f32) + right[part, :].astype(f32)).astype(
            target.dtype
        )
        return carry

    lax.fori_loop(0, rows // strip, step, 0)


class Total:
    def __init__(self, mail, near, own, mid, in_a, in_b):
        self.mail, self.near, self.own = mail, near, own
        self.mid, self.in_a, self.in_b = mid, in_a, in_b

    def first(self):
        self.over = self.mail.post(self.near.at[3], self.mid, self.mail.ring.bit_a)

    def first_a(self):
        self.for_a = self.mail.post(self.near.at[1], self.in_a, self.mail.ring.bit_a)

    def second(self):
        self.over.wait_recv()
        add_near(self.near.at[2], self.near.at[2], self.mid)
        self.for_b = self.mail.post(self.near.at[2], self.in_b, self.mail.ring.bit_b)

    def arrive(self):
        self.for_a.wait_recv()
        self.for_b.wait_recv()

    def value(self, part):
        return self.own[part, :] + self.in_a[part, :].astype(f32) + self.in_b[part, :].astype(f32)


def head_mask(width, head):
    lanes = lax.broadcasted_iota(jnp.int32, (1, width), 1)
    return (lanes >= head * HEAD_DIM) & (lanes < (head + 1) * HEAD_DIM)


def turn(u, cosine, signed_sine):
    width = u.shape[-1]
    half = HEAD_DIM // 2
    lanes = lax.broadcasted_iota(jnp.int32, (1, width), 1)
    lower = lanes % HEAD_DIM < half
    turned = jnp.where(lower, pltpu.roll(u, width - half, 1), pltpu.roll(u, half, 1))
    return u * cosine + turned * signed_sine


def front_kernel(
    outer, inner, seq_len,
    x_ref, gain_ref, wq_ref, wk_ref, wv_ref, cos_ref, sin_ref,
    wo_ref, wg_ref, wu_ref, wd_ref,
    act_one, w_qkv, w_o, q_out, k_out, v_out, att_out, resid_out, gains_out,
    act_two, w_g, w_u, w_d,
    cut, gain_in, x_all, far, core_in, near, own_sum, mid, in_a, in_b, act_two_own,
    send_sems, recv_sems, local_sems, far_send, far_recv,
):
    rows = wq_ref.shape[0]
    width = wq_ref.shape[1]
    hidden_rows = wd_ref.shape[0]
    narrow = width // (2 * QUAD)
    ring = Ring(outer, inner, rows)
    mail = Mail(ring, send_sems, recv_sems, local_sems)
    ring.greet()
    bits = ring.data_bits
    flat = ring.flat

    def by_place(ref, size, pieces):
        step = size // pieces
        return lambda key: [
            ref.at[
                pl.ds(
                    pl.multiple_of(ring.place(ring.flip(flat, key)) * size + p * step, 16), step
                )
            ]
            for p in range(pieces)
        ]

    def by_runs(ref):
        return lambda key: [
            ref.at[pl.ds(pl.multiple_of(start, 16), size)]
            for start, size in ring.runs(ring.flip(flat, key), rows)
        ]

    def settle(copy):
        copy.wait()
        mail.kept = [c for c in mail.kept if c is not copy]

    mine_o = w_o.at[pl.ds(pl.multiple_of(ring.place(flat) * rows, 16), rows)]
    mine_d = w_d.at[pl.ds(pl.multiple_of(ring.place(flat) * hidden_rows, 16), hidden_rows)]
    keep_o = mail.keep(wo_ref, mine_o)
    keep_d = mail.keep(wd_ref, mine_d)
    keep_x = mail.keep(x_ref, x_all.at[0])

    chunk = HEAD_DIM
    for t in range(2 * QUAD):
        for j, ref in enumerate((wq_ref, wk_ref, wv_ref)):
            parts = []
            for y in range(ring.upper_size):
                for o in range(ring.across):
                    head = ((y * 2 + t // QUAD) * ring.across + o) * QUAD + t % QUAD
                    parts.append(ref[:, head * chunk : (head + 1) * chunk])
            cut[t, :, j * narrow : (j + 1) * narrow] = jnp.concatenate(parts, axis=1)
    here = pl.ds(pl.multiple_of(flat * rows, 16), rows)
    keep_qkv = mail.keep(cut.at[ring.team(flat)], w_qkv.at[here])
    qkv_swap = []
    for delta in ring.deltas[1:]:
        other = ring.flip(flat, delta)
        qkv_swap.append(mail.post(cut.at[ring.team(other)], w_qkv.at[here], delta))

    gains_out[...] = gain_ref[...]
    gains = Adding(
        mail, gains_out, gain_in, [ring.bit_core, ring.bit_a, ring.bit_b] + bits
    )
    gains.post()
    settle(keep_o)
    spread_o = Spread(mail, by_place(w_o, rows, 1), bits)
    spread_o.begin()
    gains.take()
    gains.post()
    share_x = Share(mail, x_all, x_ref)
    share_x.first_core()
    share_x.first_a()
    settle(keep_qkv)
    for copy in qkv_swap:
        copy.wait_recv()
    spread_qkv = Spread(mail, by_runs(w_qkv), bits)
    spread_qkv.begin()
    gains.take()
    gains.post()
    share_x.first_b()
    spread_o.pass_all()

    gains.take()
    gains.post()
    share_x.second_a()
    for piece in range(spread_qkv.pieces):
        spread_qkv.pass_all(piece)
    while gains.step < len(gains.bits) - 1:
        gains.take()
        gains.post()
    spread_d = Spread(mail, by_place(w_d, hidden_rows, 2), bits)
    settle(keep_d)
    share_x.second_b()
    block = ring.span * hidden_rows
    gate_swap, up_swap = [], []
    for ref, whole, swap in ((wg_ref, w_g, gate_swap), (wu_ref, w_u, up_swap)):
        for delta in ring.deltas:
            team = ring.team(ring.flip(flat, delta))
            for y in range(ring.upper_size):
                for o in range(ring.across):
                    source = ((y * 2 + team // QUAD) * ring.across + o) * QUAD + team % QUAD
                    src = ref.at[:, pl.ds(pl.multiple_of(source * block, 128), block)]
                    dst = whole.at[here, pl.ds((y * ring.across + o) * block, block)]
                    if delta:
                        swap.append((mail.post(src, dst, delta), True))
                    else:
                        swap.append((mail.keep(src, dst), False))

    def swapped(swap):
        for copy, remote in swap:
            if remote:
                copy.wait_recv()
            else:
                settle(copy)

    spread_d.begin()
    gains.take()

    size = act_one.shape[1]
    strip = 32

    def norm_block(place):
        def norm_one(i, carry):
            part = pl.ds(pl.multiple_of(i * strip, strip), strip)
            x = x_all[place, part, :].astype(f32)
            inv = lax.rsqrt(jnp.mean(x * x, axis=-1, keepdims=True) + epsilon)
            act_one[place, part, :] = (x * inv * gains_out[0:1, :]).astype(bf16)
            return carry

        lax.fori_loop(0, size // strip, norm_one, 0)

    settle(keep_x)
    share_x.done(range(QUAD - 1))

    def norm_early(i, carry):
        norm_block(lax.rem(i, QUAD - 1) + QUAD * (i // (QUAD - 1)))
        return carry

    lax.fori_loop(0, 2 * (QUAD - 1), norm_early, 0)
    spread_o.done()
    spread_qkv.done()

    scale = HEAD_DIM**-0.5
    cosine, sine = cos_ref[...], sin_ref[...]
    per_block = act_one.shape[1] // seq_len

    def attend_block(place):
        qkv = jnp.dot(act_one[place], w_qkv[...], preferred_element_type=f32)
        causal = lax.broadcasted_iota(jnp.int32, (seq_len, seq_len), 1) <= lax.broadcasted_iota(
            jnp.int32, (seq_len, seq_len), 0
        )
        for b in range(per_block):
            span = slice(b * seq_len, (b + 1) * seq_len)
            q = turn(qkv[span, :narrow], cosine, sine).astype(bf16)
            k = turn(qkv[span, narrow : 2 * narrow], cosine, sine).astype(bf16)
            v = qkv[span, 2 * narrow :].astype(bf16)
            q_out[place, span] = q
            k_out[place, span] = k
            v_out[place, span] = v
            mixed = jnp.zeros((seq_len, narrow), f32)
            for head in range(narrow // HEAD_DIM):
                mask = head_mask(narrow, head)
                kh = jnp.where(mask, k, jnp.zeros_like(k))
                vh = jnp.where(mask, v, jnp.zeros_like(v))
                scores = lax.dot_general(
                    q, kh, (((1,), (1,)), ((), ())), preferred_element_type=f32
                )
                scores = jnp.where(causal, scores * scale, -1e30)
                top = jnp.max(scores, axis=-1, keepdims=True)
                grown = jnp.exp(scores - top)
                soft = (grown / jnp.sum(grown, axis=-1, keepdims=True)).astype(bf16)
                mixed = mixed + jnp.dot(soft, vh, preferred_element_type=f32)
            att_out[place, span] = mixed.astype(bf16)
        return jnp.dot(att_out[place], w_o[...], preferred_element_type=f32)

    def far_copy(j):
        return pltpu.make_async_remote_copy(
            src_ref=far.at[j],
            dst_ref=core_in.at[j],
            send_sem=far_send.at[j],
            recv_sem=far_recv.at[j],
            device_id=ring.where(ring.bit_core),
            device_id_type=MESH,
        )

    def far_step(j, carry):
        far[j] = attend_block(QUAD + j).astype(bf16)
        far_copy(j).start()
        return carry

    def near_step(j, carry):
        part = attend_block(j)
        far_copy(j).wait_recv()
        total = part + core_in[j].astype(f32)
        near[j] = total.astype(bf16)

        @pl.when(j == 0)
        def _():
            own_sum[...] = total

        return carry

    lax.fori_loop(0, QUAD - 1, far_step, 0)
    spread_g = Spread(mail, by_runs(w_g), bits)
    spread_u = Spread(mail, by_runs(w_u), bits)
    swapped(gate_swap)
    spread_g.begin()
    share_x.third()
    lax.fori_loop(0, QUAD - 1, near_step, 0)
    norm_block(QUAD - 1)
    share_x.done((QUAD - 1,))
    norm_block(2 * QUAD - 1)
    far_step(QUAD - 1, 0)
    near_step(QUAD - 1, 0)
    for j in range(QUAD):
        far_copy(j).wait_send()
    total = Total(mail, near, own_sum, mid, in_a, in_b)
    total.first()
    total.first_a()
    swapped(up_swap)
    spread_u.begin()
    for piece in range(spread_d.pieces):
        spread_d.pass_on(0, piece)
    total.second()
    spread_g.pass_on(0, 0)
    total.arrive()

    def norm_two(i, carry):
        part = pl.ds(pl.multiple_of(i * strip, strip), strip)
        resid = (
            x_ref[part, :].astype(f32) + total.value(part)
        )
        resid_out[part, :] = resid
        inv = lax.rsqrt(jnp.mean(resid * resid, axis=-1, keepdims=True) + epsilon)
        act_two_own[part, :] = (resid * inv * gains_out[1:2, :]).astype(bf16)
        return carry

    lax.fori_loop(0, size // strip, norm_two, 0)
    mail.keep(act_two_own, act_two.at[0])
    share_two = Share(mail, act_two, act_two_own)
    share_two.first()
    for piece in range(1, spread_g.pieces):
        spread_g.pass_on(0, piece)
    share_two.second()
    spread_u.pass_on(0)
    share_two.third()
    for stage in range(1, len(bits) - 1):
        for spread in (spread_d, spread_g, spread_u):
            spread.pass_on(stage)
    spread_d.done()
    spread_g.done()
    spread_u.done()
    share_two.done()
    mail.finish()


def front(outer, inner, seq_len, tokens, gain_rows, w_query, w_key, w_value, cosine, signed_sine, w_out, w_gate, w_up, w_down):
    size, width = tokens.shape
    rows, hidden_all = w_gate.shape
    hidden_rows = w_down.shape[0]
    narrow, hidden = width // (2 * QUAD), hidden_all // (2 * QUAD)
    span = max(1, HEAD_DIM // rows)
    places = outer * inner // (2 * QUAD)
    pieces = 2 if span == 1 else 2 * QUAD
    remote = (places - 1) * (3 * pieces + 3) + 7 + 14 * places // span + 8 + 24
    local = 8 + 2 * places // span
    vm = pl.BlockSpec(memory_space=pltpu.VMEM)
    hbm = pl.BlockSpec(memory_space=pl.ANY)
    eight = (2 * QUAD, size)
    sds = jax.ShapeDtypeStruct
    out_shape = (
        sds(eight + (width,), bf16),
        sds((width, 3 * narrow), bf16),
        sds((narrow, width), bf16),
        sds(eight + (narrow,), bf16),
        sds(eight + (narrow,), bf16),
        sds(eight + (narrow,), bf16),
        sds(eight + (narrow,), bf16),
        sds((size, width), f32),
        sds((8, width), f32),
        sds(eight + (width,), bf16),
        sds((width, hidden), bf16),
        sds((width, hidden), bf16),
        sds((hidden, width), bf16),
    )
    return pl.pallas_call(
        functools.partial(front_kernel, outer, inner, seq_len),
        out_shape=out_shape,
        in_specs=[vm] * 7 + [hbm] * 4,
        out_specs=tuple([vm] * 9 + [hbm] * 4),
        scratch_shapes=[
            pltpu.VMEM((2 * QUAD, rows, 3 * narrow), bf16),
            pltpu.VMEM((8, 8, width), f32),
            pltpu.VMEM((2 * QUAD, size, width), bf16),
            pltpu.VMEM((QUAD, size, width), bf16),
            pltpu.VMEM((QUAD, size, width), bf16),
            pltpu.VMEM((QUAD, size, width), bf16),
            pltpu.VMEM((size, width), f32),
            pltpu.VMEM((size, width), bf16),
            pltpu.VMEM((size, width), bf16),
            pltpu.VMEM((size, width), bf16),
            pltpu.VMEM((size, width), bf16),
            pltpu.SemaphoreType.DMA((remote,)),
            pltpu.SemaphoreType.DMA((remote,)),
            pltpu.SemaphoreType.DMA((local,)),
            pltpu.SemaphoreType.DMA((QUAD,)),
            pltpu.SemaphoreType.DMA((QUAD,)),
        ],
        compiler_params=pltpu.CompilerParams(
            collective_id=0, has_side_effects=True, vmem_limit_bytes=60 * 1024 * 1024
        ),
        name="front",
    )(tokens, gain_rows, w_query, w_key, w_value, cosine, signed_sine, w_out, w_gate, w_up, w_down)


def add_far(target, left, right):
    rows, width = left.shape
    strip = min(64, rows)

    def body(left_ref, right_ref, target_ref):
        target_ref[...] = (left_ref[...].astype(f32) + right_ref[...].astype(f32)).astype(
            target_ref.dtype
        )

    spec = pl.BlockSpec((strip, width), lambda i: (i, 0))
    pltpu.emit_pipeline(body, grid=(rows // strip,), in_specs=[spec, spec], out_specs=[spec])(
        left, right, target
    )


class Collect:
    def __init__(self, mail, bits, views, landed, sums, last, add):
        self.mail, self.bits, self.views = mail, bits, views
        self.landed, self.sums, self.last, self.add = landed, sums, last, add
        self.came = {}
        self.added = set()
        self.pieces = len(views(0))

    def slot(self, stage, sub, piece):
        return (2**stage - 1 + keys_below(self.bits, stage).index(sub)) * self.pieces + piece

    def current(self, sub, piece):
        if (sub, piece) not in self.added:
            return self.views(sub)[piece]
        return self.sums.at[keys_below(self.bits, len(self.bits)).index(sub) * self.pieces + piece]

    def send(self, stage, sub, piece):
        bit = self.bits[stage]
        self.came[stage, sub, piece] = self.mail.post(
            self.current(bit + sub, piece), self.landed.at[self.slot(stage, sub, piece)], bit
        )

    def start(self, which=None):
        stage = len(self.bits) - 1
        for sub in reversed(keys_below(self.bits, stage)):
            if which is None or (sub != 0) == which:
                for piece in range(self.pieces):
                    self.send(stage, sub, piece)

    def take(self, stage, sub, piece):
        self.came[stage, sub, piece].wait_recv()
        here = self.current(sub, piece)
        landed = self.landed.at[self.slot(stage, sub, piece)]
        if stage == 0:
            self.add(self.last(piece), here, landed)
            return
        place = keys_below(self.bits, len(self.bits)).index(sub) * self.pieces + piece
        self.add(self.sums.at[place], here, landed)
        self.added.add((sub, piece))
        below = self.bits[stage - 1]
        if (sub // below) % 2:
            self.send(stage - 1, sub - below, piece)

    def take_away(self, stage, piece):
        below = self.bits[stage - 1]
        for sub in keys_below(self.bits, stage):
            if (sub // below) % 2:
                self.take(stage, sub, piece)

    def take_here(self, stage, piece):
        below = self.bits[stage - 1] if stage else 0
        for sub in keys_below(self.bits, stage):
            if not stage or not (sub // below) % 2:
                self.take(stage, sub, piece)

    def finish_piece(self, piece):
        top = len(self.bits) - 1
        for stage in range(top, -1, -1):
            if stage and stage != top:
                self.take_away(stage, piece)
            self.take_here(stage, piece)


def norm_back(total, base, gain):
    inv = lax.rsqrt(jnp.mean(base * base, axis=-1, keepdims=True) + epsilon)
    scaled = gain * total
    grads = inv * scaled - base * inv**3 * jnp.mean(scaled * base, axis=-1, keepdims=True)
    return grads, total * base * inv


def back_kernel(
    outer, inner, seq_len,
    x_ref, go_ref, factor_ref, gains_ref, q_ref, k_ref, v_ref, att_ref, w_qkv, w_o, cos_ref, sin_ref,
    p_g, p_u, half_d, act_one, resid_ref, two_ref,
    out_q, out_k, out_v, out_o, gain_grads,
    out_gate, out_up, out_d, land_g, land_u, land_d, sum_g, sum_u, sum_d, fin_g, fin_u, land_qkv, land_o, grad_tokens,
    near, core_in, far, own_sum, grad_resid, branch,
    mid, in_a, in_b,
    acts, d_qkv, p_qkv, p_o, p_o_sum, sum_qkv, sum_o, fin_qkv, qkv_in, gain_in,
    send_sems, recv_sems, local_sems, far_send, far_recv, act_sems, add_buf, add_sem,
):
    size, width = x_ref.shape
    rows = out_q.shape[0]
    hidden_rows = out_d.shape[0]
    narrow = w_o.shape[0]
    hidden = p_g.shape[1]
    ring = Ring(outer, inner, rows)
    mail = Mail(ring, send_sems, recv_sems, local_sems)
    ring.greet()
    bits = ring.data_bits
    flat = ring.flat
    strip = 32
    core_partner = ring.where(ring.bit_core)

    def strips(step):
        def run(i, carry):
            step(pl.ds(pl.multiple_of(i * strip, strip), strip))
            return carry

        lax.fori_loop(0, size // strip, run, 0)

    def by_place(ref, count):
        return lambda key: [
            ref.at[pl.ds(pl.multiple_of(ring.place(ring.flip(flat, key)) * count, 16), count)]
        ]

    def by_runs(ref):
        return lambda key: [
            ref.at[pl.ds(pl.multiple_of(start, 16), count)]
            for start, count in ring.runs(ring.flip(flat, key), rows)
        ]

    def dot(left, right, left_dim, right_dim):
        return lax.dot_general(
            left, right, (((left_dim,), (right_dim,)), ((), ())), preferred_element_type=f32
        )

    run_rows = ring.runs(flat, rows)[0][1]
    top_stage = len(bits) - 1
    collect_g, collect_u = (
        Collect(
            mail, bits, by_runs(partial), landed, sums,
            lambda piece, last=last: last.at[pl.ds(piece * run_rows, run_rows)], add_far,
        )
        for partial, landed, sums, last in (
            (p_g, land_g, sum_g, fin_g), (p_u, land_u, sum_u, fin_u)
        )
    )
    share_count = half_d.shape[0] // hidden_rows

    def half_place(key):
        place = ring.place(ring.flip(flat, key)) % share_count
        return [half_d.at[pl.ds(pl.multiple_of(place * hidden_rows, 16), hidden_rows)]]

    collect_d = Collect(mail, bits[:-1], half_place, land_d, sum_d, lambda piece: out_d, add_far)

    load_resid = mail.keep(resid_ref, grad_resid)
    load_two = mail.keep(two_ref, own_sum)
    collect_d.start()
    for which in (True, False):
        collect_g.start(which)
        collect_u.start(which)
    gain_grads[...] = jnp.zeros_like(gain_grads)
    for copy in (load_resid, load_two):
        copy.wait()
        mail.kept = [c for c in mail.kept if c is not copy]

    def second_norm(part):
        resid = grad_resid[part, :]
        grads, terms = norm_back(own_sum[part, :], resid, gains_ref[1:2, :])
        grads = grads + go_ref[part, :].astype(f32) * factor_ref[part, :]
        grad_resid[part, :] = grads
        branch[0, part, :] = grads.astype(bf16)
        gain_grads[1:2, :] = gain_grads[1:2, :] + jnp.sum(terms, axis=0, keepdims=True)

    strips(second_norm)
    share = Share(mail, branch, branch.at[0])
    share.first()
    for piece in range(collect_g.pieces):
        collect_g.take_away(top_stage, piece)
    share.second()
    for piece in range(collect_u.pieces):
        collect_u.take_away(top_stage, piece)
    share.third()
    p_o_sum[...] = jnp.zeros_like(p_o_sum)
    share.done()

    scale = HEAD_DIM**-0.5
    cosine, sine = cos_ref[...], sin_ref[...]
    per_block = size // seq_len

    def attend_block(place):
        grads = branch[place]
        grad_att = dot(grads, w_o[...], 1, 1).astype(bf16)
        p_o_sum[...] = p_o_sum[...] + dot(att_ref[place], grads, 0, 0)
        causal = lax.broadcasted_iota(jnp.int32, (seq_len, seq_len), 1) <= lax.broadcasted_iota(
            jnp.int32, (seq_len, seq_len), 0
        )
        for b in range(per_block):
            span = slice(b * seq_len, (b + 1) * seq_len)
            q, k, v = q_ref[place, span], k_ref[place, span], v_ref[place, span]
            ga = grad_att[span]
            dq = jnp.zeros((seq_len, narrow), f32)
            dk = jnp.zeros((seq_len, narrow), f32)
            dv = jnp.zeros((seq_len, narrow), f32)
            for head in range(narrow // HEAD_DIM):
                mask = head_mask(narrow, head)
                kh = jnp.where(mask, k, jnp.zeros_like(k))
                vh = jnp.where(mask, v, jnp.zeros_like(v))
                qh = jnp.where(mask, q, jnp.zeros_like(q))
                gh = jnp.where(mask, ga, jnp.zeros_like(ga))
                scores = jnp.where(causal, dot(q, kh, 1, 1) * scale, -1e30)
                grown = jnp.exp(scores - jnp.max(scores, axis=-1, keepdims=True))
                soft = grown / jnp.sum(grown, axis=-1, keepdims=True)
                grad_soft = dot(ga, vh, 1, 1)
                grad_scores = (
                    soft * (grad_soft - jnp.sum(soft * grad_soft, axis=-1, keepdims=True))
                ).astype(bf16)
                dq = dq + dot(grad_scores, kh, 1, 0)
                dk = dk + dot(grad_scores, qh, 0, 0)
                dv = dv + dot(soft.astype(bf16), gh, 0, 0)
            d_qkv[place, span, :narrow] = turn(dq * scale, cosine, -sine).astype(bf16)
            d_qkv[place, span, narrow : 2 * narrow] = turn(dk * scale, cosine, -sine).astype(bf16)
            d_qkv[place, span, 2 * narrow :] = dv.astype(bf16)
        return dot(d_qkv[place], w_qkv[...], 1, 1)

    def far_copy(j):
        return pltpu.make_async_remote_copy(
            src_ref=far.at[j % 2],
            dst_ref=core_in.at[j],
            send_sem=far_send.at[j],
            recv_sem=far_recv.at[j],
            device_id=core_partner,
            device_id_type=MESH,
        )

    def far_step(i, carry):
        j = QUAD - 1 - i
        part = attend_block(QUAD + j).astype(bf16)

        @pl.when(i >= 2)
        def _():
            far_copy(j + 2).wait_send()

        far[j % 2] = part
        far_copy(j).start()
        return carry

    lax.fori_loop(0, QUAD, far_step, 0)
    for j in range(2):
        far_copy(j).wait_send()
    def near_step(i, carry):
        j = QUAD - 1 - i
        part = attend_block(j)
        far_copy(j).wait_recv()
        own_sum[...] = part + core_in[j].astype(f32)
        near[j] = own_sum[...].astype(bf16)
        return carry

    lax.fori_loop(0, QUAD, near_step, 0)
    total_one = Total(mail, near, own_sum, mid, in_a, in_b)
    total_one.first()
    total_one.first_a()

    def add_mixed(target, left, landed):
        count, across = landed.shape
        buffer = add_buf.at[pl.ds(0, count), pl.ds(0, across)]
        copy = pltpu.make_async_copy(landed, buffer, add_sem.at[0])
        copy.start()
        copy.wait()
        add_near(target, left, buffer)

    collect_o = Collect(
        mail, bits, by_place(p_o, rows), land_o, sum_o, lambda piece: out_o, add_mixed
    )
    collect_qkv = Collect(
        mail, bits, by_runs(p_qkv), land_qkv, sum_qkv,
        lambda piece: fin_qkv.at[pl.ds(piece * run_rows, run_rows)], add_mixed,
    )
    p_o[...] = p_o_sum[...].astype(bf16)
    collect_o.start()
    cut = acts.shape[3]
    cuts = width // cut
    shift = (1 - flat // (ring.count // 2)) * (cuts // 2)

    def chunk_at(i):
        return pl.multiple_of(((i + shift) % cuts) * cut, cut)

    def act_copy(i):
        return pltpu.make_async_copy(
            act_one.at[:, :, pl.ds(chunk_at(i), cut)], acts.at[i % 2], act_sems.at[i % 2]
        )

    act_copy(0).start()

    def chunk_step(i, carry):
        act_copy(i).wait()

        @pl.when(i + 1 < cuts)
        def _():
            act_copy(i + 1).start()

        left = acts[i % 2].reshape(2 * QUAD * size, cut)
        right = d_qkv[...].reshape(2 * QUAD * size, 3 * narrow)
        p_qkv[pl.ds(chunk_at(i), cut), :] = dot(left, right, 0, 0).astype(bf16)
        return carry

    lax.fori_loop(0, cuts // 2, chunk_step, 0)
    collect_qkv.start()
    total_one.second()
    lax.fori_loop(cuts // 2, cuts, chunk_step, 0)
    if len(bits) > 2:
        collect_d.take_away(top_stage - 1, 0)
    collect_d.finish_piece(0)

    block = ring.span * hidden_rows
    gu_swap = []
    team = ring.team(flat)

    def hand_out(last, ref):
        for delta in ring.deltas:
            other = ring.team(ring.flip(flat, delta))
            part = pl.ds(pl.multiple_of(other * rows, 16), rows)
            for y in range(ring.upper_size):
                for o in range(ring.across):
                    target = ((y * 2 + team // QUAD) * ring.across + o) * QUAD + team % QUAD
                    src = last.at[part, pl.ds((y * ring.across + o) * block, block)]
                    dst = ref.at[:, pl.ds(pl.multiple_of(target * block, 128), block)]
                    if delta:
                        gu_swap.append(mail.post(src, dst, delta))
                    else:
                        mail.keep(src, dst)

    for piece in range(collect_g.pieces):
        collect_g.finish_piece(piece)
    hand_out(fin_g, out_gate)
    collect_o.take_away(top_stage, 0)
    for piece in range(collect_qkv.pieces):
        collect_qkv.take_away(top_stage, piece)
    for piece in range(collect_u.pieces):
        collect_u.finish_piece(piece)
    hand_out(fin_u, out_up)
    total_one.arrive()

    def first_norm(part):
        x = x_ref[part, :].astype(f32)
        grads, terms = norm_back(total_one.value(part), x, gains_ref[0:1, :])
        grad_resid[part, :] = grad_resid[part, :] + grads
        gain_grads[0:1, :] = gain_grads[0:1, :] + jnp.sum(terms, axis=0, keepdims=True)

    strips(first_norm)
    mail.keep(grad_resid, grad_tokens)
    for step, bit in enumerate([ring.bit_core, ring.bit_a, ring.bit_b] + bits):
        copy = mail.post(gain_grads, gain_in.at[step], bit)
        copy.wait()
        mail.sent = [c for c in mail.sent if c is not copy]
        gain_grads[...] = gain_grads[...] + gain_in[step]
    for piece in range(collect_qkv.pieces):
        collect_qkv.finish_piece(piece)
    collect_o.finish_piece(0)

    swaps = []
    for delta in ring.deltas:
        other = ring.team(ring.flip(flat, delta))
        src = fin_qkv.at[pl.ds(pl.multiple_of(other * rows, 16), rows)]
        dst = qkv_in.at[team]
        if delta:
            swaps.append(mail.post(src, dst, delta))
        else:
            kept = mail.keep(src, dst)
    kept.wait()
    mail.kept = [c for c in mail.kept if c is not kept]
    for copy in swaps:
        copy.wait_recv()
    for j, ref in enumerate((out_q, out_k, out_v)):
        parts = []
        for y in range(ring.upper_size):
            for c in range(2):
                for o in range(ring.across):
                    for q in range(QUAD):
                        start = j * narrow + (y * ring.across + o) * HEAD_DIM
                        parts.append(qkv_in[c * QUAD + q, :, start : start + HEAD_DIM])
        ref[...] = jnp.concatenate(parts, axis=1).astype(f32)
    for copy in gu_swap:
        copy.wait_recv()
    mail.finish()


def back(outer, inner, seq_len, near_args, far_args):
    tokens, w_qkv, w_o = near_args[0], near_args[8], near_args[9]
    size, width = tokens.shape
    narrow = w_o.shape[0]
    hidden = far_args[0].shape[1]
    places = outer * inner // (2 * QUAD)
    rows = width // (outer * inner)
    hidden_rows = hidden // places
    span = max(1, HEAD_DIM // rows)
    pieces = 2 if span == 1 else 2 * QUAD
    run_rows = 2 * QUAD * rows // pieces
    remote = (places - 1) * (3 * pieces + 2) + 7 + 14 * places // span + 8 + 24
    local = 8 + 2 * places // span
    vm = pl.BlockSpec(memory_space=pltpu.VMEM)
    hbm = pl.BlockSpec(memory_space=pl.ANY)
    sds = jax.ShapeDtypeStruct
    out_shape = (
        sds((rows, width), f32),
        sds((rows, width), f32),
        sds((rows, width), f32),
        sds((rows, width), f32),
        sds((8, width), f32),
        sds((rows, 2 * QUAD * hidden), bf16),
        sds((rows, 2 * QUAD * hidden), bf16),
        sds((hidden_rows, width), f32),
        sds(((places - 1) * pieces, run_rows, hidden), bf16),
        sds(((places - 1) * pieces, run_rows, hidden), bf16),
        sds((places // 2, hidden_rows, width), bf16),
        sds((places // 2 * pieces, run_rows, hidden), bf16),
        sds((places // 2 * pieces, run_rows, hidden), bf16),
        sds((places // 2, hidden_rows, width), bf16),
        sds((2 * QUAD * rows, hidden), bf16),
        sds((2 * QUAD * rows, hidden), bf16),
        sds(((places - 1) * pieces, run_rows, 3 * narrow), bf16),
        sds((places - 1, rows, width), bf16),
        sds((size, width), f32),
    )
    wide = pltpu.VMEM((size, width), bf16)
    four = pltpu.VMEM((QUAD, size, width), bf16)
    cut = min(256, width // 2)
    four_sems = pltpu.SemaphoreType.DMA((QUAD,))
    return pl.pallas_call(
        functools.partial(back_kernel, outer, inner, seq_len),
        out_shape=out_shape,
        in_specs=[vm] * len(near_args) + [hbm] * len(far_args),
        out_specs=tuple([vm] * 5 + [hbm] * 14),
        scratch_shapes=[
            four, four, pltpu.VMEM((2, size, width), bf16),
            pltpu.VMEM((size, width), f32),
            pltpu.VMEM((size, width), f32),
            pltpu.VMEM((2 * QUAD, size, width), bf16),
            wide, wide, wide,
            pltpu.VMEM((2, 2 * QUAD, size, cut), bf16),
            pltpu.VMEM((2 * QUAD, size, 3 * narrow), bf16),
            pltpu.VMEM((width, 3 * narrow), bf16),
            pltpu.VMEM((narrow, width), bf16),
            pltpu.VMEM((narrow, width), f32),
            pltpu.VMEM((places // 2 * pieces, run_rows, 3 * narrow), bf16),
            pltpu.VMEM((places // 2, rows, width), bf16),
            pltpu.VMEM((2 * QUAD * rows, 3 * narrow), bf16),
            pltpu.VMEM((2 * QUAD, rows, 3 * narrow), bf16),
            pltpu.VMEM((8, 8, width), f32),
            pltpu.SemaphoreType.DMA((remote,)),
            pltpu.SemaphoreType.DMA((remote,)),
            pltpu.SemaphoreType.DMA((local,)),
            four_sems, four_sems,
            pltpu.SemaphoreType.DMA((2,)),
            pltpu.VMEM((run_rows, width), bf16),
            pltpu.SemaphoreType.DMA((1,)),
        ],
        compiler_params=pltpu.CompilerParams(
            collective_id=1, has_side_effects=True, vmem_limit_bytes=63 * 1024 * 1024
        ),
        name="back",
    )(*near_args, *far_args)


def mid_kernel(
    outer, inner, hidden_rows,
    go_ref, factor_ref,
    act_two, wg_ref, wu_ref, wd_ref, resid_ref,
    p_g, p_u, half_d, added, layer_out, dy, p_d, land_d, land_down, land_two, a_down, b_down, a_two, b_two,
    w_g, w_u, w_d, middle, cols, act_in, dy_in, act_cut, dy_cut, stage_d, dy_own,
    far_down, far_two, tmp_down, tmp_two, near_down, near_two, own_down, own_two, halves, stage,
    send_sems, recv_sems, local_sems, down_send, down_recv, two_send, two_recv, act_sems, dy_sem, tmp_sems, cut_sems, out_sems,
):
    size, width = go_ref.shape
    hidden = w_g.shape[1]
    ring = Ring(outer, inner, width // (outer * inner))
    mail = Mail(ring, send_sems, recv_sems, local_sems)
    ring.greet()
    flat = ring.flat
    strip = 32
    top_bit = ring.count // 2

    def strips(step):
        def run(i, carry):
            step(pl.ds(pl.multiple_of(i * strip, strip), strip))
            return carry

        lax.fori_loop(0, size // strip, run, 0)

    def dot(left, right, left_dim, right_dim):
        return lax.dot_general(
            left, right, (((left_dim,), (right_dim,)), ((), ())), preferred_element_type=f32
        )

    def settle(copy):
        copy.wait()
        mail.kept = [c for c in mail.kept if c is not copy]

    def pair_at(i):
        pair = i // 2
        return pair + (pair // 2) * (5 - 2 * pair)

    def block_at(i):
        return pair_at(i) + QUAD * (1 - i % 2)

    def act_copy(i):
        return pltpu.make_async_copy(
            act_two.at[block_at(i)], act_in.at[i % 2], act_sems.at[i % 2]
        )

    act_copy(0).start()
    loads = [mail.keep(wg_ref, w_g), mail.keep(wu_ref, w_u), mail.keep(wd_ref, w_d)]
    load_resid = mail.keep(resid_ref, own_down)

    def cotangent(part):
        dy_own[part, :] = (go_ref[part, :].astype(f32) * factor_ref[part, :]).astype(bf16)

    strips(cotangent)
    keep_dy = mail.keep(dy_own, dy.at[0])
    half = size // 2
    top, end = pl.ds(0, half), pl.ds(half, half)
    share = Share(mail, dy, dy_own)
    share.first()
    for copy in loads:
        settle(copy)
    settle(load_resid)
    settle(keep_dy)
    share.done((0,))

    def core_copy(kind, i):
        pair = i // 2
        source, target, send, recv = (
            (far_down, land_down, down_send, down_recv),
            (far_two, land_two, two_send, two_recv),
        )[kind]
        return pltpu.make_async_remote_copy(
            src_ref=source,
            dst_ref=target.at[pair_at(i)],
            send_sem=send.at[pair],
            recv_sem=recv.at[pair],
            device_id=ring.where(ring.bit_core),
            device_id_type=MESH,
        )

    def tmp_copy(kind, i):
        source, target = ((land_down, tmp_down), (land_two, tmp_two))[kind]
        return pltpu.make_async_copy(source.at[pair_at(i)], target, tmp_sems.at[kind])

    base = mail.used
    mail.used += 9

    def late(n):
        src, dst, bit = (
            (dy.at[1, top], dy.at[3, top], ring.bit_b),
            (dy.at[2, end], dy.at[3, end], ring.bit_a),
            (dy.at[1], dy.at[QUAD + 1], ring.bit_core),
            (dy.at[2], dy.at[QUAD + 2], ring.bit_core),
            (dy.at[3], dy.at[QUAD + 3], ring.bit_core),
            (near_two.at[2, top], halves.at[1, 0], ring.bit_b),
            (near_two.at[2, end], halves.at[1, 1], ring.bit_a),
            (near_down.at[2, top], halves.at[0, 0], ring.bit_b),
            (near_down.at[2, end], halves.at[0, 1], ring.bit_a),
        )[n]
        return pltpu.make_async_remote_copy(
            src_ref=src,
            dst_ref=dst,
            send_sem=send_sems.at[base + n],
            recv_sem=recv_sems.at[base + n],
            device_id=ring.where(bit),
            device_id_type=MESH,
        )

    def block(i, carry):
        place = block_at(i)
        other = i % 2 == 0
        pair = pair_at(i)

        @pl.when(i == 2)
        def _():
            share.from_a.wait_recv()
            late(0).start()
            late(2).start()
            share.from_b.wait_recv()
            late(1).start()
            late(3).start()
            late(2).wait_recv()

        @pl.when(i == 4)
        def _():
            late(0).wait_recv()
            late(1).wait_recv()
            late(4).start()
            late(3).wait_recv()
            late(4).wait_recv()

        @pl.when(i == 6)
        def _():
            for n in range(5, 9):
                late(n).start()

        dy_copy = pltpu.make_async_copy(dy.at[place], dy_in, dy_sem.at[0])
        dy_copy.start()

        @pl.when(jnp.logical_not(other))
        def _():
            for kind in range(2):
                core_copy(kind, i).wait_recv()
                tmp_copy(kind, i).start()

        act_copy(i).wait()

        @pl.when(i + 1 < 2 * QUAD)
        def _():
            act_copy(i + 1).start()

        act = act_in[i % 2]
        gate_pre = dot(act, w_g[...], 1, 0)
        up_proj = dot(act, w_u[...], 1, 0)
        sigmoid_gate = jax.nn.sigmoid(gate_pre)
        swish = gate_pre * sigmoid_gate
        middle[place] = (swish * up_proj).astype(bf16)
        dy_copy.wait()
        grad_middle = dot(dy_in[...], w_d[...], 1, 1)
        cols[place, :, hidden:] = (grad_middle * swish).astype(bf16)
        cols[place, :, :hidden] = (
            grad_middle * up_proj * sigmoid_gate * (1.0 + gate_pre * (1.0 - sigmoid_gate))
        ).astype(bf16)
        down = dot(middle[place], w_d[...], 1, 0)

        def give(kind, part, far, tmp, near, own):
            @pl.when(other)
            def _():
                @pl.when(i >= 2)
                def _():
                    core_copy(kind, i - 2).wait_send()

                far[...] = part.astype(bf16)
                core_copy(kind, i).start()

            @pl.when(jnp.logical_not(other))
            def _():
                tmp_copy(kind, i).wait()
                total = part + tmp[...].astype(f32)

                @pl.when(pair == 0)
                def _():
                    own[...] = total + own[...] if kind == 0 else total

                @pl.when(pair > 0)
                def _():
                    near[jnp.maximum(pair, 1) - 1] = total.astype(bf16)

        give(0, down, far_down, tmp_down, near_down, own_down)
        two = dot(cols[place, :, :hidden], w_g[...], 1, 1) + dot(
            cols[place, :, hidden:], w_u[...], 1, 1
        )
        give(1, two, far_two, tmp_two, near_two, own_two)
        return carry

    lax.fori_loop(0, 2 * QUAD, block, 0)
    for kind in range(2):
        core_copy(kind, 2 * QUAD - 2).wait_send()

    cut = act_cut.shape[3]
    cuts = width // cut
    tokens = 2 * QUAD * size

    def cut_copy(source, target, i):
        start = pl.multiple_of(i * cut, cut)
        return pltpu.make_async_copy(
            source.at[:, :, pl.ds(start, cut)], target.at[i % 2], cut_sems.at[i % 2]
        )

    def down_out(i):
        start = pl.multiple_of(i * cut, cut)
        return pltpu.make_async_copy(
            stage_d.at[i % 2], p_d.at[:, pl.ds(start, cut)], out_sems.at[i % 2]
        )

    cut_copy(dy, dy_cut, 0).start()

    def down_step(i, carry):
        cut_copy(dy, dy_cut, i).wait()

        @pl.when(i + 1 < cuts)
        def _():
            cut_copy(dy, dy_cut, i + 1).start()

        turned = dot(
            dy_cut[i % 2].reshape(tokens, cut), middle[...].reshape(tokens, hidden), 0, 0
        )

        @pl.when(i >= 2)
        def _():
            down_out(i - 2).wait()

        stage_d[i % 2] = turned.T.astype(bf16)
        down_out(i).start()
        return carry

    lax.fori_loop(0, cuts, down_step, 0)
    cut_copy(act_two, act_cut, 0).start()
    for i in (cuts - 2, cuts - 1):
        down_out(i).wait()
    upper = flat // top_bit
    rows_half = hidden // 2
    away = pl.ds(pl.multiple_of((1 - upper) * rows_half, 16), rows_half)
    kept = pl.ds(pl.multiple_of(upper * rows_half, 16), rows_half)
    sum_d = mail.post(p_d.at[away], land_d, top_bit)

    second = {}
    for kind, near, to_a, to_b in ((1, near_two, a_two, b_two), (0, near_down, a_down, b_down)):
        late(7 - 2 * kind).wait_recv()
        add_near(near.at[0, top], near.at[0, top], halves.at[kind, 0])
        second["a", kind] = mail.post(near.at[0], to_a, ring.bit_a)
        late(8 - 2 * kind).wait_recv()
        add_near(near.at[1, end], near.at[1, end], halves.at[kind, 1])
        second["b", kind] = mail.post(near.at[1], to_b, ring.bit_b)

    def stage_out(i):
        rows = pl.ds(pl.multiple_of(i * cut, cut), cut)
        return [
            pltpu.make_async_copy(
                stage.at[i % 2, :, pl.ds(j * hidden, hidden)],
                target.at[rows],
                out_sems.at[2 + 2 * j + i % 2],
            )
            for j, target in enumerate((p_g, p_u))
        ]

    def gate_step(i, carry):
        cut_copy(act_two, act_cut, i).wait()

        @pl.when(i + 1 < cuts)
        def _():
            cut_copy(act_two, act_cut, i + 1).start()

        @pl.when(i >= 2)
        def _():
            for copy in stage_out(i - 2):
                copy.wait()

        stage[i % 2] = dot(
            act_cut[i % 2].reshape(tokens, cut), cols[...].reshape(tokens, 2 * hidden), 0, 0
        ).astype(bf16)
        for copy in stage_out(i):
            copy.start()
        return carry

    lax.fori_loop(0, cuts, gate_step, 0)
    for i in (cuts - 2, cuts - 1):
        for copy in stage_out(i):
            copy.wait()

    for kind, own, in_a, in_b in ((1, own_two, a_two, b_two), (0, own_down, a_down, b_down)):
        second["a", kind].wait_recv()
        second["b", kind].wait_recv()
        first = mail.keep(in_a, tmp_down)
        other = mail.keep(in_b, tmp_two)
        settle(first)
        settle(other)

        def finish(part, own=own, kind=kind):
            total = own[part, :] + tmp_down[part, :].astype(f32) + tmp_two[part, :].astype(f32)
            if kind:
                own_two[part, :] = total
            else:
                far_down[part, :] = total.astype(bf16)

        strips(finish)
        if kind:
            mail.keep(own_two, added)
        else:
            mail.keep(far_down, layer_out)
    sum_d.wait_recv()
    add_far(half_d, p_d.at[kept], land_d)
    for n in range(9):
        late(n).wait_send()
    mail.finish()


def mid(outer, inner, hidden_rows, grad_out, factor_rows, act_two, w_g, w_u, w_d, resid):
    size, width = grad_out.shape
    hidden = w_g.shape[1]
    vm = pl.BlockSpec(memory_space=pltpu.VMEM)
    hbm = pl.BlockSpec(memory_space=pl.ANY)
    sds = jax.ShapeDtypeStruct
    wide = sds((size, width), bf16)
    out_shape = (
        sds((width, hidden), bf16),
        sds((width, hidden), bf16),
        sds((hidden // 2, width), bf16),
        sds((size, width), f32),
        wide,
        sds((2 * QUAD, size, width), bf16),
        sds((hidden, width), bf16),
        sds((hidden // 2, width), bf16),
        sds((QUAD, size, width), bf16),
        sds((QUAD, size, width), bf16),
        wide, wide, wide, wide,
    )
    cut = min(256, width // 2)
    vw = pltpu.VMEM((size, width), bf16)
    dma = pltpu.SemaphoreType.DMA
    return pl.pallas_call(
        functools.partial(mid_kernel, outer, inner, hidden_rows),
        out_shape=out_shape,
        in_specs=[vm] * 2 + [hbm] * 5,
        out_specs=tuple([hbm] * len(out_shape)),
        scratch_shapes=[
            pltpu.VMEM((width, hidden), bf16),
            pltpu.VMEM((width, hidden), bf16),
            pltpu.VMEM((hidden, width), bf16),
            pltpu.VMEM((2 * QUAD, size, hidden), bf16),
            pltpu.VMEM((2 * QUAD, size, 2 * hidden), bf16),
            pltpu.VMEM((2, size, width), bf16),
            vw,
            pltpu.VMEM((2, 2 * QUAD, size, cut), bf16),
            pltpu.VMEM((2, 2 * QUAD, size, cut), bf16),
            pltpu.VMEM((2, hidden, cut), bf16),
            vw,
            vw, vw, vw, vw,
            pltpu.VMEM((QUAD - 1, size, width), bf16),
            pltpu.VMEM((QUAD - 1, size, width), bf16),
            pltpu.VMEM((size, width), f32),
            pltpu.VMEM((size, width), f32),
            pltpu.VMEM((2, 2, size // 2, width), bf16),
            pltpu.VMEM((2, cut, 2 * hidden), bf16),
            dma((32,)), dma((32,)), dma((16,)),
            dma((QUAD,)), dma((QUAD,)), dma((QUAD,)), dma((QUAD,)),
            dma((2,)), dma((1,)), dma((2,)), dma((2,)), dma((6,)),
        ],
        compiler_params=pltpu.CompilerParams(
            collective_id=2, has_side_effects=True, vmem_limit_bytes=63 * 1024 * 1024
        ),
        name="mid",
    )(grad_out, factor_rows, act_two, w_g, w_u, w_d, resid)


def on_device(
    tokens,
    labels,
    counts,
    grad_out,
    w_query,
    w_key,
    w_value,
    w_out,
    gain_attn,
    gain_mlp,
    w_gate,
    w_up,
    w_down,
):
    batch_size, seq_len, width = tokens.shape
    outer_count = lax.axis_size("dp")
    inner_count = lax.axis_size("fsdp")
    rows = w_query.shape[0]
    hidden_rows = w_down.shape[0]
    flat = lax.axis_index("dp") * inner_count + lax.axis_index("fsdp")
    x_rows = tokens.reshape(-1, width)

    token_total = float(seq_len * batch_size * outer_count * inner_count)
    picked_counts = jnp.sum(
        jnp.where(labels[:, None] == jnp.arange(3)[None, :], counts[None, :], 0), axis=1
    ).astype(f32)
    factor = token_total / (3.0 * picked_counts)
    cosine, sine = rope_tables(seq_len, HEAD_DIM)
    head_count = width // (2 * QUAD) // HEAD_DIM
    sign = jnp.where(jnp.arange(HEAD_DIM) < HEAD_DIM // 2, -1.0, 1.0)
    wide_cosine = jnp.tile(cosine, (1, head_count))
    wide_sine = jnp.tile(sine * sign, (1, head_count))
    gain_rows = lax.dynamic_update_slice(
        jnp.zeros((8, width), f32),
        jnp.stack([gain_attn, gain_mlp]).astype(f32),
        (0, flat * rows),
    )
    factor_rows = jnp.repeat(factor, seq_len)[:, None]
    (
        act_one, w_qkv, w_o, q_rot, k_rot, values, attended, resid, gains, act_two, w_g, w_u, w_d,
    ) = front(
        outer_count, inner_count, seq_len,
        x_rows, gain_rows,
        w_query, w_key, w_value,
        wide_cosine, wide_sine,
        w_out, w_gate, w_up, w_down,
    )
    p_g, p_u, half_d, added, layer_out = mid(
        outer_count, inner_count, w_down.shape[0], grad_out.reshape(-1, width), factor_rows,
        act_two, w_g, w_u, w_d, resid,
    )[:5]
    layer_out = layer_out.reshape(tokens.shape)
    results = back(
        outer_count, inner_count, seq_len,
        (
            x_rows, grad_out.reshape(-1, width), factor_rows, gains, q_rot, k_rot, values, attended,
            w_qkv, w_o, wide_cosine, wide_sine,
        ),
        (p_g, p_u, half_d, act_one, resid, added),
    )
    query_grad, key_grad, value_grad, out_grad, gain_grads = results[:5]
    gate_grad, up_grad, down_grad = (a.astype(f32) for a in results[5:8])
    grad_tokens = results[-1]
    gain_grads = lax.dynamic_slice(gain_grads, (0, flat * rows), (2, rows))
    return (
        layer_out,
        grad_tokens.reshape(tokens.shape),
        query_grad,
        key_grad,
        value_grad,
        out_grad,
        gain_grads[0],
        gain_grads[1],
        gate_grad,
        up_grad,
        down_grad,
    )


def solution(mesh):
    rows = P(AXES, None)
    vector = P(AXES)
    three = P(AXES, None, None)
    in_specs = (three, vector, P(), three, rows, rows, rows, rows, vector, vector, rows, rows, rows)
    out_specs = (three, three, rows, rows, rows, rows, vector, vector, rows, rows, rows)
    return jax.shard_map(
        on_device, mesh=mesh, in_specs=in_specs, out_specs=out_specs, check_vma=False
    )
```

```python
import functools

import jax
import jax.numpy as jnp
from jax import lax
from jax.experimental import pallas as pl
from jax.experimental.pallas import tpu as pltpu
from jax.sharding import PartitionSpec as P

HEAD_DIM = 64
AXES = ("dp", "fsdp")
QUAD = 4

epsilon = 1e-05
rope_base = 130000.0
bf16 = jnp.bfloat16
f32 = jnp.float32
MESH = pl.DeviceIdType.MESH


def rope_tables(seq_len, head_dim):
    half_dim = head_dim // 2
    frequency = rope_base ** (-(jnp.arange(half_dim).astype(f32) * 2.0) / head_dim)
    angles = jnp.arange(seq_len).astype(f32)[:, None] * frequency[None, :]
    angles = jnp.concatenate([angles, angles], axis=1)
    return (jnp.cos(angles), jnp.sin(angles))


class Ring:
    def __init__(self, outer, inner, rows):
        self.known = {}
        self.count = outer * inner
        self.inner = inner
        self.span = max(1, HEAD_DIM // rows)
        self.bit_a = self.span
        self.bit_b = 2 * self.span
        self.bit_core = inner
        self.low = powers(1, self.span)
        self.mid = powers(QUAD * self.span, inner)
        self.upper = powers(2 * inner, self.count)
        self.data_bits = self.low + self.mid + self.upper
        self.deltas = [
            (self.bit_core if t // QUAD else 0) + (t % QUAD) * self.span for t in range(2 * QUAD)
        ]
        self.across = inner // (QUAD * self.span)
        self.upper_size = outer // 2
        self.flat = lax.axis_index("dp") * inner + lax.axis_index("fsdp")

    def flip(self, flat, bits):
        bit = 1
        while bit <= bits:
            if bits & bit:
                flat = flat + bit * (1 - 2 * ((flat // bit) % 2))
            bit *= 2
        return flat

    def where(self, bits):
        if bits not in self.known:
            other = self.flip(self.flat, bits)
            self.known[bits] = (other // self.inner, other % self.inner)
        return self.known[bits]

    def team(self, flat):
        return ((flat // self.inner) % 2) * QUAD + (flat // self.span) % QUAD

    def place(self, flat):
        return (
            (flat // (2 * self.inner)) * self.across + (flat % self.inner) // (QUAD * self.span)
        ) * self.span + flat % self.span

    def runs(self, flat, rows):
        lowest = flat - self.span * ((flat // self.span) % QUAD)
        lowest = lowest - self.inner * ((flat // self.inner) % 2)
        found = []
        for core in range(2):
            start = lowest + core * self.inner
            if self.span == 1:
                found.append((start * rows, QUAD * rows))
            else:
                found += [((start + q * self.span) * rows, rows) for q in range(QUAD)]
        return found

    def greet(self):
        partners = self.deltas[1:] + self.data_bits
        barrier = pltpu.get_barrier_semaphore()
        for bits in partners:
            pl.semaphore_signal(barrier, 1, device_id=self.where(bits), device_id_type=MESH)
        pl.semaphore_wait(barrier, len(partners))


def powers(first, end):
    found = []
    while first < end:
        found.append(first)
        first *= 2
    return found


class Mail:
    def __init__(self, ring, send_sems, recv_sems, local_sems):
        self.ring, self.send_sems, self.recv_sems, self.local_sems = ring, send_sems, recv_sems, local_sems
        self.used = 0
        self.used_local = 0
        self.sent = []
        self.kept = []

    def post(self, src, dst, bits):
        copy = pltpu.make_async_remote_copy(
            src_ref=src,
            dst_ref=dst,
            send_sem=self.send_sems.at[self.used],
            recv_sem=self.recv_sems.at[self.used],
            device_id=self.ring.where(bits),
            device_id_type=MESH,
        )
        self.used += 1
        copy.start()
        self.sent.append(copy)
        return copy

    def keep(self, src, dst):
        copy = pltpu.make_async_copy(src, dst, self.local_sems.at[self.used_local])
        self.used_local += 1
        copy.start()
        self.kept.append(copy)
        return copy

    def drop(self, copy):
        self.sent = [c for c in self.sent if c is not copy]

    def finish(self):
        for copy in self.sent:
            copy.wait_send()
        for copy in self.kept:
            copy.wait()


class Spread:
    def __init__(self, mail, views, bits):
        self.mail, self.views, self.bits = mail, views, bits
        self.pieces = len(views(0))
        self.came = {}

    def start(self, key, piece, first):
        ref = self.views(key)[piece]
        for bit in self.bits[first:]:
            self.came[key + bit, piece] = self.mail.post(ref, ref, bit)

    def begin(self, piece=None):
        for p in range(self.pieces) if piece is None else (piece,):
            self.start(0, p, 0)

    def pass_on(self, stage, piece=None):
        for p in range(self.pieces) if piece is None else (piece,):
            for key in keys_below(self.bits, stage):
                key += self.bits[stage]
                self.came.pop((key, p)).wait_recv()
                self.start(key, p, stage + 1)

    def pass_all(self, piece=None):
        for stage in range(len(self.bits) - 1):
            self.pass_on(stage, piece)

    def done(self):
        for copy in self.came.values():
            copy.wait_recv()


def keys_below(bits, stage):
    return [
        sum(b for i, b in enumerate(bits[:stage]) if low >> i & 1) for low in range(2**stage)
    ]


class Adding:
    def __init__(self, mail, ref, came_in, bits):
        self.mail, self.ref, self.came_in, self.bits = mail, ref, came_in, bits
        self.step = 0

    def post(self):
        self.copy = self.mail.post(
            self.ref, self.came_in.at[self.step], self.bits[self.step]
        )

    def take(self):
        self.copy.wait()
        self.mail.drop(self.copy)
        self.ref[...] = self.ref[...] + self.came_in[self.step]
        self.step += 1


class Share:
    def __init__(self, mail, whole, own):
        self.mail, self.whole, self.own = mail, whole, own
        self.core = []

    def first_core(self):
        self.to_core(self.own, 0)

    def first_a(self):
        self.from_a = self.mail.post(self.own, self.whole.at[1], self.mail.ring.bit_a)

    def first_b(self):
        self.from_b = self.mail.post(self.own, self.whole.at[2], self.mail.ring.bit_b)

    def first(self):
        self.first_a()
        self.first_b()
        self.first_core()

    def to_core(self, ref, place):
        self.core.append(
            self.mail.post(ref, self.whole.at[QUAD + place], self.mail.ring.bit_core)
        )

    def second_a(self):
        self.from_a.wait_recv()
        self.to_core(self.whole.at[1], 1)

    def second_b(self):
        self.from_b.wait_recv()
        self.both = self.mail.post(self.whole.at[2], self.whole.at[3], self.mail.ring.bit_a)
        self.to_core(self.whole.at[2], 2)

    def second(self):
        self.second_a()
        self.second_b()

    def third(self):
        self.both.wait_recv()
        self.to_core(self.whole.at[3], 3)

    def done(self, places=range(QUAD)):
        for place in places:
            self.core[place].wait_recv()


def add_near(target, left, right):
    rows = left.shape[0]
    strip = min(32, rows)

    def step(i, carry):
        part = pl.ds(pl.multiple_of(i * strip, strip), strip)
        target[part, :] = (left[part, :].astype(f32) + right[part, :].astype(f32)).astype(
            target.dtype
        )
        return carry

    lax.fori_loop(0, rows // strip, step, 0)


class Total:
    def __init__(self, mail, near, own, mid, in_a, in_b):
        self.mail, self.near, self.own = mail, near, own
        self.mid, self.in_a, self.in_b = mid, in_a, in_b

    def first(self):
        self.over = self.mail.post(self.near.at[3], self.mid, self.mail.ring.bit_a)

    def first_a(self):
        self.for_a = self.mail.post(self.near.at[1], self.in_a, self.mail.ring.bit_a)

    def second(self):
        self.over.wait_recv()
        add_near(self.near.at[2], self.near.at[2], self.mid)
        self.for_b = self.mail.post(self.near.at[2], self.in_b, self.mail.ring.bit_b)

    def arrive(self):
        self.for_a.wait_recv()
        self.for_b.wait_recv()

    def value(self, part):
        return self.own[part, :] + self.in_a[part, :].astype(f32) + self.in_b[part, :].astype(f32)


def head_mask(width, head):
    lanes = lax.broadcasted_iota(jnp.int32, (1, width), 1)
    return (lanes >= head * HEAD_DIM) & (lanes < (head + 1) * HEAD_DIM)


def turn(u, cosine, signed_sine):
    width = u.shape[-1]
    half = HEAD_DIM // 2
    lanes = lax.broadcasted_iota(jnp.int32, (1, width), 1)
    lower = lanes % HEAD_DIM < half
    turned = jnp.where(lower, pltpu.roll(u, width - half, 1), pltpu.roll(u, half, 1))
    return u * cosine + turned * signed_sine


def front_kernel(
    outer, inner, seq_len,
    x_ref, gain_ref, wq_ref, wk_ref, wv_ref, cos_ref, sin_ref,
    wo_ref, wg_ref, wu_ref, wd_ref,
    act_one, w_qkv, w_o, q_out, k_out, v_out, att_out, resid_out, gains_out,
    act_two, w_g, w_u, w_d,
    cut, gain_in, x_all, far, core_in, near, own_sum, mid, in_a, in_b, act_two_own,
    send_sems, recv_sems, local_sems, far_send, far_recv,
):
    rows = wq_ref.shape[0]
    width = wq_ref.shape[1]
    hidden_rows = wd_ref.shape[0]
    narrow = width // (2 * QUAD)
    ring = Ring(outer, inner, rows)
    mail = Mail(ring, send_sems, recv_sems, local_sems)
    ring.greet()
    bits = ring.data_bits
    flat = ring.flat

    def by_place(ref, size, pieces):
        step = size // pieces
        return lambda key: [
            ref.at[
                pl.ds(
                    pl.multiple_of(ring.place(ring.flip(flat, key)) * size + p * step, 16), step
                )
            ]
            for p in range(pieces)
        ]

    def by_runs(ref):
        return lambda key: [
            ref.at[pl.ds(pl.multiple_of(start, 16), size)]
            for start, size in ring.runs(ring.flip(flat, key), rows)
        ]

    def settle(copy):
        copy.wait()
        mail.kept = [c for c in mail.kept if c is not copy]

    mine_o = w_o.at[pl.ds(pl.multiple_of(ring.place(flat) * rows, 16), rows)]
    mine_d = w_d.at[pl.ds(pl.multiple_of(ring.place(flat) * hidden_rows, 16), hidden_rows)]
    keep_o = mail.keep(wo_ref, mine_o)
    keep_d = mail.keep(wd_ref, mine_d)
    keep_x = mail.keep(x_ref, x_all.at[0])

    gains_out[...] = gain_ref[...]
    gains = Adding(
        mail, gains_out, gain_in, [ring.bit_a, ring.bit_b, ring.bit_core] + bits
    )
    gains.post()

    chunk = HEAD_DIM
    for t in range(2 * QUAD):
        for j, ref in enumerate((wq_ref, wk_ref, wv_ref)):
            parts = []
            for y in range(ring.upper_size):
                for o in range(ring.across):
                    head = ((y * 2 + t // QUAD) * ring.across + o) * QUAD + t % QUAD
                    parts.append(ref[:, head * chunk : (head + 1) * chunk])
            cut[t, :, j * narrow : (j + 1) * narrow] = jnp.concatenate(parts, axis=1)
    here = pl.ds(pl.multiple_of(flat * rows, 16), rows)
    keep_qkv = mail.keep(cut.at[ring.team(flat)], w_qkv.at[here])
    gains.take()
    gains.post()
    qkv_swap = []
    for delta in ring.deltas[1:]:
        other = ring.flip(flat, delta)
        qkv_swap.append(mail.post(cut.at[ring.team(other)], w_qkv.at[here], delta))
    share_x = Share(mail, x_all, x_ref)
    share_x.first_core()
    share_x.first_a()
    gains.take()
    gains.post()
    settle(keep_o)
    spread_o = Spread(mail, by_place(w_o, rows, 1), bits)
    gains.take()
    gains.post()
    spread_o.begin()
    share_x.first_b()
    settle(keep_qkv)
    for copy in qkv_swap:
        copy.wait_recv()
    spread_qkv = Spread(mail, by_runs(w_qkv), bits)
    spread_qkv.begin()
    while gains.step < len(gains.bits) - 1:
        gains.take()
        gains.post()
    spread_o.pass_all()
    gains.take()

    block = ring.span * hidden_rows

    def swap_columns(ref, whole):
        swap = []
        for delta in ring.deltas:
            team = ring.team(ring.flip(flat, delta))
            for y in range(ring.upper_size):
                for o in range(ring.across):
                    source = ((y * 2 + team // QUAD) * ring.across + o) * QUAD + team % QUAD
                    src = ref.at[:, pl.ds(pl.multiple_of(source * block, 128), block)]
                    dst = whole.at[here, pl.ds((y * ring.across + o) * block, block)]
                    if delta:
                        swap.append((mail.post(src, dst, delta), True))
                    else:
                        swap.append((mail.keep(src, dst), False))
        return swap

    def swapped(swap):
        for copy, remote in swap:
            if remote:
                copy.wait_recv()
            else:
                settle(copy)

    size = act_one.shape[1]
    strip = 32

    def norm_block(place):
        def norm_one(i, carry):
            part = pl.ds(pl.multiple_of(i * strip, strip), strip)
            x = x_all[place, part, :].astype(f32)
            inv = lax.rsqrt(jnp.mean(x * x, axis=-1, keepdims=True) + epsilon)
            act_one[place, part, :] = (x * inv * gains_out[0:1, :]).astype(bf16)
            return carry

        lax.fori_loop(0, size // strip, norm_one, 0)

    share_x.second_a()
    gate_swap = swap_columns(wg_ref, w_g)
    settle(keep_d)
    spread_d = Spread(mail, by_place(w_d, hidden_rows, 2), bits)
    spread_d.begin()
    settle(keep_x)
    share_x.done((0, 1))
    for place in (0, QUAD, 1, QUAD + 1):
        norm_block(place)
    share_x.second_b()
    for piece in range(spread_qkv.pieces):
        spread_qkv.pass_all(piece)
    up_swap = swap_columns(wu_ref, w_u)
    share_x.done((2,))
    for place in (2, QUAD + 2):
        norm_block(place)
    spread_o.done()
    spread_qkv.done()

    scale = HEAD_DIM**-0.5
    cosine, sine = cos_ref[...], sin_ref[...]
    per_block = act_one.shape[1] // seq_len

    def attend_block(place):
        qkv = jnp.dot(act_one[place], w_qkv[...], preferred_element_type=f32)
        causal = lax.broadcasted_iota(jnp.int32, (seq_len, seq_len), 1) <= lax.broadcasted_iota(
            jnp.int32, (seq_len, seq_len), 0
        )
        for b in range(per_block):
            span = slice(b * seq_len, (b + 1) * seq_len)
            q = turn(qkv[span, :narrow], cosine, sine).astype(bf16)
            k = turn(qkv[span, narrow : 2 * narrow], cosine, sine).astype(bf16)
            v = qkv[span, 2 * narrow :].astype(bf16)
            q_out[place, span] = q
            k_out[place, span] = k
            v_out[place, span] = v
            mixed = jnp.zeros((seq_len, narrow), f32)
            for head in range(narrow // HEAD_DIM):
                mask = head_mask(narrow, head)
                kh = jnp.where(mask, k, jnp.zeros_like(k))
                vh = jnp.where(mask, v, jnp.zeros_like(v))
                scores = lax.dot_general(
                    q, kh, (((1,), (1,)), ((), ())), preferred_element_type=f32
                )
                scores = jnp.where(causal, scores * scale, -1e30)
                top = jnp.max(scores, axis=-1, keepdims=True)
                grown = jnp.exp(scores - top)
                soft = (grown / jnp.sum(grown, axis=-1, keepdims=True)).astype(bf16)
                mixed = mixed + jnp.dot(soft, vh, preferred_element_type=f32)
            att_out[place, span] = mixed.astype(bf16)
        return jnp.dot(att_out[place], w_o[...], preferred_element_type=f32)

    def far_copy(j):
        return pltpu.make_async_remote_copy(
            src_ref=far.at[j],
            dst_ref=core_in.at[j],
            send_sem=far_send.at[j],
            recv_sem=far_recv.at[j],
            device_id=ring.where(ring.bit_core),
            device_id_type=MESH,
        )

    def far_step(j, carry):
        far[j] = attend_block(QUAD + j).astype(bf16)
        far_copy(j).start()
        return carry

    def near_step(j, carry):
        part = attend_block(j)
        far_copy(j).wait_recv()
        total = part + core_in[j].astype(f32)
        near[j] = total.astype(bf16)

        @pl.when(j == 0)
        def _():
            own_sum[...] = total

        return carry

    spread_g = Spread(mail, by_runs(w_g), bits)
    spread_u = Spread(mail, by_runs(w_u), bits)
    lax.fori_loop(0, QUAD - 1, far_step, 0)
    share_x.third()
    swapped(gate_swap)
    spread_g.begin()
    lax.fori_loop(0, QUAD - 1, near_step, 0)
    norm_block(QUAD - 1)
    share_x.done((QUAD - 1,))
    norm_block(2 * QUAD - 1)
    far_step(QUAD - 1, 0)
    near_step(QUAD - 1, 0)
    for j in range(QUAD):
        far_copy(j).wait_send()
    total = Total(mail, near, own_sum, mid, in_a, in_b)
    total.first()
    total.first_a()
    swapped(up_swap)
    spread_u.begin()
    for piece in range(spread_d.pieces):
        spread_d.pass_on(0, piece)
    total.second()
    spread_g.pass_on(0, 0)
    total.arrive()

    def norm_two(i, carry):
        part = pl.ds(pl.multiple_of(i * strip, strip), strip)
        resid = (
            x_ref[part, :].astype(f32) + total.value(part)
        )
        resid_out[part, :] = resid
        inv = lax.rsqrt(jnp.mean(resid * resid, axis=-1, keepdims=True) + epsilon)
        act_two_own[part, :] = (resid * inv * gains_out[1:2, :]).astype(bf16)
        return carry

    lax.fori_loop(0, size // strip, norm_two, 0)
    mail.keep(act_two_own, act_two.at[0])
    share_two = Share(mail, act_two, act_two_own)
    share_two.first()
    for piece in range(1, spread_g.pieces):
        spread_g.pass_on(0, piece)
    share_two.second()
    spread_u.pass_on(0)
    share_two.third()
    for stage in range(1, len(bits) - 1):
        for spread in (spread_d, spread_g, spread_u):
            spread.pass_on(stage)
    spread_d.done()
    spread_g.done()
    spread_u.done()
    share_two.done()
    mail.finish()


def front(outer, inner, seq_len, tokens, gain_rows, w_query, w_key, w_value, cosine, signed_sine, w_out, w_gate, w_up, w_down):
    size, width = tokens.shape
    rows, hidden_all = w_gate.shape
    hidden_rows = w_down.shape[0]
    narrow, hidden = width // (2 * QUAD), hidden_all // (2 * QUAD)
    span = max(1, HEAD_DIM // rows)
    places = outer * inner // (2 * QUAD)
    pieces = 2 if span == 1 else 2 * QUAD
    remote = (places - 1) * (3 * pieces + 3) + 7 + 14 * places // span + 8 + 24
    local = 8 + 2 * places // span
    vm = pl.BlockSpec(memory_space=pltpu.VMEM)
    hbm = pl.BlockSpec(memory_space=pl.ANY)
    eight = (2 * QUAD, size)
    sds = jax.ShapeDtypeStruct
    out_shape = (
        sds(eight + (width,), bf16),
        sds((width, 3 * narrow), bf16),
        sds((narrow, width), bf16),
        sds(eight + (narrow,), bf16),
        sds(eight + (narrow,), bf16),
        sds(eight + (narrow,), bf16),
        sds(eight + (narrow,), bf16),
        sds((size, width), f32),
        sds((8, width), f32),
        sds(eight + (width,), bf16),
        sds((width, hidden), bf16),
        sds((width, hidden), bf16),
        sds((hidden, width), bf16),
    )
    return pl.pallas_call(
        functools.partial(front_kernel, outer, inner, seq_len),
        out_shape=out_shape,
        in_specs=[vm] * 7 + [hbm] * 4,
        out_specs=tuple([vm] * 9 + [hbm] * 4),
        scratch_shapes=[
            pltpu.VMEM((2 * QUAD, rows, 3 * narrow), bf16),
            pltpu.VMEM((8, 8, width), f32),
            pltpu.VMEM((2 * QUAD, size, width), bf16),
            pltpu.VMEM((QUAD, size, width), bf16),
            pltpu.VMEM((QUAD, size, width), bf16),
            pltpu.VMEM((QUAD, size, width), bf16),
            pltpu.VMEM((size, width), f32),
            pltpu.VMEM((size, width), bf16),
            pltpu.VMEM((size, width), bf16),
            pltpu.VMEM((size, width), bf16),
            pltpu.VMEM((size, width), bf16),
            pltpu.SemaphoreType.DMA((remote,)),
            pltpu.SemaphoreType.DMA((remote,)),
            pltpu.SemaphoreType.DMA((local,)),
            pltpu.SemaphoreType.DMA((QUAD,)),
            pltpu.SemaphoreType.DMA((QUAD,)),
        ],
        compiler_params=pltpu.CompilerParams(
            collective_id=0, has_side_effects=True, vmem_limit_bytes=60 * 1024 * 1024
        ),
        name="front",
    )(tokens, gain_rows, w_query, w_key, w_value, cosine, signed_sine, w_out, w_gate, w_up, w_down)


def add_far(target, left, right):
    rows, width = left.shape
    strip = min(64, rows)

    def body(left_ref, right_ref, target_ref):
        target_ref[...] = (left_ref[...].astype(f32) + right_ref[...].astype(f32)).astype(
            target_ref.dtype
        )

    spec = pl.BlockSpec((strip, width), lambda i: (i, 0))
    pltpu.emit_pipeline(body, grid=(rows // strip,), in_specs=[spec, spec], out_specs=[spec])(
        left, right, target
    )


class Collect:
    def __init__(self, mail, bits, views, landed, sums, last, add):
        self.mail, self.bits, self.views = mail, bits, views
        self.landed, self.sums, self.last, self.add = landed, sums, last, add
        self.came = {}
        self.added = set()
        self.pieces = len(views(0))

    def slot(self, stage, sub, piece):
        return (2**stage - 1 + keys_below(self.bits, stage).index(sub)) * self.pieces + piece

    def current(self, sub, piece):
        if (sub, piece) not in self.added:
            return self.views(sub)[piece]
        return self.sums.at[keys_below(self.bits, len(self.bits)).index(sub) * self.pieces + piece]

    def send(self, stage, sub, piece):
        bit = self.bits[stage]
        self.came[stage, sub, piece] = self.mail.post(
            self.current(bit + sub, piece), self.landed.at[self.slot(stage, sub, piece)], bit
        )

    def start(self, which=None):
        stage = len(self.bits) - 1
        for sub in reversed(keys_below(self.bits, stage)):
            if which is None or (sub != 0) == which:
                for piece in range(self.pieces):
                    self.send(stage, sub, piece)

    def take(self, stage, sub, piece):
        self.came[stage, sub, piece].wait_recv()
        here = self.current(sub, piece)
        landed = self.landed.at[self.slot(stage, sub, piece)]
        if stage == 0:
            self.add(self.last(piece), here, landed)
            return
        place = keys_below(self.bits, len(self.bits)).index(sub) * self.pieces + piece
        self.add(self.sums.at[place], here, landed)
        self.added.add((sub, piece))
        below = self.bits[stage - 1]
        if (sub // below) % 2:
            self.send(stage - 1, sub - below, piece)

    def take_away(self, stage, piece):
        below = self.bits[stage - 1]
        for sub in keys_below(self.bits, stage):
            if (sub // below) % 2:
                self.take(stage, sub, piece)

    def take_here(self, stage, piece):
        below = self.bits[stage - 1] if stage else 0
        for sub in keys_below(self.bits, stage):
            if not stage or not (sub // below) % 2:
                self.take(stage, sub, piece)

    def finish_piece(self, piece):
        top = len(self.bits) - 1
        for stage in range(top, -1, -1):
            if stage and stage != top:
                self.take_away(stage, piece)
            self.take_here(stage, piece)


def norm_back(total, base, gain):
    inv = lax.rsqrt(jnp.mean(base * base, axis=-1, keepdims=True) + epsilon)
    scaled = gain * total
    grads = inv * scaled - base * inv**3 * jnp.mean(scaled * base, axis=-1, keepdims=True)
    return grads, total * base * inv


def back_kernel(
    outer, inner, seq_len,
    x_ref, go_ref, factor_ref, gains_ref, q_ref, k_ref, v_ref, att_ref, w_qkv, w_o, cos_ref, sin_ref,
    p_g, p_u, half_d, act_one, resid_ref, two_ref,
    out_q, out_k, out_v, out_o, gain_grads,
    out_gate, out_up, out_d, land_g, land_u, land_d, sum_g, sum_u, sum_d, fin_g, fin_u, land_qkv, land_o, grad_tokens,
    near, core_in, far, own_sum, grad_resid, branch,
    mid, in_a, in_b,
    acts, d_qkv, p_qkv, p_o, p_o_sum, sum_qkv, sum_o, fin_qkv, qkv_in, gain_in,
    send_sems, recv_sems, local_sems, far_send, far_recv, act_sems, add_buf, add_sem,
):
    size, width = x_ref.shape
    rows = out_q.shape[0]
    hidden_rows = out_d.shape[0]
    narrow = w_o.shape[0]
    hidden = p_g.shape[1]
    ring = Ring(outer, inner, rows)
    mail = Mail(ring, send_sems, recv_sems, local_sems)
    ring.greet()
    bits = ring.data_bits
    flat = ring.flat
    strip = 32
    core_partner = ring.where(ring.bit_core)

    def strips(step):
        def run(i, carry):
            step(pl.ds(pl.multiple_of(i * strip, strip), strip))
            return carry

        lax.fori_loop(0, size // strip, run, 0)

    def by_place(ref, count):
        return lambda key: [
            ref.at[pl.ds(pl.multiple_of(ring.place(ring.flip(flat, key)) * count, 16), count)]
        ]

    def by_runs(ref):
        return lambda key: [
            ref.at[pl.ds(pl.multiple_of(start, 16), count)]
            for start, count in ring.runs(ring.flip(flat, key), rows)
        ]

    def dot(left, right, left_dim, right_dim):
        return lax.dot_general(
            left, right, (((left_dim,), (right_dim,)), ((), ())), preferred_element_type=f32
        )

    run_rows = ring.runs(flat, rows)[0][1]
    top_stage = len(bits) - 1
    collect_g, collect_u = (
        Collect(
            mail, bits, by_runs(partial), landed, sums,
            lambda piece, last=last: last.at[pl.ds(piece * run_rows, run_rows)], add_far,
        )
        for partial, landed, sums, last in (
            (p_g, land_g, sum_g, fin_g), (p_u, land_u, sum_u, fin_u)
        )
    )
    share_count = half_d.shape[0] // hidden_rows

    def half_place(key):
        place = ring.place(ring.flip(flat, key)) % share_count
        return [half_d.at[pl.ds(pl.multiple_of(place * hidden_rows, 16), hidden_rows)]]

    collect_d = Collect(mail, bits[:-1], half_place, land_d, sum_d, lambda piece: out_d, add_far)

    load_resid = mail.keep(resid_ref, grad_resid)
    load_two = mail.keep(two_ref, own_sum)
    collect_d.start()
    for which in (True, False):
        collect_g.start(which)
        collect_u.start(which)
    gain_grads[...] = jnp.zeros_like(gain_grads)
    for copy in (load_resid, load_two):
        copy.wait()
        mail.kept = [c for c in mail.kept if c is not copy]

    def second_norm(part):
        resid = grad_resid[part, :]
        grads, terms = norm_back(own_sum[part, :], resid, gains_ref[1:2, :])
        grads = grads + go_ref[part, :].astype(f32) * factor_ref[part, :]
        grad_resid[part, :] = grads
        branch[0, part, :] = grads.astype(bf16)
        gain_grads[1:2, :] = gain_grads[1:2, :] + jnp.sum(terms, axis=0, keepdims=True)

    strips(second_norm)
    share = Share(mail, branch, branch.at[0])
    share.first()
    for piece in range(collect_g.pieces):
        collect_g.take_away(top_stage, piece)
    share.second()
    for piece in range(collect_u.pieces):
        collect_u.take_away(top_stage, piece)
    share.third()
    p_o_sum[...] = jnp.zeros_like(p_o_sum)
    share.done()

    scale = HEAD_DIM**-0.5
    cosine, sine = cos_ref[...], sin_ref[...]
    per_block = size // seq_len

    def attend_block(place):
        grads = branch[place]
        grad_att = dot(grads, w_o[...], 1, 1).astype(bf16)
        p_o_sum[...] = p_o_sum[...] + dot(att_ref[place], grads, 0, 0)
        causal = lax.broadcasted_iota(jnp.int32, (seq_len, seq_len), 1) <= lax.broadcasted_iota(
            jnp.int32, (seq_len, seq_len), 0
        )
        for b in range(per_block):
            span = slice(b * seq_len, (b + 1) * seq_len)
            q, k, v = q_ref[place, span], k_ref[place, span], v_ref[place, span]
            ga = grad_att[span]
            dq = jnp.zeros((seq_len, narrow), f32)
            dk = jnp.zeros((seq_len, narrow), f32)
            dv = jnp.zeros((seq_len, narrow), f32)
            for head in range(narrow // HEAD_DIM):
                mask = head_mask(narrow, head)
                kh = jnp.where(mask, k, jnp.zeros_like(k))
                vh = jnp.where(mask, v, jnp.zeros_like(v))
                qh = jnp.where(mask, q, jnp.zeros_like(q))
                gh = jnp.where(mask, ga, jnp.zeros_like(ga))
                scores = jnp.where(causal, dot(q, kh, 1, 1) * scale, -1e30)
                grown = jnp.exp(scores - jnp.max(scores, axis=-1, keepdims=True))
                soft = grown / jnp.sum(grown, axis=-1, keepdims=True)
                grad_soft = dot(ga, vh, 1, 1)
                grad_scores = (
                    soft * (grad_soft - jnp.sum(soft * grad_soft, axis=-1, keepdims=True))
                ).astype(bf16)
                dq = dq + dot(grad_scores, kh, 1, 0)
                dk = dk + dot(grad_scores, qh, 0, 0)
                dv = dv + dot(soft.astype(bf16), gh, 0, 0)
            d_qkv[place, span, :narrow] = turn(dq * scale, cosine, -sine).astype(bf16)
            d_qkv[place, span, narrow : 2 * narrow] = turn(dk * scale, cosine, -sine).astype(bf16)
            d_qkv[place, span, 2 * narrow :] = dv.astype(bf16)
        return dot(d_qkv[place], w_qkv[...], 1, 1)

    def far_copy(j):
        return pltpu.make_async_remote_copy(
            src_ref=far.at[j % 2],
            dst_ref=core_in.at[j],
            send_sem=far_send.at[j],
            recv_sem=far_recv.at[j],
            device_id=core_partner,
            device_id_type=MESH,
        )

    def far_step(i, carry):
        j = QUAD - 1 - i
        part = attend_block(QUAD + j).astype(bf16)

        @pl.when(i >= 2)
        def _():
            far_copy(j + 2).wait_send()

        far[j % 2] = part
        far_copy(j).start()
        return carry

    lax.fori_loop(0, QUAD, far_step, 0)
    for j in range(2):
        far_copy(j).wait_send()
    def near_step(i, carry):
        j = QUAD - 1 - i
        part = attend_block(j)
        far_copy(j).wait_recv()
        own_sum[...] = part + core_in[j].astype(f32)
        near[j] = own_sum[...].astype(bf16)
        return carry

    lax.fori_loop(0, QUAD, near_step, 0)
    total_one = Total(mail, near, own_sum, mid, in_a, in_b)
    total_one.first()
    total_one.first_a()

    def add_mixed(target, left, landed):
        count, across = landed.shape
        buffer = add_buf.at[pl.ds(0, count), pl.ds(0, across)]
        copy = pltpu.make_async_copy(landed, buffer, add_sem.at[0])
        copy.start()
        copy.wait()
        add_near(target, left, buffer)

    collect_o = Collect(
        mail, bits, by_place(p_o, rows), land_o, sum_o, lambda piece: out_o, add_mixed
    )
    collect_qkv = Collect(
        mail, bits, by_runs(p_qkv), land_qkv, sum_qkv,
        lambda piece: fin_qkv.at[pl.ds(piece * run_rows, run_rows)], add_mixed,
    )
    p_o[...] = p_o_sum[...].astype(bf16)
    collect_o.start()
    cut = acts.shape[3]
    cuts = width // cut
    shift = (1 - flat // (ring.count // 2)) * (cuts // 2)

    def chunk_at(i):
        return pl.multiple_of(((i + shift) % cuts) * cut, cut)

    def act_copy(i):
        return pltpu.make_async_copy(
            act_one.at[:, :, pl.ds(chunk_at(i), cut)], acts.at[i % 2], act_sems.at[i % 2]
        )

    act_copy(0).start()

    def chunk_step(i, carry):
        act_copy(i).wait()

        @pl.when(i + 1 < cuts)
        def _():
            act_copy(i + 1).start()

        left = acts[i % 2].reshape(2 * QUAD * size, cut)
        right = d_qkv[...].reshape(2 * QUAD * size, 3 * narrow)
        p_qkv[pl.ds(chunk_at(i), cut), :] = dot(left, right, 0, 0).astype(bf16)
        return carry

    lax.fori_loop(0, cuts // 2, chunk_step, 0)
    collect_qkv.start()
    total_one.second()
    lax.fori_loop(cuts // 2, cuts, chunk_step, 0)
    if len(bits) > 2:
        collect_d.take_away(top_stage - 1, 0)
    collect_d.finish_piece(0)

    block = ring.span * hidden_rows
    gu_swap = []
    team = ring.team(flat)

    def hand_out(last, ref):
        for delta in ring.deltas:
            other = ring.team(ring.flip(flat, delta))
            part = pl.ds(pl.multiple_of(other * rows, 16), rows)
            for y in range(ring.upper_size):
                for o in range(ring.across):
                    target = ((y * 2 + team // QUAD) * ring.across + o) * QUAD + team % QUAD
                    src = last.at[part, pl.ds((y * ring.across + o) * block, block)]
                    dst = ref.at[:, pl.ds(pl.multiple_of(target * block, 128), block)]
                    if delta:
                        gu_swap.append(mail.post(src, dst, delta))
                    else:
                        mail.keep(src, dst)

    for piece in range(collect_g.pieces):
        collect_g.finish_piece(piece)
    hand_out(fin_g, out_gate)
    collect_o.take_away(top_stage, 0)
    for piece in range(collect_qkv.pieces):
        collect_qkv.take_away(top_stage, piece)
    for piece in range(collect_u.pieces):
        collect_u.finish_piece(piece)
    hand_out(fin_u, out_up)
    total_one.arrive()

    def first_norm(part):
        x = x_ref[part, :].astype(f32)
        grads, terms = norm_back(total_one.value(part), x, gains_ref[0:1, :])
        grad_resid[part, :] = grad_resid[part, :] + grads
        gain_grads[0:1, :] = gain_grads[0:1, :] + jnp.sum(terms, axis=0, keepdims=True)

    strips(first_norm)
    mail.keep(grad_resid, grad_tokens)
    for step, bit in enumerate([ring.bit_core, ring.bit_a, ring.bit_b] + bits):
        copy = mail.post(gain_grads, gain_in.at[step], bit)
        copy.wait()
        mail.sent = [c for c in mail.sent if c is not copy]
        gain_grads[...] = gain_grads[...] + gain_in[step]
    for piece in range(collect_qkv.pieces):
        collect_qkv.finish_piece(piece)
    collect_o.finish_piece(0)

    swaps = []
    for delta in ring.deltas:
        other = ring.team(ring.flip(flat, delta))
        src = fin_qkv.at[pl.ds(pl.multiple_of(other * rows, 16), rows)]
        dst = qkv_in.at[team]
        if delta:
            swaps.append(mail.post(src, dst, delta))
        else:
            kept = mail.keep(src, dst)
    kept.wait()
    mail.kept = [c for c in mail.kept if c is not kept]
    for copy in swaps:
        copy.wait_recv()
    for j, ref in enumerate((out_q, out_k, out_v)):
        parts = []
        for y in range(ring.upper_size):
            for c in range(2):
                for o in range(ring.across):
                    for q in range(QUAD):
                        start = j * narrow + (y * ring.across + o) * HEAD_DIM
                        parts.append(qkv_in[c * QUAD + q, :, start : start + HEAD_DIM])
        ref[...] = jnp.concatenate(parts, axis=1).astype(f32)
    for copy in gu_swap:
        copy.wait_recv()
    mail.finish()


def back(outer, inner, seq_len, near_args, far_args):
    tokens, w_qkv, w_o = near_args[0], near_args[8], near_args[9]
    size, width = tokens.shape
    narrow = w_o.shape[0]
    hidden = far_args[0].shape[1]
    places = outer * inner // (2 * QUAD)
    rows = width // (outer * inner)
    hidden_rows = hidden // places
    span = max(1, HEAD_DIM // rows)
    pieces = 2 if span == 1 else 2 * QUAD
    run_rows = 2 * QUAD * rows // pieces
    remote = (places - 1) * (3 * pieces + 2) + 7 + 14 * places // span + 8 + 24
    local = 8 + 2 * places // span
    vm = pl.BlockSpec(memory_space=pltpu.VMEM)
    hbm = pl.BlockSpec(memory_space=pl.ANY)
    sds = jax.ShapeDtypeStruct
    out_shape = (
        sds((rows, width), f32),
        sds((rows, width), f32),
        sds((rows, width), f32),
        sds((rows, width), f32),
        sds((8, width), f32),
        sds((rows, 2 * QUAD * hidden), bf16),
        sds((rows, 2 * QUAD * hidden), bf16),
        sds((hidden_rows, width), f32),
        sds(((places - 1) * pieces, run_rows, hidden), bf16),
        sds(((places - 1) * pieces, run_rows, hidden), bf16),
        sds((places // 2, hidden_rows, width), bf16),
        sds((places // 2 * pieces, run_rows, hidden), bf16),
        sds((places // 2 * pieces, run_rows, hidden), bf16),
        sds((places // 2, hidden_rows, width), bf16),
        sds((2 * QUAD * rows, hidden), bf16),
        sds((2 * QUAD * rows, hidden), bf16),
        sds(((places - 1) * pieces, run_rows, 3 * narrow), bf16),
        sds((places - 1, rows, width), bf16),
        sds((size, width), f32),
    )
    wide = pltpu.VMEM((size, width), bf16)
    four = pltpu.VMEM((QUAD, size, width), bf16)
    cut = min(256, width // 2)
    four_sems = pltpu.SemaphoreType.DMA((QUAD,))
    return pl.pallas_call(
        functools.partial(back_kernel, outer, inner, seq_len),
        out_shape=out_shape,
        in_specs=[vm] * len(near_args) + [hbm] * len(far_args),
        out_specs=tuple([vm] * 5 + [hbm] * 14),
        scratch_shapes=[
            four, four, pltpu.VMEM((2, size, width), bf16),
            pltpu.VMEM((size, width), f32),
            pltpu.VMEM((size, width), f32),
            pltpu.VMEM((2 * QUAD, size, width), bf16),
            wide, wide, wide,
            pltpu.VMEM((2, 2 * QUAD, size, cut), bf16),
            pltpu.VMEM((2 * QUAD, size, 3 * narrow), bf16),
            pltpu.VMEM((width, 3 * narrow), bf16),
            pltpu.VMEM((narrow, width), bf16),
            pltpu.VMEM((narrow, width), f32),
            pltpu.VMEM((places // 2 * pieces, run_rows, 3 * narrow), bf16),
            pltpu.VMEM((places // 2, rows, width), bf16),
            pltpu.VMEM((2 * QUAD * rows, 3 * narrow), bf16),
            pltpu.VMEM((2 * QUAD, rows, 3 * narrow), bf16),
            pltpu.VMEM((8, 8, width), f32),
            pltpu.SemaphoreType.DMA((remote,)),
            pltpu.SemaphoreType.DMA((remote,)),
            pltpu.SemaphoreType.DMA((local,)),
            four_sems, four_sems,
            pltpu.SemaphoreType.DMA((2,)),
            pltpu.VMEM((run_rows, width), bf16),
            pltpu.SemaphoreType.DMA((1,)),
        ],
        compiler_params=pltpu.CompilerParams(
            collective_id=1, has_side_effects=True, vmem_limit_bytes=63 * 1024 * 1024
        ),
        name="back",
    )(*near_args, *far_args)


def mid_kernel(
    outer, inner, hidden_rows,
    go_ref, factor_ref,
    act_two, wg_ref, wu_ref, wd_ref, resid_ref,
    p_g, p_u, half_d, added, layer_out, dy, p_d, land_d, land_down, land_two, a_down, b_down, a_two, b_two,
    w_g, w_u, w_d, middle, cols, act_in, dy_in, act_cut, dy_cut, stage_d, dy_own,
    far_down, far_two, tmp_down, tmp_two, near_down, near_two, own_down, own_two, halves, stage,
    send_sems, recv_sems, local_sems, down_send, down_recv, two_send, two_recv, act_sems, dy_sem, tmp_sems, cut_sems, out_sems, pd_send, pd_recv,
):
    size, width = go_ref.shape
    hidden = w_g.shape[1]
    ring = Ring(outer, inner, width // (outer * inner))
    mail = Mail(ring, send_sems, recv_sems, local_sems)
    ring.greet()
    flat = ring.flat
    strip = 32
    top_bit = ring.count // 2

    def strips(step):
        def run(i, carry):
            step(pl.ds(pl.multiple_of(i * strip, strip), strip))
            return carry

        lax.fori_loop(0, size // strip, run, 0)

    def dot(left, right, left_dim, right_dim):
        return lax.dot_general(
            left, right, (((left_dim,), (right_dim,)), ((), ())), preferred_element_type=f32
        )

    def settle(copy):
        copy.wait()
        mail.kept = [c for c in mail.kept if c is not copy]

    def pair_at(i):
        return i + (i // 2) * (5 - 2 * i)

    def pair_copies(source, target, sems, i):
        pair = pair_at(i)
        return [
            pltpu.make_async_copy(source.at[pair], target.at[pl.ds(0, size)], sems.at[0]),
            pltpu.make_async_copy(source.at[QUAD + pair], target.at[pl.ds(size, size)], sems.at[1]),
        ]

    def act_copies(i):
        return pair_copies(act_two, act_in.at[i % 2], act_sems.at[i % 2], i)

    for copy in act_copies(0):
        copy.start()
    loads = [mail.keep(wg_ref, w_g), mail.keep(wu_ref, w_u), mail.keep(wd_ref, w_d)]
    load_resid = mail.keep(resid_ref, own_down)

    def cotangent(part):
        dy_own[part, :] = (go_ref[part, :].astype(f32) * factor_ref[part, :]).astype(bf16)

    strips(cotangent)
    keep_dy = mail.keep(dy_own, dy.at[0])
    half = size // 2
    top, end = pl.ds(0, half), pl.ds(half, half)
    share = Share(mail, dy, dy_own)
    share.first()
    for copy in loads:
        settle(copy)
    settle(load_resid)
    settle(keep_dy)
    share.done((0,))

    def core_copy(kind, i):
        source, target, send, recv = (
            (far_down, land_down, down_send, down_recv),
            (far_two, land_two, two_send, two_recv),
        )[kind]
        return pltpu.make_async_remote_copy(
            src_ref=source,
            dst_ref=target.at[pair_at(i)],
            send_sem=send.at[i],
            recv_sem=recv.at[i],
            device_id=ring.where(ring.bit_core),
            device_id_type=MESH,
        )

    def tmp_copy(kind, i):
        source, target = ((land_down, tmp_down), (land_two, tmp_two))[kind]
        return pltpu.make_async_copy(source.at[pair_at(i)], target, tmp_sems.at[kind])

    base = mail.used
    mail.used += 9

    def late(n):
        src, dst, bit = (
            (dy.at[1, top], dy.at[3, top], ring.bit_b),
            (dy.at[2, end], dy.at[3, end], ring.bit_a),
            (dy.at[1], dy.at[QUAD + 1], ring.bit_core),
            (dy.at[2], dy.at[QUAD + 2], ring.bit_core),
            (dy.at[3], dy.at[QUAD + 3], ring.bit_core),
            (near_two.at[2, top], halves.at[1, 0], ring.bit_b),
            (near_two.at[2, end], halves.at[1, 1], ring.bit_a),
            (near_down.at[2, top], halves.at[0, 0], ring.bit_b),
            (near_down.at[2, end], halves.at[0, 1], ring.bit_a),
        )[n]
        return pltpu.make_async_remote_copy(
            src_ref=src,
            dst_ref=dst,
            send_sem=send_sems.at[base + n],
            recv_sem=recv_sems.at[base + n],
            device_id=ring.where(bit),
            device_id_type=MESH,
        )

    def join(kind, i):
        pair = pair_at(i)
        tmp, near, own = ((tmp_down, near_down, own_down), (tmp_two, near_two, own_two))[kind]
        core_copy(kind, i).wait_recv()
        tmp_copy(kind, i).start()
        tmp_copy(kind, i).wait()

        @pl.when(pair == 0)
        def _():
            add_near(own, own, tmp)

        @pl.when(pair > 0)
        def _():
            here = near.at[jnp.maximum(pair, 1) - 1]
            add_near(here, here, tmp)

    wide = min(512, width)
    piece = min(256, hidden)

    def give(kind, i, left, product, far, near, own):
        pair = pair_at(i)

        @pl.when(i >= 1)
        def _():
            join(kind, i - 1)
            core_copy(kind, i - 1).wait_send()

        @pl.when(i == 3)
        def _():
            late(7 - 2 * kind).start()
            late(8 - 2 * kind).start()

        for c in range(width // wide):
            part = slice(c * wide, (c + 1) * wide)
            whole = product(left, part)
            far[:, part] = whole[size:].astype(bf16)
            mine = whole[:size]

            @pl.when(pair == 0)
            def _():
                own[:, part] = mine + own[:, part] if kind == 0 else mine

            @pl.when(pair > 0)
            def _():
                near[jnp.maximum(pair, 1) - 1, :, part] = mine.astype(bf16)

        core_copy(kind, i).start()

    second = {}

    def pass_sums(kind):
        near, to_a, to_b = ((near_down, a_down, b_down), (near_two, a_two, b_two))[kind]
        join(kind, QUAD - 1)
        late(7 - 2 * kind).wait_recv()
        add_near(near.at[0, top], near.at[0, top], halves.at[kind, 0])
        second["a", kind] = mail.post(near.at[0], to_a, ring.bit_a)
        late(8 - 2 * kind).wait_recv()
        add_near(near.at[1, end], near.at[1, end], halves.at[kind, 1])
        second["b", kind] = mail.post(near.at[1], to_b, ring.bit_b)
        core_copy(kind, QUAD - 1).wait_send()

    def ahead(i, carry):
        pair = pair_at(i)

        @pl.when(i == 2)
        def _():
            share.from_a.wait_recv()
            late(0).start()
            late(2).start()
            share.from_b.wait_recv()
            late(1).start()
            late(3).start()

        @pl.when(i == 3)
        def _():
            late(0).wait_recv()
            late(1).wait_recv()
            late(4).start()

        for copy in act_copies(i):
            copy.wait()

        @pl.when(i + 1 < QUAD)
        def _():
            for copy in act_copies(i + 1):
                copy.start()

        act = act_in[i % 2]
        for c in range(hidden // piece):
            part = slice(c * piece, (c + 1) * piece)
            up_part = slice(hidden + c * piece, hidden + (c + 1) * piece)
            gate_pre = dot(act, w_g[:, part], 1, 0)
            up_proj = dot(act, w_u[:, part], 1, 0)
            ready = (gate_pre * jax.nn.sigmoid(gate_pre) * up_proj).astype(bf16)
            for rows, place in ((slice(0, size), pair), (slice(size, None), QUAD + pair)):
                middle[place, :, part] = ready[rows]
                cols[place, :, part] = gate_pre[rows].astype(bf16)
                cols[place, :, up_part] = up_proj[rows].astype(bf16)

        give(
            0, i,
            jnp.concatenate([middle[pair], middle[QUAD + pair]], axis=0),
            lambda left, part: dot(left, w_d[:, part], 1, 0),
            far_down, near_down, own_down,
        )
        return carry

    lax.fori_loop(0, QUAD, ahead, 0)
    pass_sums(0)
    for n in (2, 3, 4):
        late(n).wait_recv()

    cut = act_cut.shape[3]
    cuts = width // cut
    tokens = 2 * QUAD * size

    def cut_copy(source, target, i):
        start = pl.multiple_of(i * cut, cut)
        return pltpu.make_async_copy(
            source.at[:, :, pl.ds(start, cut)], target.at[i % 2], cut_sems.at[i % 2]
        )

    def down_out(i):
        start = pl.multiple_of(i * cut, cut)
        return pltpu.make_async_copy(
            stage_d.at[i % 2], p_d.at[:, pl.ds(start, cut)], out_sems.at[i % 2]
        )

    upper = flat // top_bit
    rows_half = hidden // 2
    away = pl.ds(pl.multiple_of((1 - upper) * rows_half, 16), rows_half)
    kept = pl.ds(pl.multiple_of(upper * rows_half, 16), rows_half)

    def down_send_at(i):
        part = pl.ds(pl.multiple_of(i * cut, cut), cut)
        return pltpu.make_async_remote_copy(
            src_ref=p_d.at[away, part],
            dst_ref=land_d.at[:, part],
            send_sem=pd_send.at[i],
            recv_sem=pd_recv.at[i],
            device_id=ring.where(top_bit),
            device_id_type=MESH,
        )

    cut_copy(dy, dy_cut, 0).start()

    def down_step(i, carry):
        cut_copy(dy, dy_cut, i).wait()

        @pl.when(i + 1 < cuts)
        def _():
            cut_copy(dy, dy_cut, i + 1).start()

        turned = dot(
            dy_cut[i % 2].reshape(tokens, cut), middle[...].reshape(tokens, hidden), 0, 0
        )

        stage_d[i % 2] = turned.T.astype(bf16)
        down_out(i).start()

        @pl.when(i >= 1)
        def _():
            down_out(i - 1).wait()
            down_send_at(i - 1).start()

        return carry

    lax.fori_loop(0, cuts, down_step, 0)
    cut_copy(act_two, act_cut, 0).start()
    down_out(cuts - 1).wait()
    down_send_at(cuts - 1).start()

    def behind(i, carry):
        pair = pair_at(i)
        dy_copies = pair_copies(dy, dy_in, dy_sem, i)
        for copy in dy_copies:
            copy.start()
        for copy in dy_copies:
            copy.wait()
        grads = dy_in[...]
        for c in range(hidden // piece):
            part = slice(c * piece, (c + 1) * piece)
            up_part = slice(hidden + c * piece, hidden + (c + 1) * piece)
            grad_middle = dot(grads, w_d[part, :], 1, 1)
            for rows, place in ((slice(0, size), pair), (slice(size, None), QUAD + pair)):
                gate_pre = cols[place, :, part].astype(f32)
                up_proj = cols[place, :, up_part].astype(f32)
                sigmoid_gate = jax.nn.sigmoid(gate_pre)
                swish = gate_pre * sigmoid_gate
                came = grad_middle[rows]
                cols[place, :, up_part] = (came * swish).astype(bf16)
                cols[place, :, part] = (
                    came * up_proj * sigmoid_gate * (1.0 + gate_pre * (1.0 - sigmoid_gate))
                ).astype(bf16)

        give(
            1, i,
            jnp.concatenate([cols[pair], cols[QUAD + pair]], axis=0),
            lambda left, part: dot(left[:, :hidden], w_g[part, :], 1, 1)
            + dot(left[:, hidden:], w_u[part, :], 1, 1),
            far_two, near_two, own_two,
        )
        return carry

    lax.fori_loop(0, QUAD, behind, 0)
    pass_sums(1)

    def stage_out(i):
        rows = pl.ds(pl.multiple_of(i * cut, cut), cut)
        return [
            pltpu.make_async_copy(
                stage.at[i % 2, :, pl.ds(j * hidden, hidden)],
                target.at[rows],
                out_sems.at[2 + 2 * j + i % 2],
            )
            for j, target in enumerate((p_g, p_u))
        ]

    def gate_step(i, carry):
        cut_copy(act_two, act_cut, i).wait()

        @pl.when(i + 1 < cuts)
        def _():
            cut_copy(act_two, act_cut, i + 1).start()

        @pl.when(i >= 2)
        def _():
            for copy in stage_out(i - 2):
                copy.wait()

        stage[i % 2] = dot(
            act_cut[i % 2].reshape(tokens, cut), cols[...].reshape(tokens, 2 * hidden), 0, 0
        ).astype(bf16)
        for copy in stage_out(i):
            copy.start()
        return carry

    lax.fori_loop(0, cuts, gate_step, 0)
    for i in (cuts - 2, cuts - 1):
        for copy in stage_out(i):
            copy.wait()

    for kind, own, in_a, in_b in ((1, own_two, a_two, b_two), (0, own_down, a_down, b_down)):
        second["a", kind].wait_recv()
        second["b", kind].wait_recv()
        first = mail.keep(in_a, tmp_down)
        other = mail.keep(in_b, tmp_two)
        settle(first)
        settle(other)

        def finish(part, own=own, kind=kind):
            total = own[part, :] + tmp_down[part, :].astype(f32) + tmp_two[part, :].astype(f32)
            if kind:
                own_two[part, :] = total
            else:
                far_down[part, :] = total.astype(bf16)

        strips(finish)
        if kind:
            mail.keep(own_two, added)
        else:
            mail.keep(far_down, layer_out)
    for i in range(cuts):
        down_send_at(i).wait()
    add_far(half_d, p_d.at[kept], land_d)
    for n in range(9):
        late(n).wait_send()
    mail.finish()


def mid(outer, inner, hidden_rows, grad_out, factor_rows, act_two, w_g, w_u, w_d, resid):
    size, width = grad_out.shape
    hidden = w_g.shape[1]
    vm = pl.BlockSpec(memory_space=pltpu.VMEM)
    hbm = pl.BlockSpec(memory_space=pl.ANY)
    sds = jax.ShapeDtypeStruct
    wide = sds((size, width), bf16)
    out_shape = (
        sds((width, hidden), bf16),
        sds((width, hidden), bf16),
        sds((hidden // 2, width), bf16),
        sds((size, width), f32),
        wide,
        sds((2 * QUAD, size, width), bf16),
        sds((hidden, width), bf16),
        sds((hidden // 2, width), bf16),
        sds((QUAD, size, width), bf16),
        sds((QUAD, size, width), bf16),
        wide, wide, wide, wide,
    )
    cut = min(256, width // 2)
    vw = pltpu.VMEM((size, width), bf16)
    dma = pltpu.SemaphoreType.DMA
    return pl.pallas_call(
        functools.partial(mid_kernel, outer, inner, hidden_rows),
        out_shape=out_shape,
        in_specs=[vm] * 2 + [hbm] * 5,
        out_specs=tuple([hbm] * len(out_shape)),
        scratch_shapes=[
            pltpu.VMEM((width, hidden), bf16),
            pltpu.VMEM((width, hidden), bf16),
            pltpu.VMEM((hidden, width), bf16),
            pltpu.VMEM((2 * QUAD, size, hidden), bf16),
            pltpu.VMEM((2 * QUAD, size, 2 * hidden), bf16),
            pltpu.VMEM((2, 2 * size, width), bf16),
            pltpu.VMEM((2 * size, width), bf16),
            pltpu.VMEM((2, 2 * QUAD, size, cut), bf16),
            pltpu.VMEM((2, 2 * QUAD, size, cut), bf16),
            pltpu.VMEM((2, hidden, cut), bf16),
            vw,
            vw, vw, vw, vw,
            pltpu.VMEM((QUAD - 1, size, width), bf16),
            pltpu.VMEM((QUAD - 1, size, width), bf16),
            pltpu.VMEM((size, width), f32),
            pltpu.VMEM((size, width), f32),
            pltpu.VMEM((2, 2, size // 2, width), bf16),
            pltpu.VMEM((2, cut, 2 * hidden), bf16),
            dma((32,)), dma((32,)), dma((16,)),
            dma((QUAD,)), dma((QUAD,)), dma((QUAD,)), dma((QUAD,)),
            dma((2, 2)), dma((2,)), dma((2,)), dma((2,)), dma((6,)),
            dma((width // cut,)), dma((width // cut,)),
        ],
        compiler_params=pltpu.CompilerParams(
            collective_id=2, has_side_effects=True, vmem_limit_bytes=63 * 1024 * 1024
        ),
        name="mid",
    )(grad_out, factor_rows, act_two, w_g, w_u, w_d, resid)


def on_device(
    tokens,
    labels,
    counts,
    grad_out,
    w_query,
    w_key,
    w_value,
    w_out,
    gain_attn,
    gain_mlp,
    w_gate,
    w_up,
    w_down,
):
    batch_size, seq_len, width = tokens.shape
    outer_count = lax.axis_size("dp")
    inner_count = lax.axis_size("fsdp")
    rows = w_query.shape[0]
    hidden_rows = w_down.shape[0]
    flat = lax.axis_index("dp") * inner_count + lax.axis_index("fsdp")
    x_rows = tokens.reshape(-1, width)

    token_total = float(seq_len * batch_size * outer_count * inner_count)
    picked_counts = jnp.sum(
        jnp.where(labels[:, None] == jnp.arange(3)[None, :], counts[None, :], 0), axis=1
    ).astype(f32)
    factor = token_total / (3.0 * picked_counts)
    cosine, sine = rope_tables(seq_len, HEAD_DIM)
    head_count = width // (2 * QUAD) // HEAD_DIM
    sign = jnp.where(jnp.arange(HEAD_DIM) < HEAD_DIM // 2, -1.0, 1.0)
    wide_cosine = jnp.tile(cosine, (1, head_count))
    wide_sine = jnp.tile(sine * sign, (1, head_count))
    gain_rows = lax.dynamic_update_slice(
        jnp.zeros((8, width), f32),
        jnp.stack([gain_attn, gain_mlp]).astype(f32),
        (0, flat * rows),
    )
    factor_rows = jnp.repeat(factor, seq_len)[:, None]
    (
        act_one, w_qkv, w_o, q_rot, k_rot, values, attended, resid, gains, act_two, w_g, w_u, w_d,
    ) = front(
        outer_count, inner_count, seq_len,
        x_rows, gain_rows,
        w_query, w_key, w_value,
        wide_cosine, wide_sine,
        w_out, w_gate, w_up, w_down,
    )
    p_g, p_u, half_d, added, layer_out = mid(
        outer_count, inner_count, w_down.shape[0], grad_out.reshape(-1, width), factor_rows,
        act_two, w_g, w_u, w_d, resid,
    )[:5]
    layer_out = layer_out.reshape(tokens.shape)
    results = back(
        outer_count, inner_count, seq_len,
        (
            x_rows, grad_out.reshape(-1, width), factor_rows, gains, q_rot, k_rot, values, attended,
            w_qkv, w_o, wide_cosine, wide_sine,
        ),
        (p_g, p_u, half_d, act_one, resid, added),
    )
    query_grad, key_grad, value_grad, out_grad, gain_grads = results[:5]
    gate_grad, up_grad, down_grad = (a.astype(f32) for a in results[5:8])
    grad_tokens = results[-1]
    gain_grads = lax.dynamic_slice(gain_grads, (0, flat * rows), (2, rows))
    return (
        layer_out,
        grad_tokens.reshape(tokens.shape),
        query_grad,
        key_grad,
        value_grad,
        out_grad,
        gain_grads[0],
        gain_grads[1],
        gate_grad,
        up_grad,
        down_grad,
    )


def solution(mesh):
    rows = P(AXES, None)
    vector = P(AXES)
    three = P(AXES, None, None)
    in_specs = (three, vector, P(), three, rows, rows, rows, rows, vector, vector, rows, rows, rows)
    out_specs = (three, three, rows, rows, rows, rows, vector, vector, rows, rows, rows)
    return jax.shard_map(
        on_device, mesh=mesh, in_specs=in_specs, out_specs=out_specs, check_vma=False
    )
```

```python
import functools

import jax
import jax.numpy as jnp
from jax import lax
from jax.experimental import pallas as pl
from jax.experimental.pallas import tpu as pltpu
from jax.sharding import PartitionSpec as P

HEAD_DIM = 64
AXES = ("dp", "fsdp")
QUAD = 4

epsilon = 1e-05
rope_base = 130000.0
bf16 = jnp.bfloat16
f32 = jnp.float32
MESH = pl.DeviceIdType.MESH


def rope_tables(seq_len, head_dim):
    half_dim = head_dim // 2
    frequency = rope_base ** (-(jnp.arange(half_dim).astype(f32) * 2.0) / head_dim)
    angles = jnp.arange(seq_len).astype(f32)[:, None] * frequency[None, :]
    angles = jnp.concatenate([angles, angles], axis=1)
    return (jnp.cos(angles), jnp.sin(angles))


class Ring:
    def __init__(self, outer, inner, rows):
        self.known = {}
        self.count = outer * inner
        self.inner = inner
        self.span = max(1, HEAD_DIM // rows)
        self.bit_a = self.span
        self.bit_b = 2 * self.span
        self.bit_core = inner
        self.low = powers(1, self.span)
        self.mid = powers(QUAD * self.span, inner)
        self.upper = powers(2 * inner, self.count)
        self.data_bits = self.low + self.mid + self.upper
        self.deltas = [
            (self.bit_core if t // QUAD else 0) + (t % QUAD) * self.span for t in range(2 * QUAD)
        ]
        self.across = inner // (QUAD * self.span)
        self.upper_size = outer // 2
        self.flat = lax.axis_index("dp") * inner + lax.axis_index("fsdp")

    def flip(self, flat, bits):
        bit = 1
        while bit <= bits:
            if bits & bit:
                flat = flat + bit * (1 - 2 * ((flat // bit) % 2))
            bit *= 2
        return flat

    def where(self, bits):
        if bits not in self.known:
            other = self.flip(self.flat, bits)
            self.known[bits] = (other // self.inner, other % self.inner)
        return self.known[bits]

    def team(self, flat):
        return ((flat // self.inner) % 2) * QUAD + (flat // self.span) % QUAD

    def place(self, flat):
        return (
            (flat // (2 * self.inner)) * self.across + (flat % self.inner) // (QUAD * self.span)
        ) * self.span + flat % self.span

    def runs(self, flat, rows):
        lowest = flat - self.span * ((flat // self.span) % QUAD)
        lowest = lowest - self.inner * ((flat // self.inner) % 2)
        found = []
        for core in range(2):
            start = lowest + core * self.inner
            if self.span == 1:
                found.append((start * rows, QUAD * rows))
            else:
                found += [((start + q * self.span) * rows, rows) for q in range(QUAD)]
        return found

    def greet(self):
        partners = self.deltas[1:] + self.data_bits
        barrier = pltpu.get_barrier_semaphore()
        for bits in partners:
            pl.semaphore_signal(barrier, 1, device_id=self.where(bits), device_id_type=MESH)
        pl.semaphore_wait(barrier, len(partners))


def powers(first, end):
    found = []
    while first < end:
        found.append(first)
        first *= 2
    return found


class Mail:
    def __init__(self, ring, send_sems, recv_sems, local_sems):
        self.ring, self.send_sems, self.recv_sems, self.local_sems = ring, send_sems, recv_sems, local_sems
        self.used = 0
        self.used_local = 0
        self.sent = []
        self.kept = []

    def post(self, src, dst, bits):
        copy = pltpu.make_async_remote_copy(
            src_ref=src,
            dst_ref=dst,
            send_sem=self.send_sems.at[self.used],
            recv_sem=self.recv_sems.at[self.used],
            device_id=self.ring.where(bits),
            device_id_type=MESH,
        )
        self.used += 1
        copy.start()
        self.sent.append(copy)
        return copy

    def keep(self, src, dst):
        copy = pltpu.make_async_copy(src, dst, self.local_sems.at[self.used_local])
        self.used_local += 1
        copy.start()
        self.kept.append(copy)
        return copy

    def drop(self, copy):
        self.sent = [c for c in self.sent if c is not copy]

    def finish(self):
        for copy in self.sent:
            copy.wait_send()
        for copy in self.kept:
            copy.wait()


class Spread:
    def __init__(self, mail, views, bits):
        self.mail, self.views, self.bits = mail, views, bits
        self.pieces = len(views(0))
        self.came = {}

    def start(self, key, piece, first):
        ref = self.views(key)[piece]
        for bit in self.bits[first:]:
            self.came[key + bit, piece] = self.mail.post(ref, ref, bit)

    def begin(self, piece=None):
        for p in range(self.pieces) if piece is None else (piece,):
            self.start(0, p, 0)

    def pass_on(self, stage, piece=None):
        for p in range(self.pieces) if piece is None else (piece,):
            for key in keys_below(self.bits, stage):
                key += self.bits[stage]
                self.came.pop((key, p)).wait_recv()
                self.start(key, p, stage + 1)

    def pass_all(self, piece=None):
        for stage in range(len(self.bits) - 1):
            self.pass_on(stage, piece)

    def done(self):
        for copy in self.came.values():
            copy.wait_recv()


def keys_below(bits, stage):
    return [
        sum(b for i, b in enumerate(bits[:stage]) if low >> i & 1) for low in range(2**stage)
    ]


class Adding:
    def __init__(self, mail, ref, came_in, bits):
        self.mail, self.ref, self.came_in, self.bits = mail, ref, came_in, bits
        self.step = 0

    def post(self):
        self.copy = self.mail.post(
            self.ref, self.came_in.at[self.step], self.bits[self.step]
        )

    def take(self):
        self.copy.wait()
        self.mail.drop(self.copy)
        self.ref[...] = self.ref[...] + self.came_in[self.step]
        self.step += 1


class Share:
    def __init__(self, mail, whole, own):
        self.mail, self.whole, self.own = mail, whole, own
        self.core = []

    def first_core(self):
        self.to_core(self.own, 0)

    def first_a(self):
        self.from_a = self.mail.post(self.own, self.whole.at[1], self.mail.ring.bit_a)

    def first_b(self):
        self.from_b = self.mail.post(self.own, self.whole.at[2], self.mail.ring.bit_b)

    def first(self):
        self.first_a()
        self.first_b()
        self.first_core()

    def to_core(self, ref, place):
        self.core.append(
            self.mail.post(ref, self.whole.at[QUAD + place], self.mail.ring.bit_core)
        )

    def second_a(self):
        self.from_a.wait_recv()
        self.to_core(self.whole.at[1], 1)

    def second_b(self):
        self.from_b.wait_recv()
        self.both = self.mail.post(self.whole.at[2], self.whole.at[3], self.mail.ring.bit_a)
        self.to_core(self.whole.at[2], 2)

    def second(self):
        self.second_a()
        self.second_b()

    def third(self):
        self.both.wait_recv()
        self.to_core(self.whole.at[3], 3)

    def done(self, places=range(QUAD)):
        for place in places:
            self.core[place].wait_recv()


def add_near(target, left, right):
    rows = left.shape[0]
    strip = min(32, rows)

    def step(i, carry):
        part = pl.ds(pl.multiple_of(i * strip, strip), strip)
        target[part, :] = (left[part, :].astype(f32) + right[part, :].astype(f32)).astype(
            target.dtype
        )
        return carry

    lax.fori_loop(0, rows // strip, step, 0)


class Total:
    def __init__(self, mail, near, own, mid, in_a, in_b):
        self.mail, self.near, self.own = mail, near, own
        self.mid, self.in_a, self.in_b = mid, in_a, in_b

    def first(self):
        self.over = self.mail.post(self.near.at[3], self.mid, self.mail.ring.bit_a)

    def first_a(self):
        self.for_a = self.mail.post(self.near.at[1], self.in_a, self.mail.ring.bit_a)

    def second(self):
        self.over.wait_recv()
        add_near(self.near.at[2], self.near.at[2], self.mid)
        self.for_b = self.mail.post(self.near.at[2], self.in_b, self.mail.ring.bit_b)

    def arrive(self):
        self.for_a.wait_recv()
        self.for_b.wait_recv()

    def value(self, part):
        return self.own[part, :] + self.in_a[part, :].astype(f32) + self.in_b[part, :].astype(f32)


def head_mask(width, head):
    lanes = lax.broadcasted_iota(jnp.int32, (1, width), 1)
    return (lanes >= head * HEAD_DIM) & (lanes < (head + 1) * HEAD_DIM)


def turn(u, cosine, signed_sine):
    width = u.shape[-1]
    half = HEAD_DIM // 2
    lanes = lax.broadcasted_iota(jnp.int32, (1, width), 1)
    lower = lanes % HEAD_DIM < half
    turned = jnp.where(lower, pltpu.roll(u, width - half, 1), pltpu.roll(u, half, 1))
    return u * cosine + turned * signed_sine


def front_kernel(
    outer, inner, seq_len,
    x_ref, gain_ref, wq_ref, wk_ref, wv_ref, cos_ref, sin_ref,
    wo_ref, wg_ref, wu_ref, wd_ref,
    act_one_far, w_qkv_far, w_o_far, q_far, k_far, v_far, att_far, resid_far, gains_out,
    act_two, w_g, w_u, w_d,
    act_one, w_qkv, w_o, q_out, k_out, v_out, att_out, resid_out,
    cut, gain_in, x_all, far, core_in, near, own_sum, mid, in_a, in_b, act_two_own,
    send_sems, recv_sems, local_sems, far_send, far_recv,
):
    rows = wq_ref.shape[0]
    width = wq_ref.shape[1]
    hidden_rows = wd_ref.shape[0]
    narrow = width // (2 * QUAD)
    ring = Ring(outer, inner, rows)
    mail = Mail(ring, send_sems, recv_sems, local_sems)
    ring.greet()
    bits = ring.data_bits
    flat = ring.flat

    def by_place(ref, size, pieces):
        step = size // pieces
        return lambda key: [
            ref.at[
                pl.ds(
                    pl.multiple_of(ring.place(ring.flip(flat, key)) * size + p * step, 16), step
                )
            ]
            for p in range(pieces)
        ]

    def by_runs(ref):
        return lambda key: [
            ref.at[pl.ds(pl.multiple_of(start, 16), size)]
            for start, size in ring.runs(ring.flip(flat, key), rows)
        ]

    def settle(copy):
        copy.wait()
        mail.kept = [c for c in mail.kept if c is not copy]

    mine_o = w_o.at[pl.ds(pl.multiple_of(ring.place(flat) * rows, 16), rows)]
    mine_d = w_d.at[pl.ds(pl.multiple_of(ring.place(flat) * hidden_rows, 16), hidden_rows)]
    keep_o = mail.keep(wo_ref, mine_o)
    keep_d = mail.keep(wd_ref, mine_d)
    keep_x = mail.keep(x_ref, x_all.at[0])

    gains_out[...] = gain_ref[...]
    gains = Adding(
        mail, gains_out, gain_in, [ring.bit_a, ring.bit_b, ring.bit_core] + bits
    )
    gains.post()

    chunk = HEAD_DIM
    for t in range(2 * QUAD):
        for j, ref in enumerate((wq_ref, wk_ref, wv_ref)):
            parts = []
            for y in range(ring.upper_size):
                for o in range(ring.across):
                    head = ((y * 2 + t // QUAD) * ring.across + o) * QUAD + t % QUAD
                    parts.append(ref[:, head * chunk : (head + 1) * chunk])
            cut[t, :, j * narrow : (j + 1) * narrow] = jnp.concatenate(parts, axis=1)
    here = pl.ds(pl.multiple_of(flat * rows, 16), rows)
    keep_qkv = mail.keep(cut.at[ring.team(flat)], w_qkv.at[here])
    gains.take()
    gains.post()
    qkv_swap = []
    for delta in ring.deltas[1:]:
        other = ring.flip(flat, delta)
        qkv_swap.append(mail.post(cut.at[ring.team(other)], w_qkv.at[here], delta))
    share_x = Share(mail, x_all, x_ref)
    share_x.first_core()
    share_x.first_a()
    gains.take()
    gains.post()
    settle(keep_o)
    spread_o = Spread(mail, by_place(w_o, rows, 1), bits)
    gains.take()
    gains.post()
    spread_o.begin()
    share_x.first_b()
    settle(keep_qkv)
    for copy in qkv_swap:
        copy.wait_recv()
    spread_qkv = Spread(mail, by_runs(w_qkv), bits)
    spread_qkv.begin()
    while gains.step < len(gains.bits) - 1:
        gains.take()
        gains.post()
    spread_o.pass_all()
    gains.take()

    block = ring.span * hidden_rows

    def swap_columns(ref, whole):
        swap = []
        for delta in ring.deltas:
            team = ring.team(ring.flip(flat, delta))
            for y in range(ring.upper_size):
                for o in range(ring.across):
                    source = ((y * 2 + team // QUAD) * ring.across + o) * QUAD + team % QUAD
                    src = ref.at[:, pl.ds(pl.multiple_of(source * block, 128), block)]
                    dst = whole.at[here, pl.ds((y * ring.across + o) * block, block)]
                    if delta:
                        swap.append((mail.post(src, dst, delta), True))
                    else:
                        swap.append((mail.keep(src, dst), False))
        return swap

    def swapped(swap):
        for copy, remote in swap:
            if remote:
                copy.wait_recv()
            else:
                settle(copy)

    size = act_one.shape[1]
    strip = 32

    def norm_block(place):
        def norm_one(i, carry):
            part = pl.ds(pl.multiple_of(i * strip, strip), strip)
            x = x_all[place, part, :].astype(f32)
            inv = lax.rsqrt(jnp.mean(x * x, axis=-1, keepdims=True) + epsilon)
            act_one[place, part, :] = (x * inv * gains_out[0:1, :]).astype(bf16)
            return carry

        lax.fori_loop(0, size // strip, norm_one, 0)

    share_x.second_a()
    gate_swap = swap_columns(wg_ref, w_g)
    settle(keep_d)
    spread_d = Spread(mail, by_place(w_d, hidden_rows, 2), bits)
    spread_d.begin()
    settle(keep_x)
    share_x.done((0, 1))
    for place in (0, QUAD, 1, QUAD + 1):
        norm_block(place)
    share_x.second_b()
    for piece in range(spread_qkv.pieces):
        spread_qkv.pass_all(piece)
    up_swap = swap_columns(wu_ref, w_u)
    share_x.done((2,))
    for place in (2, QUAD + 2):
        norm_block(place)
    spread_o.done()
    spread_qkv.done()
    mail.keep(w_o, w_o_far)
    mail.keep(w_qkv, w_qkv_far)

    scale = HEAD_DIM**-0.5
    cosine, sine = cos_ref[...], sin_ref[...]
    per_block = act_one.shape[1] // seq_len

    def attend_block(place):
        qkv = jnp.dot(act_one[place], w_qkv[...], preferred_element_type=f32)
        causal = lax.broadcasted_iota(jnp.int32, (seq_len, seq_len), 1) <= lax.broadcasted_iota(
            jnp.int32, (seq_len, seq_len), 0
        )
        for b in range(per_block):
            span = slice(b * seq_len, (b + 1) * seq_len)
            q = turn(qkv[span, :narrow], cosine, sine).astype(bf16)
            k = turn(qkv[span, narrow : 2 * narrow], cosine, sine).astype(bf16)
            v = qkv[span, 2 * narrow :].astype(bf16)
            q_out[place, span] = q
            k_out[place, span] = k
            v_out[place, span] = v
            mixed = jnp.zeros((seq_len, narrow), f32)
            for head in range(narrow // HEAD_DIM):
                mask = head_mask(narrow, head)
                kh = jnp.where(mask, k, jnp.zeros_like(k))
                vh = jnp.where(mask, v, jnp.zeros_like(v))
                scores = lax.dot_general(
                    q, kh, (((1,), (1,)), ((), ())), preferred_element_type=f32
                )
                scores = jnp.where(causal, scores * scale, -1e30)
                top = jnp.max(scores, axis=-1, keepdims=True)
                grown = jnp.exp(scores - top)
                soft = (grown / jnp.sum(grown, axis=-1, keepdims=True)).astype(bf16)
                mixed = mixed + jnp.dot(soft, vh, preferred_element_type=f32)
            att_out[place, span] = mixed.astype(bf16)
        return jnp.dot(att_out[place], w_o[...], preferred_element_type=f32)

    def far_copy(j):
        return pltpu.make_async_remote_copy(
            src_ref=far.at[j],
            dst_ref=core_in.at[j],
            send_sem=far_send.at[j],
            recv_sem=far_recv.at[j],
            device_id=ring.where(ring.bit_core),
            device_id_type=MESH,
        )

    def far_step(j, carry):
        far[j] = attend_block(QUAD + j).astype(bf16)
        far_copy(j).start()
        return carry

    def near_step(j, carry):
        part = attend_block(j)
        far_copy(j).wait_recv()
        total = part + core_in[j].astype(f32)
        near[j] = total.astype(bf16)

        @pl.when(j == 0)
        def _():
            own_sum[...] = total

        return carry

    spread_g = Spread(mail, by_runs(w_g), bits)
    spread_u = Spread(mail, by_runs(w_u), bits)
    lax.fori_loop(0, QUAD - 1, far_step, 0)
    share_x.third()
    swapped(gate_swap)
    spread_g.begin()
    lax.fori_loop(0, QUAD - 1, near_step, 0)
    norm_block(QUAD - 1)
    share_x.done((QUAD - 1,))
    norm_block(2 * QUAD - 1)
    mail.keep(act_one, act_one_far)
    far_step(QUAD - 1, 0)
    near_step(QUAD - 1, 0)
    for j in range(QUAD):
        far_copy(j).wait_send()
    for here, far_off in ((q_out, q_far), (k_out, k_far), (v_out, v_far), (att_out, att_far)):
        mail.keep(here, far_off)
    total = Total(mail, near, own_sum, mid, in_a, in_b)
    total.first()
    total.first_a()
    swapped(up_swap)
    spread_u.begin()
    for piece in range(spread_d.pieces):
        spread_d.pass_on(0, piece)
    total.second()
    spread_g.pass_on(0, 0)
    total.arrive()

    def norm_two(i, carry):
        part = pl.ds(pl.multiple_of(i * strip, strip), strip)
        resid = (
            x_ref[part, :].astype(f32) + total.value(part)
        )
        resid_out[part, :] = resid
        inv = lax.rsqrt(jnp.mean(resid * resid, axis=-1, keepdims=True) + epsilon)
        act_two_own[part, :] = (resid * inv * gains_out[1:2, :]).astype(bf16)
        return carry

    lax.fori_loop(0, size // strip, norm_two, 0)
    mail.keep(act_two_own, act_two.at[0])
    mail.keep(resid_out, resid_far)
    share_two = Share(mail, act_two, act_two_own)
    share_two.first()
    for piece in range(1, spread_g.pieces):
        spread_g.pass_on(0, piece)
    share_two.second()
    spread_u.pass_on(0)
    share_two.third()
    for stage in range(1, len(bits) - 1):
        for spread in (spread_d, spread_g, spread_u):
            spread.pass_on(stage)
    spread_d.done()
    spread_g.done()
    spread_u.done()
    share_two.done()
    mail.finish()


def front(outer, inner, seq_len, tokens, gain_rows, w_query, w_key, w_value, cosine, signed_sine, w_out, w_gate, w_up, w_down):
    size, width = tokens.shape
    rows, hidden_all = w_gate.shape
    hidden_rows = w_down.shape[0]
    narrow, hidden = width // (2 * QUAD), hidden_all // (2 * QUAD)
    span = max(1, HEAD_DIM // rows)
    places = outer * inner // (2 * QUAD)
    pieces = 2 if span == 1 else 2 * QUAD
    remote = (places - 1) * (3 * pieces + 3) + 7 + 14 * places // span + 8 + 24
    local = 24 + 2 * places // span
    vm = pl.BlockSpec(memory_space=pltpu.VMEM)
    hbm = pl.BlockSpec(memory_space=pl.ANY)
    eight = (2 * QUAD, size)
    sds = jax.ShapeDtypeStruct
    out_shape = (
        sds(eight + (width,), bf16),
        sds((width, 3 * narrow), bf16),
        sds((narrow, width), bf16),
        sds(eight + (narrow,), bf16),
        sds(eight + (narrow,), bf16),
        sds(eight + (narrow,), bf16),
        sds(eight + (narrow,), bf16),
        sds((size, width), f32),
        sds((8, width), f32),
        sds(eight + (width,), bf16),
        sds((width, hidden), bf16),
        sds((width, hidden), bf16),
        sds((hidden, width), bf16),
    )
    return pl.pallas_call(
        functools.partial(front_kernel, outer, inner, seq_len),
        out_shape=out_shape,
        in_specs=[vm] * 7 + [hbm] * 4,
        out_specs=tuple([hbm] * 8 + [vm] + [hbm] * 4),
        scratch_shapes=[pltpu.VMEM(s.shape, s.dtype) for s in out_shape[:8]]
        + [
            pltpu.VMEM((2 * QUAD, rows, 3 * narrow), bf16),
            pltpu.VMEM((8, 8, width), f32),
            pltpu.VMEM((2 * QUAD, size, width), bf16),
            pltpu.VMEM((QUAD, size, width), bf16),
            pltpu.VMEM((QUAD, size, width), bf16),
            pltpu.VMEM((QUAD, size, width), bf16),
            pltpu.VMEM((size, width), f32),
            pltpu.VMEM((size, width), bf16),
            pltpu.VMEM((size, width), bf16),
            pltpu.VMEM((size, width), bf16),
            pltpu.VMEM((size, width), bf16),
            pltpu.SemaphoreType.DMA((remote,)),
            pltpu.SemaphoreType.DMA((remote,)),
            pltpu.SemaphoreType.DMA((local,)),
            pltpu.SemaphoreType.DMA((QUAD,)),
            pltpu.SemaphoreType.DMA((QUAD,)),
        ],
        compiler_params=pltpu.CompilerParams(
            collective_id=0, has_side_effects=True, vmem_limit_bytes=60 * 1024 * 1024
        ),
        name="front",
    )(tokens, gain_rows, w_query, w_key, w_value, cosine, signed_sine, w_out, w_gate, w_up, w_down)


def add_far(target, left, right):
    rows, width = left.shape
    strip = min(64, rows)

    def body(left_ref, right_ref, target_ref):
        target_ref[...] = (left_ref[...].astype(f32) + right_ref[...].astype(f32)).astype(
            target_ref.dtype
        )

    spec = pl.BlockSpec((strip, width), lambda i: (i, 0))
    pltpu.emit_pipeline(body, grid=(rows // strip,), in_specs=[spec, spec], out_specs=[spec])(
        left, right, target
    )


class Collect:
    def __init__(self, mail, bits, views, landed, sums, last, add):
        self.mail, self.bits, self.views = mail, bits, views
        self.landed, self.sums, self.last, self.add = landed, sums, last, add
        self.came = {}
        self.added = set()
        self.pieces = len(views(0))

    def slot(self, stage, sub, piece):
        return (2**stage - 1 + keys_below(self.bits, stage).index(sub)) * self.pieces + piece

    def current(self, sub, piece):
        if (sub, piece) not in self.added:
            return self.views(sub)[piece]
        return self.sums.at[keys_below(self.bits, len(self.bits)).index(sub) * self.pieces + piece]

    def send(self, stage, sub, piece):
        bit = self.bits[stage]
        self.came[stage, sub, piece] = self.mail.post(
            self.current(bit + sub, piece), self.landed.at[self.slot(stage, sub, piece)], bit
        )

    def start(self, which=None):
        stage = len(self.bits) - 1
        for sub in reversed(keys_below(self.bits, stage)):
            if which is None or (sub != 0) == which:
                for piece in range(self.pieces):
                    self.send(stage, sub, piece)

    def take(self, stage, sub, piece):
        self.came[stage, sub, piece].wait_recv()
        here = self.current(sub, piece)
        landed = self.landed.at[self.slot(stage, sub, piece)]
        if stage == 0:
            self.add(self.last(piece), here, landed)
            return
        place = keys_below(self.bits, len(self.bits)).index(sub) * self.pieces + piece
        self.add(self.sums.at[place], here, landed)
        self.added.add((sub, piece))
        below = self.bits[stage - 1]
        if (sub // below) % 2:
            self.send(stage - 1, sub - below, piece)

    def take_away(self, stage, piece):
        below = self.bits[stage - 1]
        for sub in keys_below(self.bits, stage):
            if (sub // below) % 2:
                self.take(stage, sub, piece)

    def take_here(self, stage, piece):
        below = self.bits[stage - 1] if stage else 0
        for sub in keys_below(self.bits, stage):
            if not stage or not (sub // below) % 2:
                self.take(stage, sub, piece)

    def finish_piece(self, piece):
        top = len(self.bits) - 1
        for stage in range(top, -1, -1):
            if stage and stage != top:
                self.take_away(stage, piece)
            self.take_here(stage, piece)


def norm_back(total, base, gain):
    inv = lax.rsqrt(jnp.mean(base * base, axis=-1, keepdims=True) + epsilon)
    scaled = gain * total
    grads = inv * scaled - base * inv**3 * jnp.mean(scaled * base, axis=-1, keepdims=True)
    return grads, total * base * inv


def back_kernel(
    outer, inner, seq_len,
    x_ref, go_ref, factor_ref, gains_ref, cos_ref, sin_ref,
    q_far, k_far, v_far, att_far, w_qkv_far, w_o_far,
    p_g, p_u, half_d, act_one, resid_ref, two_ref,
    out_q, out_k, out_v, out_o, gain_grads,
    out_gate, out_up, out_d, land_g, land_u, land_d, sum_g, sum_u, sum_d, fin_g, fin_u, land_qkv, land_o, grad_tokens,
    q_ref, k_ref, v_ref, att_ref, w_qkv, w_o,
    near, core_in, far, own_sum, grad_resid, branch,
    mid, in_a, in_b,
    acts, d_qkv, p_qkv, p_o, p_o_sum, sum_qkv, sum_o, fin_qkv, qkv_in, gain_in,
    send_sems, recv_sems, local_sems, far_send, far_recv, act_sems, add_buf, add_sem,
):
    size, width = x_ref.shape
    rows = out_q.shape[0]
    hidden_rows = out_d.shape[0]
    narrow = w_o.shape[0]
    hidden = p_g.shape[1]
    ring = Ring(outer, inner, rows)
    mail = Mail(ring, send_sems, recv_sems, local_sems)
    ring.greet()
    bits = ring.data_bits
    flat = ring.flat
    strip = 32
    core_partner = ring.where(ring.bit_core)

    def strips(step):
        def run(i, carry):
            step(pl.ds(pl.multiple_of(i * strip, strip), strip))
            return carry

        lax.fori_loop(0, size // strip, run, 0)

    def by_place(ref, count):
        return lambda key: [
            ref.at[pl.ds(pl.multiple_of(ring.place(ring.flip(flat, key)) * count, 16), count)]
        ]

    def by_runs(ref):
        return lambda key: [
            ref.at[pl.ds(pl.multiple_of(start, 16), count)]
            for start, count in ring.runs(ring.flip(flat, key), rows)
        ]

    def dot(left, right, left_dim, right_dim):
        return lax.dot_general(
            left, right, (((left_dim,), (right_dim,)), ((), ())), preferred_element_type=f32
        )

    run_rows = ring.runs(flat, rows)[0][1]
    top_stage = len(bits) - 1
    collect_g, collect_u = (
        Collect(
            mail, bits, by_runs(partial), landed, sums,
            lambda piece, last=last: last.at[pl.ds(piece * run_rows, run_rows)], add_far,
        )
        for partial, landed, sums, last in (
            (p_g, land_g, sum_g, fin_g), (p_u, land_u, sum_u, fin_u)
        )
    )
    share_count = half_d.shape[0] // hidden_rows

    def half_place(key):
        place = ring.place(ring.flip(flat, key)) % share_count
        return [half_d.at[pl.ds(pl.multiple_of(place * hidden_rows, 16), hidden_rows)]]

    collect_d = Collect(mail, bits[:-1], half_place, land_d, sum_d, lambda piece: out_d, add_far)

    load_resid = mail.keep(resid_ref, grad_resid)
    load_two = mail.keep(two_ref, own_sum)
    loads = [
        mail.keep(far_off, here)
        for far_off, here in (
            (w_o_far, w_o), (att_far, att_ref), (q_far, q_ref), (k_far, k_ref), (v_far, v_ref), (w_qkv_far, w_qkv),
        )
    ]
    collect_d.start()
    for which in (True, False):
        collect_g.start(which)
        collect_u.start(which)
    gain_grads[...] = jnp.zeros_like(gain_grads)
    for copy in (load_resid, load_two):
        copy.wait()
        mail.kept = [c for c in mail.kept if c is not copy]

    def second_norm(part):
        resid = grad_resid[part, :]
        grads, terms = norm_back(own_sum[part, :], resid, gains_ref[1:2, :])
        grads = grads + go_ref[part, :].astype(f32) * factor_ref[part, :]
        grad_resid[part, :] = grads
        branch[0, part, :] = grads.astype(bf16)
        gain_grads[1:2, :] = gain_grads[1:2, :] + jnp.sum(terms, axis=0, keepdims=True)

    strips(second_norm)
    share = Share(mail, branch, branch.at[0])
    share.first()
    for piece in range(collect_g.pieces):
        collect_g.take_away(top_stage, piece)
    share.second()
    for piece in range(collect_u.pieces):
        collect_u.take_away(top_stage, piece)
    share.third()
    p_o_sum[...] = jnp.zeros_like(p_o_sum)
    for copy in loads:
        copy.wait()
        mail.kept = [c for c in mail.kept if c is not copy]
    share.done()

    scale = HEAD_DIM**-0.5
    cosine, sine = cos_ref[...], sin_ref[...]
    per_block = size // seq_len

    def attend_block(place):
        grads = branch[place]
        grad_att = dot(grads, w_o[...], 1, 1).astype(bf16)
        p_o_sum[...] = p_o_sum[...] + dot(att_ref[place], grads, 0, 0)
        causal = lax.broadcasted_iota(jnp.int32, (seq_len, seq_len), 1) <= lax.broadcasted_iota(
            jnp.int32, (seq_len, seq_len), 0
        )
        for b in range(per_block):
            span = slice(b * seq_len, (b + 1) * seq_len)
            q, k, v = q_ref[place, span], k_ref[place, span], v_ref[place, span]
            ga = grad_att[span]
            dq = jnp.zeros((seq_len, narrow), f32)
            dk = jnp.zeros((seq_len, narrow), f32)
            dv = jnp.zeros((seq_len, narrow), f32)
            for head in range(narrow // HEAD_DIM):
                mask = head_mask(narrow, head)
                kh = jnp.where(mask, k, jnp.zeros_like(k))
                vh = jnp.where(mask, v, jnp.zeros_like(v))
                qh = jnp.where(mask, q, jnp.zeros_like(q))
                gh = jnp.where(mask, ga, jnp.zeros_like(ga))
                scores = jnp.where(causal, dot(q, kh, 1, 1) * scale, -1e30)
                grown = jnp.exp(scores - jnp.max(scores, axis=-1, keepdims=True))
                soft = grown / jnp.sum(grown, axis=-1, keepdims=True)
                grad_soft = dot(ga, vh, 1, 1)
                grad_scores = (
                    soft * (grad_soft - jnp.sum(soft * grad_soft, axis=-1, keepdims=True))
                ).astype(bf16)
                dq = dq + dot(grad_scores, kh, 1, 0)
                dk = dk + dot(grad_scores, qh, 0, 0)
                dv = dv + dot(soft.astype(bf16), gh, 0, 0)
            d_qkv[place, span, :narrow] = turn(dq * scale, cosine, -sine).astype(bf16)
            d_qkv[place, span, narrow : 2 * narrow] = turn(dk * scale, cosine, -sine).astype(bf16)
            d_qkv[place, span, 2 * narrow :] = dv.astype(bf16)
        return dot(d_qkv[place], w_qkv[...], 1, 1)

    def far_copy(j):
        return pltpu.make_async_remote_copy(
            src_ref=far.at[j % 2],
            dst_ref=core_in.at[j],
            send_sem=far_send.at[j],
            recv_sem=far_recv.at[j],
            device_id=core_partner,
            device_id_type=MESH,
        )

    def far_step(i, carry):
        j = QUAD - 1 - i
        part = attend_block(QUAD + j).astype(bf16)

        @pl.when(i >= 2)
        def _():
            far_copy(j + 2).wait_send()

        far[j % 2] = part
        far_copy(j).start()
        return carry

    lax.fori_loop(0, QUAD, far_step, 0)
    for j in range(2):
        far_copy(j).wait_send()
    def near_step(i, carry):
        j = QUAD - 1 - i
        part = attend_block(j)
        far_copy(j).wait_recv()
        own_sum[...] = part + core_in[j].astype(f32)
        near[j] = own_sum[...].astype(bf16)
        return carry

    lax.fori_loop(0, QUAD, near_step, 0)
    total_one = Total(mail, near, own_sum, mid, in_a, in_b)
    total_one.first()
    total_one.first_a()

    def add_mixed(target, left, landed):
        count, across = landed.shape
        buffer = add_buf.at[pl.ds(0, count), pl.ds(0, across)]
        copy = pltpu.make_async_copy(landed, buffer, add_sem.at[0])
        copy.start()
        copy.wait()
        add_near(target, left, buffer)

    collect_o = Collect(
        mail, bits, by_place(p_o, rows), land_o, sum_o, lambda piece: out_o, add_mixed
    )
    collect_qkv = Collect(
        mail, bits, by_runs(p_qkv), land_qkv, sum_qkv,
        lambda piece: fin_qkv.at[pl.ds(piece * run_rows, run_rows)], add_mixed,
    )
    p_o[...] = p_o_sum[...].astype(bf16)
    collect_o.start()
    cut = acts.shape[3]
    cuts = width // cut
    shift = (1 - flat // (ring.count // 2)) * (cuts // 2)

    def chunk_at(i):
        return pl.multiple_of(((i + shift) % cuts) * cut, cut)

    def act_copy(i):
        return pltpu.make_async_copy(
            act_one.at[:, :, pl.ds(chunk_at(i), cut)], acts.at[i % 2], act_sems.at[i % 2]
        )

    act_copy(0).start()

    def chunk_step(i, carry):
        act_copy(i).wait()

        @pl.when(i + 1 < cuts)
        def _():
            act_copy(i + 1).start()

        left = acts[i % 2].reshape(2 * QUAD * size, cut)
        right = d_qkv[...].reshape(2 * QUAD * size, 3 * narrow)
        p_qkv[pl.ds(chunk_at(i), cut), :] = dot(left, right, 0, 0).astype(bf16)
        return carry

    lax.fori_loop(0, cuts // 2, chunk_step, 0)
    collect_qkv.start()
    total_one.second()
    lax.fori_loop(cuts // 2, cuts, chunk_step, 0)
    if len(bits) > 2:
        collect_d.take_away(top_stage - 1, 0)
    collect_d.finish_piece(0)

    block = ring.span * hidden_rows
    gu_swap = []
    team = ring.team(flat)

    def hand_out(last, ref):
        for delta in ring.deltas:
            other = ring.team(ring.flip(flat, delta))
            part = pl.ds(pl.multiple_of(other * rows, 16), rows)
            for y in range(ring.upper_size):
                for o in range(ring.across):
                    target = ((y * 2 + team // QUAD) * ring.across + o) * QUAD + team % QUAD
                    src = last.at[part, pl.ds((y * ring.across + o) * block, block)]
                    dst = ref.at[:, pl.ds(pl.multiple_of(target * block, 128), block)]
                    if delta:
                        gu_swap.append(mail.post(src, dst, delta))
                    else:
                        mail.keep(src, dst)

    for piece in range(collect_g.pieces):
        collect_g.finish_piece(piece)
    hand_out(fin_g, out_gate)
    collect_o.take_away(top_stage, 0)
    for piece in range(collect_qkv.pieces):
        collect_qkv.take_away(top_stage, piece)
    for piece in range(collect_u.pieces):
        collect_u.finish_piece(piece)
    hand_out(fin_u, out_up)
    total_one.arrive()

    def first_norm(part):
        x = x_ref[part, :].astype(f32)
        grads, terms = norm_back(total_one.value(part), x, gains_ref[0:1, :])
        grad_resid[part, :] = grad_resid[part, :] + grads
        gain_grads[0:1, :] = gain_grads[0:1, :] + jnp.sum(terms, axis=0, keepdims=True)

    strips(first_norm)
    mail.keep(grad_resid, grad_tokens)
    for step, bit in enumerate([ring.bit_core, ring.bit_a, ring.bit_b] + bits):
        copy = mail.post(gain_grads, gain_in.at[step], bit)
        copy.wait()
        mail.sent = [c for c in mail.sent if c is not copy]
        gain_grads[...] = gain_grads[...] + gain_in[step]
    for piece in range(collect_qkv.pieces):
        collect_qkv.finish_piece(piece)
    collect_o.finish_piece(0)

    swaps = []
    for delta in ring.deltas:
        other = ring.team(ring.flip(flat, delta))
        src = fin_qkv.at[pl.ds(pl.multiple_of(other * rows, 16), rows)]
        dst = qkv_in.at[team]
        if delta:
            swaps.append(mail.post(src, dst, delta))
        else:
            kept = mail.keep(src, dst)
    kept.wait()
    mail.kept = [c for c in mail.kept if c is not kept]
    for copy in swaps:
        copy.wait_recv()
    for j, ref in enumerate((out_q, out_k, out_v)):
        parts = []
        for y in range(ring.upper_size):
            for c in range(2):
                for o in range(ring.across):
                    for q in range(QUAD):
                        start = j * narrow + (y * ring.across + o) * HEAD_DIM
                        parts.append(qkv_in[c * QUAD + q, :, start : start + HEAD_DIM])
        ref[...] = jnp.concatenate(parts, axis=1).astype(f32)
    for copy in gu_swap:
        copy.wait_recv()
    mail.finish()


def back(outer, inner, seq_len, near_args, far_args):
    tokens, w_qkv, w_o = near_args[0], far_args[4], far_args[5]
    size, width = tokens.shape
    narrow = w_o.shape[0]
    hidden = far_args[6].shape[1]
    places = outer * inner // (2 * QUAD)
    rows = width // (outer * inner)
    hidden_rows = hidden // places
    span = max(1, HEAD_DIM // rows)
    pieces = 2 if span == 1 else 2 * QUAD
    run_rows = 2 * QUAD * rows // pieces
    remote = (places - 1) * (3 * pieces + 2) + 7 + 14 * places // span + 8 + 24
    local = 20 + 2 * places // span
    vm = pl.BlockSpec(memory_space=pltpu.VMEM)
    hbm = pl.BlockSpec(memory_space=pl.ANY)
    sds = jax.ShapeDtypeStruct
    out_shape = (
        sds((rows, width), f32),
        sds((rows, width), f32),
        sds((rows, width), f32),
        sds((rows, width), f32),
        sds((8, width), f32),
        sds((rows, 2 * QUAD * hidden), bf16),
        sds((rows, 2 * QUAD * hidden), bf16),
        sds((hidden_rows, width), f32),
        sds(((places - 1) * pieces, run_rows, hidden), bf16),
        sds(((places - 1) * pieces, run_rows, hidden), bf16),
        sds((places // 2, hidden_rows, width), bf16),
        sds((places // 2 * pieces, run_rows, hidden), bf16),
        sds((places // 2 * pieces, run_rows, hidden), bf16),
        sds((places // 2, hidden_rows, width), bf16),
        sds((2 * QUAD * rows, hidden), bf16),
        sds((2 * QUAD * rows, hidden), bf16),
        sds(((places - 1) * pieces, run_rows, 3 * narrow), bf16),
        sds((places - 1, rows, width), bf16),
        sds((size, width), f32),
    )
    wide = pltpu.VMEM((size, width), bf16)
    four = pltpu.VMEM((QUAD, size, width), bf16)
    cut = min(256, width // 2)
    four_sems = pltpu.SemaphoreType.DMA((QUAD,))
    return pl.pallas_call(
        functools.partial(back_kernel, outer, inner, seq_len),
        out_shape=out_shape,
        in_specs=[vm] * len(near_args) + [hbm] * len(far_args),
        out_specs=tuple([vm] * 5 + [hbm] * 14),
        scratch_shapes=[pltpu.VMEM(a.shape, a.dtype) for a in (*far_args[:4], w_qkv, w_o)]
        + [
            four, four, pltpu.VMEM((2, size, width), bf16),
            pltpu.VMEM((size, width), f32),
            pltpu.VMEM((size, width), f32),
            pltpu.VMEM((2 * QUAD, size, width), bf16),
            wide, wide, wide,
            pltpu.VMEM((2, 2 * QUAD, size, cut), bf16),
            pltpu.VMEM((2 * QUAD, size, 3 * narrow), bf16),
            pltpu.VMEM((width, 3 * narrow), bf16),
            pltpu.VMEM((narrow, width), bf16),
            pltpu.VMEM((narrow, width), f32),
            pltpu.VMEM((places // 2 * pieces, run_rows, 3 * narrow), bf16),
            pltpu.VMEM((places // 2, rows, width), bf16),
            pltpu.VMEM((2 * QUAD * rows, 3 * narrow), bf16),
            pltpu.VMEM((2 * QUAD, rows, 3 * narrow), bf16),
            pltpu.VMEM((8, 8, width), f32),
            pltpu.SemaphoreType.DMA((remote,)),
            pltpu.SemaphoreType.DMA((remote,)),
            pltpu.SemaphoreType.DMA((local,)),
            four_sems, four_sems,
            pltpu.SemaphoreType.DMA((2,)),
            pltpu.VMEM((run_rows, width), bf16),
            pltpu.SemaphoreType.DMA((1,)),
        ],
        compiler_params=pltpu.CompilerParams(
            collective_id=1, has_side_effects=True, vmem_limit_bytes=63 * 1024 * 1024
        ),
        name="back",
    )(*near_args, *far_args)


def mid_kernel(
    outer, inner, hidden_rows,
    go_ref, factor_ref,
    act_two, wg_ref, wu_ref, wd_ref, resid_ref,
    p_g, p_u, half_d, added, layer_out, dy, p_d, land_d, a_down, b_down, a_two, b_two,
    w_g, w_u, w_d, middle, cols, act_in, dy_in, act_cut, dy_cut, stage_d, dy_own,
    far_down, far_two, tmp_down, tmp_two, near_down, near_two, own_down, own_two, halves, stage,
    send_sems, recv_sems, local_sems, down_send, down_recv, two_send, two_recv, act_sems, dy_sem, cut_sems, out_sems, pd_send, pd_recv,
):
    size, width = go_ref.shape
    hidden = w_g.shape[1]
    ring = Ring(outer, inner, width // (outer * inner))
    mail = Mail(ring, send_sems, recv_sems, local_sems)
    ring.greet()
    flat = ring.flat
    strip = 32
    top_bit = ring.count // 2

    def strips(step):
        def run(i, carry):
            step(pl.ds(pl.multiple_of(i * strip, strip), strip))
            return carry

        lax.fori_loop(0, size // strip, run, 0)

    def dot(left, right, left_dim, right_dim):
        return lax.dot_general(
            left, right, (((left_dim,), (right_dim,)), ((), ())), preferred_element_type=f32
        )

    def settle(copy):
        copy.wait()
        mail.kept = [c for c in mail.kept if c is not copy]

    def pair_at(i):
        return i + (i // 2) * (5 - 2 * i)

    def pair_copies(source, target, sems, i):
        pair = pair_at(i)
        return [
            pltpu.make_async_copy(source.at[pair], target.at[pl.ds(0, size)], sems.at[0]),
            pltpu.make_async_copy(source.at[QUAD + pair], target.at[pl.ds(size, size)], sems.at[1]),
        ]

    def act_copies(i):
        return pair_copies(act_two, act_in.at[i % 2], act_sems.at[i % 2], i)

    for copy in act_copies(0):
        copy.start()
    loads = [mail.keep(wg_ref, w_g), mail.keep(wu_ref, w_u), mail.keep(wd_ref, w_d)]
    load_resid = mail.keep(resid_ref, own_down)

    def cotangent(part):
        dy_own[part, :] = (go_ref[part, :].astype(f32) * factor_ref[part, :]).astype(bf16)

    strips(cotangent)
    keep_dy = mail.keep(dy_own, dy.at[0])
    half = size // 2
    top, end = pl.ds(0, half), pl.ds(half, half)
    share = Share(mail, dy, dy_own)
    share.first()
    for copy in loads:
        settle(copy)
    settle(load_resid)
    settle(keep_dy)
    share.done((0,))

    def core_copy(kind, i):
        source, target, send, recv = (
            (far_down, tmp_down, down_send, down_recv),
            (far_two, tmp_two, two_send, two_recv),
        )[kind]
        return pltpu.make_async_remote_copy(
            src_ref=source,
            dst_ref=target.at[i % 2],
            send_sem=send.at[i],
            recv_sem=recv.at[i],
            device_id=ring.where(ring.bit_core),
            device_id_type=MESH,
        )

    base = mail.used
    mail.used += 9

    def late(n):
        src, dst, bit = (
            (dy.at[1, top], dy.at[3, top], ring.bit_b),
            (dy.at[2, end], dy.at[3, end], ring.bit_a),
            (dy.at[1], dy.at[QUAD + 1], ring.bit_core),
            (dy.at[2], dy.at[QUAD + 2], ring.bit_core),
            (dy.at[3], dy.at[QUAD + 3], ring.bit_core),
            (near_two.at[2, top], halves.at[1, 0], ring.bit_b),
            (near_two.at[2, end], halves.at[1, 1], ring.bit_a),
            (near_down.at[2, top], halves.at[0, 0], ring.bit_b),
            (near_down.at[2, end], halves.at[0, 1], ring.bit_a),
        )[n]
        return pltpu.make_async_remote_copy(
            src_ref=src,
            dst_ref=dst,
            send_sem=send_sems.at[base + n],
            recv_sem=recv_sems.at[base + n],
            device_id=ring.where(bit),
            device_id_type=MESH,
        )

    def join(kind, i):
        pair = pair_at(i)
        tmp, near, own = ((tmp_down, near_down, own_down), (tmp_two, near_two, own_two))[kind]
        core_copy(kind, i).wait_recv()
        tmp = tmp.at[i % 2]

        @pl.when(pair == 0)
        def _():
            add_near(own, own, tmp)

        @pl.when(pair > 0)
        def _():
            here = near.at[jnp.maximum(pair, 1) - 1]
            add_near(here, here, tmp)

    wide = min(512, width)
    piece = min(256, hidden)

    def give(kind, i, left, product, far, near, own):
        pair = pair_at(i)

        @pl.when(i >= 1)
        def _():
            join(kind, i - 1)
            core_copy(kind, i - 1).wait_send()

        @pl.when(i == 3)
        def _():
            late(7 - 2 * kind).start()
            late(8 - 2 * kind).start()

        for c in range(width // wide):
            part = slice(c * wide, (c + 1) * wide)
            whole = product(left, part)
            far[:, part] = whole[size:].astype(bf16)
            mine = whole[:size]

            @pl.when(pair == 0)
            def _():
                own[:, part] = mine + own[:, part] if kind == 0 else mine

            @pl.when(pair > 0)
            def _():
                near[jnp.maximum(pair, 1) - 1, :, part] = mine.astype(bf16)

        core_copy(kind, i).start()

    second = {}

    def pass_sums(kind):
        near, to_a, to_b = ((near_down, a_down, b_down), (near_two, a_two, b_two))[kind]
        join(kind, QUAD - 1)
        late(7 - 2 * kind).wait_recv()
        add_near(near.at[0, top], near.at[0, top], halves.at[kind, 0])
        second["a", kind] = mail.post(near.at[0], to_a, ring.bit_a)
        late(8 - 2 * kind).wait_recv()
        add_near(near.at[1, end], near.at[1, end], halves.at[kind, 1])
        second["b", kind] = mail.post(near.at[1], to_b, ring.bit_b)
        core_copy(kind, QUAD - 1).wait_send()

    def ahead(i, carry):
        pair = pair_at(i)

        @pl.when(i == 2)
        def _():
            share.from_a.wait_recv()
            late(0).start()
            late(2).start()
            share.from_b.wait_recv()
            late(1).start()
            late(3).start()

        @pl.when(i == 3)
        def _():
            late(0).wait_recv()
            late(1).wait_recv()
            late(4).start()

        for copy in act_copies(i):
            copy.wait()

        @pl.when(i + 1 < QUAD)
        def _():
            for copy in act_copies(i + 1):
                copy.start()

        act = act_in[i % 2]
        for c in range(hidden // piece):
            part = slice(c * piece, (c + 1) * piece)
            up_part = slice(hidden + c * piece, hidden + (c + 1) * piece)
            gate_pre = dot(act, w_g[:, part], 1, 0)
            up_proj = dot(act, w_u[:, part], 1, 0)
            ready = (gate_pre * jax.nn.sigmoid(gate_pre) * up_proj).astype(bf16)
            for rows, place in ((slice(0, size), pair), (slice(size, None), QUAD + pair)):
                middle[place, :, part] = ready[rows]
                cols[place, :, part] = gate_pre[rows].astype(bf16)
                cols[place, :, up_part] = up_proj[rows].astype(bf16)

        give(
            0, i,
            jnp.concatenate([middle[pair], middle[QUAD + pair]], axis=0),
            lambda left, part: dot(left, w_d[:, part], 1, 0),
            far_down, near_down, own_down,
        )
        return carry

    lax.fori_loop(0, QUAD, ahead, 0)
    pass_sums(0)
    for n in (2, 3, 4):
        late(n).wait_recv()

    cut = act_cut.shape[3]
    cuts = width // cut
    tokens = 2 * QUAD * size

    def cut_copy(source, target, i):
        start = pl.multiple_of(i * cut, cut)
        return pltpu.make_async_copy(
            source.at[:, :, pl.ds(start, cut)], target.at[i % 2], cut_sems.at[i % 2]
        )

    def down_out(i):
        start = pl.multiple_of(i * cut, cut)
        return pltpu.make_async_copy(
            stage_d.at[i % 2], p_d.at[:, pl.ds(start, cut)], out_sems.at[i % 2]
        )

    upper = flat // top_bit
    rows_half = hidden // 2
    away = pl.ds(pl.multiple_of((1 - upper) * rows_half, 16), rows_half)
    kept = pl.ds(pl.multiple_of(upper * rows_half, 16), rows_half)

    def down_send_at(i):
        part = pl.ds(pl.multiple_of(i * cut, cut), cut)
        return pltpu.make_async_remote_copy(
            src_ref=p_d.at[away, part],
            dst_ref=land_d.at[:, part],
            send_sem=pd_send.at[i],
            recv_sem=pd_recv.at[i],
            device_id=ring.where(top_bit),
            device_id_type=MESH,
        )

    cut_copy(dy, dy_cut, 0).start()

    def down_step(i, carry):
        cut_copy(dy, dy_cut, i).wait()

        @pl.when(i + 1 < cuts)
        def _():
            cut_copy(dy, dy_cut, i + 1).start()

        turned = dot(
            dy_cut[i % 2].reshape(tokens, cut), middle[...].reshape(tokens, hidden), 0, 0
        )

        stage_d[i % 2] = turned.T.astype(bf16)
        down_out(i).start()

        @pl.when(i >= 1)
        def _():
            down_out(i - 1).wait()
            down_send_at(i - 1).start()

        return carry

    lax.fori_loop(0, cuts, down_step, 0)
    cut_copy(act_two, act_cut, 0).start()
    down_out(cuts - 1).wait()
    down_send_at(cuts - 1).start()

    def behind(i, carry):
        pair = pair_at(i)
        dy_copies = pair_copies(dy, dy_in, dy_sem, i)
        for copy in dy_copies:
            copy.start()
        for copy in dy_copies:
            copy.wait()
        grads = dy_in[...]
        for c in range(hidden // piece):
            part = slice(c * piece, (c + 1) * piece)
            up_part = slice(hidden + c * piece, hidden + (c + 1) * piece)
            grad_middle = dot(grads, w_d[part, :], 1, 1)
            for rows, place in ((slice(0, size), pair), (slice(size, None), QUAD + pair)):
                gate_pre = cols[place, :, part].astype(f32)
                up_proj = cols[place, :, up_part].astype(f32)
                sigmoid_gate = jax.nn.sigmoid(gate_pre)
                swish = gate_pre * sigmoid_gate
                came = grad_middle[rows]
                cols[place, :, up_part] = (came * swish).astype(bf16)
                cols[place, :, part] = (
                    came * up_proj * sigmoid_gate * (1.0 + gate_pre * (1.0 - sigmoid_gate))
                ).astype(bf16)

        give(
            1, i,
            jnp.concatenate([cols[pair], cols[QUAD + pair]], axis=0),
            lambda left, part: dot(left[:, :hidden], w_g[part, :], 1, 1)
            + dot(left[:, hidden:], w_u[part, :], 1, 1),
            far_two, near_two, own_two,
        )
        return carry

    lax.fori_loop(0, QUAD, behind, 0)
    pass_sums(1)

    def stage_out(i):
        rows = pl.ds(pl.multiple_of(i * cut, cut), cut)
        return [
            pltpu.make_async_copy(
                stage.at[i % 2, :, pl.ds(j * hidden, hidden)],
                target.at[rows],
                out_sems.at[2 + 2 * j + i % 2],
            )
            for j, target in enumerate((p_g, p_u))
        ]

    def gate_step(i, carry):
        cut_copy(act_two, act_cut, i).wait()

        @pl.when(i + 1 < cuts)
        def _():
            cut_copy(act_two, act_cut, i + 1).start()

        @pl.when(i >= 2)
        def _():
            for copy in stage_out(i - 2):
                copy.wait()

        stage[i % 2] = dot(
            act_cut[i % 2].reshape(tokens, cut), cols[...].reshape(tokens, 2 * hidden), 0, 0
        ).astype(bf16)
        for copy in stage_out(i):
            copy.start()
        return carry

    lax.fori_loop(0, cuts, gate_step, 0)
    for i in (cuts - 2, cuts - 1):
        for copy in stage_out(i):
            copy.wait()

    for kind, own, in_a, in_b in ((1, own_two, a_two, b_two), (0, own_down, a_down, b_down)):
        second["a", kind].wait_recv()
        second["b", kind].wait_recv()
        first = mail.keep(in_a, tmp_down.at[0])
        other = mail.keep(in_b, tmp_two.at[0])
        settle(first)
        settle(other)

        def finish(part, own=own, kind=kind):
            total = own[part, :] + tmp_down[0, part, :].astype(f32) + tmp_two[0, part, :].astype(f32)
            if kind:
                own_two[part, :] = total
            else:
                far_down[part, :] = total.astype(bf16)

        strips(finish)
        if kind:
            mail.keep(own_two, added)
        else:
            mail.keep(far_down, layer_out)
    for i in range(cuts):
        down_send_at(i).wait()
    add_far(half_d, p_d.at[kept], land_d)
    for n in range(9):
        late(n).wait_send()
    mail.finish()


def mid(outer, inner, hidden_rows, grad_out, factor_rows, act_two, w_g, w_u, w_d, resid):
    size, width = grad_out.shape
    hidden = w_g.shape[1]
    vm = pl.BlockSpec(memory_space=pltpu.VMEM)
    hbm = pl.BlockSpec(memory_space=pl.ANY)
    sds = jax.ShapeDtypeStruct
    wide = sds((size, width), bf16)
    out_shape = (
        sds((width, hidden), bf16),
        sds((width, hidden), bf16),
        sds((hidden // 2, width), bf16),
        sds((size, width), f32),
        wide,
        sds((2 * QUAD, size, width), bf16),
        sds((hidden, width), bf16),
        sds((hidden // 2, width), bf16),
        wide, wide, wide, wide,
    )
    cut = min(256, width // 2)
    vw = pltpu.VMEM((size, width), bf16)
    dma = pltpu.SemaphoreType.DMA
    return pl.pallas_call(
        functools.partial(mid_kernel, outer, inner, hidden_rows),
        out_shape=out_shape,
        in_specs=[vm] * 2 + [hbm] * 5,
        out_specs=tuple([hbm] * len(out_shape)),
        scratch_shapes=[
            pltpu.VMEM((width, hidden), bf16),
            pltpu.VMEM((width, hidden), bf16),
            pltpu.VMEM((hidden, width), bf16),
            pltpu.VMEM((2 * QUAD, size, hidden), bf16),
            pltpu.VMEM((2 * QUAD, size, 2 * hidden), bf16),
            pltpu.VMEM((2, 2 * size, width), bf16),
            pltpu.VMEM((2 * size, width), bf16),
            pltpu.VMEM((2, 2 * QUAD, size, cut), bf16),
            pltpu.VMEM((2, 2 * QUAD, size, cut), bf16),
            pltpu.VMEM((2, hidden, cut), bf16),
            vw,
            vw, vw,
            pltpu.VMEM((2, size, width), bf16),
            pltpu.VMEM((2, size, width), bf16),
            pltpu.VMEM((QUAD - 1, size, width), bf16),
            pltpu.VMEM((QUAD - 1, size, width), bf16),
            pltpu.VMEM((size, width), f32),
            pltpu.VMEM((size, width), f32),
            pltpu.VMEM((2, 2, size // 2, width), bf16),
            pltpu.VMEM((2, cut, 2 * hidden), bf16),
            dma((32,)), dma((32,)), dma((16,)),
            dma((QUAD,)), dma((QUAD,)), dma((QUAD,)), dma((QUAD,)),
            dma((2, 2)), dma((2,)), dma((2,)), dma((6,)),
            dma((width // cut,)), dma((width // cut,)),
        ],
        compiler_params=pltpu.CompilerParams(
            collective_id=2, has_side_effects=True, vmem_limit_bytes=63 * 1024 * 1024
        ),
        name="mid",
    )(grad_out, factor_rows, act_two, w_g, w_u, w_d, resid)


def on_device(
    tokens,
    labels,
    counts,
    grad_out,
    w_query,
    w_key,
    w_value,
    w_out,
    gain_attn,
    gain_mlp,
    w_gate,
    w_up,
    w_down,
):
    batch_size, seq_len, width = tokens.shape
    outer_count = lax.axis_size("dp")
    inner_count = lax.axis_size("fsdp")
    rows = w_query.shape[0]
    hidden_rows = w_down.shape[0]
    flat = lax.axis_index("dp") * inner_count + lax.axis_index("fsdp")
    x_rows = tokens.reshape(-1, width)

    token_total = float(seq_len * batch_size * outer_count * inner_count)
    picked_counts = jnp.sum(
        jnp.where(labels[:, None] == jnp.arange(3)[None, :], counts[None, :], 0), axis=1
    ).astype(f32)
    factor = token_total / (3.0 * picked_counts)
    cosine, sine = rope_tables(seq_len, HEAD_DIM)
    head_count = width // (2 * QUAD) // HEAD_DIM
    sign = jnp.where(jnp.arange(HEAD_DIM) < HEAD_DIM // 2, -1.0, 1.0)
    wide_cosine = jnp.tile(cosine, (1, head_count))
    wide_sine = jnp.tile(sine * sign, (1, head_count))
    gain_rows = lax.dynamic_update_slice(
        jnp.zeros((8, width), f32),
        jnp.stack([gain_attn, gain_mlp]).astype(f32),
        (0, flat * rows),
    )
    factor_rows = jnp.repeat(factor, seq_len)[:, None]
    (
        act_one, w_qkv, w_o, q_rot, k_rot, values, attended, resid, gains, act_two, w_g, w_u, w_d,
    ) = front(
        outer_count, inner_count, seq_len,
        x_rows, gain_rows,
        w_query, w_key, w_value,
        wide_cosine, wide_sine,
        w_out, w_gate, w_up, w_down,
    )
    p_g, p_u, half_d, added, layer_out = mid(
        outer_count, inner_count, w_down.shape[0], grad_out.reshape(-1, width), factor_rows,
        act_two, w_g, w_u, w_d, resid,
    )[:5]
    layer_out = layer_out.reshape(tokens.shape)
    results = back(
        outer_count, inner_count, seq_len,
        (
            x_rows, grad_out.reshape(-1, width), factor_rows, gains, wide_cosine, wide_sine,
        ),
        (q_rot, k_rot, values, attended, w_qkv, w_o, p_g, p_u, half_d, act_one, resid, added),
    )
    query_grad, key_grad, value_grad, out_grad, gain_grads = results[:5]
    gate_grad, up_grad, down_grad = (a.astype(f32) for a in results[5:8])
    grad_tokens = results[-1]
    gain_grads = lax.dynamic_slice(gain_grads, (0, flat * rows), (2, rows))
    return (
        layer_out,
        grad_tokens.reshape(tokens.shape),
        query_grad,
        key_grad,
        value_grad,
        out_grad,
        gain_grads[0],
        gain_grads[1],
        gate_grad,
        up_grad,
        down_grad,
    )


def solution(mesh):
    rows = P(AXES, None)
    vector = P(AXES)
    three = P(AXES, None, None)
    in_specs = (three, vector, P(), three, rows, rows, rows, rows, vector, vector, rows, rows, rows)
    out_specs = (three, three, rows, rows, rows, rows, vector, vector, rows, rows, rows)
    return jax.shard_map(
        on_device, mesh=mesh, in_specs=in_specs, out_specs=out_specs, check_vma=False
    )
```

```python
import functools

import jax
import jax.numpy as jnp
from jax import lax
from jax.experimental import pallas as pl
from jax.experimental.pallas import tpu as pltpu
from jax.sharding import PartitionSpec as P

HEAD_DIM = 64
AXES = ("dp", "fsdp")
QUAD = 4

epsilon = 1e-05
rope_base = 130000.0
bf16 = jnp.bfloat16
f32 = jnp.float32
MESH = pl.DeviceIdType.MESH


def rope_tables(seq_len, head_dim):
    half_dim = head_dim // 2
    frequency = rope_base ** (-(jnp.arange(half_dim).astype(f32) * 2.0) / head_dim)
    angles = jnp.arange(seq_len).astype(f32)[:, None] * frequency[None, :]
    angles = jnp.concatenate([angles, angles], axis=1)
    return (jnp.cos(angles), jnp.sin(angles))


class Ring:
    def __init__(self, outer, inner, rows):
        self.known = {}
        self.count = outer * inner
        self.inner = inner
        self.span = max(1, HEAD_DIM // rows)
        self.bit_a = self.span
        self.bit_b = 2 * self.span
        self.bit_core = inner
        self.low = powers(1, self.span)
        self.mid = powers(QUAD * self.span, inner)
        self.upper = powers(2 * inner, self.count)
        self.data_bits = self.low + self.mid + self.upper
        self.deltas = [
            (self.bit_core if t // QUAD else 0) + (t % QUAD) * self.span for t in range(2 * QUAD)
        ]
        self.across = inner // (QUAD * self.span)
        self.upper_size = outer // 2
        self.flat = lax.axis_index("dp") * inner + lax.axis_index("fsdp")

    def flip(self, flat, bits):
        bit = 1
        while bit <= bits:
            if bits & bit:
                flat = flat + bit * (1 - 2 * ((flat // bit) % 2))
            bit *= 2
        return flat

    def where(self, bits):
        if bits not in self.known:
            other = self.flip(self.flat, bits)
            self.known[bits] = (other // self.inner, other % self.inner)
        return self.known[bits]

    def team(self, flat):
        return ((flat // self.inner) % 2) * QUAD + (flat // self.span) % QUAD

    def place(self, flat):
        return (
            (flat // (2 * self.inner)) * self.across + (flat % self.inner) // (QUAD * self.span)
        ) * self.span + flat % self.span

    def runs(self, flat, rows):
        lowest = flat - self.span * ((flat // self.span) % QUAD)
        lowest = lowest - self.inner * ((flat // self.inner) % 2)
        found = []
        for core in range(2):
            start = lowest + core * self.inner
            if self.span == 1:
                found.append((start * rows, QUAD * rows))
            else:
                found += [((start + q * self.span) * rows, rows) for q in range(QUAD)]
        return found

    def greet(self):
        partners = self.deltas[1:] + self.data_bits
        barrier = pltpu.get_barrier_semaphore()
        for bits in partners:
            pl.semaphore_signal(barrier, 1, device_id=self.where(bits), device_id_type=MESH)
        pl.semaphore_wait(barrier, len(partners))


def powers(first, end):
    found = []
    while first < end:
        found.append(first)
        first *= 2
    return found


class Mail:
    def __init__(self, ring, send_sems, recv_sems, local_sems):
        self.ring, self.send_sems, self.recv_sems, self.local_sems = ring, send_sems, recv_sems, local_sems
        self.used = 0
        self.used_local = 0
        self.sent = []
        self.kept = []

    def post(self, src, dst, bits):
        copy = pltpu.make_async_remote_copy(
            src_ref=src,
            dst_ref=dst,
            send_sem=self.send_sems.at[self.used],
            recv_sem=self.recv_sems.at[self.used],
            device_id=self.ring.where(bits),
            device_id_type=MESH,
        )
        self.used += 1
        copy.start()
        self.sent.append(copy)
        return copy

    def keep(self, src, dst):
        copy = pltpu.make_async_copy(src, dst, self.local_sems.at[self.used_local])
        self.used_local += 1
        copy.start()
        self.kept.append(copy)
        return copy

    def drop(self, copy):
        self.sent = [c for c in self.sent if c is not copy]

    def finish(self):
        for copy in self.sent:
            copy.wait_send()
        for copy in self.kept:
            copy.wait()


class Spread:
    def __init__(self, mail, views, bits):
        self.mail, self.views, self.bits = mail, views, bits
        self.pieces = len(views(0))
        self.came = {}

    def start(self, key, piece, first):
        ref = self.views(key)[piece]
        for bit in self.bits[first:]:
            self.came[key + bit, piece] = self.mail.post(ref, ref, bit)

    def begin(self, piece=None):
        for p in range(self.pieces) if piece is None else (piece,):
            self.start(0, p, 0)

    def pass_on(self, stage, piece=None):
        for p in range(self.pieces) if piece is None else (piece,):
            for key in keys_below(self.bits, stage):
                key += self.bits[stage]
                self.came.pop((key, p)).wait_recv()
                self.start(key, p, stage + 1)

    def pass_all(self, piece=None):
        for stage in range(len(self.bits) - 1):
            self.pass_on(stage, piece)

    def done(self):
        for copy in self.came.values():
            copy.wait_recv()


def keys_below(bits, stage):
    return [
        sum(b for i, b in enumerate(bits[:stage]) if low >> i & 1) for low in range(2**stage)
    ]


class Adding:
    def __init__(self, mail, ref, came_in, bits):
        self.mail, self.ref, self.came_in, self.bits = mail, ref, came_in, bits
        self.step = 0

    def post(self):
        self.copy = self.mail.post(
            self.ref, self.came_in.at[self.step], self.bits[self.step]
        )

    def take(self):
        self.copy.wait()
        self.mail.drop(self.copy)
        self.ref[...] = self.ref[...] + self.came_in[self.step]
        self.step += 1


class Share:
    def __init__(self, mail, whole, own):
        self.mail, self.whole, self.own = mail, whole, own
        self.core = []

    def first_core(self):
        self.to_core(self.own, 0)

    def first_a(self):
        self.from_a = self.mail.post(self.own, self.whole.at[1], self.mail.ring.bit_a)

    def first_b(self):
        self.from_b = self.mail.post(self.own, self.whole.at[2], self.mail.ring.bit_b)

    def first(self):
        self.first_a()
        self.first_b()
        self.first_core()

    def to_core(self, ref, place):
        self.core.append(
            self.mail.post(ref, self.whole.at[QUAD + place], self.mail.ring.bit_core)
        )

    def second_a(self):
        self.from_a.wait_recv()
        self.to_core(self.whole.at[1], 1)

    def second_b(self):
        self.from_b.wait_recv()
        self.both = self.mail.post(self.whole.at[2], self.whole.at[3], self.mail.ring.bit_a)
        self.to_core(self.whole.at[2], 2)

    def second(self):
        self.second_a()
        self.second_b()

    def third(self):
        self.both.wait_recv()
        self.to_core(self.whole.at[3], 3)

    def done(self, places=range(QUAD)):
        for place in places:
            self.core[place].wait_recv()


def add_near(target, left, right):
    rows = left.shape[0]
    strip = min(32, rows)

    def step(i, carry):
        part = pl.ds(pl.multiple_of(i * strip, strip), strip)
        target[part, :] = (left[part, :].astype(f32) + right[part, :].astype(f32)).astype(
            target.dtype
        )
        return carry

    lax.fori_loop(0, rows // strip, step, 0)


class Total:
    def __init__(self, mail, near, own, mid, in_a, in_b):
        self.mail, self.near, self.own = mail, near, own
        self.mid, self.in_a, self.in_b = mid, in_a, in_b

    def first(self):
        self.over = self.mail.post(self.near.at[3], self.mid, self.mail.ring.bit_a)

    def first_a(self):
        self.for_a = self.mail.post(self.near.at[1], self.in_a, self.mail.ring.bit_a)

    def second(self):
        self.over.wait_recv()
        add_near(self.near.at[2], self.near.at[2], self.mid)
        self.for_b = self.mail.post(self.near.at[2], self.in_b, self.mail.ring.bit_b)

    def arrive(self):
        self.for_a.wait_recv()
        self.for_b.wait_recv()

    def value(self, part):
        return self.own[part, :] + self.in_a[part, :].astype(f32) + self.in_b[part, :].astype(f32)


def head_mask(width, head):
    lanes = lax.broadcasted_iota(jnp.int32, (1, width), 1)
    return (lanes >= head * HEAD_DIM) & (lanes < (head + 1) * HEAD_DIM)


def turn(u, cosine, signed_sine):
    width = u.shape[-1]
    half = HEAD_DIM // 2
    lanes = lax.broadcasted_iota(jnp.int32, (1, width), 1)
    lower = lanes % HEAD_DIM < half
    turned = jnp.where(lower, pltpu.roll(u, width - half, 1), pltpu.roll(u, half, 1))
    return u * cosine + turned * signed_sine


def front_kernel(
    outer, inner, seq_len,
    x_ref, gain_ref, wq_ref, wk_ref, wv_ref, cos_ref, sin_ref,
    wo_ref, wg_ref, wu_ref, wd_ref,
    act_one_far, w_qkv_far, w_o_far, q_far, k_far, v_far, att_far, resid_far, gains_out,
    act_two, w_g, w_u, w_d,
    act_one, w_qkv, w_o, q_out, k_out, v_out, att_out, resid_out,
    cut, gain_in, x_all, far, core_in, near, own_sum, mid, in_a, in_b, act_two_own,
    send_sems, recv_sems, local_sems, far_send, far_recv,
):
    rows = wq_ref.shape[0]
    width = wq_ref.shape[1]
    hidden_rows = wd_ref.shape[0]
    narrow = width // (2 * QUAD)
    ring = Ring(outer, inner, rows)
    mail = Mail(ring, send_sems, recv_sems, local_sems)
    ring.greet()
    bits = ring.data_bits
    flat = ring.flat

    def by_place(ref, size, pieces):
        step = size // pieces
        return lambda key: [
            ref.at[
                pl.ds(
                    pl.multiple_of(ring.place(ring.flip(flat, key)) * size + p * step, 16), step
                )
            ]
            for p in range(pieces)
        ]

    def by_runs(ref):
        return lambda key: [
            ref.at[pl.ds(pl.multiple_of(start, 16), size)]
            for start, size in ring.runs(ring.flip(flat, key), rows)
        ]

    def settle(copy):
        copy.wait()
        mail.kept = [c for c in mail.kept if c is not copy]

    mine_o = w_o.at[pl.ds(pl.multiple_of(ring.place(flat) * rows, 16), rows)]
    mine_d = w_d.at[pl.ds(pl.multiple_of(ring.place(flat) * hidden_rows, 16), hidden_rows)]
    keep_o = mail.keep(wo_ref, mine_o)
    keep_d = mail.keep(wd_ref, mine_d)
    keep_x = mail.keep(x_ref, x_all.at[0])

    gains_out[...] = gain_ref[...]
    gains = Adding(
        mail, gains_out, gain_in, [ring.bit_a, ring.bit_b, ring.bit_core] + bits
    )
    gains.post()

    chunk = HEAD_DIM
    for t in range(2 * QUAD):
        for j, ref in enumerate((wq_ref, wk_ref, wv_ref)):
            parts = []
            for y in range(ring.upper_size):
                for o in range(ring.across):
                    head = ((y * 2 + t // QUAD) * ring.across + o) * QUAD + t % QUAD
                    parts.append(ref[:, head * chunk : (head + 1) * chunk])
            cut[t, :, j * narrow : (j + 1) * narrow] = jnp.concatenate(parts, axis=1)
    here = pl.ds(pl.multiple_of(flat * rows, 16), rows)
    keep_qkv = mail.keep(cut.at[ring.team(flat)], w_qkv.at[here])
    gains.take()
    gains.post()
    qkv_swap = []
    for delta in ring.deltas[1:]:
        other = ring.flip(flat, delta)
        qkv_swap.append(mail.post(cut.at[ring.team(other)], w_qkv.at[here], delta))
    share_x = Share(mail, x_all, x_ref)
    share_x.first_core()
    share_x.first_a()
    gains.take()
    gains.post()
    settle(keep_o)
    spread_o = Spread(mail, by_place(w_o, rows, 1), bits)
    gains.take()
    gains.post()
    spread_o.begin()
    share_x.first_b()
    settle(keep_qkv)
    for copy in qkv_swap:
        copy.wait_recv()
    spread_qkv = Spread(mail, by_runs(w_qkv), bits)
    spread_qkv.begin()
    while gains.step < len(gains.bits) - 1:
        gains.take()
        gains.post()
    spread_o.pass_all()
    gains.take()

    block = ring.span * hidden_rows

    def swap_columns(ref, whole):
        swap = []
        for delta in ring.deltas:
            team = ring.team(ring.flip(flat, delta))
            for y in range(ring.upper_size):
                for o in range(ring.across):
                    source = ((y * 2 + team // QUAD) * ring.across + o) * QUAD + team % QUAD
                    src = ref.at[:, pl.ds(pl.multiple_of(source * block, 128), block)]
                    dst = whole.at[here, pl.ds((y * ring.across + o) * block, block)]
                    if delta:
                        swap.append((mail.post(src, dst, delta), True))
                    else:
                        swap.append((mail.keep(src, dst), False))
        return swap

    def swapped(swap):
        for copy, remote in swap:
            if remote:
                copy.wait_recv()
            else:
                settle(copy)

    size = act_one.shape[1]
    strip = 32

    def norm_block(place):
        def norm_one(i, carry):
            part = pl.ds(pl.multiple_of(i * strip, strip), strip)
            x = x_all[place, part, :].astype(f32)
            inv = lax.rsqrt(jnp.mean(x * x, axis=-1, keepdims=True) + epsilon)
            act_one[place, part, :] = (x * inv * gains_out[0:1, :]).astype(bf16)
            return carry

        lax.fori_loop(0, size // strip, norm_one, 0)

    share_x.second_a()
    gate_swap = swap_columns(wg_ref, w_g)
    settle(keep_d)
    spread_d = Spread(mail, by_place(w_d, hidden_rows, 2), bits)
    spread_d.begin()
    settle(keep_x)
    share_x.done((0, 1))
    for place in (0, QUAD, 1, QUAD + 1):
        norm_block(place)
    share_x.second_b()
    for piece in range(spread_qkv.pieces):
        spread_qkv.pass_all(piece)
    up_swap = swap_columns(wu_ref, w_u)
    share_x.done((2,))
    for place in (2, QUAD + 2):
        norm_block(place)
    spread_o.done()
    spread_qkv.done()
    mail.keep(w_o, w_o_far)
    mail.keep(w_qkv, w_qkv_far)

    scale = HEAD_DIM**-0.5
    cosine, sine = cos_ref[...], sin_ref[...]
    per_block = act_one.shape[1] // seq_len

    def attend_block(place):
        qkv = jnp.dot(act_one[place], w_qkv[...], preferred_element_type=f32)
        causal = lax.broadcasted_iota(jnp.int32, (seq_len, seq_len), 1) <= lax.broadcasted_iota(
            jnp.int32, (seq_len, seq_len), 0
        )
        for b in range(per_block):
            span = slice(b * seq_len, (b + 1) * seq_len)
            q = turn(qkv[span, :narrow], cosine, sine).astype(bf16)
            k = turn(qkv[span, narrow : 2 * narrow], cosine, sine).astype(bf16)
            v = qkv[span, 2 * narrow :].astype(bf16)
            q_out[place, span] = q
            k_out[place, span] = k
            v_out[place, span] = v
            mixed = jnp.zeros((seq_len, narrow), f32)
            for head in range(narrow // HEAD_DIM):
                mask = head_mask(narrow, head)
                kh = jnp.where(mask, k, jnp.zeros_like(k))
                vh = jnp.where(mask, v, jnp.zeros_like(v))
                scores = lax.dot_general(
                    q, kh, (((1,), (1,)), ((), ())), preferred_element_type=f32
                )
                scores = jnp.where(causal, scores * scale, -1e30)
                top = jnp.max(scores, axis=-1, keepdims=True)
                grown = jnp.exp(scores - top)
                soft = (grown / jnp.sum(grown, axis=-1, keepdims=True)).astype(bf16)
                mixed = mixed + jnp.dot(soft, vh, preferred_element_type=f32)
            att_out[place, span] = mixed.astype(bf16)
        return jnp.dot(att_out[place], w_o[...], preferred_element_type=f32)

    def far_copy(j):
        return pltpu.make_async_remote_copy(
            src_ref=far.at[j],
            dst_ref=core_in.at[j],
            send_sem=far_send.at[j],
            recv_sem=far_recv.at[j],
            device_id=ring.where(ring.bit_core),
            device_id_type=MESH,
        )

    def far_step(j, carry):
        far[j] = attend_block(QUAD + j).astype(bf16)
        far_copy(j).start()
        return carry

    def near_step(j, carry):
        part = attend_block(j)
        far_copy(j).wait_recv()
        total = part + core_in[j].astype(f32)
        near[j] = total.astype(bf16)

        @pl.when(j == 0)
        def _():
            own_sum[...] = total

        return carry

    spread_g = Spread(mail, by_runs(w_g), bits)
    spread_u = Spread(mail, by_runs(w_u), bits)
    lax.fori_loop(0, QUAD - 1, far_step, 0)
    share_x.third()
    swapped(gate_swap)
    spread_g.begin()
    lax.fori_loop(0, QUAD - 1, near_step, 0)
    norm_block(QUAD - 1)
    share_x.done((QUAD - 1,))
    norm_block(2 * QUAD - 1)
    mail.keep(act_one, act_one_far)
    far_step(QUAD - 1, 0)
    near_step(QUAD - 1, 0)
    for j in range(QUAD):
        far_copy(j).wait_send()
    for here, far_off in ((q_out, q_far), (k_out, k_far), (v_out, v_far), (att_out, att_far)):
        mail.keep(here, far_off)
    total = Total(mail, near, own_sum, mid, in_a, in_b)
    total.first()
    total.first_a()
    swapped(up_swap)
    spread_u.begin()
    for piece in range(spread_d.pieces):
        spread_d.pass_on(0, piece)
    total.second()
    spread_g.pass_on(0, 0)
    total.arrive()

    def norm_two(i, carry):
        part = pl.ds(pl.multiple_of(i * strip, strip), strip)
        resid = (
            x_ref[part, :].astype(f32) + total.value(part)
        )
        resid_out[part, :] = resid
        inv = lax.rsqrt(jnp.mean(resid * resid, axis=-1, keepdims=True) + epsilon)
        act_two_own[part, :] = (resid * inv * gains_out[1:2, :]).astype(bf16)
        return carry

    lax.fori_loop(0, size // strip, norm_two, 0)
    mail.keep(act_two_own, act_two.at[0])
    mail.keep(resid_out, resid_far)
    share_two = Share(mail, act_two, act_two_own)
    share_two.first()
    for piece in range(1, spread_g.pieces):
        spread_g.pass_on(0, piece)
    share_two.second()
    spread_u.pass_on(0)
    share_two.third()
    for stage in range(1, len(bits) - 1):
        for spread in (spread_d, spread_g, spread_u):
            spread.pass_on(stage)
    spread_d.done()
    spread_g.done()
    spread_u.done()
    share_two.done()
    mail.finish()


def front(outer, inner, seq_len, tokens, gain_rows, w_query, w_key, w_value, cosine, signed_sine, w_out, w_gate, w_up, w_down):
    size, width = tokens.shape
    rows, hidden_all = w_gate.shape
    hidden_rows = w_down.shape[0]
    narrow, hidden = width // (2 * QUAD), hidden_all // (2 * QUAD)
    span = max(1, HEAD_DIM // rows)
    places = outer * inner // (2 * QUAD)
    pieces = 2 if span == 1 else 2 * QUAD
    remote = (places - 1) * (3 * pieces + 3) + 7 + 14 * places // span + 8 + 24
    local = 24 + 2 * places // span
    vm = pl.BlockSpec(memory_space=pltpu.VMEM)
    hbm = pl.BlockSpec(memory_space=pl.ANY)
    eight = (2 * QUAD, size)
    sds = jax.ShapeDtypeStruct
    out_shape = (
        sds(eight + (width,), bf16),
        sds((width, 3 * narrow), bf16),
        sds((narrow, width), bf16),
        sds(eight + (narrow,), bf16),
        sds(eight + (narrow,), bf16),
        sds(eight + (narrow,), bf16),
        sds(eight + (narrow,), bf16),
        sds((size, width), f32),
        sds((8, width), f32),
        sds(eight + (width,), bf16),
        sds((width, hidden), bf16),
        sds((width, hidden), bf16),
        sds((hidden, width), bf16),
    )
    return pl.pallas_call(
        functools.partial(front_kernel, outer, inner, seq_len),
        out_shape=out_shape,
        in_specs=[vm] * 7 + [hbm] * 4,
        out_specs=tuple([hbm] * 8 + [vm] + [hbm] * 4),
        scratch_shapes=[pltpu.VMEM(s.shape, s.dtype) for s in out_shape[:8]]
        + [
            pltpu.VMEM((2 * QUAD, rows, 3 * narrow), bf16),
            pltpu.VMEM((8, 8, width), f32),
            pltpu.VMEM((2 * QUAD, size, width), bf16),
            pltpu.VMEM((QUAD, size, width), bf16),
            pltpu.VMEM((QUAD, size, width), bf16),
            pltpu.VMEM((QUAD, size, width), bf16),
            pltpu.VMEM((size, width), f32),
            pltpu.VMEM((size, width), bf16),
            pltpu.VMEM((size, width), bf16),
            pltpu.VMEM((size, width), bf16),
            pltpu.VMEM((size, width), bf16),
            pltpu.SemaphoreType.DMA((remote,)),
            pltpu.SemaphoreType.DMA((remote,)),
            pltpu.SemaphoreType.DMA((local,)),
            pltpu.SemaphoreType.DMA((QUAD,)),
            pltpu.SemaphoreType.DMA((QUAD,)),
        ],
        compiler_params=pltpu.CompilerParams(
            collective_id=0, has_side_effects=True, vmem_limit_bytes=60 * 1024 * 1024
        ),
        name="front",
    )(tokens, gain_rows, w_query, w_key, w_value, cosine, signed_sine, w_out, w_gate, w_up, w_down)


def add_far(target, left, right):
    rows, width = left.shape
    strip = min(64, rows)

    def body(left_ref, right_ref, target_ref):
        target_ref[...] = (left_ref[...].astype(f32) + right_ref[...].astype(f32)).astype(
            target_ref.dtype
        )

    spec = pl.BlockSpec((strip, width), lambda i: (i, 0))
    pltpu.emit_pipeline(body, grid=(rows // strip,), in_specs=[spec, spec], out_specs=[spec])(
        left, right, target
    )


class Collect:
    def __init__(self, mail, bits, views, landed, sums, last, add):
        self.mail, self.bits, self.views = mail, bits, views
        self.landed, self.sums, self.last, self.add = landed, sums, last, add
        self.came = {}
        self.added = set()
        self.pieces = len(views(0))

    def slot(self, stage, sub, piece):
        return (2**stage - 1 + keys_below(self.bits, stage).index(sub)) * self.pieces + piece

    def current(self, sub, piece):
        if (sub, piece) not in self.added:
            return self.views(sub)[piece]
        return self.sums.at[keys_below(self.bits, len(self.bits)).index(sub) * self.pieces + piece]

    def send(self, stage, sub, piece):
        bit = self.bits[stage]
        self.came[stage, sub, piece] = self.mail.post(
            self.current(bit + sub, piece), self.landed.at[self.slot(stage, sub, piece)], bit
        )

    def start(self, which=None):
        stage = len(self.bits) - 1
        for sub in reversed(keys_below(self.bits, stage)):
            if which is None or (sub != 0) == which:
                for piece in range(self.pieces):
                    self.send(stage, sub, piece)

    def take(self, stage, sub, piece):
        self.came[stage, sub, piece].wait_recv()
        here = self.current(sub, piece)
        landed = self.landed.at[self.slot(stage, sub, piece)]
        if stage == 0:
            self.add(self.last(piece), here, landed)
            return
        place = keys_below(self.bits, len(self.bits)).index(sub) * self.pieces + piece
        self.add(self.sums.at[place], here, landed)
        self.added.add((sub, piece))
        below = self.bits[stage - 1]
        if (sub // below) % 2:
            self.send(stage - 1, sub - below, piece)

    def take_away(self, stage, piece):
        below = self.bits[stage - 1]
        for sub in keys_below(self.bits, stage):
            if (sub // below) % 2:
                self.take(stage, sub, piece)

    def take_here(self, stage, piece):
        below = self.bits[stage - 1] if stage else 0
        for sub in keys_below(self.bits, stage):
            if not stage or not (sub // below) % 2:
                self.take(stage, sub, piece)

    def finish_piece(self, piece):
        top = len(self.bits) - 1
        for stage in range(top, -1, -1):
            if stage and stage != top:
                self.take_away(stage, piece)
            self.take_here(stage, piece)


def norm_back(total, base, gain):
    inv = lax.rsqrt(jnp.mean(base * base, axis=-1, keepdims=True) + epsilon)
    scaled = gain * total
    grads = inv * scaled - base * inv**3 * jnp.mean(scaled * base, axis=-1, keepdims=True)
    return grads, total * base * inv


def back_kernel(
    outer, inner, seq_len,
    x_ref, go_ref, factor_ref, gains_ref, cos_ref, sin_ref,
    q_far, k_far, v_far, att_far, w_qkv_far, w_o_far,
    p_g, p_u, half_d, act_one, resid_ref, two_ref,
    out_q, out_k, out_v, out_o, gain_grads,
    out_gate, out_up, out_d, land_g, land_u, land_d, sum_g, sum_u, sum_d, fin_g, fin_u, land_qkv, land_o, grad_tokens,
    q_ref, k_ref, v_ref, att_ref, w_qkv, w_o,
    near, core_in, far, own_sum, grad_resid, branch,
    mid, in_a, in_b,
    acts, d_qkv, p_qkv, p_o, p_o_sum, sum_qkv, sum_o, fin_qkv, qkv_in, gain_in,
    send_sems, recv_sems, local_sems, far_send, far_recv, act_sems, add_buf, add_sem,
):
    size, width = x_ref.shape
    rows = out_q.shape[0]
    hidden_rows = out_d.shape[0]
    narrow = w_o.shape[0]
    hidden = p_g.shape[1]
    ring = Ring(outer, inner, rows)
    mail = Mail(ring, send_sems, recv_sems, local_sems)
    ring.greet()
    bits = ring.data_bits
    flat = ring.flat
    strip = 32
    core_partner = ring.where(ring.bit_core)

    def strips(step):
        def run(i, carry):
            step(pl.ds(pl.multiple_of(i * strip, strip), strip))
            return carry

        lax.fori_loop(0, size // strip, run, 0)

    def by_place(ref, count):
        return lambda key: [
            ref.at[pl.ds(pl.multiple_of(ring.place(ring.flip(flat, key)) * count, 16), count)]
        ]

    def by_runs(ref):
        return lambda key: [
            ref.at[pl.ds(pl.multiple_of(start, 16), count)]
            for start, count in ring.runs(ring.flip(flat, key), rows)
        ]

    def dot(left, right, left_dim, right_dim):
        return lax.dot_general(
            left, right, (((left_dim,), (right_dim,)), ((), ())), preferred_element_type=f32
        )

    run_rows = ring.runs(flat, rows)[0][1]
    top_stage = len(bits) - 1
    collect_g, collect_u = (
        Collect(
            mail, bits, by_runs(partial), landed, sums,
            lambda piece, last=last: last.at[pl.ds(piece * run_rows, run_rows)], add_far,
        )
        for partial, landed, sums, last in (
            (p_g, land_g, sum_g, fin_g), (p_u, land_u, sum_u, fin_u)
        )
    )
    share_count = half_d.shape[0] // hidden_rows

    def half_place(key):
        place = ring.place(ring.flip(flat, key)) % share_count
        return [half_d.at[pl.ds(pl.multiple_of(place * hidden_rows, 16), hidden_rows)]]

    collect_d = Collect(mail, bits[:-1], half_place, land_d, sum_d, lambda piece: out_d, add_far)

    load_resid = mail.keep(resid_ref, grad_resid)
    load_two = mail.keep(two_ref, own_sum)
    loads = [
        mail.keep(far_off, here)
        for far_off, here in (
            (w_o_far, w_o), (att_far, att_ref), (q_far, q_ref), (k_far, k_ref), (v_far, v_ref), (w_qkv_far, w_qkv),
        )
    ]
    collect_d.start()
    for which in (True, False):
        collect_g.start(which)
        collect_u.start(which)
    gain_grads[...] = jnp.zeros_like(gain_grads)
    for copy in (load_resid, load_two):
        copy.wait()
        mail.kept = [c for c in mail.kept if c is not copy]

    def second_norm(part):
        resid = grad_resid[part, :]
        grads, terms = norm_back(own_sum[part, :], resid, gains_ref[1:2, :])
        grads = grads + go_ref[part, :].astype(f32) * factor_ref[part, :]
        grad_resid[part, :] = grads
        branch[0, part, :] = grads.astype(bf16)
        gain_grads[1:2, :] = gain_grads[1:2, :] + jnp.sum(terms, axis=0, keepdims=True)

    strips(second_norm)
    share = Share(mail, branch, branch.at[0])
    share.first()
    for piece in range(collect_g.pieces):
        collect_g.take_away(top_stage, piece)
    share.second()
    for piece in range(collect_u.pieces):
        collect_u.take_away(top_stage, piece)
    share.third()
    p_o_sum[...] = jnp.zeros_like(p_o_sum)
    for copy in loads:
        copy.wait()
        mail.kept = [c for c in mail.kept if c is not copy]
    share.done()

    scale = HEAD_DIM**-0.5
    cosine, sine = cos_ref[...], sin_ref[...]
    per_block = size // seq_len

    def attend_block(place):
        grads = branch[place]
        grad_att = dot(grads, w_o[...], 1, 1).astype(bf16)
        p_o_sum[...] = p_o_sum[...] + dot(att_ref[place], grads, 0, 0)
        causal = lax.broadcasted_iota(jnp.int32, (seq_len, seq_len), 1) <= lax.broadcasted_iota(
            jnp.int32, (seq_len, seq_len), 0
        )
        for b in range(per_block):
            span = slice(b * seq_len, (b + 1) * seq_len)
            q, k, v = q_ref[place, span], k_ref[place, span], v_ref[place, span]
            ga = grad_att[span]
            dq = jnp.zeros((seq_len, narrow), f32)
            dk = jnp.zeros((seq_len, narrow), f32)
            dv = jnp.zeros((seq_len, narrow), f32)
            for head in range(narrow // HEAD_DIM):
                mask = head_mask(narrow, head)
                kh = jnp.where(mask, k, jnp.zeros_like(k))
                vh = jnp.where(mask, v, jnp.zeros_like(v))
                qh = jnp.where(mask, q, jnp.zeros_like(q))
                gh = jnp.where(mask, ga, jnp.zeros_like(ga))
                scores = jnp.where(causal, dot(q, kh, 1, 1) * scale, -1e30)
                grown = jnp.exp(scores - jnp.max(scores, axis=-1, keepdims=True))
                soft = grown / jnp.sum(grown, axis=-1, keepdims=True)
                grad_soft = dot(ga, vh, 1, 1)
                grad_scores = (
                    soft * (grad_soft - jnp.sum(soft * grad_soft, axis=-1, keepdims=True))
                ).astype(bf16)
                dq = dq + dot(grad_scores, kh, 1, 0)
                dk = dk + dot(grad_scores, qh, 0, 0)
                dv = dv + dot(soft.astype(bf16), gh, 0, 0)
            d_qkv[place, span, :narrow] = turn(dq * scale, cosine, -sine).astype(bf16)
            d_qkv[place, span, narrow : 2 * narrow] = turn(dk * scale, cosine, -sine).astype(bf16)
            d_qkv[place, span, 2 * narrow :] = dv.astype(bf16)
        return dot(d_qkv[place], w_qkv[...], 1, 1)

    def far_copy(j):
        return pltpu.make_async_remote_copy(
            src_ref=far.at[j % 2],
            dst_ref=core_in.at[j],
            send_sem=far_send.at[j],
            recv_sem=far_recv.at[j],
            device_id=core_partner,
            device_id_type=MESH,
        )

    def far_step(i, carry):
        j = QUAD - 1 - i
        part = attend_block(QUAD + j).astype(bf16)

        @pl.when(i >= 2)
        def _():
            far_copy(j + 2).wait_send()

        far[j % 2] = part
        far_copy(j).start()
        return carry

    lax.fori_loop(0, QUAD, far_step, 0)
    for j in range(2):
        far_copy(j).wait_send()
    def near_step(i, carry):
        j = QUAD - 1 - i
        part = attend_block(j)
        far_copy(j).wait_recv()
        own_sum[...] = part + core_in[j].astype(f32)
        near[j] = own_sum[...].astype(bf16)
        return carry

    lax.fori_loop(0, QUAD, near_step, 0)
    total_one = Total(mail, near, own_sum, mid, in_a, in_b)
    total_one.first()
    total_one.first_a()

    def add_mixed(target, left, landed):
        count, across = landed.shape
        buffer = add_buf.at[pl.ds(0, count), pl.ds(0, across)]
        copy = pltpu.make_async_copy(landed, buffer, add_sem.at[0])
        copy.start()
        copy.wait()
        add_near(target, left, buffer)

    collect_o = Collect(
        mail, bits, by_place(p_o, rows), land_o, sum_o, lambda piece: out_o, add_mixed
    )
    collect_qkv = Collect(
        mail, bits, by_runs(p_qkv), land_qkv, sum_qkv,
        lambda piece: fin_qkv.at[pl.ds(piece * run_rows, run_rows)], add_mixed,
    )
    p_o[...] = p_o_sum[...].astype(bf16)
    collect_o.start()
    cut = acts.shape[3]
    cuts = width // cut
    shift = (1 - flat // (ring.count // 2)) * (cuts // 2)

    def chunk_at(i):
        return pl.multiple_of(((i + shift) % cuts) * cut, cut)

    def act_copy(i):
        return pltpu.make_async_copy(
            act_one.at[:, :, pl.ds(chunk_at(i), cut)], acts.at[i % 2], act_sems.at[i % 2]
        )

    act_copy(0).start()

    def chunk_step(i, carry):
        act_copy(i).wait()

        @pl.when(i + 1 < cuts)
        def _():
            act_copy(i + 1).start()

        left = acts[i % 2].reshape(2 * QUAD * size, cut)
        right = d_qkv[...].reshape(2 * QUAD * size, 3 * narrow)
        p_qkv[pl.ds(chunk_at(i), cut), :] = dot(left, right, 0, 0).astype(bf16)
        return carry

    lax.fori_loop(0, cuts // 2, chunk_step, 0)
    collect_qkv.start()
    total_one.second()
    lax.fori_loop(cuts // 2, cuts, chunk_step, 0)
    if len(bits) > 2:
        collect_d.take_away(top_stage - 1, 0)
    collect_d.finish_piece(0)

    block = ring.span * hidden_rows
    gu_swap = []
    team = ring.team(flat)

    def hand_out(last, ref):
        for delta in ring.deltas:
            other = ring.team(ring.flip(flat, delta))
            part = pl.ds(pl.multiple_of(other * rows, 16), rows)
            for y in range(ring.upper_size):
                for o in range(ring.across):
                    target = ((y * 2 + team // QUAD) * ring.across + o) * QUAD + team % QUAD
                    src = last.at[part, pl.ds((y * ring.across + o) * block, block)]
                    dst = ref.at[:, pl.ds(pl.multiple_of(target * block, 128), block)]
                    if delta:
                        gu_swap.append(mail.post(src, dst, delta))
                    else:
                        mail.keep(src, dst)

    for piece in range(collect_g.pieces):
        collect_g.finish_piece(piece)
    hand_out(fin_g, out_gate)
    collect_o.take_away(top_stage, 0)
    for piece in range(collect_qkv.pieces):
        collect_qkv.take_away(top_stage, piece)
    for piece in range(collect_u.pieces):
        collect_u.finish_piece(piece)
    hand_out(fin_u, out_up)
    total_one.arrive()

    def first_norm(part):
        x = x_ref[part, :].astype(f32)
        grads, terms = norm_back(total_one.value(part), x, gains_ref[0:1, :])
        grad_resid[part, :] = grad_resid[part, :] + grads
        gain_grads[0:1, :] = gain_grads[0:1, :] + jnp.sum(terms, axis=0, keepdims=True)

    strips(first_norm)
    mail.keep(grad_resid, grad_tokens)
    gains = Adding(
        mail, gain_grads, gain_in, [ring.bit_core] + bits[::-1] + [ring.bit_a, ring.bit_b]
    )
    gains.post()
    collect_o.finish_piece(0)
    gains.take()
    gains.post()
    for piece in range(collect_qkv.pieces):
        collect_qkv.finish_piece(piece)
        if gains.step < len(gains.bits) - 1:
            gains.take()
            gains.post()

    swaps = []
    for delta in ring.deltas:
        other = ring.team(ring.flip(flat, delta))
        src = fin_qkv.at[pl.ds(pl.multiple_of(other * rows, 16), rows)]
        dst = qkv_in.at[team]
        if delta:
            swaps.append(mail.post(src, dst, delta))
        else:
            kept = mail.keep(src, dst)
    kept.wait()
    mail.kept = [c for c in mail.kept if c is not kept]
    gains.take()
    while gains.step < len(gains.bits):
        gains.post()
        gains.take()
    for copy in swaps:
        copy.wait_recv()
    for j, ref in enumerate((out_q, out_k, out_v)):
        parts = []
        for y in range(ring.upper_size):
            for c in range(2):
                for o in range(ring.across):
                    for q in range(QUAD):
                        start = j * narrow + (y * ring.across + o) * HEAD_DIM
                        parts.append(qkv_in[c * QUAD + q, :, start : start + HEAD_DIM])
        ref[...] = jnp.concatenate(parts, axis=1).astype(f32)
    for copy in gu_swap:
        copy.wait_recv()
    mail.finish()


def back(outer, inner, seq_len, near_args, far_args):
    tokens, w_qkv, w_o = near_args[0], far_args[4], far_args[5]
    size, width = tokens.shape
    narrow = w_o.shape[0]
    hidden = far_args[6].shape[1]
    places = outer * inner // (2 * QUAD)
    rows = width // (outer * inner)
    hidden_rows = hidden // places
    span = max(1, HEAD_DIM // rows)
    pieces = 2 if span == 1 else 2 * QUAD
    run_rows = 2 * QUAD * rows // pieces
    remote = (places - 1) * (3 * pieces + 2) + 7 + 14 * places // span + 8 + 24
    local = 20 + 2 * places // span
    vm = pl.BlockSpec(memory_space=pltpu.VMEM)
    hbm = pl.BlockSpec(memory_space=pl.ANY)
    sds = jax.ShapeDtypeStruct
    out_shape = (
        sds((rows, width), f32),
        sds((rows, width), f32),
        sds((rows, width), f32),
        sds((rows, width), f32),
        sds((8, width), f32),
        sds((rows, 2 * QUAD * hidden), bf16),
        sds((rows, 2 * QUAD * hidden), bf16),
        sds((hidden_rows, width), f32),
        sds(((places - 1) * pieces, run_rows, hidden), bf16),
        sds(((places - 1) * pieces, run_rows, hidden), bf16),
        sds((places // 2, hidden_rows, width), bf16),
        sds((places // 2 * pieces, run_rows, hidden), bf16),
        sds((places // 2 * pieces, run_rows, hidden), bf16),
        sds((places // 2, hidden_rows, width), bf16),
        sds((2 * QUAD * rows, hidden), bf16),
        sds((2 * QUAD * rows, hidden), bf16),
        sds(((places - 1) * pieces, run_rows, 3 * narrow), bf16),
        sds((places - 1, rows, width), bf16),
        sds((size, width), f32),
    )
    wide = pltpu.VMEM((size, width), bf16)
    four = pltpu.VMEM((QUAD, size, width), bf16)
    cut = min(256, width // 2)
    four_sems = pltpu.SemaphoreType.DMA((QUAD,))
    return pl.pallas_call(
        functools.partial(back_kernel, outer, inner, seq_len),
        out_shape=out_shape,
        in_specs=[vm] * len(near_args) + [hbm] * len(far_args),
        out_specs=tuple([vm] * 5 + [hbm] * 14),
        scratch_shapes=[pltpu.VMEM(a.shape, a.dtype) for a in (*far_args[:4], w_qkv, w_o)]
        + [
            four, four, pltpu.VMEM((2, size, width), bf16),
            pltpu.VMEM((size, width), f32),
            pltpu.VMEM((size, width), f32),
            pltpu.VMEM((2 * QUAD, size, width), bf16),
            wide, wide, wide,
            pltpu.VMEM((2, 2 * QUAD, size, cut), bf16),
            pltpu.VMEM((2 * QUAD, size, 3 * narrow), bf16),
            pltpu.VMEM((width, 3 * narrow), bf16),
            pltpu.VMEM((narrow, width), bf16),
            pltpu.VMEM((narrow, width), f32),
            pltpu.VMEM((places // 2 * pieces, run_rows, 3 * narrow), bf16),
            pltpu.VMEM((places // 2, rows, width), bf16),
            pltpu.VMEM((2 * QUAD * rows, 3 * narrow), bf16),
            pltpu.VMEM((2 * QUAD, rows, 3 * narrow), bf16),
            pltpu.VMEM((8, 8, width), f32),
            pltpu.SemaphoreType.DMA((remote,)),
            pltpu.SemaphoreType.DMA((remote,)),
            pltpu.SemaphoreType.DMA((local,)),
            four_sems, four_sems,
            pltpu.SemaphoreType.DMA((2,)),
            pltpu.VMEM((run_rows, width), bf16),
            pltpu.SemaphoreType.DMA((1,)),
        ],
        compiler_params=pltpu.CompilerParams(
            collective_id=1, has_side_effects=True, vmem_limit_bytes=63 * 1024 * 1024
        ),
        name="back",
    )(*near_args, *far_args)


def mid_kernel(
    outer, inner, hidden_rows,
    go_ref, factor_ref,
    act_two, wg_ref, wu_ref, wd_ref, resid_ref,
    p_g, p_u, half_d, added, layer_out, dy, p_d, land_d, a_down, b_down, a_two, b_two,
    w_g, w_u, w_d, middle, cols, act_in, dy_in, act_cut, dy_cut, stage_d, dy_own,
    far_down, far_two, tmp_down, tmp_two, near_down, near_two, own_down, own_two, halves, stage,
    send_sems, recv_sems, local_sems, down_send, down_recv, two_send, two_recv, act_sems, dy_sem, cut_sems, out_sems, pd_send, pd_recv,
):
    size, width = go_ref.shape
    hidden = w_g.shape[1]
    ring = Ring(outer, inner, width // (outer * inner))
    mail = Mail(ring, send_sems, recv_sems, local_sems)
    ring.greet()
    flat = ring.flat
    strip = 32
    top_bit = ring.count // 2

    def strips(step):
        def run(i, carry):
            step(pl.ds(pl.multiple_of(i * strip, strip), strip))
            return carry

        lax.fori_loop(0, size // strip, run, 0)

    def dot(left, right, left_dim, right_dim):
        return lax.dot_general(
            left, right, (((left_dim,), (right_dim,)), ((), ())), preferred_element_type=f32
        )

    def settle(copy):
        copy.wait()
        mail.kept = [c for c in mail.kept if c is not copy]

    def pair_at(i):
        return i + (i // 2) * (5 - 2 * i)

    def pair_copies(source, target, sems, i):
        pair = pair_at(i)
        return [
            pltpu.make_async_copy(source.at[pair], target.at[pl.ds(0, size)], sems.at[0]),
            pltpu.make_async_copy(source.at[QUAD + pair], target.at[pl.ds(size, size)], sems.at[1]),
        ]

    def act_copies(i):
        return pair_copies(act_two, act_in.at[i % 2], act_sems.at[i % 2], i)

    for copy in act_copies(0):
        copy.start()
    loads = [mail.keep(wg_ref, w_g), mail.keep(wu_ref, w_u), mail.keep(wd_ref, w_d)]
    load_resid = mail.keep(resid_ref, own_down)

    def cotangent(part):
        dy_own[part, :] = (go_ref[part, :].astype(f32) * factor_ref[part, :]).astype(bf16)

    strips(cotangent)
    keep_dy = mail.keep(dy_own, dy.at[0])
    half = size // 2
    top, end = pl.ds(0, half), pl.ds(half, half)
    share = Share(mail, dy, dy_own)
    share.first()
    for copy in loads:
        settle(copy)
    settle(load_resid)
    settle(keep_dy)
    share.done((0,))

    def core_copy(kind, i):
        source, target, send, recv = (
            (far_down, tmp_down, down_send, down_recv),
            (far_two, tmp_two, two_send, two_recv),
        )[kind]
        return pltpu.make_async_remote_copy(
            src_ref=source,
            dst_ref=target.at[i % 2],
            send_sem=send.at[i],
            recv_sem=recv.at[i],
            device_id=ring.where(ring.bit_core),
            device_id_type=MESH,
        )

    base = mail.used
    mail.used += 9

    def late(n):
        src, dst, bit = (
            (dy.at[1, top], dy.at[3, top], ring.bit_b),
            (dy.at[2, end], dy.at[3, end], ring.bit_a),
            (dy.at[1], dy.at[QUAD + 1], ring.bit_core),
            (dy.at[2], dy.at[QUAD + 2], ring.bit_core),
            (dy.at[3], dy.at[QUAD + 3], ring.bit_core),
            (near_two.at[2, top], halves.at[1, 0], ring.bit_b),
            (near_two.at[2, end], halves.at[1, 1], ring.bit_a),
            (near_down.at[2, top], halves.at[0, 0], ring.bit_b),
            (near_down.at[2, end], halves.at[0, 1], ring.bit_a),
        )[n]
        return pltpu.make_async_remote_copy(
            src_ref=src,
            dst_ref=dst,
            send_sem=send_sems.at[base + n],
            recv_sem=recv_sems.at[base + n],
            device_id=ring.where(bit),
            device_id_type=MESH,
        )

    def join(kind, i):
        pair = pair_at(i)
        tmp, near, own = ((tmp_down, near_down, own_down), (tmp_two, near_two, own_two))[kind]
        core_copy(kind, i).wait_recv()
        tmp = tmp.at[i % 2]

        @pl.when(pair == 0)
        def _():
            add_near(own, own, tmp)

        @pl.when(pair > 0)
        def _():
            here = near.at[jnp.maximum(pair, 1) - 1]
            add_near(here, here, tmp)

    wide = min(512, width)
    piece = min(256, hidden)

    def give(kind, i, left, product, far, near, own):
        pair = pair_at(i)

        @pl.when(i >= 1)
        def _():
            join(kind, i - 1)
            core_copy(kind, i - 1).wait_send()

        @pl.when(i == 3)
        def _():
            late(7 - 2 * kind).start()
            late(8 - 2 * kind).start()

        for c in range(width // wide):
            part = slice(c * wide, (c + 1) * wide)
            whole = product(left, part)
            far[:, part] = whole[size:].astype(bf16)
            mine = whole[:size]

            @pl.when(pair == 0)
            def _():
                own[:, part] = mine + own[:, part] if kind == 0 else mine

            @pl.when(pair > 0)
            def _():
                near[jnp.maximum(pair, 1) - 1, :, part] = mine.astype(bf16)

        core_copy(kind, i).start()

    second = {}

    def pass_sums(kind):
        near, to_a, to_b = ((near_down, a_down, b_down), (near_two, a_two, b_two))[kind]
        join(kind, QUAD - 1)
        late(7 - 2 * kind).wait_recv()
        add_near(near.at[0, top], near.at[0, top], halves.at[kind, 0])
        second["a", kind] = mail.post(near.at[0], to_a, ring.bit_a)
        late(8 - 2 * kind).wait_recv()
        add_near(near.at[1, end], near.at[1, end], halves.at[kind, 1])
        second["b", kind] = mail.post(near.at[1], to_b, ring.bit_b)
        core_copy(kind, QUAD - 1).wait_send()

    def ahead(i, carry):
        pair = pair_at(i)

        @pl.when(i == 2)
        def _():
            share.from_a.wait_recv()
            late(0).start()
            late(2).start()
            share.from_b.wait_recv()
            late(1).start()
            late(3).start()

        @pl.when(i == 3)
        def _():
            late(0).wait_recv()
            late(1).wait_recv()
            late(4).start()

        for copy in act_copies(i):
            copy.wait()

        @pl.when(i + 1 < QUAD)
        def _():
            for copy in act_copies(i + 1):
                copy.start()

        act = act_in[i % 2]
        for c in range(hidden // piece):
            part = slice(c * piece, (c + 1) * piece)
            up_part = slice(hidden + c * piece, hidden + (c + 1) * piece)
            gate_pre = dot(act, w_g[:, part], 1, 0)
            up_proj = dot(act, w_u[:, part], 1, 0)
            ready = (gate_pre * jax.nn.sigmoid(gate_pre) * up_proj).astype(bf16)
            for rows, place in ((slice(0, size), pair), (slice(size, None), QUAD + pair)):
                middle[place, :, part] = ready[rows]
                cols[place, :, part] = gate_pre[rows].astype(bf16)
                cols[place, :, up_part] = up_proj[rows].astype(bf16)

        give(
            0, i,
            jnp.concatenate([middle[pair], middle[QUAD + pair]], axis=0),
            lambda left, part: dot(left, w_d[:, part], 1, 0),
            far_down, near_down, own_down,
        )
        return carry

    lax.fori_loop(0, QUAD, ahead, 0)
    pass_sums(0)
    for n in (2, 3, 4):
        late(n).wait_recv()

    cut = act_cut.shape[3]
    cuts = width // cut
    tokens = 2 * QUAD * size

    def cut_copy(source, target, i):
        start = pl.multiple_of(i * cut, cut)
        return pltpu.make_async_copy(
            source.at[:, :, pl.ds(start, cut)], target.at[i % 2], cut_sems.at[i % 2]
        )

    def down_out(i):
        start = pl.multiple_of(i * cut, cut)
        return pltpu.make_async_copy(
            stage_d.at[i % 2], p_d.at[:, pl.ds(start, cut)], out_sems.at[i % 2]
        )

    upper = flat // top_bit
    rows_half = hidden // 2
    away = pl.ds(pl.multiple_of((1 - upper) * rows_half, 16), rows_half)
    kept = pl.ds(pl.multiple_of(upper * rows_half, 16), rows_half)

    def down_send_at(i):
        part = pl.ds(pl.multiple_of(i * cut, cut), cut)
        return pltpu.make_async_remote_copy(
            src_ref=p_d.at[away, part],
            dst_ref=land_d.at[:, part],
            send_sem=pd_send.at[i],
            recv_sem=pd_recv.at[i],
            device_id=ring.where(top_bit),
            device_id_type=MESH,
        )

    cut_copy(dy, dy_cut, 0).start()

    def down_step(i, carry):
        cut_copy(dy, dy_cut, i).wait()

        @pl.when(i + 1 < cuts)
        def _():
            cut_copy(dy, dy_cut, i + 1).start()

        turned = dot(
            dy_cut[i % 2].reshape(tokens, cut), middle[...].reshape(tokens, hidden), 0, 0
        )

        stage_d[i % 2] = turned.T.astype(bf16)
        down_out(i).start()

        @pl.when(i >= 1)
        def _():
            down_out(i - 1).wait()
            down_send_at(i - 1).start()

        return carry

    lax.fori_loop(0, cuts, down_step, 0)
    cut_copy(act_two, act_cut, 0).start()
    down_out(cuts - 1).wait()
    down_send_at(cuts - 1).start()

    def behind(i, carry):
        pair = pair_at(i)
        dy_copies = pair_copies(dy, dy_in, dy_sem, i)
        for copy in dy_copies:
            copy.start()
        for copy in dy_copies:
            copy.wait()
        grads = dy_in[...]
        for c in range(hidden // piece):
            part = slice(c * piece, (c + 1) * piece)
            up_part = slice(hidden + c * piece, hidden + (c + 1) * piece)
            grad_middle = dot(grads, w_d[part, :], 1, 1)
            for rows, place in ((slice(0, size), pair), (slice(size, None), QUAD + pair)):
                gate_pre = cols[place, :, part].astype(f32)
                up_proj = cols[place, :, up_part].astype(f32)
                sigmoid_gate = jax.nn.sigmoid(gate_pre)
                swish = gate_pre * sigmoid_gate
                came = grad_middle[rows]
                cols[place, :, up_part] = (came * swish).astype(bf16)
                cols[place, :, part] = (
                    came * up_proj * sigmoid_gate * (1.0 + gate_pre * (1.0 - sigmoid_gate))
                ).astype(bf16)

        give(
            1, i,
            jnp.concatenate([cols[pair], cols[QUAD + pair]], axis=0),
            lambda left, part: dot(left[:, :hidden], w_g[part, :], 1, 1)
            + dot(left[:, hidden:], w_u[part, :], 1, 1),
            far_two, near_two, own_two,
        )
        return carry

    lax.fori_loop(0, QUAD, behind, 0)
    pass_sums(1)

    def stage_out(i):
        rows = pl.ds(pl.multiple_of(i * cut, cut), cut)
        return [
            pltpu.make_async_copy(
                stage.at[i % 2, :, pl.ds(j * hidden, hidden)],
                target.at[rows],
                out_sems.at[2 + 2 * j + i % 2],
            )
            for j, target in enumerate((p_g, p_u))
        ]

    def gate_step(i, carry):
        cut_copy(act_two, act_cut, i).wait()

        @pl.when(i + 1 < cuts)
        def _():
            cut_copy(act_two, act_cut, i + 1).start()

        @pl.when(i >= 2)
        def _():
            for copy in stage_out(i - 2):
                copy.wait()

        stage[i % 2] = dot(
            act_cut[i % 2].reshape(tokens, cut), cols[...].reshape(tokens, 2 * hidden), 0, 0
        ).astype(bf16)
        for copy in stage_out(i):
            copy.start()
        return carry

    lax.fori_loop(0, cuts, gate_step, 0)
    for i in (cuts - 2, cuts - 1):
        for copy in stage_out(i):
            copy.wait()

    for kind, own, in_a, in_b in ((1, own_two, a_two, b_two), (0, own_down, a_down, b_down)):
        second["a", kind].wait_recv()
        second["b", kind].wait_recv()
        first = mail.keep(in_a, tmp_down.at[0])
        other = mail.keep(in_b, tmp_two.at[0])
        settle(first)
        settle(other)

        def finish(part, own=own, kind=kind):
            total = own[part, :] + tmp_down[0, part, :].astype(f32) + tmp_two[0, part, :].astype(f32)
            if kind:
                own_two[part, :] = total
            else:
                far_down[part, :] = total.astype(bf16)

        strips(finish)
        if kind:
            mail.keep(own_two, added)
        else:
            mail.keep(far_down, layer_out)
    for i in range(cuts):
        down_send_at(i).wait()
    add_far(half_d, p_d.at[kept], land_d)
    for n in range(9):
        late(n).wait_send()
    mail.finish()


def mid(outer, inner, hidden_rows, grad_out, factor_rows, act_two, w_g, w_u, w_d, resid):
    size, width = grad_out.shape
    hidden = w_g.shape[1]
    vm = pl.BlockSpec(memory_space=pltpu.VMEM)
    hbm = pl.BlockSpec(memory_space=pl.ANY)
    sds = jax.ShapeDtypeStruct
    wide = sds((size, width), bf16)
    out_shape = (
        sds((width, hidden), bf16),
        sds((width, hidden), bf16),
        sds((hidden // 2, width), bf16),
        sds((size, width), f32),
        wide,
        sds((2 * QUAD, size, width), bf16),
        sds((hidden, width), bf16),
        sds((hidden // 2, width), bf16),
        wide, wide, wide, wide,
    )
    cut = min(256, width // 2)
    vw = pltpu.VMEM((size, width), bf16)
    dma = pltpu.SemaphoreType.DMA
    return pl.pallas_call(
        functools.partial(mid_kernel, outer, inner, hidden_rows),
        out_shape=out_shape,
        in_specs=[vm] * 2 + [hbm] * 5,
        out_specs=tuple([hbm] * len(out_shape)),
        scratch_shapes=[
            pltpu.VMEM((width, hidden), bf16),
            pltpu.VMEM((width, hidden), bf16),
            pltpu.VMEM((hidden, width), bf16),
            pltpu.VMEM((2 * QUAD, size, hidden), bf16),
            pltpu.VMEM((2 * QUAD, size, 2 * hidden), bf16),
            pltpu.VMEM((2, 2 * size, width), bf16),
            pltpu.VMEM((2 * size, width), bf16),
            pltpu.VMEM((2, 2 * QUAD, size, cut), bf16),
            pltpu.VMEM((2, 2 * QUAD, size, cut), bf16),
            pltpu.VMEM((2, hidden, cut), bf16),
            vw,
            vw, vw,
            pltpu.VMEM((2, size, width), bf16),
            pltpu.VMEM((2, size, width), bf16),
            pltpu.VMEM((QUAD - 1, size, width), bf16),
            pltpu.VMEM((QUAD - 1, size, width), bf16),
            pltpu.VMEM((size, width), f32),
            pltpu.VMEM((size, width), f32),
            pltpu.VMEM((2, 2, size // 2, width), bf16),
            pltpu.VMEM((2, cut, 2 * hidden), bf16),
            dma((32,)), dma((32,)), dma((16,)),
            dma((QUAD,)), dma((QUAD,)), dma((QUAD,)), dma((QUAD,)),
            dma((2, 2)), dma((2,)), dma((2,)), dma((6,)),
            dma((width // cut,)), dma((width // cut,)),
        ],
        compiler_params=pltpu.CompilerParams(
            collective_id=2, has_side_effects=True, vmem_limit_bytes=63 * 1024 * 1024
        ),
        name="mid",
    )(grad_out, factor_rows, act_two, w_g, w_u, w_d, resid)


def on_device(
    tokens,
    labels,
    counts,
    grad_out,
    w_query,
    w_key,
    w_value,
    w_out,
    gain_attn,
    gain_mlp,
    w_gate,
    w_up,
    w_down,
):
    batch_size, seq_len, width = tokens.shape
    outer_count = lax.axis_size("dp")
    inner_count = lax.axis_size("fsdp")
    rows = w_query.shape[0]
    hidden_rows = w_down.shape[0]
    flat = lax.axis_index("dp") * inner_count + lax.axis_index("fsdp")
    x_rows = tokens.reshape(-1, width)

    token_total = float(seq_len * batch_size * outer_count * inner_count)
    picked_counts = jnp.sum(
        jnp.where(labels[:, None] == jnp.arange(3)[None, :], counts[None, :], 0), axis=1
    ).astype(f32)
    factor = token_total / (3.0 * picked_counts)
    cosine, sine = rope_tables(seq_len, HEAD_DIM)
    head_count = width // (2 * QUAD) // HEAD_DIM
    sign = jnp.where(jnp.arange(HEAD_DIM) < HEAD_DIM // 2, -1.0, 1.0)
    wide_cosine = jnp.tile(cosine, (1, head_count))
    wide_sine = jnp.tile(sine * sign, (1, head_count))
    gain_rows = lax.dynamic_update_slice(
        jnp.zeros((8, width), f32),
        jnp.stack([gain_attn, gain_mlp]).astype(f32),
        (0, flat * rows),
    )
    factor_rows = jnp.repeat(factor, seq_len)[:, None]
    (
        act_one, w_qkv, w_o, q_rot, k_rot, values, attended, resid, gains, act_two, w_g, w_u, w_d,
    ) = front(
        outer_count, inner_count, seq_len,
        x_rows, gain_rows,
        w_query, w_key, w_value,
        wide_cosine, wide_sine,
        w_out, w_gate, w_up, w_down,
    )
    p_g, p_u, half_d, added, layer_out = mid(
        outer_count, inner_count, w_down.shape[0], grad_out.reshape(-1, width), factor_rows,
        act_two, w_g, w_u, w_d, resid,
    )[:5]
    layer_out = layer_out.reshape(tokens.shape)
    results = back(
        outer_count, inner_count, seq_len,
        (
            x_rows, grad_out.reshape(-1, width), factor_rows, gains, wide_cosine, wide_sine,
        ),
        (q_rot, k_rot, values, attended, w_qkv, w_o, p_g, p_u, half_d, act_one, resid, added),
    )
    query_grad, key_grad, value_grad, out_grad, gain_grads = results[:5]
    gate_grad, up_grad, down_grad = (a.astype(f32) for a in results[5:8])
    grad_tokens = results[-1]
    gain_grads = lax.dynamic_slice(gain_grads, (0, flat * rows), (2, rows))
    return (
        layer_out,
        grad_tokens.reshape(tokens.shape),
        query_grad,
        key_grad,
        value_grad,
        out_grad,
        gain_grads[0],
        gain_grads[1],
        gate_grad,
        up_grad,
        down_grad,
    )


def solution(mesh):
    rows = P(AXES, None)
    vector = P(AXES)
    three = P(AXES, None, None)
    in_specs = (three, vector, P(), three, rows, rows, rows, rows, vector, vector, rows, rows, rows)
    out_specs = (three, three, rows, rows, rows, rows, vector, vector, rows, rows, rows)
    return jax.shard_map(
        on_device, mesh=mesh, in_specs=in_specs, out_specs=out_specs, check_vma=False
    )
```

```python
import functools

import jax
import jax.numpy as jnp
from jax import lax
from jax.experimental import pallas as pl
from jax.experimental.pallas import tpu as pltpu
from jax.sharding import PartitionSpec as P

HEAD_DIM = 64
AXES = ("dp", "fsdp")
QUAD = 4

epsilon = 1e-05
rope_base = 130000.0
bf16 = jnp.bfloat16
f32 = jnp.float32
MESH = pl.DeviceIdType.MESH


def rope_tables(seq_len, head_dim):
    half_dim = head_dim // 2
    frequency = rope_base ** (-(jnp.arange(half_dim).astype(f32) * 2.0) / head_dim)
    angles = jnp.arange(seq_len).astype(f32)[:, None] * frequency[None, :]
    angles = jnp.concatenate([angles, angles], axis=1)
    return (jnp.cos(angles), jnp.sin(angles))


class Ring:
    def __init__(self, outer, inner, rows):
        self.known = {}
        self.count = outer * inner
        self.inner = inner
        self.span = max(1, HEAD_DIM // rows)
        self.bit_a = self.span
        self.bit_b = 2 * self.span
        self.bit_core = inner
        self.low = powers(1, self.span)
        self.mid = powers(QUAD * self.span, inner)
        self.upper = powers(2 * inner, self.count)
        self.data_bits = self.low + self.mid + self.upper
        self.deltas = [
            (self.bit_core if t // QUAD else 0) + (t % QUAD) * self.span for t in range(2 * QUAD)
        ]
        self.across = inner // (QUAD * self.span)
        self.upper_size = outer // 2
        self.flat = lax.axis_index("dp") * inner + lax.axis_index("fsdp")

    def flip(self, flat, bits):
        bit = 1
        while bit <= bits:
            if bits & bit:
                flat = flat + bit * (1 - 2 * ((flat // bit) % 2))
            bit *= 2
        return flat

    def where(self, bits):
        if bits not in self.known:
            other = self.flip(self.flat, bits)
            self.known[bits] = (other // self.inner, other % self.inner)
        return self.known[bits]

    def team(self, flat):
        return ((flat // self.inner) % 2) * QUAD + (flat // self.span) % QUAD

    def place(self, flat):
        return (
            (flat // (2 * self.inner)) * self.across + (flat % self.inner) // (QUAD * self.span)
        ) * self.span + flat % self.span

    def runs(self, flat, rows):
        lowest = flat - self.span * ((flat // self.span) % QUAD)
        lowest = lowest - self.inner * ((flat // self.inner) % 2)
        found = []
        for core in range(2):
            start = lowest + core * self.inner
            if self.span == 1:
                found.append((start * rows, QUAD * rows))
            else:
                found += [((start + q * self.span) * rows, rows) for q in range(QUAD)]
        return found

    def greet(self):
        partners = self.deltas[1:] + self.data_bits
        barrier = pltpu.get_barrier_semaphore()
        for bits in partners:
            pl.semaphore_signal(barrier, 1, device_id=self.where(bits), device_id_type=MESH)
        pl.semaphore_wait(barrier, len(partners))


def powers(first, end):
    found = []
    while first < end:
        found.append(first)
        first *= 2
    return found


class Mail:
    def __init__(self, ring, send_sems, recv_sems, local_sems):
        self.ring, self.send_sems, self.recv_sems, self.local_sems = ring, send_sems, recv_sems, local_sems
        self.used = 0
        self.used_local = 0
        self.sent = []
        self.kept = []

    def post(self, src, dst, bits):
        copy = pltpu.make_async_remote_copy(
            src_ref=src,
            dst_ref=dst,
            send_sem=self.send_sems.at[self.used],
            recv_sem=self.recv_sems.at[self.used],
            device_id=self.ring.where(bits),
            device_id_type=MESH,
        )
        self.used += 1
        copy.start()
        self.sent.append(copy)
        return copy

    def keep(self, src, dst):
        copy = pltpu.make_async_copy(src, dst, self.local_sems.at[self.used_local])
        self.used_local += 1
        copy.start()
        self.kept.append(copy)
        return copy

    def drop(self, copy):
        self.sent = [c for c in self.sent if c is not copy]

    def finish(self):
        for copy in self.sent:
            copy.wait_send()
        for copy in self.kept:
            copy.wait()


class Spread:
    def __init__(self, mail, views, bits):
        self.mail, self.views, self.bits = mail, views, bits
        self.pieces = len(views(0))
        self.came = {}

    def start(self, key, piece, first):
        ref = self.views(key)[piece]
        for bit in self.bits[first:]:
            self.came[key + bit, piece] = self.mail.post(ref, ref, bit)

    def begin(self, piece=None):
        for p in range(self.pieces) if piece is None else (piece,):
            self.start(0, p, 0)

    def pass_on(self, stage, piece=None):
        for p in range(self.pieces) if piece is None else (piece,):
            for key in keys_below(self.bits, stage):
                key += self.bits[stage]
                self.came.pop((key, p)).wait_recv()
                self.start(key, p, stage + 1)

    def pass_all(self, piece=None):
        for stage in range(len(self.bits) - 1):
            self.pass_on(stage, piece)

    def done(self):
        for copy in self.came.values():
            copy.wait_recv()


def keys_below(bits, stage):
    return [
        sum(b for i, b in enumerate(bits[:stage]) if low >> i & 1) for low in range(2**stage)
    ]


class Adding:
    def __init__(self, mail, ref, came_in, bits):
        self.mail, self.ref, self.came_in, self.bits = mail, ref, came_in, bits
        self.step = 0

    def post(self):
        self.copy = self.mail.post(
            self.ref, self.came_in.at[self.step], self.bits[self.step]
        )

    def take(self):
        self.copy.wait()
        self.mail.drop(self.copy)
        self.ref[...] = self.ref[...] + self.came_in[self.step]
        self.step += 1


class Share:
    def __init__(self, mail, whole, own):
        self.mail, self.whole, self.own = mail, whole, own
        self.core = []

    def first_core(self):
        self.to_core(self.own, 0)

    def first_a(self):
        self.from_a = self.mail.post(self.own, self.whole.at[1], self.mail.ring.bit_a)

    def first_b(self):
        self.from_b = self.mail.post(self.own, self.whole.at[2], self.mail.ring.bit_b)

    def first(self):
        self.first_a()
        self.first_b()
        self.first_core()

    def to_core(self, ref, place):
        self.core.append(
            self.mail.post(ref, self.whole.at[QUAD + place], self.mail.ring.bit_core)
        )

    def second_a(self):
        self.from_a.wait_recv()
        self.to_core(self.whole.at[1], 1)

    def second_b(self):
        self.from_b.wait_recv()
        self.both = self.mail.post(self.whole.at[2], self.whole.at[3], self.mail.ring.bit_a)
        self.to_core(self.whole.at[2], 2)

    def second(self):
        self.second_a()
        self.second_b()

    def third(self):
        self.both.wait_recv()
        self.to_core(self.whole.at[3], 3)

    def done(self, places=range(QUAD)):
        for place in places:
            self.core[place].wait_recv()


def add_near(target, left, right):
    rows = left.shape[0]
    strip = min(32, rows)

    def step(i, carry):
        part = pl.ds(pl.multiple_of(i * strip, strip), strip)
        target[part, :] = (left[part, :].astype(f32) + right[part, :].astype(f32)).astype(
            target.dtype
        )
        return carry

    lax.fori_loop(0, rows // strip, step, 0)


class Total:
    def __init__(self, mail, near, own, mid, in_a, in_b):
        self.mail, self.near, self.own = mail, near, own
        self.mid, self.in_a, self.in_b = mid, in_a, in_b

    def first(self):
        self.over = self.mail.post(self.near.at[3], self.mid, self.mail.ring.bit_a)

    def first_a(self):
        self.for_a = self.mail.post(self.near.at[1], self.in_a, self.mail.ring.bit_a)

    def second(self):
        self.over.wait_recv()
        add_near(self.near.at[2], self.near.at[2], self.mid)
        self.for_b = self.mail.post(self.near.at[2], self.in_b, self.mail.ring.bit_b)

    def arrive(self):
        self.for_a.wait_recv()
        self.for_b.wait_recv()

    def value(self, part):
        return self.own[part, :] + self.in_a[part, :].astype(f32) + self.in_b[part, :].astype(f32)


def head_mask(width, head):
    lanes = lax.broadcasted_iota(jnp.int32, (1, width), 1)
    return (lanes >= head * HEAD_DIM) & (lanes < (head + 1) * HEAD_DIM)


def turn(u, cosine, signed_sine):
    width = u.shape[-1]
    half = HEAD_DIM // 2
    lanes = lax.broadcasted_iota(jnp.int32, (1, width), 1)
    lower = lanes % HEAD_DIM < half
    turned = jnp.where(lower, pltpu.roll(u, width - half, 1), pltpu.roll(u, half, 1))
    return u * cosine + turned * signed_sine


def front_kernel(
    outer, inner, seq_len,
    x_ref, gain_ref, wq_ref, wk_ref, wv_ref, cos_ref, sin_ref,
    wo_ref, wg_ref, wu_ref, wd_ref,
    act_one_far, w_qkv_far, w_o_far, q_far, k_far, v_far, att_far, resid_far, gains_out,
    act_two, w_g, w_u, w_d,
    act_one, w_qkv, w_o, q_out, k_out, v_out, att_out, resid_out,
    cut, gain_in, x_all, far, core_in, near, own_sum, mid, in_a, in_b, act_two_own,
    send_sems, recv_sems, local_sems, far_send, far_recv,
):
    rows = wq_ref.shape[0]
    width = wq_ref.shape[1]
    hidden_rows = wd_ref.shape[0]
    narrow = width // (2 * QUAD)
    ring = Ring(outer, inner, rows)
    mail = Mail(ring, send_sems, recv_sems, local_sems)
    ring.greet()
    bits = ring.data_bits
    flat = ring.flat

    def by_place(ref, size, pieces):
        step = size // pieces
        return lambda key: [
            ref.at[
                pl.ds(
                    pl.multiple_of(ring.place(ring.flip(flat, key)) * size + p * step, 16), step
                )
            ]
            for p in range(pieces)
        ]

    def by_runs(ref):
        return lambda key: [
            ref.at[pl.ds(pl.multiple_of(start, 16), size)]
            for start, size in ring.runs(ring.flip(flat, key), rows)
        ]

    def settle(copy):
        copy.wait()
        mail.kept = [c for c in mail.kept if c is not copy]

    mine_o = w_o.at[pl.ds(pl.multiple_of(ring.place(flat) * rows, 16), rows)]
    mine_d = w_d.at[pl.ds(pl.multiple_of(ring.place(flat) * hidden_rows, 16), hidden_rows)]
    keep_o = mail.keep(wo_ref, mine_o)
    keep_d = mail.keep(wd_ref, mine_d)
    keep_x = mail.keep(x_ref, x_all.at[0])

    gains_out[...] = gain_ref[...]
    gains = Adding(
        mail, gains_out, gain_in, [ring.bit_a, ring.bit_b, ring.bit_core] + bits
    )
    gains.post()

    chunk = HEAD_DIM
    for t in range(2 * QUAD):
        for j, ref in enumerate((wq_ref, wk_ref, wv_ref)):
            parts = []
            for y in range(ring.upper_size):
                for o in range(ring.across):
                    head = ((y * 2 + t // QUAD) * ring.across + o) * QUAD + t % QUAD
                    parts.append(ref[:, head * chunk : (head + 1) * chunk])
            cut[t, :, j * narrow : (j + 1) * narrow] = jnp.concatenate(parts, axis=1)
    here = pl.ds(pl.multiple_of(flat * rows, 16), rows)
    keep_qkv = mail.keep(cut.at[ring.team(flat)], w_qkv.at[here])
    gains.take()
    gains.post()
    qkv_swap = []
    for delta in ring.deltas[1:]:
        other = ring.flip(flat, delta)
        qkv_swap.append(mail.post(cut.at[ring.team(other)], w_qkv.at[here], delta))
    share_x = Share(mail, x_all, x_ref)
    share_x.first_core()
    share_x.first_a()
    gains.take()
    gains.post()
    settle(keep_o)
    spread_o = Spread(mail, by_place(w_o, rows, 1), bits)
    gains.take()
    gains.post()
    spread_o.begin()
    share_x.first_b()
    settle(keep_qkv)
    for copy in qkv_swap:
        copy.wait_recv()
    spread_qkv = Spread(mail, by_runs(w_qkv), bits)
    spread_qkv.begin()
    while gains.step < len(gains.bits) - 1:
        gains.take()
        gains.post()
    spread_o.pass_all()
    gains.take()

    block = ring.span * hidden_rows

    def swap_columns(ref, whole):
        swap = []
        for delta in ring.deltas:
            team = ring.team(ring.flip(flat, delta))
            for y in range(ring.upper_size):
                for o in range(ring.across):
                    source = ((y * 2 + team // QUAD) * ring.across + o) * QUAD + team % QUAD
                    src = ref.at[:, pl.ds(pl.multiple_of(source * block, 128), block)]
                    dst = whole.at[here, pl.ds((y * ring.across + o) * block, block)]
                    if delta:
                        swap.append((mail.post(src, dst, delta), True))
                    else:
                        swap.append((mail.keep(src, dst), False))
        return swap

    def swapped(swap):
        for copy, remote in swap:
            if remote:
                copy.wait_recv()
            else:
                settle(copy)

    size = act_one.shape[1]
    strip = 32

    def norm_block(place):
        def norm_one(i, carry):
            part = pl.ds(pl.multiple_of(i * strip, strip), strip)
            x = x_all[place, part, :].astype(f32)
            inv = lax.rsqrt(jnp.mean(x * x, axis=-1, keepdims=True) + epsilon)
            act_one[place, part, :] = (x * inv * gains_out[0:1, :]).astype(bf16)
            return carry

        lax.fori_loop(0, size // strip, norm_one, 0)

    share_x.second_a()
    gate_swap = swap_columns(wg_ref, w_g)
    settle(keep_d)
    spread_d = Spread(mail, by_place(w_d, hidden_rows, 2), bits)
    spread_d.begin()
    settle(keep_x)
    share_x.done((0, 1))
    for place in (0, QUAD, 1, QUAD + 1):
        norm_block(place)
    share_x.second_b()
    for piece in range(spread_qkv.pieces):
        spread_qkv.pass_all(piece)
    up_swap = swap_columns(wu_ref, w_u)
    share_x.done((2,))
    for place in (2, QUAD + 2):
        norm_block(place)
    spread_o.done()
    spread_qkv.done()
    mail.keep(w_o, w_o_far)
    mail.keep(w_qkv, w_qkv_far)

    scale = HEAD_DIM**-0.5
    cosine, sine = cos_ref[...], sin_ref[...]
    per_block = act_one.shape[1] // seq_len

    def attend_block(place):
        qkv = jnp.dot(act_one[place], w_qkv[...], preferred_element_type=f32)
        causal = lax.broadcasted_iota(jnp.int32, (seq_len, seq_len), 1) <= lax.broadcasted_iota(
            jnp.int32, (seq_len, seq_len), 0
        )
        for b in range(per_block):
            span = slice(b * seq_len, (b + 1) * seq_len)
            q = turn(qkv[span, :narrow], cosine, sine).astype(bf16)
            k = turn(qkv[span, narrow : 2 * narrow], cosine, sine).astype(bf16)
            v = qkv[span, 2 * narrow :].astype(bf16)
            q_out[place, span] = q
            k_out[place, span] = k
            v_out[place, span] = v
            mixed = jnp.zeros((seq_len, narrow), f32)
            for head in range(narrow // HEAD_DIM):
                mask = head_mask(narrow, head)
                kh = jnp.where(mask, k, jnp.zeros_like(k))
                vh = jnp.where(mask, v, jnp.zeros_like(v))
                scores = lax.dot_general(
                    q, kh, (((1,), (1,)), ((), ())), preferred_element_type=f32
                )
                scores = jnp.where(causal, scores * scale, -1e30)
                top = jnp.max(scores, axis=-1, keepdims=True)
                grown = jnp.exp(scores - top)
                soft = (grown / jnp.sum(grown, axis=-1, keepdims=True)).astype(bf16)
                mixed = mixed + jnp.dot(soft, vh, preferred_element_type=f32)
            att_out[place, span] = mixed.astype(bf16)
        return jnp.dot(att_out[place], w_o[...], preferred_element_type=f32)

    def far_copy(j):
        return pltpu.make_async_remote_copy(
            src_ref=far.at[j],
            dst_ref=core_in.at[j],
            send_sem=far_send.at[j],
            recv_sem=far_recv.at[j],
            device_id=ring.where(ring.bit_core),
            device_id_type=MESH,
        )

    def far_step(j, carry):
        far[j] = attend_block(QUAD + j).astype(bf16)
        far_copy(j).start()
        return carry

    def near_step(j, carry):
        part = attend_block(j)
        far_copy(j).wait_recv()
        total = part + core_in[j].astype(f32)
        near[j] = total.astype(bf16)

        @pl.when(j == 0)
        def _():
            own_sum[...] = total

        return carry

    spread_g = Spread(mail, by_runs(w_g), bits)
    spread_u = Spread(mail, by_runs(w_u), bits)
    lax.fori_loop(0, QUAD - 1, far_step, 0)
    share_x.third()
    swapped(gate_swap)
    spread_g.begin()
    lax.fori_loop(0, QUAD - 1, near_step, 0)
    norm_block(QUAD - 1)
    share_x.done((QUAD - 1,))
    norm_block(2 * QUAD - 1)
    mail.keep(act_one, act_one_far)
    far_step(QUAD - 1, 0)
    near_step(QUAD - 1, 0)
    for j in range(QUAD):
        far_copy(j).wait_send()
    for here, far_off in ((q_out, q_far), (k_out, k_far), (v_out, v_far), (att_out, att_far)):
        mail.keep(here, far_off)
    total = Total(mail, near, own_sum, mid, in_a, in_b)
    total.first()
    total.first_a()
    swapped(up_swap)
    spread_u.begin()
    for piece in range(spread_d.pieces):
        spread_d.pass_on(0, piece)
    total.second()
    spread_g.pass_on(0, 0)
    total.arrive()

    def norm_two(i, carry):
        part = pl.ds(pl.multiple_of(i * strip, strip), strip)
        resid = (
            x_ref[part, :].astype(f32) + total.value(part)
        )
        resid_out[part, :] = resid
        inv = lax.rsqrt(jnp.mean(resid * resid, axis=-1, keepdims=True) + epsilon)
        act_two_own[part, :] = (resid * inv * gains_out[1:2, :]).astype(bf16)
        return carry

    lax.fori_loop(0, size // strip, norm_two, 0)
    mail.keep(act_two_own, act_two.at[0])
    mail.keep(resid_out, resid_far)
    share_two = Share(mail, act_two, act_two_own)
    share_two.first()
    for piece in range(1, spread_g.pieces):
        spread_g.pass_on(0, piece)
    share_two.second()
    spread_u.pass_on(0)
    share_two.third()
    for stage in range(1, len(bits) - 1):
        for spread in (spread_d, spread_g, spread_u):
            spread.pass_on(stage)
    spread_d.done()
    spread_g.done()
    spread_u.done()
    share_two.done()
    mail.finish()


def front(outer, inner, seq_len, tokens, gain_rows, w_query, w_key, w_value, cosine, signed_sine, w_out, w_gate, w_up, w_down):
    size, width = tokens.shape
    rows, hidden_all = w_gate.shape
    hidden_rows = w_down.shape[0]
    narrow, hidden = width // (2 * QUAD), hidden_all // (2 * QUAD)
    span = max(1, HEAD_DIM // rows)
    places = outer * inner // (2 * QUAD)
    pieces = 2 if span == 1 else 2 * QUAD
    remote = (places - 1) * (3 * pieces + 3) + 7 + 14 * places // span + 8 + 24
    local = 24 + 2 * places // span
    vm = pl.BlockSpec(memory_space=pltpu.VMEM)
    hbm = pl.BlockSpec(memory_space=pl.ANY)
    eight = (2 * QUAD, size)
    sds = jax.ShapeDtypeStruct
    out_shape = (
        sds(eight + (width,), bf16),
        sds((width, 3 * narrow), bf16),
        sds((narrow, width), bf16),
        sds(eight + (narrow,), bf16),
        sds(eight + (narrow,), bf16),
        sds(eight + (narrow,), bf16),
        sds(eight + (narrow,), bf16),
        sds((size, width), f32),
        sds((8, width), f32),
        sds(eight + (width,), bf16),
        sds((width, hidden), bf16),
        sds((width, hidden), bf16),
        sds((hidden, width), bf16),
    )
    return pl.pallas_call(
        functools.partial(front_kernel, outer, inner, seq_len),
        out_shape=out_shape,
        in_specs=[vm] * 7 + [hbm] * 4,
        out_specs=tuple([hbm] * 8 + [vm] + [hbm] * 4),
        scratch_shapes=[pltpu.VMEM(s.shape, s.dtype) for s in out_shape[:8]]
        + [
            pltpu.VMEM((2 * QUAD, rows, 3 * narrow), bf16),
            pltpu.VMEM((8, 8, width), f32),
            pltpu.VMEM((2 * QUAD, size, width), bf16),
            pltpu.VMEM((QUAD, size, width), bf16),
            pltpu.VMEM((QUAD, size, width), bf16),
            pltpu.VMEM((QUAD, size, width), bf16),
            pltpu.VMEM((size, width), f32),
            pltpu.VMEM((size, width), bf16),
            pltpu.VMEM((size, width), bf16),
            pltpu.VMEM((size, width), bf16),
            pltpu.VMEM((size, width), bf16),
            pltpu.SemaphoreType.DMA((remote,)),
            pltpu.SemaphoreType.DMA((remote,)),
            pltpu.SemaphoreType.DMA((local,)),
            pltpu.SemaphoreType.DMA((QUAD,)),
            pltpu.SemaphoreType.DMA((QUAD,)),
        ],
        compiler_params=pltpu.CompilerParams(
            collective_id=0, has_side_effects=True, vmem_limit_bytes=60 * 1024 * 1024
        ),
        name="front",
    )(tokens, gain_rows, w_query, w_key, w_value, cosine, signed_sine, w_out, w_gate, w_up, w_down)


def add_far(target, left, right):
    rows, width = left.shape
    strip = min(rows, max(16, 131072 // width))

    def body(left_ref, right_ref, target_ref):
        target_ref[...] = (left_ref[...].astype(f32) + right_ref[...].astype(f32)).astype(
            target_ref.dtype
        )

    spec = pl.BlockSpec((strip, width), lambda i: (i, 0))
    pltpu.emit_pipeline(body, grid=(rows // strip,), in_specs=[spec, spec], out_specs=[spec])(
        left, right, target
    )


class Collect:
    def __init__(self, mail, bits, views, landed, sums, last, add):
        self.mail, self.bits, self.views = mail, bits, views
        self.landed, self.sums, self.last, self.add = landed, sums, last, add
        self.came = {}
        self.added = set()
        self.pieces = len(views(0))

    def slot(self, stage, sub, piece):
        return (2**stage - 1 + keys_below(self.bits, stage).index(sub)) * self.pieces + piece

    def current(self, sub, piece):
        if (sub, piece) not in self.added:
            return self.views(sub)[piece]
        return self.sums.at[keys_below(self.bits, len(self.bits)).index(sub) * self.pieces + piece]

    def send(self, stage, sub, piece):
        bit = self.bits[stage]
        self.came[stage, sub, piece] = self.mail.post(
            self.current(bit + sub, piece), self.landed.at[self.slot(stage, sub, piece)], bit
        )

    def start(self, which=None):
        stage = len(self.bits) - 1
        for sub in reversed(keys_below(self.bits, stage)):
            if which is None or (sub != 0) == which:
                for piece in range(self.pieces):
                    self.send(stage, sub, piece)

    def take(self, stage, sub, piece):
        self.came[stage, sub, piece].wait_recv()
        here = self.current(sub, piece)
        landed = self.landed.at[self.slot(stage, sub, piece)]
        if stage == 0:
            self.add(self.last(piece), here, landed)
            return
        place = keys_below(self.bits, len(self.bits)).index(sub) * self.pieces + piece
        self.add(self.sums.at[place], here, landed)
        self.added.add((sub, piece))
        below = self.bits[stage - 1]
        if (sub // below) % 2:
            self.send(stage - 1, sub - below, piece)

    def take_away(self, stage, piece):
        below = self.bits[stage - 1]
        for sub in keys_below(self.bits, stage):
            if (sub // below) % 2:
                self.take(stage, sub, piece)

    def take_here(self, stage, piece):
        below = self.bits[stage - 1] if stage else 0
        for sub in keys_below(self.bits, stage):
            if not stage or not (sub // below) % 2:
                self.take(stage, sub, piece)

    def finish_piece(self, piece):
        top = len(self.bits) - 1
        for stage in range(top, -1, -1):
            if stage and stage != top:
                self.take_away(stage, piece)
            self.take_here(stage, piece)


def norm_back(total, base, gain):
    inv = lax.rsqrt(jnp.mean(base * base, axis=-1, keepdims=True) + epsilon)
    scaled = gain * total
    grads = inv * scaled - base * inv**3 * jnp.mean(scaled * base, axis=-1, keepdims=True)
    return grads, total * base * inv


def back_kernel(
    outer, inner, seq_len,
    x_ref, go_ref, factor_ref, gains_ref, cos_ref, sin_ref,
    q_far, k_far, v_far, att_far, w_qkv_far, w_o_far,
    p_g, p_u, half_d, act_one, resid_ref, two_ref,
    out_q, out_k, out_v, out_o, gain_grads,
    out_gate, out_up, out_d, land_g, land_u, land_d, sum_g, sum_u, sum_d, fin_g, fin_u, land_qkv, land_o, grad_tokens,
    q_ref, k_ref, v_ref, att_ref, w_qkv, w_o,
    near, core_in, far, own_sum, grad_resid, branch,
    mid, in_a, in_b,
    acts, d_qkv, p_qkv, p_o, p_o_sum, sum_qkv, sum_o, fin_qkv, qkv_in, gain_in,
    send_sems, recv_sems, local_sems, far_send, far_recv, act_sems, add_buf, add_sem,
):
    size, width = x_ref.shape
    rows = out_q.shape[0]
    hidden_rows = out_d.shape[0]
    narrow = w_o.shape[0]
    hidden = p_g.shape[1]
    ring = Ring(outer, inner, rows)
    mail = Mail(ring, send_sems, recv_sems, local_sems)
    ring.greet()
    bits = ring.data_bits
    flat = ring.flat
    strip = 32
    core_partner = ring.where(ring.bit_core)

    def strips(step):
        def run(i, carry):
            step(pl.ds(pl.multiple_of(i * strip, strip), strip))
            return carry

        lax.fori_loop(0, size // strip, run, 0)

    def by_place(ref, count):
        return lambda key: [
            ref.at[pl.ds(pl.multiple_of(ring.place(ring.flip(flat, key)) * count, 16), count)]
        ]

    def by_runs(ref):
        return lambda key: [
            ref.at[pl.ds(pl.multiple_of(start, 16), count)]
            for start, count in ring.runs(ring.flip(flat, key), rows)
        ]

    def dot(left, right, left_dim, right_dim):
        return lax.dot_general(
            left, right, (((left_dim,), (right_dim,)), ((), ())), preferred_element_type=f32
        )

    run_rows = ring.runs(flat, rows)[0][1]
    top_stage = len(bits) - 1
    collect_g, collect_u = (
        Collect(
            mail, bits, by_runs(partial), landed, sums,
            lambda piece, last=last: last.at[pl.ds(piece * run_rows, run_rows)], add_far,
        )
        for partial, landed, sums, last in (
            (p_g, land_g, sum_g, fin_g), (p_u, land_u, sum_u, fin_u)
        )
    )
    share_count = half_d.shape[0] // hidden_rows

    def half_place(key):
        place = ring.place(ring.flip(flat, key)) % share_count
        return [half_d.at[pl.ds(pl.multiple_of(place * hidden_rows, 16), hidden_rows)]]

    collect_d = Collect(mail, bits[:-1], half_place, land_d, sum_d, lambda piece: out_d, add_far)

    load_resid = mail.keep(resid_ref, grad_resid)
    load_two = mail.keep(two_ref, own_sum)
    loads = [
        mail.keep(far_off, here)
        for far_off, here in (
            (w_o_far, w_o), (att_far, att_ref), (q_far, q_ref), (k_far, k_ref), (v_far, v_ref), (w_qkv_far, w_qkv),
        )
    ]
    collect_d.start()
    for which in (True, False):
        collect_g.start(which)
        collect_u.start(which)
    gain_grads[...] = jnp.zeros_like(gain_grads)
    for copy in (load_resid, load_two):
        copy.wait()
        mail.kept = [c for c in mail.kept if c is not copy]

    def second_norm(part):
        resid = grad_resid[part, :]
        grads, terms = norm_back(own_sum[part, :], resid, gains_ref[1:2, :])
        grads = grads + go_ref[part, :].astype(f32) * factor_ref[part, :]
        grad_resid[part, :] = grads
        branch[0, part, :] = grads.astype(bf16)
        gain_grads[1:2, :] = gain_grads[1:2, :] + jnp.sum(terms, axis=0, keepdims=True)

    strips(second_norm)
    share = Share(mail, branch, branch.at[0])
    share.first()
    for piece in range(collect_g.pieces):
        collect_g.take_away(top_stage, piece)
    share.second()
    for piece in range(collect_u.pieces):
        collect_u.take_away(top_stage, piece)
    share.third()
    p_o_sum[...] = jnp.zeros_like(p_o_sum)
    for copy in loads:
        copy.wait()
        mail.kept = [c for c in mail.kept if c is not copy]
    share.done()

    scale = HEAD_DIM**-0.5
    cosine, sine = cos_ref[...], sin_ref[...]
    per_block = size // seq_len

    def attend_block(place):
        grads = branch[place]
        grad_att = dot(grads, w_o[...], 1, 1).astype(bf16)
        p_o_sum[...] = p_o_sum[...] + dot(att_ref[place], grads, 0, 0)
        causal = lax.broadcasted_iota(jnp.int32, (seq_len, seq_len), 1) <= lax.broadcasted_iota(
            jnp.int32, (seq_len, seq_len), 0
        )
        for b in range(per_block):
            span = slice(b * seq_len, (b + 1) * seq_len)
            q, k, v = q_ref[place, span], k_ref[place, span], v_ref[place, span]
            ga = grad_att[span]
            dq = jnp.zeros((seq_len, narrow), f32)
            dk = jnp.zeros((seq_len, narrow), f32)
            dv = jnp.zeros((seq_len, narrow), f32)
            for head in range(narrow // HEAD_DIM):
                mask = head_mask(narrow, head)
                kh = jnp.where(mask, k, jnp.zeros_like(k))
                vh = jnp.where(mask, v, jnp.zeros_like(v))
                qh = jnp.where(mask, q, jnp.zeros_like(q))
                gh = jnp.where(mask, ga, jnp.zeros_like(ga))
                scores = jnp.where(causal, dot(q, kh, 1, 1) * scale, -1e30)
                grown = jnp.exp(scores - jnp.max(scores, axis=-1, keepdims=True))
                soft = grown / jnp.sum(grown, axis=-1, keepdims=True)
                grad_soft = dot(ga, vh, 1, 1)
                grad_scores = (
                    soft * (grad_soft - jnp.sum(soft * grad_soft, axis=-1, keepdims=True))
                ).astype(bf16)
                dq = dq + dot(grad_scores, kh, 1, 0)
                dk = dk + dot(grad_scores, qh, 0, 0)
                dv = dv + dot(soft.astype(bf16), gh, 0, 0)
            d_qkv[place, span, :narrow] = turn(dq * scale, cosine, -sine).astype(bf16)
            d_qkv[place, span, narrow : 2 * narrow] = turn(dk * scale, cosine, -sine).astype(bf16)
            d_qkv[place, span, 2 * narrow :] = dv.astype(bf16)
        return dot(d_qkv[place], w_qkv[...], 1, 1)

    def far_copy(j):
        return pltpu.make_async_remote_copy(
            src_ref=far.at[j % 2],
            dst_ref=core_in.at[j],
            send_sem=far_send.at[j],
            recv_sem=far_recv.at[j],
            device_id=core_partner,
            device_id_type=MESH,
        )

    def far_step(i, carry):
        j = QUAD - 1 - i
        part = attend_block(QUAD + j).astype(bf16)

        @pl.when(i >= 2)
        def _():
            far_copy(j + 2).wait_send()

        far[j % 2] = part
        far_copy(j).start()
        return carry

    lax.fori_loop(0, QUAD, far_step, 0)
    for j in range(2):
        far_copy(j).wait_send()
    def near_step(i, carry):
        j = QUAD - 1 - i
        part = attend_block(j)
        far_copy(j).wait_recv()
        own_sum[...] = part + core_in[j].astype(f32)
        near[j] = own_sum[...].astype(bf16)
        return carry

    lax.fori_loop(0, QUAD, near_step, 0)
    total_one = Total(mail, near, own_sum, mid, in_a, in_b)
    total_one.first()
    total_one.first_a()

    def add_mixed(target, left, landed):
        count, across = landed.shape
        buffer = add_buf.at[pl.ds(0, count), pl.ds(0, across)]
        copy = pltpu.make_async_copy(landed, buffer, add_sem.at[0])
        copy.start()
        copy.wait()
        add_near(target, left, buffer)

    collect_o = Collect(
        mail, bits, by_place(p_o, rows), land_o, sum_o, lambda piece: out_o, add_mixed
    )
    collect_qkv = Collect(
        mail, bits, by_runs(p_qkv), land_qkv, sum_qkv,
        lambda piece: fin_qkv.at[pl.ds(piece * run_rows, run_rows)], add_mixed,
    )
    p_o[...] = p_o_sum[...].astype(bf16)
    collect_o.start()
    cut = acts.shape[3]
    cuts = width // cut
    shift = (1 - flat // (ring.count // 2)) * (cuts // 2)

    def chunk_at(i):
        return pl.multiple_of(((i + shift) % cuts) * cut, cut)

    def act_copy(i):
        return pltpu.make_async_copy(
            act_one.at[:, :, pl.ds(chunk_at(i), cut)], acts.at[i % 2], act_sems.at[i % 2]
        )

    act_copy(0).start()

    def chunk_step(i, carry):
        act_copy(i).wait()

        @pl.when(i + 1 < cuts)
        def _():
            act_copy(i + 1).start()

        left = acts[i % 2].reshape(2 * QUAD * size, cut)
        right = d_qkv[...].reshape(2 * QUAD * size, 3 * narrow)
        p_qkv[pl.ds(chunk_at(i), cut), :] = dot(left, right, 0, 0).astype(bf16)
        return carry

    lax.fori_loop(0, cuts // 2, chunk_step, 0)
    collect_qkv.start()
    total_one.second()
    lax.fori_loop(cuts // 2, cuts, chunk_step, 0)
    if len(bits) > 2:
        collect_d.take_away(top_stage - 1, 0)
    collect_d.finish_piece(0)

    block = ring.span * hidden_rows
    gu_swap = []
    team = ring.team(flat)

    def hand_out(last, ref):
        for delta in ring.deltas:
            other = ring.team(ring.flip(flat, delta))
            part = pl.ds(pl.multiple_of(other * rows, 16), rows)
            for y in range(ring.upper_size):
                for o in range(ring.across):
                    target = ((y * 2 + team // QUAD) * ring.across + o) * QUAD + team % QUAD
                    src = last.at[part, pl.ds((y * ring.across + o) * block, block)]
                    dst = ref.at[:, pl.ds(pl.multiple_of(target * block, 128), block)]
                    if delta:
                        gu_swap.append(mail.post(src, dst, delta))
                    else:
                        mail.keep(src, dst)

    for piece in range(collect_g.pieces):
        collect_g.finish_piece(piece)
    hand_out(fin_g, out_gate)
    collect_o.take_away(top_stage, 0)
    for piece in range(collect_qkv.pieces):
        collect_qkv.take_away(top_stage, piece)
    for piece in range(collect_u.pieces):
        collect_u.finish_piece(piece)
    hand_out(fin_u, out_up)
    total_one.arrive()

    def first_norm(part):
        x = x_ref[part, :].astype(f32)
        grads, terms = norm_back(total_one.value(part), x, gains_ref[0:1, :])
        grad_resid[part, :] = grad_resid[part, :] + grads
        gain_grads[0:1, :] = gain_grads[0:1, :] + jnp.sum(terms, axis=0, keepdims=True)

    strips(first_norm)
    mail.keep(grad_resid, grad_tokens)
    gains = Adding(
        mail, gain_grads, gain_in, [ring.bit_core] + bits[::-1] + [ring.bit_a, ring.bit_b]
    )
    gains.post()
    collect_o.finish_piece(0)
    gains.take()
    gains.post()
    for piece in range(collect_qkv.pieces):
        collect_qkv.finish_piece(piece)
        if gains.step < len(gains.bits) - 1:
            gains.take()
            gains.post()

    swaps = []
    for delta in ring.deltas:
        other = ring.team(ring.flip(flat, delta))
        src = fin_qkv.at[pl.ds(pl.multiple_of(other * rows, 16), rows)]
        dst = qkv_in.at[team]
        if delta:
            swaps.append(mail.post(src, dst, delta))
        else:
            kept = mail.keep(src, dst)
    kept.wait()
    mail.kept = [c for c in mail.kept if c is not kept]
    gains.take()
    while gains.step < len(gains.bits):
        gains.post()
        gains.take()
    for copy in swaps:
        copy.wait_recv()
    for j, ref in enumerate((out_q, out_k, out_v)):
        parts = []
        for y in range(ring.upper_size):
            for c in range(2):
                for o in range(ring.across):
                    for q in range(QUAD):
                        start = j * narrow + (y * ring.across + o) * HEAD_DIM
                        parts.append(qkv_in[c * QUAD + q, :, start : start + HEAD_DIM])
        ref[...] = jnp.concatenate(parts, axis=1).astype(f32)
    for copy in gu_swap:
        copy.wait_recv()
    mail.finish()


def back(outer, inner, seq_len, near_args, far_args):
    tokens, w_qkv, w_o = near_args[0], far_args[4], far_args[5]
    size, width = tokens.shape
    narrow = w_o.shape[0]
    hidden = far_args[6].shape[1]
    places = outer * inner // (2 * QUAD)
    rows = width // (outer * inner)
    hidden_rows = hidden // places
    span = max(1, HEAD_DIM // rows)
    pieces = 2 if span == 1 else 2 * QUAD
    run_rows = 2 * QUAD * rows // pieces
    remote = (places - 1) * (3 * pieces + 2) + 7 + 14 * places // span + 8 + 24
    local = 20 + 2 * places // span
    vm = pl.BlockSpec(memory_space=pltpu.VMEM)
    hbm = pl.BlockSpec(memory_space=pl.ANY)
    sds = jax.ShapeDtypeStruct
    out_shape = (
        sds((rows, width), f32),
        sds((rows, width), f32),
        sds((rows, width), f32),
        sds((rows, width), f32),
        sds((8, width), f32),
        sds((rows, 2 * QUAD * hidden), bf16),
        sds((rows, 2 * QUAD * hidden), bf16),
        sds((hidden_rows, width), f32),
        sds(((places - 1) * pieces, run_rows, hidden), bf16),
        sds(((places - 1) * pieces, run_rows, hidden), bf16),
        sds((places // 2, hidden_rows, width), bf16),
        sds((places // 2 * pieces, run_rows, hidden), bf16),
        sds((places // 2 * pieces, run_rows, hidden), bf16),
        sds((places // 2, hidden_rows, width), bf16),
        sds((2 * QUAD * rows, hidden), bf16),
        sds((2 * QUAD * rows, hidden), bf16),
        sds(((places - 1) * pieces, run_rows, 3 * narrow), bf16),
        sds((places - 1, rows, width), bf16),
        sds((size, width), f32),
    )
    wide = pltpu.VMEM((size, width), bf16)
    four = pltpu.VMEM((QUAD, size, width), bf16)
    cut = min(256, width // 2)
    four_sems = pltpu.SemaphoreType.DMA((QUAD,))
    return pl.pallas_call(
        functools.partial(back_kernel, outer, inner, seq_len),
        out_shape=out_shape,
        in_specs=[vm] * len(near_args) + [hbm] * len(far_args),
        out_specs=tuple([vm] * 5 + [hbm] * 14),
        scratch_shapes=[pltpu.VMEM(a.shape, a.dtype) for a in (*far_args[:4], w_qkv, w_o)]
        + [
            four, four, pltpu.VMEM((2, size, width), bf16),
            pltpu.VMEM((size, width), f32),
            pltpu.VMEM((size, width), f32),
            pltpu.VMEM((2 * QUAD, size, width), bf16),
            wide, wide, wide,
            pltpu.VMEM((2, 2 * QUAD, size, cut), bf16),
            pltpu.VMEM((2 * QUAD, size, 3 * narrow), bf16),
            pltpu.VMEM((width, 3 * narrow), bf16),
            pltpu.VMEM((narrow, width), bf16),
            pltpu.VMEM((narrow, width), f32),
            pltpu.VMEM((places // 2 * pieces, run_rows, 3 * narrow), bf16),
            pltpu.VMEM((places // 2, rows, width), bf16),
            pltpu.VMEM((2 * QUAD * rows, 3 * narrow), bf16),
            pltpu.VMEM((2 * QUAD, rows, 3 * narrow), bf16),
            pltpu.VMEM((8, 8, width), f32),
            pltpu.SemaphoreType.DMA((remote,)),
            pltpu.SemaphoreType.DMA((remote,)),
            pltpu.SemaphoreType.DMA((local,)),
            four_sems, four_sems,
            pltpu.SemaphoreType.DMA((2,)),
            pltpu.VMEM((run_rows, width), bf16),
            pltpu.SemaphoreType.DMA((1,)),
        ],
        compiler_params=pltpu.CompilerParams(
            collective_id=1, has_side_effects=True, vmem_limit_bytes=63 * 1024 * 1024
        ),
        name="back",
    )(*near_args, *far_args)


def mid_kernel(
    outer, inner, hidden_rows,
    go_ref, factor_ref,
    act_two, wg_ref, wu_ref, wd_ref, resid_ref,
    p_g, p_u, half_d, added, layer_out, dy, p_d, land_d, a_down, b_down, a_two, b_two,
    w_g, w_u, w_d, middle, cols, act_in, dy_in, act_cut, dy_cut, stage_d, dy_own,
    far_down, far_two, tmp_down, tmp_two, near_down, near_two, own_down, own_two, halves, stage,
    send_sems, recv_sems, local_sems, down_send, down_recv, two_send, two_recv, act_sems, dy_sem, cut_sems, out_sems, pd_send, pd_recv,
):
    size, width = go_ref.shape
    hidden = w_g.shape[1]
    ring = Ring(outer, inner, width // (outer * inner))
    mail = Mail(ring, send_sems, recv_sems, local_sems)
    ring.greet()
    flat = ring.flat
    strip = 32
    top_bit = ring.count // 2

    def strips(step):
        def run(i, carry):
            step(pl.ds(pl.multiple_of(i * strip, strip), strip))
            return carry

        lax.fori_loop(0, size // strip, run, 0)

    def dot(left, right, left_dim, right_dim):
        return lax.dot_general(
            left, right, (((left_dim,), (right_dim,)), ((), ())), preferred_element_type=f32
        )

    def settle(copy):
        copy.wait()
        mail.kept = [c for c in mail.kept if c is not copy]

    def pair_at(i):
        return i + (i // 2) * (5 - 2 * i)

    def pair_copies(source, target, sems, i):
        pair = pair_at(i)
        return [
            pltpu.make_async_copy(source.at[pair], target.at[pl.ds(0, size)], sems.at[0]),
            pltpu.make_async_copy(source.at[QUAD + pair], target.at[pl.ds(size, size)], sems.at[1]),
        ]

    def act_copies(i):
        return pair_copies(act_two, act_in.at[i % 2], act_sems.at[i % 2], i)

    for copy in act_copies(0):
        copy.start()
    loads = [mail.keep(wg_ref, w_g), mail.keep(wu_ref, w_u), mail.keep(wd_ref, w_d)]
    load_resid = mail.keep(resid_ref, own_down)

    def cotangent(part):
        dy_own[part, :] = (go_ref[part, :].astype(f32) * factor_ref[part, :]).astype(bf16)

    strips(cotangent)
    keep_dy = mail.keep(dy_own, dy.at[0])
    half = size // 2
    top, end = pl.ds(0, half), pl.ds(half, half)
    share = Share(mail, dy, dy_own)
    share.first()
    for copy in loads:
        settle(copy)
    settle(load_resid)
    settle(keep_dy)
    share.done((0,))

    def core_copy(kind, i):
        source, target, send, recv = (
            (far_down, tmp_down, down_send, down_recv),
            (far_two, tmp_two, two_send, two_recv),
        )[kind]
        return pltpu.make_async_remote_copy(
            src_ref=source,
            dst_ref=target.at[i % 2],
            send_sem=send.at[i],
            recv_sem=recv.at[i],
            device_id=ring.where(ring.bit_core),
            device_id_type=MESH,
        )

    base = mail.used
    mail.used += 9

    def late(n):
        src, dst, bit = (
            (dy.at[1, top], dy.at[3, top], ring.bit_b),
            (dy.at[2, end], dy.at[3, end], ring.bit_a),
            (dy.at[1], dy.at[QUAD + 1], ring.bit_core),
            (dy.at[2], dy.at[QUAD + 2], ring.bit_core),
            (dy.at[3], dy.at[QUAD + 3], ring.bit_core),
            (near_two.at[2, top], halves.at[1, 0], ring.bit_b),
            (near_two.at[2, end], halves.at[1, 1], ring.bit_a),
            (near_down.at[2, top], halves.at[0, 0], ring.bit_b),
            (near_down.at[2, end], halves.at[0, 1], ring.bit_a),
        )[n]
        return pltpu.make_async_remote_copy(
            src_ref=src,
            dst_ref=dst,
            send_sem=send_sems.at[base + n],
            recv_sem=recv_sems.at[base + n],
            device_id=ring.where(bit),
            device_id_type=MESH,
        )

    def join(kind, i):
        pair = pair_at(i)
        tmp, near, own = ((tmp_down, near_down, own_down), (tmp_two, near_two, own_two))[kind]
        core_copy(kind, i).wait_recv()
        tmp = tmp.at[i % 2]

        @pl.when(pair == 0)
        def _():
            add_near(own, own, tmp)

        @pl.when(pair > 0)
        def _():
            here = near.at[jnp.maximum(pair, 1) - 1]
            add_near(here, here, tmp)

    wide = min(512, width)
    piece = min(256, hidden)

    def give(kind, i, left, product, far, near, own):
        pair = pair_at(i)

        @pl.when(i >= 1)
        def _():
            join(kind, i - 1)
            core_copy(kind, i - 1).wait_send()

        @pl.when(i == 3)
        def _():
            late(7 - 2 * kind).start()
            late(8 - 2 * kind).start()

        for c in range(width // wide):
            part = slice(c * wide, (c + 1) * wide)
            whole = product(left, part)
            far[:, part] = whole[size:].astype(bf16)
            mine = whole[:size]

            @pl.when(pair == 0)
            def _():
                own[:, part] = mine + own[:, part] if kind == 0 else mine

            @pl.when(pair > 0)
            def _():
                near[jnp.maximum(pair, 1) - 1, :, part] = mine.astype(bf16)

        core_copy(kind, i).start()

    second = {}

    def pass_sums(kind):
        near, to_a, to_b = ((near_down, a_down, b_down), (near_two, a_two, b_two))[kind]
        join(kind, QUAD - 1)
        late(7 - 2 * kind).wait_recv()
        add_near(near.at[0, top], near.at[0, top], halves.at[kind, 0])
        second["a", kind] = mail.post(near.at[0], to_a, ring.bit_a)
        late(8 - 2 * kind).wait_recv()
        add_near(near.at[1, end], near.at[1, end], halves.at[kind, 1])
        second["b", kind] = mail.post(near.at[1], to_b, ring.bit_b)
        core_copy(kind, QUAD - 1).wait_send()

    def ahead(i, carry):
        pair = pair_at(i)

        @pl.when(i == 2)
        def _():
            share.from_a.wait_recv()
            late(0).start()
            late(2).start()
            share.from_b.wait_recv()
            late(1).start()
            late(3).start()

        @pl.when(i == 3)
        def _():
            late(0).wait_recv()
            late(1).wait_recv()
            late(4).start()

        for copy in act_copies(i):
            copy.wait()

        @pl.when(i + 1 < QUAD)
        def _():
            for copy in act_copies(i + 1):
                copy.start()

        act = act_in[i % 2]
        for c in range(hidden // piece):
            part = slice(c * piece, (c + 1) * piece)
            up_part = slice(hidden + c * piece, hidden + (c + 1) * piece)
            gate_pre = dot(act, w_g[:, part], 1, 0)
            up_proj = dot(act, w_u[:, part], 1, 0)
            ready = (gate_pre * jax.nn.sigmoid(gate_pre) * up_proj).astype(bf16)
            for rows, place in ((slice(0, size), pair), (slice(size, None), QUAD + pair)):
                middle[place, :, part] = ready[rows]
                cols[place, :, part] = gate_pre[rows].astype(bf16)
                cols[place, :, up_part] = up_proj[rows].astype(bf16)

        give(
            0, i,
            jnp.concatenate([middle[pair], middle[QUAD + pair]], axis=0),
            lambda left, part: dot(left, w_d[:, part], 1, 0),
            far_down, near_down, own_down,
        )
        return carry

    lax.fori_loop(0, QUAD, ahead, 0)
    pass_sums(0)
    for n in (2, 3, 4):
        late(n).wait_recv()

    cut = act_cut.shape[3]
    cuts = width // cut
    tokens = 2 * QUAD * size

    def cut_copy(source, target, i):
        start = pl.multiple_of(i * cut, cut)
        return pltpu.make_async_copy(
            source.at[:, :, pl.ds(start, cut)], target.at[i % 2], cut_sems.at[i % 2]
        )

    def down_out(i):
        start = pl.multiple_of(i * cut, cut)
        return pltpu.make_async_copy(
            stage_d.at[i % 2], p_d.at[:, pl.ds(start, cut)], out_sems.at[i % 2]
        )

    upper = flat // top_bit
    rows_half = hidden // 2
    away = pl.ds(pl.multiple_of((1 - upper) * rows_half, 16), rows_half)
    kept = pl.ds(pl.multiple_of(upper * rows_half, 16), rows_half)

    def down_send_at(i):
        part = pl.ds(pl.multiple_of(i * cut, cut), cut)
        return pltpu.make_async_remote_copy(
            src_ref=p_d.at[away, part],
            dst_ref=land_d.at[:, part],
            send_sem=pd_send.at[i],
            recv_sem=pd_recv.at[i],
            device_id=ring.where(top_bit),
            device_id_type=MESH,
        )

    cut_copy(dy, dy_cut, 0).start()

    def down_step(i, carry):
        cut_copy(dy, dy_cut, i).wait()

        @pl.when(i + 1 < cuts)
        def _():
            cut_copy(dy, dy_cut, i + 1).start()

        turned = dot(
            dy_cut[i % 2].reshape(tokens, cut), middle[...].reshape(tokens, hidden), 0, 0
        )

        stage_d[i % 2] = turned.T.astype(bf16)
        down_out(i).start()

        @pl.when(i >= 1)
        def _():
            down_out(i - 1).wait()
            down_send_at(i - 1).start()

        return carry

    lax.fori_loop(0, cuts, down_step, 0)
    cut_copy(act_two, act_cut, 0).start()
    down_out(cuts - 1).wait()
    down_send_at(cuts - 1).start()

    def behind(i, carry):
        pair = pair_at(i)
        dy_copies = pair_copies(dy, dy_in, dy_sem, i)
        for copy in dy_copies:
            copy.start()
        for copy in dy_copies:
            copy.wait()
        grads = dy_in[...]
        for c in range(hidden // piece):
            part = slice(c * piece, (c + 1) * piece)
            up_part = slice(hidden + c * piece, hidden + (c + 1) * piece)
            grad_middle = dot(grads, w_d[part, :], 1, 1)
            for rows, place in ((slice(0, size), pair), (slice(size, None), QUAD + pair)):
                gate_pre = cols[place, :, part].astype(f32)
                up_proj = cols[place, :, up_part].astype(f32)
                sigmoid_gate = jax.nn.sigmoid(gate_pre)
                swish = gate_pre * sigmoid_gate
                came = grad_middle[rows]
                cols[place, :, up_part] = (came * swish).astype(bf16)
                cols[place, :, part] = (
                    came * up_proj * sigmoid_gate * (1.0 + gate_pre * (1.0 - sigmoid_gate))
                ).astype(bf16)

        give(
            1, i,
            jnp.concatenate([cols[pair], cols[QUAD + pair]], axis=0),
            lambda left, part: dot(left[:, :hidden], w_g[part, :], 1, 1)
            + dot(left[:, hidden:], w_u[part, :], 1, 1),
            far_two, near_two, own_two,
        )
        return carry

    lax.fori_loop(0, QUAD, behind, 0)
    pass_sums(1)

    def stage_out(i):
        rows = pl.ds(pl.multiple_of(i * cut, cut), cut)
        return [
            pltpu.make_async_copy(
                stage.at[i % 2, :, pl.ds(j * hidden, hidden)],
                target.at[rows],
                out_sems.at[2 + 2 * j + i % 2],
            )
            for j, target in enumerate((p_g, p_u))
        ]

    def gate_step(i, carry):
        cut_copy(act_two, act_cut, i).wait()

        @pl.when(i + 1 < cuts)
        def _():
            cut_copy(act_two, act_cut, i + 1).start()

        @pl.when(i >= 2)
        def _():
            for copy in stage_out(i - 2):
                copy.wait()

        stage[i % 2] = dot(
            act_cut[i % 2].reshape(tokens, cut), cols[...].reshape(tokens, 2 * hidden), 0, 0
        ).astype(bf16)
        for copy in stage_out(i):
            copy.start()
        return carry

    lax.fori_loop(0, cuts, gate_step, 0)
    for i in (cuts - 2, cuts - 1):
        for copy in stage_out(i):
            copy.wait()

    for kind, own, in_a, in_b in ((1, own_two, a_two, b_two), (0, own_down, a_down, b_down)):
        second["a", kind].wait_recv()
        second["b", kind].wait_recv()
        first = mail.keep(in_a, tmp_down.at[0])
        other = mail.keep(in_b, tmp_two.at[0])
        settle(first)
        settle(other)

        def finish(part, own=own, kind=kind):
            total = own[part, :] + tmp_down[0, part, :].astype(f32) + tmp_two[0, part, :].astype(f32)
            if kind:
                own_two[part, :] = total
            else:
                far_down[part, :] = total.astype(bf16)

        strips(finish)
        if kind:
            mail.keep(own_two, added)
        else:
            mail.keep(far_down, layer_out)
    for i in range(cuts):
        down_send_at(i).wait()
    add_far(half_d, p_d.at[kept], land_d)
    for n in range(9):
        late(n).wait_send()
    mail.finish()


def mid(outer, inner, hidden_rows, grad_out, factor_rows, act_two, w_g, w_u, w_d, resid):
    size, width = grad_out.shape
    hidden = w_g.shape[1]
    vm = pl.BlockSpec(memory_space=pltpu.VMEM)
    hbm = pl.BlockSpec(memory_space=pl.ANY)
    sds = jax.ShapeDtypeStruct
    wide = sds((size, width), bf16)
    out_shape = (
        sds((width, hidden), bf16),
        sds((width, hidden), bf16),
        sds((hidden // 2, width), bf16),
        sds((size, width), f32),
        wide,
        sds((2 * QUAD, size, width), bf16),
        sds((hidden, width), bf16),
        sds((hidden // 2, width), bf16),
        wide, wide, wide, wide,
    )
    cut = min(256, width // 2)
    vw = pltpu.VMEM((size, width), bf16)
    dma = pltpu.SemaphoreType.DMA
    return pl.pallas_call(
        functools.partial(mid_kernel, outer, inner, hidden_rows),
        out_shape=out_shape,
        in_specs=[vm] * 2 + [hbm] * 5,
        out_specs=tuple([hbm] * len(out_shape)),
        scratch_shapes=[
            pltpu.VMEM((width, hidden), bf16),
            pltpu.VMEM((width, hidden), bf16),
            pltpu.VMEM((hidden, width), bf16),
            pltpu.VMEM((2 * QUAD, size, hidden), bf16),
            pltpu.VMEM((2 * QUAD, size, 2 * hidden), bf16),
            pltpu.VMEM((2, 2 * size, width), bf16),
            pltpu.VMEM((2 * size, width), bf16),
            pltpu.VMEM((2, 2 * QUAD, size, cut), bf16),
            pltpu.VMEM((2, 2 * QUAD, size, cut), bf16),
            pltpu.VMEM((2, hidden, cut), bf16),
            vw,
            vw, vw,
            pltpu.VMEM((2, size, width), bf16),
            pltpu.VMEM((2, size, width), bf16),
            pltpu.VMEM((QUAD - 1, size, width), bf16),
            pltpu.VMEM((QUAD - 1, size, width), bf16),
            pltpu.VMEM((size, width), f32),
            pltpu.VMEM((size, width), f32),
            pltpu.VMEM((2, 2, size // 2, width), bf16),
            pltpu.VMEM((2, cut, 2 * hidden), bf16),
            dma((32,)), dma((32,)), dma((16,)),
            dma((QUAD,)), dma((QUAD,)), dma((QUAD,)), dma((QUAD,)),
            dma((2, 2)), dma((2,)), dma((2,)), dma((6,)),
            dma((width // cut,)), dma((width // cut,)),
        ],
        compiler_params=pltpu.CompilerParams(
            collective_id=2, has_side_effects=True, vmem_limit_bytes=63 * 1024 * 1024
        ),
        name="mid",
    )(grad_out, factor_rows, act_two, w_g, w_u, w_d, resid)


def on_device(
    tokens,
    labels,
    counts,
    grad_out,
    w_query,
    w_key,
    w_value,
    w_out,
    gain_attn,
    gain_mlp,
    w_gate,
    w_up,
    w_down,
):
    batch_size, seq_len, width = tokens.shape
    outer_count = lax.axis_size("dp")
    inner_count = lax.axis_size("fsdp")
    rows = w_query.shape[0]
    hidden_rows = w_down.shape[0]
    flat = lax.axis_index("dp") * inner_count + lax.axis_index("fsdp")
    x_rows = tokens.reshape(-1, width)

    token_total = float(seq_len * batch_size * outer_count * inner_count)
    picked_counts = jnp.sum(
        jnp.where(labels[:, None] == jnp.arange(3)[None, :], counts[None, :], 0), axis=1
    ).astype(f32)
    factor = token_total / (3.0 * picked_counts)
    cosine, sine = rope_tables(seq_len, HEAD_DIM)
    head_count = width // (2 * QUAD) // HEAD_DIM
    sign = jnp.where(jnp.arange(HEAD_DIM) < HEAD_DIM // 2, -1.0, 1.0)
    wide_cosine = jnp.tile(cosine, (1, head_count))
    wide_sine = jnp.tile(sine * sign, (1, head_count))
    gain_rows = lax.dynamic_update_slice(
        jnp.zeros((8, width), f32),
        jnp.stack([gain_attn, gain_mlp]).astype(f32),
        (0, flat * rows),
    )
    factor_rows = jnp.repeat(factor, seq_len)[:, None]
    (
        act_one, w_qkv, w_o, q_rot, k_rot, values, attended, resid, gains, act_two, w_g, w_u, w_d,
    ) = front(
        outer_count, inner_count, seq_len,
        x_rows, gain_rows,
        w_query, w_key, w_value,
        wide_cosine, wide_sine,
        w_out, w_gate, w_up, w_down,
    )
    p_g, p_u, half_d, added, layer_out = mid(
        outer_count, inner_count, w_down.shape[0], grad_out.reshape(-1, width), factor_rows,
        act_two, w_g, w_u, w_d, resid,
    )[:5]
    layer_out = layer_out.reshape(tokens.shape)
    results = back(
        outer_count, inner_count, seq_len,
        (
            x_rows, grad_out.reshape(-1, width), factor_rows, gains, wide_cosine, wide_sine,
        ),
        (q_rot, k_rot, values, attended, w_qkv, w_o, p_g, p_u, half_d, act_one, resid, added),
    )
    query_grad, key_grad, value_grad, out_grad, gain_grads = results[:5]
    gate_grad, up_grad, down_grad = (a.astype(f32) for a in results[5:8])
    grad_tokens = results[-1]
    gain_grads = lax.dynamic_slice(gain_grads, (0, flat * rows), (2, rows))
    return (
        layer_out,
        grad_tokens.reshape(tokens.shape),
        query_grad,
        key_grad,
        value_grad,
        out_grad,
        gain_grads[0],
        gain_grads[1],
        gate_grad,
        up_grad,
        down_grad,
    )


def solution(mesh):
    rows = P(AXES, None)
    vector = P(AXES)
    three = P(AXES, None, None)
    in_specs = (three, vector, P(), three, rows, rows, rows, rows, vector, vector, rows, rows, rows)
    out_specs = (three, three, rows, rows, rows, rows, vector, vector, rows, rows, rows)
    return jax.shard_map(
        on_device, mesh=mesh, in_specs=in_specs, out_specs=out_specs, check_vma=False
    )
```
